32 devices in a mesh: dp: 8 (over y, x, core), tensor: 4 (over z).
Axes of the slice: x: 2, y: 2, z: 4, core: 2. Of those that a mesh axis runs over, the one named last changes fastest.
Arguments:
- tokens: bfloat16 [8192, 2048], P(('dp', 'tensor')), may hold values from -6 to 6
- cotangent: bfloat16 [8192, 2048], P(('dp', 'tensor')), may hold values from -6 to 6
- seg_ids: int32 [8, 1024], P('dp'), may hold values from 0 to 15, never falling along the last dimension, each value on 1 to 512 neighbouring positions
- keep_mask: int32 [8, 1024], P('dp'), may hold values from 0 to 1, as said below
- routes: int32 [8192, 8], P('dp'), may hold values from 0 to 15, all different within a row; in each aligned block of 1024 rows (0 to 1023, 1024 to 2047, ...) at most 768 rows name the same one
- attn_gain: float32 [2048], replicated, may hold values from 0.1 to 1.9
- w_query: bfloat16 [2048, 2048], P(None, 'tensor'), may hold values from -0.125 to 0.125
- w_key: bfloat16 [2048, 2048], P(None, 'tensor'), may hold values from -0.125 to 0.125
- w_value: bfloat16 [2048, 2048], P(None, 'tensor'), may hold values from -0.125 to 0.125
- w_out: bfloat16 [2048, 2048], P(None, 'tensor'), may hold values from -0.5 to 0.5
- q_gain: float32 [2048], P('tensor'), may hold values from 0.1 to 1.9
- k_gain: float32 [2048], P('tensor'), may hold values from 0.1 to 1.9
- ffn_gain: float32 [2048], replicated, may hold values from 0.1 to 1.9
- router: bfloat16 [2048, 16], replicated, may hold values from -0.06591797 to 0.06591797
- w_gate: bfloat16 [16, 2048, 1024], P(None, None, 'tensor'), may hold values from -0.125 to 0.125
- w_up: bfloat16 [16, 2048, 1024], P(None, None, 'tensor'), may hold values from -0.125 to 0.125
- w_down: bfloat16 [16, 2048, 1024], P(None, None, 'tensor'), may hold values from -1.5 to 1.5
Outputs:
- layer_out: bfloat16 [8192, 2048], P(('dp', 'tensor'))
- tokens_grad: float32 [8192, 2048], P(('dp', 'tensor'))
- w_query_grad: float32 [2048, 2048], P('dp', 'tensor')
- w_key_grad: float32 [2048, 2048], P('dp', 'tensor')
- w_value_grad: float32 [2048, 2048], P('dp', 'tensor')
- w_out_grad: float32 [2048, 2048], P('dp', 'tensor')
- attn_gain_grad: float32 [2048], replicated
- q_gain_grad: float32 [2048], replicated
- k_gain_grad: float32 [2048], replicated
- ffn_gain_grad: float32 [2048], replicated
- router_grad: float32 [2048, 16], replicated
- w_gate_grad: float32 [16, 2048, 1024], P('dp', None, 'tensor')
- w_up_grad: float32 [16, 2048, 1024], P('dp', None, 'tensor')
- w_down_grad: float32 [16, 2048, 1024], P('dp', None, 'tensor')
The draws below stay inside these ranges and needn't reach their ends.
Inputs may be any that keep to these rules, and one draw needn't show every extreme that they name: `seg_ids`: numbers never fall along a sequence; a run of equal numbers is one document of at most 512 positions. `keep_mask`: the zeros of a sequence, if any, form its tail. `routes`: each row names 8 different experts; within the rows of one index of dp (aligned blocks of 1024 rows) no expert is named by more than 768 rows.
All inputs are finite; a program needn't handle non-finite values.
Results may differ from the reference program's by a relative error of at most 0.015.
Values may be sent and summed in bfloat16 or wider, within the bound.
No kernel may reach another device: no remote copies, remote signals or barrier semaphores. Data moves between devices by JAX's collectives and lax.ppermute only.
A program may use at most 448 MiB of HBM per device.

```python
import math
import jax
import jax.numpy as jnp
import numpy as np
from jax import lax

D = 2048
HEADS = 16
HEAD = 128
FF = 1024
TOPK = 8
EXPERTS = 16
LEN = 1024
SEQS = 1
TOK_GROUP = 1024
CAP = 768
TOKENS = 8192
NSEQ = 8
SEG_COUNT = 16
SEG_MOST = 512
N_DP = 8


def draw_keep_mask(key, part):
    key = jax.random.fold_in(key, 11)
    tails = jax.random.randint(key, (NSEQ, 1), 0, LEN // 4 + 1)
    places = jnp.arange(LEN, dtype=jnp.int32)[None, :]
    return (places < LEN - tails).astype(jnp.int32)


def strengthened(values, own_key, source, target, shards_of, factor):
    def block_of(dim):
        return (jnp.arange(values.shape[dim]) // (values.shape[dim] // shards_of)).reshape((-1,) + (1,) * (values.ndim - 1 - dim))

    one_side = jax.random.permutation(own_key, shards_of)[block_of(target)]
    far = (block_of(target) + shards_of // 2) % shards_of
    return jnp.where((block_of(source) == one_side) | (block_of(source) == far), factor * values, values)


def steps_of(rng, extent, cuts, least, top_value):
    factor_of = 1.0
    for axis_at, blocks in cuts:
        draws = jax.random.uniform(jax.random.fold_in(jax.random.fold_in(rng, 6), axis_at), (blocks,), jnp.float32, least / len(cuts), top_value / len(cuts))
        factor_of = factor_of * jnp.repeat(jnp.exp(draws), extent[axis_at] // blocks).reshape((-1,) + (1,) * (len(extent) - 1 - axis_at))
    return factor_of


def split_up(amount, total, reach, slope):
    portions = [(1 << 20) // math.isqrt(rank ** slope) + 1 for rank in range(2, amount + 1)]
    surplus, given = total - reach - (amount - 1), [1] * (amount - 1)
    while surplus > 0:
        movable = [i for i in range(amount - 1) if given[i] < reach]
        pool, remaining = sum([portions[i] for i in movable]), surplus
        for i in movable:
            more = min(reach - given[i], max(1, remaining * portions[i] // pool), surplus)
            given[i] = given[i] + more
            surplus = surplus - more
    return np.array([reach] + given)


def uneven_parts(stream_key, count, total, most, skew):
    if count == 2:
        one = jax.random.randint(stream_key, (), max(1, total - most), min(most, total - 1) + 1)
        return jnp.stack([one, total - one])
    sizes = jnp.asarray(split_up(count, total, most, skew), jnp.int32)
    pairs = (count - 1) // 2
    donor, sink = sizes[1:1 + 2 * pairs:2], sizes[2:2 + 2 * pairs:2]
    slack = jnp.minimum(donor - 1, most - sink)
    shifted = jax.random.randint(jax.random.fold_in(stream_key, 1), (pairs,), 0, 1 << 20) % (slack + 1)
    sizes = sizes.at[1:1 + 2 * pairs:2].set(donor - shifted).at[2:2 + 2 * pairs:2].set(sink + shifted)
    return sizes[jax.random.permutation(jax.random.fold_in(stream_key, 2), count)]


def deal_out(key, own, number, rows, amount, top, most, skew):
    sequence = jax.random.permutation(key, amount)
    heavy_load, usual = portions_of(amount, rows * top, most, skew, True), portions_of(amount, rows * top, most, skew, False)
    places = jnp.arange(amount)

    def named(tallies, turn):
        used = int((tallies > 0).sum())
        fixed = max(1, used // 4)
        passed = fixed + (places - fixed + turn * (used - fixed)) % max(1, amount - fixed)
        return jnp.zeros((amount,), jnp.int32).at[sequence[jnp.where(places < fixed, places, passed)]].set(jnp.asarray(tallies, jnp.int32))

    tallies = jnp.where(number % 4 == 0, named(heavy_load, number // 4), named(usual, number - number // 4 - 1))
    mixed = jax.random.permutation(jax.random.fold_in(own, 3), amount)
    source_of, taker = mixed[0:amount // 2 * 2:2], mixed[1:amount // 2 * 2:2]
    slack = jnp.minimum(tallies[source_of] - 1, most - tallies[taker]) // 2
    slack = jnp.where((source_of == sequence[0]) | (taker == sequence[0]) | (tallies[taker] == 0), 0, jnp.maximum(slack, 0))
    passed = jax.random.randint(jax.random.fold_in(own, 4), (amount // 2,), 0, 1 << 20) % (slack + 1)
    tallies = tallies.at[source_of].add(-passed).at[taker].add(passed)
    labels = jnp.searchsorted(jnp.cumsum(tallies), jnp.arange(rows * top), side="right").astype(jnp.int32)
    listing = labels.reshape(top, rows).T
    listing = listing[jax.random.permutation(jax.random.fold_in(own, 1), rows)]
    turn = jax.random.randint(jax.random.fold_in(own, 2), (rows, 1), 0, top)
    return jnp.take_along_axis(listing, (jnp.arange(top)[None, :] + turn) % top, axis=1)


def portions_of(amount, total, reach, slope, full):
    portions = [(1 << 20) // math.isqrt(grade ** slope) + 1 for grade in range(1, amount + 1)]
    largest = reach if full else min(reach, max(-(-total // amount), total * portions[0] // sum(portions)))
    least = 1 if total - largest >= amount - 1 else 0
    given, spare = [largest] + [least] * (amount - 1), total - largest - least * (amount - 1)
    while spare > 0:
        candidates = [i for i in range(1, amount) if given[i] < largest] or [i for i in range(1, amount) if given[i] < reach]
        whole, budget = sum([portions[i] for i in candidates]), spare
        for i in candidates:
            extra = min(reach - given[i], max(1, budget * portions[i] // whole), spare)
            given[i] = given[i] + extra
            spare = spare - extra
    return np.array(given)


def gaussian(rng, dims, scale, most, cuts=(), held_as=jnp.bfloat16):
    values = jax.random.normal(rng, dims, jnp.float32) * scale
    if len(cuts) > 0:
        values = steps_of(rng, dims, cuts, -0.22, 0.18) * values
    return jnp.clip(values, min=-most, max=most).astype(held_as)


def bell_draw_with(own_key, shape, scale, bound, shards, heavy, kind=jnp.bfloat16):
    array = scale * jax.random.normal(own_key, shape, jnp.float32)
    if shards:
        array = array * steps_of(own_key, shape, shards, -0.22, 0.18)
    return jnp.clip(strengthened(array, jax.random.fold_in(own_key, 3), *heavy), -bound, bound).astype(kind)


def setup_inputs(seed: int = 0) -> dict:
    splits = jax.random.split(jax.random.key(seed), 18)
    tokens = bell_draw_with(splits[0], (TOKENS, D), 1.0, 6.0, ((0, 32),), (0, 1, 32, 2.75))
    cotangent = gaussian(splits[1], (TOKENS, D), 1.0, 6.0, ((0, 32),))
    seg_ids = jax.vmap(lambda own: jnp.searchsorted(jnp.cumsum(uneven_parts(own, SEG_COUNT, LEN, SEG_MOST, 2)), jnp.arange(LEN), side="right"))(jax.random.split(splits[2], NSEQ)).reshape((NSEQ, LEN)).astype(jnp.int32)
    keep_mask = draw_keep_mask(jax.random.fold_in(splits[17], 71), 0)
    routes_keys = jax.random.split(jax.random.fold_in(splits[4], 1), TOKENS // TOK_GROUP)
    routes_turns = jax.random.permutation(jax.random.fold_in(splits[4], 3), TOKENS // TOK_GROUP)
    routes = jax.vmap(lambda own, number: deal_out(jax.random.fold_in(splits[4], 2), own, number, TOK_GROUP, EXPERTS, TOPK, CAP, 1))(routes_keys, routes_turns).reshape((TOKENS, TOPK))
    attn_gain = jnp.clip(1.0 + 0.18 * jax.random.normal(splits[5], (D,), jnp.float32), 0.1, 1.9)
    w_query = gaussian(splits[6], (D, D), D ** -0.5, 0.125, ((1, 4),))
    w_key = gaussian(splits[7], (D, D), D ** -0.5, 0.125, ((1, 4),))
    w_value = gaussian(splits[8], (D, D), D ** -0.5, 0.125, ((1, 4),))
    w_out = gaussian(splits[9], (D, D), (D // 16) ** -0.5, 0.5, ((1, 4),))
    q_gain = jnp.clip(1.0 + 0.18 * jax.random.normal(splits[10], (D,), jnp.float32), 0.1, 1.9)
    k_gain = jnp.clip(1.0 + 0.18 * jax.random.normal(splits[11], (D,), jnp.float32), 0.1, 1.9)
    ffn_gain = jnp.clip(1.0 + 0.18 * jax.random.normal(splits[12], (D,), jnp.float32), 0.1, 1.9)
    router = gaussian(splits[13], (D, EXPERTS), (0.5 / D ** 0.5), 0.06591797)
    w_gate = gaussian(splits[14], (EXPERTS, D, FF), D ** -0.5, 0.125, ((2, 4),))
    w_up = gaussian(splits[15], (EXPERTS, D, FF), D ** -0.5, 0.125, ((2, 4),))
    w_down = gaussian(splits[16], (EXPERTS, D, FF), (FF // 64) ** -0.5, 1.5, ((2, 4),))
    return dict(tokens=tokens, cotangent=cotangent, seg_ids=seg_ids, keep_mask=keep_mask, routes=routes, attn_gain=attn_gain, w_query=w_query, w_key=w_key, w_value=w_value, w_out=w_out, q_gain=q_gain, k_gain=k_gain, ffn_gain=ffn_gain, router=router, w_gate=w_gate, w_up=w_up, w_down=w_down)


@jax.custom_vjp
def low(v):
    return lax.optimization_barrier(v.astype(jnp.bfloat16)).astype(jnp.float32)

@jax.custom_vjp
def low_back(v):
    return v

def low_keep(v):
    return (low(v), None)

def low_pass(kept, grad):
    return (grad,)

def back_keep(v):
    return (v, None)

def back_low(kept, grad):
    return (low(grad),)
low.defvjp(low_keep, low_pass)
low_back.defvjp(back_keep, back_low)
EPSILON = 1e-05
HIGHEST = lax.Precision.HIGHEST

def matmul(left, right):
    return jnp.dot(left, right, precision=HIGHEST)

def rms_scale(values):
    return lax.rsqrt(lax.optimization_barrier(jnp.mean(values * values, axis=-1, keepdims=True)) + EPSILON)

def rope_tables():
    half_width = HEAD // 2
    frequency = jnp.power(10000.0, -jnp.arange(half_width, dtype=jnp.float32) * 2.0 / HEAD)
    angles = jnp.arange(LEN, dtype=jnp.float32)[:, None] * frequency[None, :]
    cosine = jnp.concatenate([jnp.cos(angles), jnp.cos(angles)], axis=1)
    sinus_table = jnp.concatenate([jnp.sin(angles), jnp.sin(angles)], axis=1)
    return (cosine[:, None, :], sinus_table[:, None, :])

def rotate(values, cosine, sinus_table):
    half_width = values.shape[-1] // 2
    turned = jnp.concatenate([-values[..., half_width:], values[..., :half_width]], axis=-1)
    return values * cosine + turned * sinus_table

def mask_table(seg_rows, keep_rows):
    places = jnp.arange(LEN)
    causal = places[None, :] <= places[:, None]
    itself = places[None, :] == places[:, None]
    same_doc = seg_rows[:, :, None] == seg_rows[:, None, :]
    live = (keep_rows[:, None, :] == 1) | itself[None]
    return same_doc & causal[None] & live

def attend_head(query_head, key_head, value_head, allowed):
    scores = low_back(jnp.einsum('sqd,skd->sqk', query_head, key_head, precision=HIGHEST) * HEAD ** (-0.5))
    scores = jnp.where(allowed, scores, -1e+30)
    weights = jax.nn.softmax(scores, axis=-1)
    return jnp.einsum('sqk,skd->sqd', low(weights), value_head, precision=HIGHEST)

def block_forward(x_rows, params, seg_rows, keep_rows, route_rows):
    w_query, w_key, w_value, w_out, attn_gain, q_gain, k_gain, ffn_gain, router, w_gate, w_up, w_down = params
    normed = low(x_rows * rms_scale(x_rows) * attn_gain)
    query_raw = low_back(matmul(normed, w_query))
    key_raw = low_back(matmul(normed, w_key))
    value_low = low(low_back(matmul(normed, w_value)))
    query_normed = query_raw * rms_scale(query_raw) * q_gain
    key_normed = key_raw * rms_scale(key_raw) * k_gain
    cosine, sinus_table = rope_tables()
    shape_four = (SEQS, LEN, HEADS, HEAD)
    query_low = low(rotate(query_normed.reshape(shape_four), cosine, sinus_table))
    key_low = low(rotate(key_normed.reshape(shape_four), cosine, sinus_table))
    value_heads = value_low.reshape(shape_four)
    allowed = mask_table(seg_rows, keep_rows)
    head_function = jax.checkpoint(attend_head)

    def one_head(operands):
        return head_function(operands[0], operands[1], operands[2], allowed)
    heads_out = lax.map(one_head, (jnp.transpose(query_low, (2, 0, 1, 3)), jnp.transpose(key_low, (2, 0, 1, 3)), jnp.transpose(value_heads, (2, 0, 1, 3))))
    attended = low(low_back(jnp.transpose(heads_out, (1, 2, 0, 3)).reshape(TOK_GROUP, D)))
    middle = x_rows + low_back(matmul(attended, w_out.T))
    ffn_in = low(middle * rms_scale(middle) * ffn_gain)
    logits = low_back(matmul(ffn_in, router))
    expert_probs = jax.nn.softmax(logits, axis=-1)
    routed = lax.optimization_barrier(jnp.sum((route_rows[:, :, None] == jnp.arange(EXPERTS)[None, None, :]).astype(jnp.float32), axis=1))
    combine = expert_probs * routed

    def expert_step(running, operands):
        gate_w, up_w, down_w, column = operands
        pre_gate = low_back(matmul(ffn_in, gate_w))
        pre_up = low_back(matmul(ffn_in, up_w))
        inner_act = low(jax.nn.silu(pre_gate) * pre_up)
        result = low_back(matmul(inner_act, down_w.T))
        return (running + column[:, None] * result, None)
    expert_total, unused = lax.scan(jax.checkpoint(expert_step), jnp.zeros((TOK_GROUP, D), jnp.float32), (w_gate, w_up, w_down, combine.T))
    return middle + low_back(expert_total)

def reference(tokens, cotangent, seg_ids, keep_mask, routes, attn_gain, w_query, w_key, w_value, w_out, q_gain, k_gain, ffn_gain, router, w_gate, w_up, w_down):
    params = (w_query.astype(jnp.float32), w_key.astype(jnp.float32), w_value.astype(jnp.float32), w_out.astype(jnp.float32), attn_gain, q_gain, k_gain, ffn_gain, router.astype(jnp.float32), w_gate.astype(jnp.float32), w_up.astype(jnp.float32), w_down.astype(jnp.float32))
    operands = (tokens.astype(jnp.float32).reshape(N_DP, TOK_GROUP, D), cotangent.astype(jnp.float32).reshape(N_DP, TOK_GROUP, D), seg_ids.reshape(N_DP, SEQS, LEN), keep_mask.reshape(N_DP, SEQS, LEN), routes.reshape(N_DP, TOK_GROUP, TOPK))

    def group_step(totals, pieces):
        x_rows, grad_rows, seg_rows, keep_rows, route_rows = pieces

        def forward(x_in, weights):
            return block_forward(x_in, weights, seg_rows, keep_rows, route_rows)
        layer_value, pullback = jax.vjp(forward, x_rows, params)
        x_grad, weight_grads = pullback(grad_rows)
        totals = tuple((left + right for left, right in zip(totals, weight_grads)))
        return (totals, (layer_value.astype(jnp.bfloat16), x_grad))
    start_sums = tuple((jnp.zeros_like(member) for member in params))
    totals, (outs_all, grads_all) = lax.scan(group_step, start_sums, operands)
    return (outs_all.reshape(TOKENS, D), grads_all.reshape(TOKENS, D), totals[0], totals[1], totals[2], totals[3], totals[4], totals[5], totals[6], totals[7], totals[8], totals[9], totals[10], totals[11])
```

```python
import functools

import jax
import jax.numpy as jnp
from jax import lax
from jax.experimental import pallas as pl
from jax.experimental.pallas import tpu as pltpu
from jax.sharding import PartitionSpec as P

D = 2048
HEAD = 128
DOC = 512
LANES = 128
EPSILON = 1e-05
MASKED = -1e30
CHUNKS = 2
VMEM = 56 * 1024 * 1024
bf16 = jnp.bfloat16
f32 = jnp.float32


def nn(left, right):
    return lax.dot_general(left, right, (((1,), (0,)), ((), ())), preferred_element_type=f32)


def nt(left, right):
    return lax.dot_general(left, right, (((1,), (1,)), ((), ())), preferred_element_type=f32)


def tn(left, right):
    return lax.dot_general(left, right, (((0,), (0,)), ((), ())), preferred_element_type=f32)


def params():
    return pltpu.CompilerParams(vmem_limit_bytes=VMEM)


def cost(flops, moved, special=0):
    return pl.CostEstimate(flops=flops, bytes_accessed=moved, transcendentals=special)


def rms_scale(values):
    return lax.rsqrt(jnp.mean(values * values, axis=-1, keepdims=True) + EPSILON)


def norm_back(grad_values, values, scale_col, gain_vec):
    weighted = grad_values * gain_vec
    inner_mean = jnp.mean(weighted * values, axis=-1, keepdims=True)
    return scale_col * weighted - values * (scale_col * scale_col * scale_col) * inner_mean


def rope_tables(length, width):
    half_width = width // 2
    frequency = jnp.power(10000.0, -jnp.arange(half_width, dtype=f32) * 2.0 / width)
    angles = jnp.arange(length, dtype=f32)[:, None] * frequency[None, :]
    cosine, sine = jnp.cos(angles), jnp.sin(angles)
    return jnp.concatenate([cosine, cosine], axis=1), jnp.concatenate([-sine, sine], axis=1)


def key_start(query_start):
    return max(0, query_start - DOC)


def fill_bias(bias, seg_col, seg_row, keep_row, block):
    length = seg_col.shape[0]
    for start in range(0, length, block):
        first, stop = key_start(start), start + block
        query_pos = start + lax.broadcasted_iota(jnp.int32, (block, stop - first), 0)
        key_pos = first + lax.broadcasted_iota(jnp.int32, (block, stop - first), 1)
        same = seg_col[start:stop, :] == seg_row[:, first:stop]
        live = (keep_row[:, first:stop] == 1) | (key_pos == query_pos)
        allowed = same & live & (key_pos <= query_pos)
        bias[start:stop, : stop - first] = jnp.where(allowed, 0.0, MASKED)


def turned(values):
    return pltpu.roll(values, values.shape[1] // 2, 1)


def attend_kernel(
    block, qraw, kraw, value, q_scale, k_scale, q_gain, k_gain, cosine, sine,
    seg_col, seg_row, keep_row, q_out, k_out, o_out, lse_out, bias,
):
    @pl.when(pl.program_id(0) == 0)
    def _():
        fill_bias(bias, seg_col, seg_row, keep_row, block)

    def rotated(raw, scale, gain):
        normed = raw[...] * scale[...] * gain[...]
        return (normed * cosine[...] + turned(normed) * sine[...]).astype(bf16)

    q_out[...] = rotated(qraw, q_scale, q_gain)
    k_out[...] = rotated(kraw, k_scale, k_gain)
    length = seg_col.shape[0]
    for start in range(0, length, block):
        first, stop = key_start(start), start + block
        scores = nt(q_out[start:stop, :], k_out[first:stop, :]) * HEAD ** (-0.5)
        scores = scores + bias[start:stop, : stop - first]
        top = jnp.max(scores, axis=1, keepdims=True)
        powers = jnp.exp(scores - top)
        total = jnp.sum(powers, axis=1, keepdims=True)
        weights = (powers * (1.0 / total)).astype(bf16)
        o_out[start:stop, :] = nn(weights, value[first:stop, :]).astype(bf16)
        lse_out[start:stop, :] = jnp.broadcast_to(top + jnp.log(total), (block, HEAD))


def attend(qraw, kraw, value, q_scale, k_scale, q_gain, k_gain, cosine, sine, seg, keep):
    length, width = qraw.shape
    block = min(256, length)
    span = min(DOC + block, length)
    head = pl.BlockSpec((length, HEAD), lambda h: (0, h))
    gain = pl.BlockSpec((1, HEAD), lambda h: (0, h))
    whole = lambda *shape: pl.BlockSpec(shape, lambda h: (0, 0))
    return pl.pallas_call(
        functools.partial(attend_kernel, block),
        grid=(width // HEAD,),
        in_specs=[head, head, head, whole(length, 1), whole(length, 1), gain, gain]
        + [whole(length, HEAD), whole(length, HEAD), whole(length, 1), whole(1, length), whole(1, length)],
        out_specs=[head, head, head, head],
        out_shape=[jax.ShapeDtypeStruct((length, width), t) for t in (bf16, bf16, bf16, f32)],
        scratch_shapes=[pltpu.VMEM((length, span), f32)],
        compiler_params=params(),
        cost_estimate=cost(4 * length * span * width, 18 * length * width, length * span * width // HEAD),
        name="attend",
    )(qraw, kraw, value, q_scale, k_scale, q_gain[None], k_gain[None], cosine, sine, seg[:, None], seg[None], keep[None])


def attend_back_kernel(
    block, query, key, value, out_grad, lse, qraw, kraw, q_scale, k_scale, q_gain, k_gain, cosine, sine,
    seg_col, seg_row, keep_row, dq_out, dk_out, dv_out, qdot_out, kdot_out, qg_out, kg_out, bias, dk_sum, dv_sum,
):
    at = pl.program_id(0)

    @pl.when(at == 0)
    def _():
        fill_bias(bias, seg_col, seg_row, keep_row, block)
        qdot_out[...] = jnp.zeros_like(qdot_out)
        kdot_out[...] = jnp.zeros_like(kdot_out)

    dk_sum[...] = jnp.zeros_like(dk_sum)
    dv_sum[...] = jnp.zeros_like(dv_sum)
    length = seg_col.shape[0]
    scale = HEAD ** (-0.5)
    for start in range(0, length, block):
        first, stop = key_start(start), start + block
        rows, keys = slice(start, stop), slice(first, stop)
        scores = nt(query[rows, :], key[keys, :]) * scale + bias[rows, : stop - first]
        weights = jnp.exp(scores - lse[rows, :1])
        prob_grad = nt(out_grad[rows, :], value[keys, :])
        inner = jnp.sum(weights * prob_grad, axis=1, keepdims=True)
        score_grad = (weights * (prob_grad - inner)).astype(bf16)
        dq_out[rows, :] = nn(score_grad, key[keys, :]) * scale
        dk_sum[keys, :] += tn(score_grad, query[rows, :])
        dv_sum[keys, :] += tn(weights.astype(bf16), out_grad[rows, :])

    def unrotated(grad):
        return grad * cosine[...] + turned(grad * sine[...])

    dv_out[...] = dv_sum[...].astype(bf16)
    dq = unrotated(dq_out[...])
    dk = unrotated(dk_sum[...] * scale)
    dq_out[...] = dq
    dk_out[...] = dk
    dq = dq * qraw[...]
    dk = dk * kraw[...]
    qg_out[...] = jnp.sum(dq * q_scale[...], axis=0, keepdims=True)
    kg_out[...] = jnp.sum(dk * k_scale[...], axis=0, keepdims=True)
    qdot_out[...] += jnp.sum(dq * q_gain[...], axis=1, keepdims=True)
    kdot_out[...] += jnp.sum(dk * k_gain[...], axis=1, keepdims=True)


def attend_back(query, key, value, out_grad, lse, qraw, kraw, q_scale, k_scale, q_gain, k_gain, cosine, sine, seg, keep):
    length, width = qraw.shape
    block = min(256, length)
    span = min(DOC + block, length)
    head = pl.BlockSpec((length, HEAD), lambda h: (0, h))
    gain = pl.BlockSpec((1, HEAD), lambda h: (0, h))
    whole = lambda *shape: pl.BlockSpec(shape, lambda h: (0, 0))
    sds = jax.ShapeDtypeStruct
    return pl.pallas_call(
        functools.partial(attend_back_kernel, block),
        grid=(width // HEAD,),
        in_specs=[head] * 7
        + [whole(length, 1), whole(length, 1), gain, gain]
        + [whole(length, HEAD), whole(length, HEAD), whole(length, 1), whole(1, length), whole(1, length)],
        out_specs=[head, head, head, whole(length, 1), whole(length, 1), gain, gain],
        out_shape=[sds((length, width), f32), sds((length, width), f32), sds((length, width), bf16)]
        + [sds((length, 1), f32), sds((length, 1), f32), sds((1, width), f32), sds((1, width), f32)],
        scratch_shapes=[pltpu.VMEM((length, span), f32), pltpu.VMEM((length, HEAD), f32), pltpu.VMEM((length, HEAD), f32)],
        compiler_params=params(),
        cost_estimate=cost(10 * length * span * width, 32 * length * width, length * span * width // HEAD),
        name="attend_back",
    )(query, key, value, out_grad, lse, qraw, kraw, q_scale, k_scale, q_gain[None], k_gain[None], cosine, sine, seg[:, None], seg[None], keep[None])


def up_back_kernel(grad, down_w, out):
    width = down_w.shape[2]
    for at in range(down_w.shape[0]):
        out[:, at * width : (at + 1) * width] = nn(grad[...], down_w[at]).astype(out.dtype)


def up_back(grad, down_w):
    rows, features = grad.shape
    experts, _, width = down_w.shape
    step = 2 if experts % 2 == 0 else 1
    return pl.pallas_call(
        up_back_kernel,
        grid=(experts // step,),
        in_specs=[pl.BlockSpec((rows, features), lambda e: (0, 0)), pl.BlockSpec((step, features, width), lambda e: (e, 0, 0))],
        out_specs=pl.BlockSpec((rows, step * width), lambda e: (0, e)),
        out_shape=jax.ShapeDtypeStruct((rows, experts * width), bf16),
        compiler_params=params(),
        cost_estimate=cost(2 * rows * features * experts * width, 2 * (rows + experts * width) * features),
        name="up_back",
    )(grad, down_w)


def expert_kernel(block, rows_in, back, routed, router, gate_w, up_w, act_out, dgate_out, dup_out, grad_out, comb, dcomb, total):
    at = pl.program_id(0)
    rows, features = rows_in.shape
    lane = lax.broadcasted_iota(jnp.int32, (block, LANES), 1)

    @pl.when(at == 0)
    def _():
        experts = pl.num_programs(0)
        for start in range(0, rows, block):
            here = slice(start, start + block)
            logits = jnp.where(lane < experts, nn(rows_in[here, :], router[...]), MASKED)
            powers = jnp.exp(logits - jnp.max(logits, axis=1, keepdims=True))
            probs = powers / jnp.sum(powers, axis=1, keepdims=True)
            comb[here, :] = probs * routed[here, :]
        total[...] = jnp.zeros_like(total)
        dcomb[...] = jnp.zeros_like(dcomb)

    gate, up = gate_w[0], up_w[0]
    mine = lane == at
    for start in range(0, rows, block):
        here = slice(start, start + block)
        taken = rows_in[here, :]
        pre_gate = nn(taken, gate)
        pre_up = nn(taken, up)
        behind = back[here, :].astype(f32)
        share = jnp.sum(jnp.where(mine, comb[here, :], 0.0), axis=1, keepdims=True)
        sigmoid = 0.5 * jnp.tanh(0.5 * pre_gate) + 0.5
        active = pre_gate * sigmoid
        inner = active * pre_up
        share_grad = jnp.sum(inner * behind, axis=1, keepdims=True)
        dcomb[here, :] = jnp.where(mine, share_grad, dcomb[here, :])
        act_out[here, :] = (inner * share).astype(bf16)
        inner_grad = behind * share
        dgate = (inner_grad * pre_up * (sigmoid + active * (1.0 - sigmoid))).astype(bf16)
        dup = (inner_grad * active).astype(bf16)
        dgate_out[here, :] = dgate
        dup_out[here, :] = dup
        total[here, :] += nt(dgate, gate) + nt(dup, up)

    @pl.when(at == pl.num_programs(0) - 1)
    def _():
        grad_out[:, :features] = total[...].astype(bf16)
        grad_out[:, features:] = dcomb[...].astype(bf16)


def experts_block(rows_in, back, routed, router, gate_w, up_w):
    rows, features = rows_in.shape
    experts, _, width = gate_w.shape
    block = min(512, rows)
    whole = lambda *shape: pl.BlockSpec(shape, lambda e: (0, 0))
    column = pl.BlockSpec((rows, width), lambda e: (0, e))
    weight = pl.BlockSpec((1, features, width), lambda e: (e, 0, 0))
    wide = jax.ShapeDtypeStruct((rows, experts * width), bf16)
    return pl.pallas_call(
        functools.partial(expert_kernel, block),
        grid=(experts,),
        in_specs=[whole(rows, features), column, whole(rows, LANES), whole(features, LANES), weight, weight],
        out_specs=[column, column, column, whole(rows, features + LANES)],
        out_shape=[wide, wide, wide, jax.ShapeDtypeStruct((rows, features + LANES), bf16)],
        scratch_shapes=[pltpu.VMEM((rows, LANES), f32), pltpu.VMEM((rows, LANES), f32), pltpu.VMEM((rows, features), f32)],
        compiler_params=params(),
        cost_estimate=cost(8 * rows * features * experts * width, 4 * experts * width * (features + 2 * rows), rows * experts * width),
        name="experts",
    )(rows_in, back, routed, router, gate_w, up_w)


def wgrad_kernel(count, block, *refs):
    lefts, rights, out = refs[:count], refs[count : 2 * count], refs[2 * count]
    for start in range(0, out.shape[1], block):
        here = slice(start, start + block)
        total = nn(lefts[0][here, :], rights[0][...])
        for left, right in zip(lefts[1:], rights[1:]):
            total = total + nn(left[here, :], right[...])
        out[0, here, :] = total.astype(out.dtype)


def wgrad(lefts, rights, experts):
    features = lefts[0].shape[0]
    width = rights[0].shape[1] // experts
    rows = sum(left.shape[1] for left in lefts)
    return pl.pallas_call(
        functools.partial(wgrad_kernel, len(lefts), min(512, features)),
        grid=(experts,),
        in_specs=[pl.BlockSpec(left.shape, lambda e: (0, 0)) for left in lefts]
        + [pl.BlockSpec((right.shape[0], width), lambda e: (0, e)) for right in rights],
        out_specs=pl.BlockSpec((1, features, width), lambda e: (e, 0, 0)),
        out_shape=jax.ShapeDtypeStruct((experts, features, width), bf16),
        compiler_params=params(),
        cost_estimate=cost(2 * rows * features * experts * width, 2 * (rows + experts * width) * features),
        name="wgrad",
    )(*lefts, *rights)


def down_kernel(act, down_w, out):
    joined = jnp.concatenate([down_w[e] for e in range(down_w.shape[0])], axis=1)
    out[...] = nt(act[...], joined).astype(out.dtype)


def down(act, down_w):
    rows = act.shape[0]
    experts, features, width = down_w.shape
    block = min(256, features)
    return pl.pallas_call(
        down_kernel,
        grid=(features // block,),
        in_specs=[pl.BlockSpec(act.shape, lambda n: (0, 0)), pl.BlockSpec((experts, block, width), lambda n: (0, n, 0))],
        out_specs=pl.BlockSpec((rows, block), lambda n: (0, n)),
        out_shape=jax.ShapeDtypeStruct((rows, features), bf16),
        compiler_params=params(),
        cost_estimate=cost(2 * rows * features * experts * width, 2 * (rows + experts * width) * features),
        name="down",
    )(act, down_w)


def gather_rows(values):
    return lax.all_gather(values, "tensor", axis=0, tiled=True)


def scatter_rows(values):
    return lax.psum_scatter(values, "tensor", scatter_dimension=0, tiled=True)


def dp_scatter(values):
    return lax.psum_scatter(values, "dp", scatter_dimension=0, tiled=True)


def exchange_sum(values, axes):
    for axis in axes:
        size = lax.axis_size(axis)
        step = 1
        while step < size:
            values = values + lax.ppermute(values, axis, [(i, i ^ step) for i in range(size)])
            step *= 2
    return values


def local(
    tokens, cotangent, seg_ids, keep_mask, routes, attn_gain, w_query, w_key, w_value, w_out,
    q_gain, k_gain, ffn_gain, router, w_gate, w_up, w_down,
):
    parts = lax.axis_size("tensor")
    part_at = lax.axis_index("tensor")
    shard_rows, features = tokens.shape
    group_rows = shard_rows * parts
    _, length = seg_ids.shape
    local_width = w_query.shape[1]
    experts = w_gate.shape[0]
    chunk_rows = shard_rows // CHUNKS
    chunks = range(CHUNKS)
    own = [slice(c * chunk_rows, (c + 1) * chunk_rows) for c in chunks]

    def chunk_of(values, c):
        width = values.shape[1]
        return values.reshape(parts, CHUNKS, chunk_rows, width)[:, c].reshape(parts * chunk_rows, width)

    def in_order(pieces):
        width = pieces[0].shape[1]
        stacked = jnp.stack([piece.reshape(parts, chunk_rows, width) for piece in pieces], axis=1)
        return stacked.reshape(group_rows, width)

    inputs = tokens.astype(f32)
    first_scale = rms_scale(inputs)
    normed_all = gather_rows((inputs * first_scale * attn_gain).astype(bf16))
    grad_all = [gather_rows(cotangent[own[c]]) for c in chunks]
    backs = [up_back(grad_all[c], w_down) for c in chunks]

    qraw = nn(normed_all, w_query)
    kraw = nn(normed_all, w_key)
    value = nn(normed_all, w_value).astype(bf16)
    squares = exchange_sum(jnp.stack([jnp.sum(qraw * qraw, axis=1), jnp.sum(kraw * kraw, axis=1)]), ("tensor",))
    q_scale, k_scale = (lax.rsqrt(squares[i] / features + EPSILON)[:, None] for i in range(2))
    cosine, sine = rope_tables(length, HEAD)
    query, key, attended, lse = attend(
        qraw, kraw, value, q_scale, k_scale, q_gain, k_gain, cosine, sine, seg_ids[0], keep_mask[0]
    )

    expert_ids = jnp.arange(LANES)
    routed = jnp.sum((routes[:, :, None] == expert_ids[None, None, :]).astype(f32), axis=1)
    router_wide = jnp.pad(router, ((0, 0), (0, LANES - experts)))
    middles, scales, ffn_own, ffn_all = [], [], [], []
    for c in chunks:
        summed = scatter_rows(nt(chunk_of(attended, c), w_out).astype(bf16))
        middle = inputs[own[c]] + summed.astype(f32)
        scale = rms_scale(middle)
        normed = (middle * scale * ffn_gain).astype(bf16)
        middles.append(middle)
        scales.append(scale)
        ffn_own.append(normed)
        ffn_all.append(gather_rows(normed))

    acts, dgates, dups, middle_grads, middle_all = [], [], [], [], []
    ffn_gain_part = 0.0
    router_part = 0.0
    routed_own = lax.dynamic_slice_in_dim(routed, part_at * shard_rows, shard_rows, 0)[:, :experts]
    for c in chunks:
        act, dgate, dup, grads = experts_block(ffn_all[c], backs[c], chunk_of(routed, c), router_wide, w_gate, w_up)
        acts.append(act)
        dgates.append(dgate)
        dups.append(dup)
        grads = scatter_rows(grads).astype(f32)
        share_grad = grads[:, features : features + experts] * routed_own[own[c]]
        probs = jax.nn.softmax(nn(ffn_own[c], router), axis=-1)
        logit_grad = (probs * (share_grad - jnp.sum(share_grad * probs, axis=-1, keepdims=True))).astype(bf16)
        ffn_grad = grads[:, :features] + nt(logit_grad, router)
        router_part = router_part + tn(ffn_own[c], logit_grad)
        ffn_gain_part = ffn_gain_part + jnp.sum(ffn_grad * middles[c] * scales[c], axis=0)
        middle_grad = cotangent[own[c]].astype(f32) + norm_back(ffn_grad, middles[c], scales[c], ffn_gain)
        middle_grads.append(middle_grad)
        middle_all.append(gather_rows(middle_grad.astype(bf16)))

    layer_out = jnp.concatenate(
        [(middles[c] + scatter_rows(down(acts[c], w_down)).astype(f32)).astype(bf16) for c in chunks]
    )
    ffn_t = [rows.T for rows in ffn_all]
    grad_t = [rows.T for rows in grad_all]
    gate_done = dp_scatter(wgrad(ffn_t, dgates, experts)).astype(f32)
    up_done = dp_scatter(wgrad(ffn_t, dups, experts)).astype(f32)
    down_done = dp_scatter(wgrad(grad_t, acts, experts)).astype(f32)

    attended_grad = in_order([nn(rows, w_out).astype(bf16) for rows in middle_all])
    dqn, dkn, dvalue, qdot, kdot, q_gain_part, k_gain_part = attend_back(
        query, key, value, attended_grad, lse, qraw, kraw, q_scale, k_scale, q_gain, k_gain, cosine, sine,
        seg_ids[0], keep_mask[0],
    )
    dots = exchange_sum(jnp.stack([qdot[:, 0], kdot[:, 0]]), ("tensor",)) / features

    def raw_grad(grad, raw, scale, gain, dot):
        return (scale * gain * grad - raw * (scale * scale * scale) * dot[:, None]).astype(bf16)

    dqraw = raw_grad(dqn, qraw, q_scale, q_gain, dots[0])
    dkraw = raw_grad(dkn, kraw, k_scale, k_gain, dots[1])
    normed_part = nt(dqraw, w_query) + nt(dkraw, w_key) + nt(dvalue, w_value)
    normed_grad = scatter_rows(normed_part.astype(bf16)).astype(f32)
    normed_t = normed_all.T
    attn_grads = [nn(normed_t, dqraw), nn(normed_t, dkraw), nn(normed_t, dvalue)]
    attn_gain_part = sum(
        jnp.sum(grad * weight.astype(f32), axis=1) for grad, weight in zip(attn_grads, (w_query, w_key, w_value))
    ) / attn_gain
    out_grad = sum(tn(middle_all[c], chunk_of(attended, c)) for c in chunks)
    attn_grads = jnp.concatenate([grad.astype(bf16) for grad in attn_grads + [out_grad]], axis=1)
    attn_done = dp_scatter(attn_grads).astype(f32)
    query_done, key_done, value_done, out_done = (
        attn_done[:, i * local_width : (i + 1) * local_width] for i in range(4)
    )
    tokens_grad = jnp.concatenate(middle_grads) + norm_back(normed_grad, inputs, first_scale, attn_gain)

    def placed(part):
        return lax.dynamic_update_slice_in_dim(jnp.zeros((features,), f32), part, part_at * local_width, 0)

    early = exchange_sum(jnp.concatenate([router_part.T, ffn_gain_part[None]]), ("dp", "tensor"))
    late = exchange_sum(jnp.stack([attn_gain_part, placed(q_gain_part[0]), placed(k_gain_part[0])]), ("dp", "tensor"))
    return (
        layer_out, tokens_grad, query_done, key_done, value_done, out_done,
        late[0], late[1], late[2], early[experts], early[:experts].T, gate_done, up_done, down_done,
    )


def solution(mesh):
    rows = P(("dp", "tensor"), None)
    column = P(None, "tensor")
    expert = P(None, None, "tensor")
    in_specs = (
        rows, rows, P("dp", None), P("dp", None), P("dp", None), P(), column, column, column, column,
        P("tensor"), P("tensor"), P(), P(), expert, expert, expert,
    )
    block = P("dp", "tensor")
    expert_out = P("dp", None, "tensor")
    out_specs = (
        rows, rows, block, block, block, block, P(), P(), P(), P(), P(), expert_out, expert_out, expert_out,
    )
    return jax.shard_map(local, mesh=mesh, in_specs=in_specs, out_specs=out_specs, check_vma=False)
```

```python
import functools

import jax
import jax.numpy as jnp
from jax import lax
from jax.experimental import pallas as pl
from jax.experimental.pallas import tpu as pltpu
from jax.sharding import PartitionSpec as P

D = 2048
HEAD = 128
DOC = 512
LANES = 128
EPSILON = 1e-05
MASKED = -1e30
CHUNKS = 2
VMEM = 56 * 1024 * 1024
bf16 = jnp.bfloat16
f32 = jnp.float32


def nn(left, right):
    return lax.dot_general(left, right, (((1,), (0,)), ((), ())), preferred_element_type=f32)


def nt(left, right):
    return lax.dot_general(left, right, (((1,), (1,)), ((), ())), preferred_element_type=f32)


def tn(left, right):
    return lax.dot_general(left, right, (((0,), (0,)), ((), ())), preferred_element_type=f32)


def params():
    return pltpu.CompilerParams(vmem_limit_bytes=VMEM)


PACE = 0.8


def cost(flops, moved, special=0):
    return pl.CostEstimate(flops=int(1.5 * PACE * flops + 6e4 * PACE * special), bytes_accessed=moved // 8, transcendentals=0)


def rms_scale(values):
    return lax.rsqrt(jnp.mean(values * values, axis=-1, keepdims=True) + EPSILON)


def norm_back(grad_values, values, scale_col, gain_vec):
    weighted = grad_values * gain_vec
    inner_mean = jnp.mean(weighted * values, axis=-1, keepdims=True)
    return scale_col * weighted - values * (scale_col * scale_col * scale_col) * inner_mean


def rope_tables(length, width):
    half_width = width // 2
    frequency = jnp.power(10000.0, -jnp.arange(half_width, dtype=f32) * 2.0 / width)
    angles = jnp.arange(length, dtype=f32)[:, None] * frequency[None, :]
    cosine, sine = jnp.cos(angles), jnp.sin(angles)
    return jnp.concatenate([cosine, cosine], axis=1), jnp.concatenate([-sine, sine], axis=1)


def key_start(query_start):
    return max(0, query_start - DOC)


def fill_bias(bias, seg_col, seg_row, keep_row, block):
    length = seg_col.shape[0]
    for start in range(0, length, block):
        first, stop = key_start(start), start + block
        query_pos = start + lax.broadcasted_iota(jnp.int32, (block, stop - first), 0)
        key_pos = first + lax.broadcasted_iota(jnp.int32, (block, stop - first), 1)
        same = seg_col[start:stop, :] == seg_row[:, first:stop]
        live = (keep_row[:, first:stop] == 1) | (key_pos == query_pos)
        allowed = same & live & (key_pos <= query_pos)
        bias[start:stop, : stop - first] = jnp.where(allowed, 0.0, MASKED)


def turned(values):
    return pltpu.roll(values, values.shape[1] // 2, 1)


def project_kernel(rows_in, w_query, w_key, w_value, q_out, k_out, v_out, squares_out):
    ones = jnp.ones((8, q_out.shape[1]), f32)
    for at, (weight, out) in enumerate(((w_query, q_out), (w_key, k_out))):
        raw = nn(rows_in[...], weight[...])
        out[...] = raw
        sums = lax.dot_general(
            ones, raw * raw, (((1,), (1,)), ((), ())), precision=lax.Precision.HIGHEST, preferred_element_type=f32
        )
        squares_out[at : at + 1, :] = sums[:1]
    v_out[...] = nn(rows_in[...], w_value[...]).astype(bf16)


def project(rows_in, w_query, w_key, w_value):
    rows, features = rows_in.shape
    width = w_query.shape[1]
    block = min(256, rows)
    row = lambda columns: pl.BlockSpec((block, columns), lambda r: (r, 0))
    weight = pl.BlockSpec((features, width), lambda r: (0, 0))
    sds = jax.ShapeDtypeStruct
    return pl.pallas_call(
        project_kernel,
        grid=(rows // block,),
        in_specs=[row(features), weight, weight, weight],
        out_specs=[row(width), row(width), row(width), pl.BlockSpec((2, block), lambda r: (0, r))],
        out_shape=[sds((rows, width), f32), sds((rows, width), f32), sds((rows, width), bf16), sds((2, rows), f32)],
        compiler_params=params(),
        cost_estimate=cost(6 * rows * features * width, 2 * (rows + 3 * width) * features),
        name="project",
    )(rows_in, w_query, w_key, w_value)


def project_back_kernel(
    rows_in, dqn, dkn, dvalue, qraw, kraw, q_scale, k_scale, q_dot, k_dot, q_gain, k_gain,
    w_query, w_key, w_value, part_out, dq_out, dk_out, gain_out,
):
    @pl.when(pl.program_id(0) == 0)
    def _():
        gain_out[...] = jnp.zeros_like(gain_out)

    def raw_grad(grad, raw, scale, gain, dot):
        cube = scale[...] * scale[...] * scale[...]
        return (scale[...] * (gain[...] * grad[...]) - raw[...] * (cube * dot[...])).astype(bf16)

    dq = raw_grad(dqn, qraw, q_scale, q_gain, q_dot)
    dk = raw_grad(dkn, kraw, k_scale, k_gain, k_dot)
    dq_out[...] = dq
    dk_out[...] = dk
    part = nt(dq, w_query[...]) + nt(dk, w_key[...]) + nt(dvalue[...], w_value[...])
    part_out[...] = part.astype(bf16)
    gain_out[...] += jnp.sum(part * rows_in[...].astype(f32), axis=0, keepdims=True)


def project_back(rows_in, dqn, dkn, dvalue, qraw, kraw, q_scale, k_scale, q_dot, k_dot, q_gain, k_gain, w_query, w_key, w_value):
    rows, features = rows_in.shape
    width = w_query.shape[1]
    block = min(256, rows)
    row = lambda columns: pl.BlockSpec((block, columns), lambda r: (r, 0))
    whole = lambda *shape: pl.BlockSpec(shape, lambda r: (0, 0))
    sds = jax.ShapeDtypeStruct
    return pl.pallas_call(
        project_back_kernel,
        grid=(rows // block,),
        in_specs=[row(features)] + [row(width)] * 5 + [row(1)] * 4 + [whole(1, width)] * 2 + [whole(features, width)] * 3,
        out_specs=[row(features), row(width), row(width), whole(1, features)],
        out_shape=[sds((rows, features), bf16), sds((rows, width), bf16), sds((rows, width), bf16), sds((1, features), f32)],
        compiler_params=params(),
        cost_estimate=cost(6 * rows * features * width, 2 * (rows + 3 * width) * features),
        name="project_back",
    )(rows_in, dqn, dkn, dvalue, qraw, kraw, q_scale, k_scale, q_dot, k_dot, q_gain[None], k_gain[None], w_query, w_key, w_value)


def attention_wgrad_kernel(count, extra, order, *refs):
    rows_in = refs[0]
    middles = refs[1 : 1 + count]
    sides = refs[1 + count : 4 + count]
    attended = refs[4 + count : 4 + 2 * count]
    outs = refs[4 + 2 * count + extra :]
    totals = [tn(rows_in[...], side[...]) for side in sides]
    total = tn(middles[0][...], attended[0][...])
    for left, right in zip(middles[1:], attended[1:]):
        total = total + tn(left[...], right[...])
    totals.append(total)
    half = outs[0].shape[2]
    for at, total in enumerate(totals):
        if extra:
            total = total + refs[4 + 2 * count][0, at].astype(f32)
        for place, out in enumerate(outs):
            out[0, at] = total[place * half : (place + 1) * half, :].astype(bf16)


def attention_wgrad(rows_in, middles, sides, attended, order, blocks, added=None):
    features = rows_in.shape[1]
    width = sides[0].shape[1]
    block = features // blocks
    extra = [] if added is None else [added]
    outs = 1 + len(extra)
    left = lambda values: pl.BlockSpec((values.shape[0], block), lambda i, ids: (0, ids[i]))
    right = lambda values: pl.BlockSpec(values.shape, lambda i, ids: (0, 0))
    out = lambda parts: pl.BlockSpec((1, 4, block // parts, width), lambda i, ids: (i, 0, 0, 0))
    result = pl.pallas_call(
        functools.partial(attention_wgrad_kernel, len(middles), len(extra)),
        grid_spec=pltpu.PrefetchScalarGridSpec(
            num_scalar_prefetch=1,
            grid=(order.shape[0],),
            in_specs=[left(rows_in)] + [left(m) for m in middles] + [right(v) for v in sides] + [right(v) for v in attended]
            + [out(1) for _ in extra],
            out_specs=[out(outs)] * outs,
        ),
        out_shape=[jax.ShapeDtypeStruct((order.shape[0], 4, block // outs, width), bf16)] * outs,
        compiler_params=params(),
        cost_estimate=cost(8 * rows_in.shape[0] * features * width, 4 * features * width),
        name="attention_wgrad",
    )(order, rows_in, *middles, *sides, *attended, *extra)
    return result if extra else result[0]


def attend_kernel(
    block, qraw, kraw, value, q_scale, k_scale, q_gain, k_gain, cosine, sine,
    seg_col, seg_row, keep_row, q_out, k_out, o_out, lse_out, bias,
):
    @pl.when(pl.program_id(0) == 0)
    def _():
        fill_bias(bias, seg_col, seg_row, keep_row, block)

    def rotated(raw, scale, gain):
        normed = raw[...] * scale[...] * gain[...]
        return (normed * cosine[...] + turned(normed) * sine[...]).astype(bf16)

    q_out[...] = rotated(qraw, q_scale, q_gain)
    k_out[...] = rotated(kraw, k_scale, k_gain)
    length = seg_col.shape[0]
    for start in range(0, length, block):
        first, stop = key_start(start), start + block
        scores = nt(q_out[start:stop, :], k_out[first:stop, :]) * HEAD ** (-0.5)
        scores = scores + bias[start:stop, : stop - first]
        top = jnp.max(scores, axis=1, keepdims=True)
        powers = jnp.exp(scores - top)
        total = jnp.sum(powers, axis=1, keepdims=True)
        weights = (powers * (1.0 / total)).astype(bf16)
        o_out[start:stop, :] = nn(weights, value[first:stop, :]).astype(bf16)
        lse_out[start:stop, :] = jnp.broadcast_to(top + jnp.log(total), (block, HEAD))


def attend(qraw, kraw, value, q_scale, k_scale, q_gain, k_gain, cosine, sine, seg, keep):
    length, width = qraw.shape
    block = min(256, length)
    span = min(DOC + block, length)
    head = pl.BlockSpec((length, HEAD), lambda h: (0, h))
    gain = pl.BlockSpec((1, HEAD), lambda h: (0, h))
    whole = lambda *shape: pl.BlockSpec(shape, lambda h: (0, 0))
    return pl.pallas_call(
        functools.partial(attend_kernel, block),
        grid=(width // HEAD,),
        in_specs=[head, head, head, whole(length, 1), whole(length, 1), gain, gain]
        + [whole(length, HEAD), whole(length, HEAD), whole(length, 1), whole(1, length), whole(1, length)],
        out_specs=[head, head, head, head],
        out_shape=[jax.ShapeDtypeStruct((length, width), t) for t in (bf16, bf16, bf16, f32)],
        scratch_shapes=[pltpu.VMEM((length, span), f32)],
        compiler_params=params(),
        cost_estimate=cost(4 * length * span * width, 18 * length * width, length * span * width // HEAD),
        name="attend",
    )(qraw, kraw, value, q_scale, k_scale, q_gain[None], k_gain[None], cosine, sine, seg[:, None], seg[None], keep[None])


def attend_back_kernel(
    block, query, key, value, out_grad, lse, qraw, kraw, q_scale, k_scale, q_gain, k_gain, cosine, sine,
    seg_col, seg_row, keep_row, dq_out, dk_out, dv_out, qdot_out, kdot_out, qg_out, kg_out, bias, dk_sum, dv_sum,
):
    at = pl.program_id(0)

    @pl.when(at == 0)
    def _():
        fill_bias(bias, seg_col, seg_row, keep_row, block)
        qdot_out[...] = jnp.zeros_like(qdot_out)
        kdot_out[...] = jnp.zeros_like(kdot_out)

    dk_sum[...] = jnp.zeros_like(dk_sum)
    dv_sum[...] = jnp.zeros_like(dv_sum)
    length = seg_col.shape[0]
    scale = HEAD ** (-0.5)
    for start in range(0, length, block):
        first, stop = key_start(start), start + block
        rows, keys = slice(start, stop), slice(first, stop)
        scores = nt(query[rows, :], key[keys, :]) * scale + bias[rows, : stop - first]
        weights = jnp.exp(scores - lse[rows, :1])
        prob_grad = nt(out_grad[rows, :], value[keys, :])
        inner = jnp.sum(weights * prob_grad, axis=1, keepdims=True)
        score_grad = (weights * (prob_grad - inner)).astype(bf16)
        dq_out[rows, :] = nn(score_grad, key[keys, :]) * scale
        dk_sum[keys, :] += tn(score_grad, query[rows, :])
        dv_sum[keys, :] += tn(weights.astype(bf16), out_grad[rows, :])

    def unrotated(grad):
        return grad * cosine[...] + turned(grad * sine[...])

    dv_out[...] = dv_sum[...].astype(bf16)
    dq = unrotated(dq_out[...])
    dk = unrotated(dk_sum[...] * scale)
    dq_out[...] = dq
    dk_out[...] = dk
    dq = dq * qraw[...]
    dk = dk * kraw[...]
    qg_out[...] = jnp.sum(dq * q_scale[...], axis=0, keepdims=True)
    kg_out[...] = jnp.sum(dk * k_scale[...], axis=0, keepdims=True)
    qdot_out[...] += jnp.sum(dq * q_gain[...], axis=1, keepdims=True)
    kdot_out[...] += jnp.sum(dk * k_gain[...], axis=1, keepdims=True)


def attend_back(query, key, value, out_grad, lse, qraw, kraw, q_scale, k_scale, q_gain, k_gain, cosine, sine, seg, keep):
    length, width = qraw.shape
    block = min(256, length)
    span = min(DOC + block, length)
    head = pl.BlockSpec((length, HEAD), lambda h: (0, h))
    gain = pl.BlockSpec((1, HEAD), lambda h: (0, h))
    whole = lambda *shape: pl.BlockSpec(shape, lambda h: (0, 0))
    sds = jax.ShapeDtypeStruct
    return pl.pallas_call(
        functools.partial(attend_back_kernel, block),
        grid=(width // HEAD,),
        in_specs=[head] * 7
        + [whole(length, 1), whole(length, 1), gain, gain]
        + [whole(length, HEAD), whole(length, HEAD), whole(length, 1), whole(1, length), whole(1, length)],
        out_specs=[head, head, head, whole(length, 1), whole(length, 1), gain, gain],
        out_shape=[sds((length, width), f32), sds((length, width), f32), sds((length, width), bf16)]
        + [sds((length, 1), f32), sds((length, 1), f32), sds((1, width), f32), sds((1, width), f32)],
        scratch_shapes=[pltpu.VMEM((length, span), f32), pltpu.VMEM((length, HEAD), f32), pltpu.VMEM((length, HEAD), f32)],
        compiler_params=params(),
        cost_estimate=cost(10 * length * span * width, 32 * length * width, length * span * width // HEAD),
        name="attend_back",
    )(query, key, value, out_grad, lse, qraw, kraw, q_scale, k_scale, q_gain[None], k_gain[None], cosine, sine, seg[:, None], seg[None], keep[None])


def up_back_kernel(grad, down_w, out):
    width = down_w.shape[2]
    for at in range(down_w.shape[0]):
        out[:, at * width : (at + 1) * width] = nn(grad[...], down_w[at]).astype(out.dtype)


def up_back(grad, down_w):
    rows, features = grad.shape
    experts, _, width = down_w.shape
    step = 2 if experts % 2 == 0 else 1
    return pl.pallas_call(
        up_back_kernel,
        grid=(experts // step,),
        in_specs=[pl.BlockSpec((rows, features), lambda e: (0, 0)), pl.BlockSpec((step, features, width), lambda e: (e, 0, 0))],
        out_specs=pl.BlockSpec((rows, step * width), lambda e: (0, e)),
        out_shape=jax.ShapeDtypeStruct((rows, experts * width), bf16),
        compiler_params=params(),
        cost_estimate=cost(2 * rows * features * experts * width, 2 * (rows + experts * width) * features),
        name="up_back",
    )(grad, down_w)


def expert_kernel(block, rows_in, back, routed, router, gate_w, up_w, act_out, dgate_out, dup_out, grad_out, comb, dcomb, total):
    at = pl.program_id(0)
    rows, features = rows_in.shape
    lane = lax.broadcasted_iota(jnp.int32, (block, LANES), 1)

    @pl.when(at == 0)
    def _():
        experts = pl.num_programs(0)
        for start in range(0, rows, block):
            here = slice(start, start + block)
            logits = jnp.where(lane < experts, nn(rows_in[here, :], router[...]), MASKED)
            powers = jnp.exp(logits - jnp.max(logits, axis=1, keepdims=True))
            probs = powers / jnp.sum(powers, axis=1, keepdims=True)
            comb[here, :] = probs * routed[here, :]
        total[...] = jnp.zeros_like(total)
        dcomb[...] = jnp.zeros_like(dcomb)

    gate, up = gate_w[0], up_w[0]
    mine = lane == at
    for start in range(0, rows, block):
        here = slice(start, start + block)
        taken = rows_in[here, :]
        pre_gate = nn(taken, gate)
        pre_up = nn(taken, up)
        behind = back[here, :].astype(f32)
        share = jnp.sum(jnp.where(mine, comb[here, :], 0.0), axis=1, keepdims=True)
        sigmoid = 0.5 * jnp.tanh(0.5 * pre_gate) + 0.5
        active = pre_gate * sigmoid
        inner = active * pre_up
        share_grad = jnp.sum(inner * behind, axis=1, keepdims=True)
        dcomb[here, :] = jnp.where(mine, share_grad, dcomb[here, :])
        act_out[here, :] = (inner * share).astype(bf16)
        inner_grad = behind * share
        dgate = (inner_grad * pre_up * (sigmoid + active * (1.0 - sigmoid))).astype(bf16)
        dup = (inner_grad * active).astype(bf16)
        dgate_out[here, :] = dgate
        dup_out[here, :] = dup
        total[here, :] += nt(dgate, gate) + nt(dup, up)

    @pl.when(at == pl.num_programs(0) - 1)
    def _():
        grad_out[:, :features] = total[...].astype(bf16)
        grad_out[:, features:] = dcomb[...].astype(bf16)


def experts_block(rows_in, back, routed, router, gate_w, up_w):
    rows, features = rows_in.shape
    experts, _, width = gate_w.shape
    block = min(512, rows)
    whole = lambda *shape: pl.BlockSpec(shape, lambda e: (0, 0))
    column = pl.BlockSpec((rows, width), lambda e: (0, e))
    weight = pl.BlockSpec((1, features, width), lambda e: (e, 0, 0))
    wide = jax.ShapeDtypeStruct((rows, experts * width), bf16)
    return pl.pallas_call(
        functools.partial(expert_kernel, block),
        grid=(experts,),
        in_specs=[whole(rows, features), column, whole(rows, LANES), whole(features, LANES), weight, weight],
        out_specs=[column, column, column, whole(rows, features + LANES)],
        out_shape=[wide, wide, wide, jax.ShapeDtypeStruct((rows, features + LANES), bf16)],
        scratch_shapes=[pltpu.VMEM((rows, LANES), f32), pltpu.VMEM((rows, LANES), f32), pltpu.VMEM((rows, features), f32)],
        compiler_params=params(),
        cost_estimate=cost(8 * rows * features * experts * width, 4 * experts * width * (features + 2 * rows), rows * experts * width),
        name="experts",
    )(rows_in, back, routed, router, gate_w, up_w)


def wgrad_kernel(count, extra, per, block, order, *refs):
    lefts, rights = refs[:count], refs[count : 2 * count]
    added = refs[2 * count : 2 * count + extra]
    outs = refs[2 * count + extra :]
    at = pl.program_id(0)
    features = lefts[0].shape[1]

    def piece(start, stop):
        total = tn(lefts[0][:, start:stop], rights[0][...])
        for left, right in zip(lefts[1:], rights[1:]):
            total = total + tn(left[:, start:stop], right[...])
        return total

    if not added:
        for place, out in enumerate(outs):

            @pl.when(at // per == place)
            def _(out=out):
                for start in range(0, features, block):
                    out[0, start : start + block, :] = piece(start, start + block).astype(bf16)

        return
    half = features // 2
    for place, got in enumerate(added):

        @pl.when(at // per == place)
        def _(got=got):
            for start in range(0, features, block):
                total = piece(start, start + block) + got[0, start : start + block, :].astype(f32)
                outs[start // half][0, start % half : start % half + block, :] = total.astype(bf16)


def wgrad(lefts, rights, order, width, per, added=()):
    features = lefts[0].shape[1]
    experts = order.shape[0]
    groups = experts // per
    rows = sum(left.shape[0] for left in lefts)

    def group_spec(place):
        return pl.BlockSpec((1, features, width), lambda i, ids: (jnp.clip(i - place * per, 0, per - 1), 0, 0))

    groups_specs = [group_spec(place) for place in range(groups)]
    if added:
        out_specs = [pl.BlockSpec((1, features // 2, width), lambda i, ids: (i, 0, 0))] * 2
        out_shape = [jax.ShapeDtypeStruct((experts, features // 2, width), bf16)] * 2
    else:
        out_specs = groups_specs
        out_shape = [jax.ShapeDtypeStruct((per, features, width), bf16)] * groups
    return pl.pallas_call(
        functools.partial(wgrad_kernel, len(lefts), len(added), per, min(512, features // 2)),
        grid_spec=pltpu.PrefetchScalarGridSpec(
            num_scalar_prefetch=1,
            grid=(experts,),
            in_specs=[pl.BlockSpec(left.shape, lambda i, ids: (0, 0)) for left in lefts]
            + [pl.BlockSpec((right.shape[0], width), lambda i, ids: (0, ids[i])) for right in rights]
            + (groups_specs if added else []),
            out_specs=out_specs,
        ),
        out_shape=out_shape,
        compiler_params=params(),
        cost_estimate=cost(2 * rows * features * experts * width, 2 * (rows + 2 * experts * width) * features),
        name="wgrad",
    )(order, *lefts, *rights, *added)


def down_kernel(act, down_w, out):
    joined = jnp.concatenate([down_w[e] for e in range(down_w.shape[0])], axis=1)
    out[...] = nt(act[...], joined).astype(out.dtype)


def down(act, down_w):
    rows = act.shape[0]
    experts, features, width = down_w.shape
    block = min(256, features)
    return pl.pallas_call(
        down_kernel,
        grid=(features // block,),
        in_specs=[pl.BlockSpec(act.shape, lambda n: (0, 0)), pl.BlockSpec((experts, block, width), lambda n: (0, n, 0))],
        out_specs=pl.BlockSpec((rows, block), lambda n: (0, n)),
        out_shape=jax.ShapeDtypeStruct((rows, features), bf16),
        compiler_params=params(),
        cost_estimate=cost(2 * rows * features * experts * width, 2 * (rows + experts * width) * features),
        name="down",
    )(act, down_w)


def gate(value, *others):
    return lax.optimization_barrier((value, others))[0]


def gather_rows(values):
    return lax.all_gather(values, "tensor", axis=0, tiled=True)


def scatter_rows(values):
    return lax.psum_scatter(values, "tensor", scatter_dimension=0, tiled=True)


class Chain:
    def __init__(self, values):
        self.values = values
        self.parts = lax.axis_size("tensor")
        self.ups, self.downs = [values], [values]

    def hop(self, *others):
        step = len(self.ups)
        if step < self.parts:
            up, down = gate((self.ups[-1], self.downs[-1]), *others) if others else (self.ups[-1], self.downs[-1])
            self.sent = (up, down)
            self.ups.append(lax.ppermute(up, "tensor", [(i, i + 1) for i in range(step - 1, self.parts - 1)]))
            self.downs.append(lax.ppermute(down, "tensor", [(i, i - 1) for i in range(1, self.parts - step + 1)]))
        return self.sent

    def recv(self):
        return self.ups[-1], self.downs[-1]

    def joined(self):
        while len(self.ups) < self.parts:
            self.hop()
        parts, values = self.parts, self.values
        at = lax.axis_index("tensor")
        rows = values.shape[0]
        whole = jnp.zeros((parts * rows,) + values.shape[1:], values.dtype)
        whole = lax.dynamic_update_slice_in_dim(whole, values, at * rows, 0)
        for step in range(1, parts):
            piece = self.ups[step] + self.downs[parts - step]
            whole = lax.dynamic_update_slice_in_dim(whole, piece, lax.rem(at - step + parts, parts) * rows, 0)
        return whole


class ScatterChain:
    def __init__(self, values):
        self.parts = lax.axis_size("tensor")
        self.at = lax.axis_index("tensor")
        self.values = values
        self.rows = values.shape[0] // self.parts
        self.step = 0
        self.up = self.down = self.first = None

    def block(self, place):
        return lax.dynamic_slice_in_dim(self.values, jnp.clip(place, 0, self.parts - 1) * self.rows, self.rows, 0)

    def hop(self, *others):
        parts, step = self.parts, self.step
        if step < parts - 1:
            if step:
                self.values = gate(self.values, self.up, self.down, *others)
            up = self.block(parts - 1 - step + self.at)
            down = self.block(step - parts + 1 + self.at)
            if step:
                up = (up.astype(f32) + self.up.astype(f32)).astype(bf16)
                down = (down.astype(f32) + self.down.astype(f32)).astype(bf16)
            self.sent = (up, down)
            self.first = self.first or self.sent
            self.up = lax.ppermute(up, "tensor", [(i, i + 1) for i in range(step + 1)])
            self.down = lax.ppermute(down, "tensor", [(i, i - 1) for i in range(parts - 1 - step, parts)])
            self.step += 1
        return self.up, self.down

    def total(self):
        while self.step < self.parts - 1:
            self.hop()
        return self.block(self.at).astype(f32) + self.up.astype(f32) + self.down.astype(f32)


def pair_swap(values, step):
    size = lax.axis_size("dp")
    return lax.ppermute(values, "dp", [(i, i ^ step) for i in range(size)])


class Halving:
    def __init__(self, values):
        bits = list(range(values[0].shape[0].bit_length() - 1))
        self.kept = list(values)
        self.left = [bits[::-1], bits]
        self.got = None

    def send(self):
        if not self.left[0]:
            return ()
        self.got = []
        sent = []
        for side, downward in ((0, True), (1, False)):
            bit = self.left[side].pop(0)
            kept = self.kept[side]
            half = kept.shape[0] // 2
            if downward:
                keep, go = kept[:half], kept[half:]
            else:
                view = kept.reshape((half, 2) + kept.shape[1:])
                keep, go = view[:, 0], view[:, 1]
            sent.append(go)
            self.got.append(pair_swap(go, 2 << bit))
            self.kept[side] = keep
        return tuple(sent)

    def add(self):
        if self.got is not None:
            last = not self.left[0]
            for side in range(2):
                total = self.kept[side].astype(f32) + self.got[side].astype(f32)
                self.kept[side] = total if last else total.astype(bf16)
            self.got = None
        return tuple(self.kept)

    def done(self):
        self.add()
        while self.left[0]:
            self.send()
            self.add()
        return jnp.concatenate([kept[0].astype(f32) for kept in self.kept], axis=1)


def exchange_sum(values, axes):
    for axis in axes:
        size = lax.axis_size(axis)
        step = 1
        while step < size:
            values = values + lax.ppermute(values, axis, [(i, i ^ step) for i in range(size)])
            step *= 2
    return values


def local(
    tokens, cotangent, seg_ids, keep_mask, routes, attn_gain, w_query, w_key, w_value, w_out,
    q_gain, k_gain, ffn_gain, router, w_gate, w_up, w_down,
):
    parts = lax.axis_size("tensor")
    part_at = lax.axis_index("tensor")
    dp_size = lax.axis_size("dp")
    low_bit = lax.axis_index("dp") % 2
    shard_rows, features = tokens.shape
    group_rows = shard_rows * parts
    _, length = seg_ids.shape
    local_width = w_query.shape[1]
    experts, _, width = w_gate.shape
    per = experts // dp_size
    chunk_rows = shard_rows // CHUNKS
    chunks = range(CHUNKS)
    own = [slice(c * chunk_rows, (c + 1) * chunk_rows) for c in chunks]

    def chunk_of(values, c):
        columns = values.shape[1]
        return values.reshape(parts, CHUNKS, chunk_rows, columns)[:, c].reshape(parts * chunk_rows, columns)

    def in_order(pieces):
        columns = pieces[0].shape[1]
        stacked = jnp.stack([piece.reshape(parts, chunk_rows, columns) for piece in pieces], axis=1)
        return stacked.reshape(group_rows, columns)

    inputs = tokens.astype(f32)
    first_scale = rms_scale(inputs)
    normed_all = Chain((inputs * first_scale * attn_gain).astype(bf16)).joined()
    behind = Chain(gate(cotangent, normed_all))

    expert_ids = jnp.arange(LANES)
    routed = jnp.sum((routes[:, :, None] == expert_ids[None, None, :]).astype(f32), axis=1)
    router_wide = jnp.pad(router, ((0, 0), (0, LANES - experts)))
    routed_own = lax.dynamic_slice_in_dim(routed, part_at * shard_rows, shard_rows, 0)[:, :experts]
    cosine, sine = rope_tables(length, HEAD)
    relative = jnp.arange(dp_size // 2, dtype=jnp.int32) ^ (lax.axis_index("dp") // 2)
    own_blocks, other_blocks = 2 * relative + low_bit, 2 * relative + 1 - low_bit
    mine, theirs = (
        (blocks[:, None] * per + jnp.arange(per, dtype=jnp.int32)).reshape(-1) for blocks in (own_blocks, other_blocks)
    )

    qraw, kraw, value, squares = project(normed_all, w_query, w_key, w_value)
    squares = exchange_sum(squares, ("tensor",))
    behind.hop()
    q_scale, k_scale = (lax.rsqrt(squares[i] / features + EPSILON)[:, None] for i in range(2))
    query, key, attended, lse = attend(
        qraw, kraw, value, q_scale, k_scale, q_gain, k_gain, cosine, sine, gate(seg_ids[0], routed, router_wide, *behind.recv()), keep_mask[0]
    )
    attended_parts = [chunk_of(attended, c) for c in chunks]
    outs = [nt(attended_parts[0], w_out).astype(bf16)]
    summed = [scatter_rows(outs[0])]
    outs.append(nt(gate(attended_parts[1], outs[0]), w_out).astype(bf16))
    summed.append(scatter_rows(outs[1]))
    behind.hop(outs[1])

    grad_group = behind.joined()
    grad_all = [chunk_of(grad_group, c) for c in chunks]
    backs = [up_back(grad_all[c], w_down) for c in chunks]

    middles, scales, ffn_own = [], [], []

    def middle_of(c, total):
        middle = inputs[own[c]] + total.astype(f32)
        scale = rms_scale(middle)
        normed = (middle * scale * ffn_gain).astype(bf16)
        middles.append(middle)
        scales.append(scale)
        ffn_own.append(normed)
        return normed

    ahead = Chain(middle_of(0, summed[0]))
    ahead.hop()
    after = gather_rows(middle_of(1, gate(summed[1], *ahead.recv())))
    ahead.hop(backs[0])
    ahead.hop(backs[1])
    ffn_all = [ahead.joined(), after]
    acts, dgates, dups, expert_grads = [], [], [], []
    for c in chunks:
        here = gate(chunk_of(routed, c), *backs, *acts[-1:])
        act, dgate, dup, grads = experts_block(ffn_all[c], backs[c], here, router_wide, w_gate, w_up)
        acts.append(act)
        dgates.append(dgate)
        dups.append(dup)
        expert_grads.append(grads)
    expert_grads[0] = scatter_rows(expert_grads[0])
    second_sums = ScatterChain(expert_grads[1])

    ffn_gain_parts, router_parts, middle_grads = [], [], []

    def middle_back(c, grads):
        share_grad = grads[:, features : features + experts] * routed_own[own[c]]
        probs = jax.nn.softmax(nn(ffn_own[c], router), axis=-1)
        logit_grad = (probs * (share_grad - jnp.sum(share_grad * probs, axis=-1, keepdims=True))).astype(bf16)
        ffn_grad = grads[:, :features] + nt(logit_grad, router)
        router_parts.append(tn(ffn_own[c], logit_grad))
        ffn_gain_parts.append(jnp.sum(ffn_grad * middles[c] * scales[c], axis=0))
        middle_grads.append(cotangent[own[c]].astype(f32) + norm_back(ffn_grad, middles[c], scales[c], ffn_gain))
        return Chain(middle_grads[c].astype(bf16))

    def expert_sums(lefts, rights, ids, *others, added=()):
        return wgrad(lefts, rights, gate(ids, *others), width, per, added)

    def core_swap(pieces):
        return [pair_swap(piece, 1) for piece in pieces]

    def halving(sums):
        return Halving([half.reshape((dp_size // 2, per) + half.shape[1:]) for half in sums])

    first = middle_back(0, gate(expert_grads[0], acts[1]).astype(f32))
    second_sums.hop()
    first.hop()
    gate_sent = expert_sums(ffn_all, dgates, theirs, first.values, *second_sums.sent)
    gate_got = core_swap(gate_sent)
    second_sums.hop(*gate_sent)
    up_sent = expert_sums(ffn_all, dups, theirs, *first.hop(*gate_sent), *second_sums.sent)
    up_got = core_swap(up_sent)
    second_sums.hop(*up_sent)
    down_sent = expert_sums(grad_all, acts, theirs, *first.hop(*up_sent), *second_sums.sent)
    down_got = core_swap(down_sent)
    second = middle_back(1, gate(second_sums.total(), *down_sent))
    second.hop()
    gate_sums = expert_sums(ffn_all, dgates, mine, second.values, *first.recv(), added=gate_got)
    gate_out = halving(gate_sums)
    up_sums = expert_sums(ffn_all, dups, mine, *second.hop(*gate_sums), *gate_out.send(), added=up_got)
    up_out = halving(up_sums)
    moe_0 = down(gate(acts[0], *second.hop(*up_sums), *up_out.send()), w_down)
    moe_sum_0 = scatter_rows(moe_0)
    middle_all = [first.joined(), second.joined()]

    attended_grad = in_order([nn(rows, w_out).astype(bf16) for rows in middle_all])
    gate_late = gate_out.add()
    gate_out.send()
    dqn, dkn, dvalue, qdot, kdot, q_gain_part, k_gain_part = attend_back(
        query, key, value, attended_grad, lse, qraw, kraw, q_scale, k_scale, q_gain, k_gain, cosine, sine,
        gate(seg_ids[0], moe_0, *gate_late), keep_mask[0],
    )
    dots = exchange_sum(jnp.stack([qdot[:, 0], kdot[:, 0]]), ("tensor",)) / features
    moe_1 = down(gate(acts[1], dqn), w_down)
    moe_sum_1 = scatter_rows(moe_1)
    up_late = up_out.add()
    up_out.send()
    down_sums = expert_sums(grad_all, acts, mine, dqn, moe_1, *up_late, added=down_got)
    down_out = halving(down_sums)
    down_out.send()
    normed_part, dqraw, dkraw, attn_gain_part = project_back(
        normed_all, dqn, dkn, dvalue, qraw, kraw, q_scale, k_scale, dots[0][:, None], dots[1][:, None],
        gate(q_gain, *down_sums), k_gain, w_query, w_key, w_value,
    )
    halves = [ScatterChain(chunk_of(normed_part, c)) for c in chunks]
    for _ in range(parts - 1):
        for half in halves:
            half.hop()
    normed_grad = jnp.concatenate([half.total() for half in halves])

    def attention_sums(ids, *others, added=None):
        return attention_wgrad(
            normed_all, middle_all, (dqraw, dkraw, dvalue), attended_parts, gate(ids, *others), dp_size, added
        )

    attn_sent = attention_sums(other_blocks, *(part for half in halves for part in half.first))
    attn_got = pair_swap(attn_sent, 1)

    def placed(part):
        return lax.dynamic_update_slice_in_dim(jnp.zeros((features,), f32), part, part_at * local_width, 0)

    smalls = [attn_gain_part[0] / attn_gain, placed(q_gain_part[0]), placed(k_gain_part[0]), sum(ffn_gain_parts)]
    smalls = gate(jnp.concatenate([jnp.stack(smalls), sum(router_parts).T]), attn_sent)
    smalls = exchange_sum(smalls, ("dp", "tensor"))
    attn_out = Halving(attention_sums(own_blocks, attn_sent, added=attn_got))
    attn_out.send()
    gate_done = gate_out.done()
    up_done = up_out.done()
    down_done = down_out.done()
    query_done, key_done, value_done, out_done = attn_out.done()
    layer_out = jnp.concatenate([middles[0] + moe_sum_0.astype(f32), middles[1] + moe_sum_1.astype(f32)]).astype(bf16)
    tokens_grad = jnp.concatenate(middle_grads) + norm_back(normed_grad, inputs, first_scale, attn_gain)
    return (
        layer_out, tokens_grad, query_done, key_done, value_done, out_done,
        smalls[0], smalls[1], smalls[2], smalls[3], smalls[4:].T, gate_done, up_done, down_done,
    )


def solution(mesh):
    rows = P(("dp", "tensor"), None)
    column = P(None, "tensor")
    expert = P(None, None, "tensor")
    in_specs = (
        rows, rows, P("dp", None), P("dp", None), P("dp", None), P(), column, column, column, column,
        P("tensor"), P("tensor"), P(), P(), expert, expert, expert,
    )
    block = P("dp", "tensor")
    expert_out = P("dp", None, "tensor")
    out_specs = (
        rows, rows, block, block, block, block, P(), P(), P(), P(), P(), expert_out, expert_out, expert_out,
    )
    return jax.shard_map(local, mesh=mesh, in_specs=in_specs, out_specs=out_specs, check_vma=False)
```

```python
import functools

import jax
import jax.numpy as jnp
from jax import lax
from jax.experimental import pallas as pl
from jax.experimental.pallas import tpu as pltpu
from jax.sharding import PartitionSpec as P

D = 2048
HEAD = 128
DOC = 512
LANES = 128
EPSILON = 1e-05
MASKED = -1e30
CHUNKS = 2
VMEM = 56 * 1024 * 1024
bf16 = jnp.bfloat16
f32 = jnp.float32


def nn(left, right):
    return lax.dot_general(left, right, (((1,), (0,)), ((), ())), preferred_element_type=f32)


def nt(left, right):
    return lax.dot_general(left, right, (((1,), (1,)), ((), ())), preferred_element_type=f32)


def tn(left, right):
    return lax.dot_general(left, right, (((0,), (0,)), ((), ())), preferred_element_type=f32)


def params():
    return pltpu.CompilerParams(vmem_limit_bytes=VMEM)


PACE = 0.3


def cost(flops, moved, special=0):
    return pl.CostEstimate(flops=int(1.5 * PACE * flops + 6e4 * PACE * special), bytes_accessed=moved // 8, transcendentals=0)


def rms_scale(values):
    return lax.rsqrt(jnp.mean(values * values, axis=-1, keepdims=True) + EPSILON)


def norm_back(grad_values, values, scale_col, gain_vec):
    weighted = grad_values * gain_vec
    inner_mean = jnp.mean(weighted * values, axis=-1, keepdims=True)
    return scale_col * weighted - values * (scale_col * scale_col * scale_col) * inner_mean


def rope_tables(length, width):
    half_width = width // 2
    frequency = jnp.power(10000.0, -jnp.arange(half_width, dtype=f32) * 2.0 / width)
    angles = jnp.arange(length, dtype=f32)[:, None] * frequency[None, :]
    cosine, sine = jnp.cos(angles), jnp.sin(angles)
    return jnp.concatenate([cosine, cosine], axis=1), jnp.concatenate([-sine, sine], axis=1)


def key_start(query_start):
    return max(0, query_start - DOC)


def fill_bias(bias, seg_col, seg_row, keep_row, block):
    length = seg_col.shape[0]
    for start in range(0, length, block):
        first, stop = key_start(start), start + block
        query_pos = start + lax.broadcasted_iota(jnp.int32, (block, stop - first), 0)
        key_pos = first + lax.broadcasted_iota(jnp.int32, (block, stop - first), 1)
        same = seg_col[start:stop, :] == seg_row[:, first:stop]
        live = (keep_row[:, first:stop] == 1) | (key_pos == query_pos)
        allowed = same & live & (key_pos <= query_pos)
        bias[start:stop, : stop - first] = jnp.where(allowed, 0.0, MASKED)


def turned(values):
    return pltpu.roll(values, values.shape[1] // 2, 1)


def project_kernel(rows_in, w_query, w_key, w_value, q_out, k_out, v_out, squares_out):
    ones = jnp.ones((8, q_out.shape[1]), f32)
    for at, (weight, out) in enumerate(((w_query, q_out), (w_key, k_out))):
        raw = nn(rows_in[...], weight[...])
        out[...] = raw
        sums = lax.dot_general(
            ones, raw * raw, (((1,), (1,)), ((), ())), precision=lax.Precision.HIGHEST, preferred_element_type=f32
        )
        squares_out[at : at + 1, :] = sums[:1]
    v_out[...] = nn(rows_in[...], w_value[...]).astype(bf16)


def project(rows_in, w_query, w_key, w_value):
    rows, features = rows_in.shape
    width = w_query.shape[1]
    block = min(256, rows)
    row = lambda columns: pl.BlockSpec((block, columns), lambda r: (r, 0))
    weight = pl.BlockSpec((features, width), lambda r: (0, 0))
    sds = jax.ShapeDtypeStruct
    return pl.pallas_call(
        project_kernel,
        grid=(rows // block,),
        in_specs=[row(features), weight, weight, weight],
        out_specs=[row(width), row(width), row(width), pl.BlockSpec((2, block), lambda r: (0, r))],
        out_shape=[sds((rows, width), f32), sds((rows, width), f32), sds((rows, width), bf16), sds((2, rows), f32)],
        compiler_params=params(),
        cost_estimate=cost(6 * rows * features * width, 2 * (rows + 3 * width) * features),
        name="project",
    )(rows_in, w_query, w_key, w_value)


def project_back_kernel(
    rows_in, dqn, dkn, dvalue, qraw, kraw, q_scale, k_scale, q_dot, k_dot, q_gain, k_gain,
    w_query, w_key, w_value, part_out, dq_out, dk_out, gain_out,
):
    @pl.when(pl.program_id(0) == 0)
    def _():
        gain_out[...] = jnp.zeros_like(gain_out)

    def raw_grad(grad, raw, scale, gain, dot):
        cube = scale[...] * scale[...] * scale[...]
        return (scale[...] * (gain[...] * grad[...]) - raw[...] * (cube * dot[...])).astype(bf16)

    dq = raw_grad(dqn, qraw, q_scale, q_gain, q_dot)
    dk = raw_grad(dkn, kraw, k_scale, k_gain, k_dot)
    dq_out[...] = dq
    dk_out[...] = dk
    part = nt(dq, w_query[...]) + nt(dk, w_key[...]) + nt(dvalue[...], w_value[...])
    part_out[...] = part.astype(bf16)
    gain_out[...] += jnp.sum(part * rows_in[...].astype(f32), axis=0, keepdims=True)


def project_back(rows_in, dqn, dkn, dvalue, qraw, kraw, q_scale, k_scale, q_dot, k_dot, q_gain, k_gain, w_query, w_key, w_value):
    rows, features = rows_in.shape
    width = w_query.shape[1]
    block = min(256, rows)
    row = lambda columns: pl.BlockSpec((block, columns), lambda r: (r, 0))
    whole = lambda *shape: pl.BlockSpec(shape, lambda r: (0, 0))
    sds = jax.ShapeDtypeStruct
    return pl.pallas_call(
        project_back_kernel,
        grid=(rows // block,),
        in_specs=[row(features)] + [row(width)] * 5 + [row(1)] * 4 + [whole(1, width)] * 2 + [whole(features, width)] * 3,
        out_specs=[row(features), row(width), row(width), whole(1, features)],
        out_shape=[sds((rows, features), bf16), sds((rows, width), bf16), sds((rows, width), bf16), sds((1, features), f32)],
        compiler_params=params(),
        cost_estimate=cost(6 * rows * features * width, 2 * (rows + 3 * width) * features),
        name="project_back",
    )(rows_in, dqn, dkn, dvalue, qraw, kraw, q_scale, k_scale, q_dot, k_dot, q_gain[None], k_gain[None], w_query, w_key, w_value)


def attention_wgrad_kernel(count, extra, order, *refs):
    rows_in = refs[0]
    middles = refs[1 : 1 + count]
    sides = refs[1 + count : 4 + count]
    attended = refs[4 + count : 4 + 2 * count]
    outs = refs[4 + 2 * count + extra :]
    totals = [tn(rows_in[...], side[...]) for side in sides]
    total = tn(middles[0][...], attended[0][...])
    for left, right in zip(middles[1:], attended[1:]):
        total = total + tn(left[...], right[...])
    totals.append(total)
    half = outs[0].shape[2]
    for at, total in enumerate(totals):
        if extra:
            total = total + refs[4 + 2 * count][0, at].astype(f32)
        for place, out in enumerate(outs):
            out[0, at] = total[place * half : (place + 1) * half, :].astype(bf16)


def attention_wgrad(rows_in, middles, sides, attended, order, blocks, added=None):
    features = rows_in.shape[1]
    width = sides[0].shape[1]
    block = features // blocks
    extra = [] if added is None else [added]
    outs = 1 + len(extra)
    left = lambda values: pl.BlockSpec((values.shape[0], block), lambda i, ids: (0, ids[i]))
    right = lambda values: pl.BlockSpec(values.shape, lambda i, ids: (0, 0))
    out = lambda parts: pl.BlockSpec((1, 4, block // parts, width), lambda i, ids: (i, 0, 0, 0))
    result = pl.pallas_call(
        functools.partial(attention_wgrad_kernel, len(middles), len(extra)),
        grid_spec=pltpu.PrefetchScalarGridSpec(
            num_scalar_prefetch=1,
            grid=(order.shape[0],),
            in_specs=[left(rows_in)] + [left(m) for m in middles] + [right(v) for v in sides] + [right(v) for v in attended]
            + [out(1) for _ in extra],
            out_specs=[out(outs)] * outs,
        ),
        out_shape=[jax.ShapeDtypeStruct((order.shape[0], 4, block // outs, width), bf16)] * outs,
        compiler_params=params(),
        cost_estimate=cost(8 * rows_in.shape[0] * features * width, 4 * features * width),
        name="attention_wgrad",
    )(order, rows_in, *middles, *sides, *attended, *extra)
    return result if extra else result[0]


def attend_kernel(
    block, qraw, kraw, value, q_scale, k_scale, q_gain, k_gain, cosine, sine,
    seg_col, seg_row, keep_row, q_out, k_out, o_out, lse_out, bias,
):
    @pl.when(pl.program_id(0) == 0)
    def _():
        fill_bias(bias, seg_col, seg_row, keep_row, block)

    def rotated(raw, scale, gain):
        normed = raw[...] * scale[...] * gain[...]
        return (normed * cosine[...] + turned(normed) * sine[...]).astype(bf16)

    q_out[...] = rotated(qraw, q_scale, q_gain)
    k_out[...] = rotated(kraw, k_scale, k_gain)
    length = seg_col.shape[0]
    for start in range(0, length, block):
        first, stop = key_start(start), start + block
        scores = nt(q_out[start:stop, :], k_out[first:stop, :]) * HEAD ** (-0.5)
        scores = scores + bias[start:stop, : stop - first]
        top = jnp.max(scores, axis=1, keepdims=True)
        powers = jnp.exp(scores - top)
        total = jnp.sum(powers, axis=1, keepdims=True)
        weights = (powers * (1.0 / total)).astype(bf16)
        o_out[start:stop, :] = nn(weights, value[first:stop, :]).astype(bf16)
        lse_out[start:stop, :] = jnp.broadcast_to(top + jnp.log(total), (block, HEAD))


def attend(qraw, kraw, value, q_scale, k_scale, q_gain, k_gain, cosine, sine, seg, keep):
    length, width = qraw.shape
    block = min(256, length)
    span = min(DOC + block, length)
    head = pl.BlockSpec((length, HEAD), lambda h: (0, h))
    gain = pl.BlockSpec((1, HEAD), lambda h: (0, h))
    whole = lambda *shape: pl.BlockSpec(shape, lambda h: (0, 0))
    return pl.pallas_call(
        functools.partial(attend_kernel, block),
        grid=(width // HEAD,),
        in_specs=[head, head, head, whole(length, 1), whole(length, 1), gain, gain]
        + [whole(length, HEAD), whole(length, HEAD), whole(length, 1), whole(1, length), whole(1, length)],
        out_specs=[head, head, head, head],
        out_shape=[jax.ShapeDtypeStruct((length, width), t) for t in (bf16, bf16, bf16, f32)],
        scratch_shapes=[pltpu.VMEM((length, span), f32)],
        compiler_params=params(),
        cost_estimate=cost(4 * length * span * width, 18 * length * width, length * span * width // HEAD),
        name="attend",
    )(qraw, kraw, value, q_scale, k_scale, q_gain[None], k_gain[None], cosine, sine, seg[:, None], seg[None], keep[None])


def attend_back_kernel(
    block, query, key, value, out_grad, lse, qraw, kraw, q_scale, k_scale, q_gain, k_gain, cosine, sine,
    seg_col, seg_row, keep_row, dq_out, dk_out, dv_out, qdot_out, kdot_out, qg_out, kg_out, bias, dk_sum, dv_sum,
):
    at = pl.program_id(0)

    @pl.when(at == 0)
    def _():
        fill_bias(bias, seg_col, seg_row, keep_row, block)
        qdot_out[...] = jnp.zeros_like(qdot_out)
        kdot_out[...] = jnp.zeros_like(kdot_out)

    dk_sum[...] = jnp.zeros_like(dk_sum)
    dv_sum[...] = jnp.zeros_like(dv_sum)
    length = seg_col.shape[0]
    scale = HEAD ** (-0.5)
    for start in range(0, length, block):
        first, stop = key_start(start), start + block
        rows, keys = slice(start, stop), slice(first, stop)
        scores = nt(query[rows, :], key[keys, :]) * scale + bias[rows, : stop - first]
        weights = jnp.exp(scores - lse[rows, :1])
        prob_grad = nt(out_grad[rows, :], value[keys, :])
        inner = jnp.sum(weights * prob_grad, axis=1, keepdims=True)
        score_grad = (weights * (prob_grad - inner)).astype(bf16)
        dq_out[rows, :] = nn(score_grad, key[keys, :]) * scale
        dk_sum[keys, :] += tn(score_grad, query[rows, :])
        dv_sum[keys, :] += tn(weights.astype(bf16), out_grad[rows, :])

    def unrotated(grad):
        return grad * cosine[...] + turned(grad * sine[...])

    dv_out[...] = dv_sum[...].astype(bf16)
    dq = unrotated(dq_out[...])
    dk = unrotated(dk_sum[...] * scale)
    dq_out[...] = dq
    dk_out[...] = dk
    dq = dq * qraw[...]
    dk = dk * kraw[...]
    qg_out[...] = jnp.sum(dq * q_scale[...], axis=0, keepdims=True)
    kg_out[...] = jnp.sum(dk * k_scale[...], axis=0, keepdims=True)
    qdot_out[...] += jnp.sum(dq * q_gain[...], axis=1, keepdims=True)
    kdot_out[...] += jnp.sum(dk * k_gain[...], axis=1, keepdims=True)


def attend_back(query, key, value, out_grad, lse, qraw, kraw, q_scale, k_scale, q_gain, k_gain, cosine, sine, seg, keep):
    length, width = qraw.shape
    block = min(256, length)
    span = min(DOC + block, length)
    head = pl.BlockSpec((length, HEAD), lambda h: (0, h))
    gain = pl.BlockSpec((1, HEAD), lambda h: (0, h))
    whole = lambda *shape: pl.BlockSpec(shape, lambda h: (0, 0))
    sds = jax.ShapeDtypeStruct
    return pl.pallas_call(
        functools.partial(attend_back_kernel, block),
        grid=(width // HEAD,),
        in_specs=[head] * 7
        + [whole(length, 1), whole(length, 1), gain, gain]
        + [whole(length, HEAD), whole(length, HEAD), whole(length, 1), whole(1, length), whole(1, length)],
        out_specs=[head, head, head, whole(length, 1), whole(length, 1), gain, gain],
        out_shape=[sds((length, width), f32), sds((length, width), f32), sds((length, width), bf16)]
        + [sds((length, 1), f32), sds((length, 1), f32), sds((1, width), f32), sds((1, width), f32)],
        scratch_shapes=[pltpu.VMEM((length, span), f32), pltpu.VMEM((length, HEAD), f32), pltpu.VMEM((length, HEAD), f32)],
        compiler_params=params(),
        cost_estimate=cost(10 * length * span * width, 32 * length * width, length * span * width // HEAD),
        name="attend_back",
    )(query, key, value, out_grad, lse, qraw, kraw, q_scale, k_scale, q_gain[None], k_gain[None], cosine, sine, seg[:, None], seg[None], keep[None])


def up_back_kernel(grad, down_w, out):
    width = down_w.shape[2]
    for at in range(down_w.shape[0]):
        out[:, at * width : (at + 1) * width] = nn(grad[...], down_w[at]).astype(out.dtype)


def up_back(grad, down_w):
    rows, features = grad.shape
    experts, _, width = down_w.shape
    step = 2 if experts % 2 == 0 else 1
    return pl.pallas_call(
        up_back_kernel,
        grid=(experts // step,),
        in_specs=[pl.BlockSpec((rows, features), lambda e: (0, 0)), pl.BlockSpec((step, features, width), lambda e: (e, 0, 0))],
        out_specs=pl.BlockSpec((rows, step * width), lambda e: (0, e)),
        out_shape=jax.ShapeDtypeStruct((rows, experts * width), bf16),
        compiler_params=params(),
        cost_estimate=cost(2 * rows * features * experts * width, 2 * (rows + experts * width) * features),
        name="up_back",
    )(grad, down_w)


def expert_kernel(block, rows_in, back, routed, router, gate_w, up_w, act_out, dgate_out, dup_out, grad_out, comb, dcomb, total):
    at = pl.program_id(0)
    rows, features = rows_in.shape
    lane = lax.broadcasted_iota(jnp.int32, (block, LANES), 1)

    @pl.when(at == 0)
    def _():
        experts = pl.num_programs(0)
        for start in range(0, rows, block):
            here = slice(start, start + block)
            logits = jnp.where(lane < experts, nn(rows_in[here, :], router[...]), MASKED)
            powers = jnp.exp(logits - jnp.max(logits, axis=1, keepdims=True))
            probs = powers / jnp.sum(powers, axis=1, keepdims=True)
            comb[here, :] = probs * routed[here, :]
        total[...] = jnp.zeros_like(total)
        dcomb[...] = jnp.zeros_like(dcomb)

    gate, up = gate_w[0], up_w[0]
    mine = lane == at
    for start in range(0, rows, block):
        here = slice(start, start + block)
        taken = rows_in[here, :]
        pre_gate = nn(taken, gate)
        pre_up = nn(taken, up)
        behind = back[here, :].astype(f32)
        share = jnp.sum(jnp.where(mine, comb[here, :], 0.0), axis=1, keepdims=True)
        sigmoid = 0.5 * jnp.tanh(0.5 * pre_gate) + 0.5
        active = pre_gate * sigmoid
        inner = active * pre_up
        share_grad = jnp.sum(inner * behind, axis=1, keepdims=True)
        dcomb[here, :] = jnp.where(mine, share_grad, dcomb[here, :])
        act_out[here, :] = (inner * share).astype(bf16)
        inner_grad = behind * share
        dgate = (inner_grad * pre_up * (sigmoid + active * (1.0 - sigmoid))).astype(bf16)
        dup = (inner_grad * active).astype(bf16)
        dgate_out[here, :] = dgate
        dup_out[here, :] = dup
        total[here, :] += nt(dgate, gate) + nt(dup, up)

    @pl.when(at == pl.num_programs(0) - 1)
    def _():
        grad_out[:, :features] = total[...].astype(bf16)
        grad_out[:, features:] = dcomb[...].astype(bf16)


def experts_block(rows_in, back, routed, router, gate_w, up_w):
    rows, features = rows_in.shape
    experts, _, width = gate_w.shape
    block = min(512, rows)
    whole = lambda *shape: pl.BlockSpec(shape, lambda e: (0, 0))
    column = pl.BlockSpec((rows, width), lambda e: (0, e))
    weight = pl.BlockSpec((1, features, width), lambda e: (e, 0, 0))
    wide = jax.ShapeDtypeStruct((rows, experts * width), bf16)
    return pl.pallas_call(
        functools.partial(expert_kernel, block),
        grid=(experts,),
        in_specs=[whole(rows, features), column, whole(rows, LANES), whole(features, LANES), weight, weight],
        out_specs=[column, column, column, whole(rows, features + LANES)],
        out_shape=[wide, wide, wide, jax.ShapeDtypeStruct((rows, features + LANES), bf16)],
        scratch_shapes=[pltpu.VMEM((rows, LANES), f32), pltpu.VMEM((rows, LANES), f32), pltpu.VMEM((rows, features), f32)],
        compiler_params=params(),
        cost_estimate=cost(8 * rows * features * experts * width, 4 * experts * width * (features + 2 * rows), rows * experts * width),
        name="experts",
    )(rows_in, back, routed, router, gate_w, up_w)


def wgrad_kernel(count, extra, per, block, order, *refs):
    lefts, rights = refs[:count], refs[count : 2 * count]
    added = refs[2 * count : 2 * count + extra]
    outs = refs[2 * count + extra :]
    at = pl.program_id(0)
    features = lefts[0].shape[1]

    def piece(start, stop):
        total = tn(lefts[0][:, start:stop], rights[0][...])
        for left, right in zip(lefts[1:], rights[1:]):
            total = total + tn(left[:, start:stop], right[...])
        return total

    if not added:
        for place, out in enumerate(outs):

            @pl.when(at // per == place)
            def _(out=out):
                for start in range(0, features, block):
                    out[0, start : start + block, :] = piece(start, start + block).astype(bf16)

        return
    half = features // 2
    for place, got in enumerate(added):

        @pl.when(at // per == place)
        def _(got=got):
            for start in range(0, features, block):
                total = piece(start, start + block) + got[0, start : start + block, :].astype(f32)
                outs[start // half][0, start % half : start % half + block, :] = total.astype(bf16)


def wgrad(lefts, rights, order, width, per, added=()):
    features = lefts[0].shape[1]
    experts = order.shape[0]
    groups = experts // per
    rows = sum(left.shape[0] for left in lefts)

    def group_spec(place):
        return pl.BlockSpec((1, features, width), lambda i, ids: (jnp.clip(i - place * per, 0, per - 1), 0, 0))

    groups_specs = [group_spec(place) for place in range(groups)]
    if added:
        out_specs = [pl.BlockSpec((1, features // 2, width), lambda i, ids: (i, 0, 0))] * 2
        out_shape = [jax.ShapeDtypeStruct((experts, features // 2, width), bf16)] * 2
    else:
        out_specs = groups_specs
        out_shape = [jax.ShapeDtypeStruct((per, features, width), bf16)] * groups
    return pl.pallas_call(
        functools.partial(wgrad_kernel, len(lefts), len(added), per, min(512, features // 2)),
        grid_spec=pltpu.PrefetchScalarGridSpec(
            num_scalar_prefetch=1,
            grid=(experts,),
            in_specs=[pl.BlockSpec(left.shape, lambda i, ids: (0, 0)) for left in lefts]
            + [pl.BlockSpec((right.shape[0], width), lambda i, ids: (0, ids[i])) for right in rights]
            + (groups_specs if added else []),
            out_specs=out_specs,
        ),
        out_shape=out_shape,
        compiler_params=params(),
        cost_estimate=cost(2 * rows * features * experts * width, 2 * (rows + 2 * experts * width) * features),
        name="wgrad",
    )(order, *lefts, *rights, *added)


def down_kernel(act, down_w, out):
    joined = jnp.concatenate([down_w[e] for e in range(down_w.shape[0])], axis=1)
    out[...] = nt(act[...], joined).astype(out.dtype)


def down(act, down_w):
    rows = act.shape[0]
    experts, features, width = down_w.shape
    block = min(256, features)
    return pl.pallas_call(
        down_kernel,
        grid=(features // block,),
        in_specs=[pl.BlockSpec(act.shape, lambda n: (0, 0)), pl.BlockSpec((experts, block, width), lambda n: (0, n, 0))],
        out_specs=pl.BlockSpec((rows, block), lambda n: (0, n)),
        out_shape=jax.ShapeDtypeStruct((rows, features), bf16),
        compiler_params=params(),
        cost_estimate=cost(2 * rows * features * experts * width, 2 * (rows + experts * width) * features),
        name="down",
    )(act, down_w)


def gate(value, *others):
    return lax.optimization_barrier((value, others))[0]


def gather_rows(values):
    return lax.all_gather(values, "tensor", axis=0, tiled=True)


def scatter_rows(values):
    return lax.psum_scatter(values, "tensor", scatter_dimension=0, tiled=True)


def join_kernel(parts, slots, own, *refs):
    ups, downs, out = refs[: parts - 1], refs[parts - 1 : 2 * parts - 2], refs[2 * parts - 2]
    at = pl.program_id(0)

    @pl.when(at == 0)
    def _():
        out[...] = own[...]

    for step in range(1, parts):

        @pl.when(at == step)
        def _(step=step):
            out[...] = ups[step - 1][...] + downs[parts - 1 - step][...]


def join(slots, own, ups, downs):
    rows, columns = own.shape
    parts = len(ups) + 1
    whole = pl.BlockSpec((rows, columns), lambda i, to: (0, 0))
    return pl.pallas_call(
        functools.partial(join_kernel, parts),
        grid_spec=pltpu.PrefetchScalarGridSpec(
            num_scalar_prefetch=1,
            grid=(parts,),
            in_specs=[whole] * (2 * parts - 1),
            out_specs=pl.BlockSpec((rows, columns), lambda i, to: (to[i], 0)),
        ),
        out_shape=jax.ShapeDtypeStruct((parts * rows, columns), own.dtype),
        compiler_params=params(),
        cost_estimate=cost(0, 0),
        name="join",
    )(slots, own, *ups, *downs)


class Chain:
    def __init__(self, values):
        self.values = values
        self.parts = lax.axis_size("tensor")
        self.ups, self.downs = [values], [values]

    def hop(self, *others):
        step = len(self.ups)
        if step < self.parts:
            up, down = gate((self.ups[-1], self.downs[-1]), *others) if others else (self.ups[-1], self.downs[-1])
            self.sent = (up, down)
            self.ups.append(lax.ppermute(up, "tensor", [(i, i + 1) for i in range(step - 1, self.parts - 1)]))
            self.downs.append(lax.ppermute(down, "tensor", [(i, i - 1) for i in range(1, self.parts - step + 1)]))
        return self.sent

    def recv(self):
        return self.ups[-1], self.downs[-1]

    def joined(self):
        while len(self.ups) < self.parts:
            self.hop()
        at = lax.axis_index("tensor")
        slots = lax.rem(at - jnp.arange(self.parts, dtype=jnp.int32) + self.parts, self.parts)
        return join(slots, self.values, self.ups[1:], self.downs[1:])


def pair_swap(values, step):
    size = lax.axis_size("dp")
    return lax.ppermute(values, "dp", [(i, i ^ step) for i in range(size)])


class Halving:
    def __init__(self, values):
        bits = list(range(values[0].shape[0].bit_length() - 1))
        self.kept = list(values)
        self.left = [bits[::-1], bits]
        self.got = None

    def send(self):
        if not self.left[0]:
            return ()
        self.got = []
        sent = []
        for side, downward in ((0, True), (1, False)):
            bit = self.left[side].pop(0)
            kept = self.kept[side]
            half = kept.shape[0] // 2
            if downward:
                keep, go = kept[:half], kept[half:]
            else:
                view = kept.reshape((half, 2) + kept.shape[1:])
                keep, go = view[:, 0], view[:, 1]
            sent.append(go)
            self.got.append(pair_swap(go, 2 << bit))
            self.kept[side] = keep
        return tuple(sent)

    def add(self):
        if self.got is not None:
            last = not self.left[0]
            for side in range(2):
                total = self.kept[side].astype(f32) + self.got[side].astype(f32)
                self.kept[side] = total if last else total.astype(bf16)
            self.got = None
        return tuple(self.kept)

    def done(self):
        self.add()
        while self.left[0]:
            self.send()
            self.add()
        return jnp.concatenate([kept[0].astype(f32) for kept in self.kept], axis=1)


def exchange_sum(values, axes):
    for axis in axes:
        size = lax.axis_size(axis)
        step = 1
        while step < size:
            values = values + lax.ppermute(values, axis, [(i, i ^ step) for i in range(size)])
            step *= 2
    return values


def local(
    tokens, cotangent, seg_ids, keep_mask, routes, attn_gain, w_query, w_key, w_value, w_out,
    q_gain, k_gain, ffn_gain, router, w_gate, w_up, w_down,
):
    parts = lax.axis_size("tensor")
    part_at = lax.axis_index("tensor")
    dp_size = lax.axis_size("dp")
    low_bit = lax.axis_index("dp") % 2
    shard_rows, features = tokens.shape
    group_rows = shard_rows * parts
    _, length = seg_ids.shape
    local_width = w_query.shape[1]
    experts, _, width = w_gate.shape
    per = experts // dp_size
    chunk_rows = shard_rows // CHUNKS
    chunks = range(CHUNKS)
    own = [slice(c * chunk_rows, (c + 1) * chunk_rows) for c in chunks]

    def chunk_of(values, c):
        columns = values.shape[1]
        return values.reshape(parts, CHUNKS, chunk_rows, columns)[:, c].reshape(parts * chunk_rows, columns)

    def in_order(pieces):
        columns = pieces[0].shape[1]
        stacked = jnp.stack([piece.reshape(parts, chunk_rows, columns) for piece in pieces], axis=1)
        return stacked.reshape(group_rows, columns)

    inputs = tokens.astype(f32)
    first_scale = rms_scale(inputs)
    normed_all = gather_rows((inputs * first_scale * attn_gain).astype(bf16))
    behind = Chain(gate(cotangent, normed_all))

    expert_ids = jnp.arange(LANES)
    routed = jnp.sum((routes[:, :, None] == expert_ids[None, None, :]).astype(f32), axis=1)
    router_wide = jnp.pad(router, ((0, 0), (0, LANES - experts)))
    routed_own = lax.dynamic_slice_in_dim(routed, part_at * shard_rows, shard_rows, 0)[:, :experts]
    cosine, sine = rope_tables(length, HEAD)
    normed_all = gate(normed_all, routed, router_wide, cosine, sine)

    relative = jnp.arange(dp_size // 2, dtype=jnp.int32) ^ (lax.axis_index("dp") // 2)
    own_blocks, other_blocks = 2 * relative + low_bit, 2 * relative + 1 - low_bit
    mine, theirs = (
        (blocks[:, None] * per + jnp.arange(per, dtype=jnp.int32)).reshape(-1) for blocks in (own_blocks, other_blocks)
    )

    qraw, kraw, value, squares = project(normed_all, w_query, w_key, w_value)
    squares = exchange_sum(squares, ("tensor",))
    behind.hop()
    q_scale, k_scale = (lax.rsqrt(squares[i] / features + EPSILON)[:, None] for i in range(2))
    query, key, attended, lse = attend(
        qraw, kraw, value, q_scale, k_scale, q_gain, k_gain, cosine, sine, gate(seg_ids[0], *behind.recv()), keep_mask[0]
    )
    behind.hop()
    attended_parts = [chunk_of(gate(attended, *behind.recv()), c) for c in chunks]
    outs = [nt(attended_parts[0], w_out).astype(bf16)]
    summed = [scatter_rows(outs[0])]
    outs.append(nt(gate(attended_parts[1], outs[0]), w_out).astype(bf16))
    summed.append(scatter_rows(outs[1]))
    behind.hop(outs[1])

    grad_group = behind.joined()
    grad_all = [chunk_of(grad_group, c) for c in chunks]
    backs = [up_back(grad_all[0], w_down)]

    middles, scales, ffn_own = [], [], []

    def middle_of(c, total):
        middle = inputs[own[c]] + total.astype(f32)
        scale = rms_scale(middle)
        normed = (middle * scale * ffn_gain).astype(bf16)
        middles.append(middle)
        scales.append(scale)
        ffn_own.append(normed)
        return normed

    ahead = Chain(middle_of(0, gate(summed[0], backs[0])))
    ahead.hop()
    backs.append(up_back(gate(grad_all[1], ahead.values), w_down))
    after = gather_rows(middle_of(1, gate(summed[1], *ahead.recv())))
    ahead.hop(backs[1])
    ahead.hop()
    ffn_all = [ahead.joined(), after]
    acts, dgates, dups, expert_grads = [], [], [], []
    for c in chunks:
        here = gate(chunk_of(routed, c), *backs, *acts[-1:])
        act, dgate, dup, grads = experts_block(ffn_all[c], backs[c], here, router_wide, w_gate, w_up)
        acts.append(act)
        dgates.append(dgate)
        dups.append(dup)
        expert_grads.append(grads)
    expert_grads = [scatter_rows(grads) for grads in expert_grads]

    ffn_gain_parts, router_parts, middle_grads = [], [], []

    def middle_back(c, grads):
        share_grad = grads[:, features : features + experts] * routed_own[own[c]]
        probs = jax.nn.softmax(nn(ffn_own[c], router), axis=-1)
        logit_grad = (probs * (share_grad - jnp.sum(share_grad * probs, axis=-1, keepdims=True))).astype(bf16)
        ffn_grad = grads[:, :features] + nt(logit_grad, router)
        router_parts.append(tn(ffn_own[c], logit_grad))
        ffn_gain_parts.append(jnp.sum(ffn_grad * middles[c] * scales[c], axis=0))
        middle_grads.append(cotangent[own[c]].astype(f32) + norm_back(ffn_grad, middles[c], scales[c], ffn_gain))
        return Chain(middle_grads[c].astype(bf16))

    def expert_sums(lefts, rights, ids, *others, added=()):
        return wgrad(lefts, rights, gate(ids, *others), width, per, added)

    def core_swap(pieces):
        return [pair_swap(piece, 1) for piece in pieces]

    def halving(sums):
        return Halving([half.reshape((dp_size // 2, per) + half.shape[1:]) for half in sums])

    first = middle_back(0, gate(expert_grads[0], acts[1]).astype(f32))
    first.hop()
    gate_sent = expert_sums(ffn_all, dgates, theirs, first.values)
    gate_got = core_swap(gate_sent)
    up_sent = expert_sums(ffn_all, dups, theirs, *first.hop(*gate_sent))
    up_got = core_swap(up_sent)
    moe_0 = down(gate(acts[0], *first.hop(*up_sent)), w_down)
    moe_sum_0 = scatter_rows(moe_0)
    second = middle_back(1, gate(expert_grads[1], moe_0, *first.recv()).astype(f32))
    second.hop()
    gate_sums = expert_sums(ffn_all, dgates, mine, second.values, added=gate_got)
    gate_out = halving(gate_sums)
    up_sums = expert_sums(ffn_all, dups, mine, *second.hop(*gate_sums), *gate_out.send(), added=up_got)
    up_out = halving(up_sums)
    moe_1 = down(gate(acts[1], *second.hop(*up_sums), *up_out.send()), w_down)
    moe_sum_1 = scatter_rows(moe_1)
    middle_all = [first.joined(), second.joined()]

    attended_grad = in_order([nn(rows, w_out).astype(bf16) for rows in middle_all])
    dqn, dkn, dvalue, qdot, kdot, q_gain_part, k_gain_part = attend_back(
        query, key, value, attended_grad, lse, qraw, kraw, q_scale, k_scale, q_gain, k_gain, cosine, sine,
        gate(seg_ids[0], moe_1), keep_mask[0],
    )
    dots = exchange_sum(jnp.stack([qdot[:, 0], kdot[:, 0]]), ("tensor",)) / features
    gate_late = gate_out.add()
    gate_out.send()
    down_sent = expert_sums(grad_all, acts, theirs, dqn, *gate_late)
    down_got = core_swap(down_sent)
    normed_part, dqraw, dkraw, attn_gain_part = project_back(
        normed_all, dqn, dkn, dvalue, qraw, kraw, q_scale, k_scale, dots[0][:, None], dots[1][:, None],
        gate(q_gain, *down_sent), k_gain, w_query, w_key, w_value,
    )
    normed_grad = scatter_rows(normed_part)
    up_late = up_out.add()
    up_out.send()
    down_sums = expert_sums(grad_all, acts, mine, normed_part, *up_late, added=down_got)
    down_out = halving(down_sums)
    down_out.send()

    def attention_sums(ids, *others, added=None):
        return attention_wgrad(
            normed_all, middle_all, (dqraw, dkraw, dvalue), attended_parts, gate(ids, *others), dp_size, added
        )

    attn_sent = attention_sums(other_blocks, *down_sums)
    attn_got = pair_swap(attn_sent, 1)

    def placed(part):
        return lax.dynamic_update_slice_in_dim(jnp.zeros((features,), f32), part, part_at * local_width, 0)

    smalls = [attn_gain_part[0] / attn_gain, placed(q_gain_part[0]), placed(k_gain_part[0]), sum(ffn_gain_parts)]
    smalls = gate(jnp.concatenate([jnp.stack(smalls), sum(router_parts).T]), attn_sent)
    smalls = exchange_sum(smalls, ("dp", "tensor"))
    attn_out = Halving(attention_sums(own_blocks, attn_sent, added=attn_got))
    normed_grad = gate(normed_grad, *attn_out.send())
    gate_done = gate_out.done()
    up_done = up_out.done()
    down_done = down_out.done()
    query_done, key_done, value_done, out_done = attn_out.done()
    layer_out = jnp.concatenate([middles[0] + moe_sum_0.astype(f32), middles[1] + moe_sum_1.astype(f32)]).astype(bf16)
    tokens_grad = jnp.concatenate(middle_grads) + norm_back(normed_grad.astype(f32), inputs, first_scale, attn_gain)
    return (
        layer_out, tokens_grad, query_done, key_done, value_done, out_done,
        smalls[0], smalls[1], smalls[2], smalls[3], smalls[4:].T, gate_done, up_done, down_done,
    )


def solution(mesh):
    rows = P(("dp", "tensor"), None)
    column = P(None, "tensor")
    expert = P(None, None, "tensor")
    in_specs = (
        rows, rows, P("dp", None), P("dp", None), P("dp", None), P(), column, column, column, column,
        P("tensor"), P("tensor"), P(), P(), expert, expert, expert,
    )
    block = P("dp", "tensor")
    expert_out = P("dp", None, "tensor")
    out_specs = (
        rows, rows, block, block, block, block, P(), P(), P(), P(), P(), expert_out, expert_out, expert_out,
    )
    return jax.shard_map(local, mesh=mesh, in_specs=in_specs, out_specs=out_specs, check_vma=False)
```

```python
import functools

import jax
import jax.numpy as jnp
import numpy as np
from jax import lax
from jax.experimental import pallas as pl
from jax.experimental.pallas import tpu as pltpu
from jax.sharding import PartitionSpec as P

D = 2048
HEAD = 128
DOC = 512
LANES = 128
EPSILON = 1e-05
MASKED = -1e30
CHUNKS = 2
VMEM = 56 * 1024 * 1024
bf16 = jnp.bfloat16
f32 = jnp.float32


def nn(left, right):
    return lax.dot_general(left, right, (((1,), (0,)), ((), ())), preferred_element_type=f32)


def nt(left, right):
    return lax.dot_general(left, right, (((1,), (1,)), ((), ())), preferred_element_type=f32)


def tn(left, right):
    return lax.dot_general(left, right, (((0,), (0,)), ((), ())), preferred_element_type=f32)


def params():
    return pltpu.CompilerParams(vmem_limit_bytes=VMEM)


PACE = 0.3


def cost(flops, moved, special=0):
    return pl.CostEstimate(flops=int(1.5 * PACE * flops + 6e4 * PACE * special), bytes_accessed=moved // 8, transcendentals=0)


def rms_scale(values):
    return lax.rsqrt(jnp.mean(values * values, axis=-1, keepdims=True) + EPSILON)


def norm_back(grad_values, values, scale_col, gain_vec):
    weighted = grad_values * gain_vec
    inner_mean = jnp.mean(weighted * values, axis=-1, keepdims=True)
    return scale_col * weighted - values * (scale_col * scale_col * scale_col) * inner_mean


def rope_tables(length, width):
    angles = np.arange(length)[:, None] * 10000.0 ** (-np.arange(width // 2) * 2.0 / width)[None, :]
    cosine, sine = np.cos(angles).astype(np.float32), np.sin(angles).astype(np.float32)
    return jnp.asarray(np.concatenate([cosine, cosine], axis=1)), jnp.asarray(np.concatenate([-sine, sine], axis=1))


def key_start(query_start):
    return max(0, query_start - DOC)


def fill_bias(bias, seg_col, seg_row, keep_row, block):
    length = seg_col.shape[0]
    for start in range(0, length, block):
        first, stop = key_start(start), start + block
        query_pos = start + lax.broadcasted_iota(jnp.int32, (block, stop - first), 0)
        key_pos = first + lax.broadcasted_iota(jnp.int32, (block, stop - first), 1)
        same = seg_col[start:stop, :] == seg_row[:, first:stop]
        live = (keep_row[:, first:stop] == 1) | (key_pos == query_pos)
        allowed = same & live & (key_pos <= query_pos)
        bias[start:stop, : stop - first] = jnp.where(allowed, 0.0, MASKED)


def turned(values):
    return pltpu.roll(values, values.shape[1] // 2, 1)


def project_kernel(rows_in, w_query, w_key, w_value, q_out, k_out, v_out, squares_out):
    ones = jnp.ones((8, q_out.shape[1]), f32)
    for at, (weight, out) in enumerate(((w_query, q_out), (w_key, k_out))):
        raw = nn(rows_in[...], weight[...])
        out[...] = raw
        sums = lax.dot_general(
            ones, raw * raw, (((1,), (1,)), ((), ())), precision=lax.Precision.HIGHEST, preferred_element_type=f32
        )
        squares_out[at : at + 1, :] = sums[:1]
    v_out[...] = nn(rows_in[...], w_value[...]).astype(bf16)


def project(rows_in, w_query, w_key, w_value):
    rows, features = rows_in.shape
    width = w_query.shape[1]
    block = min(256, rows)
    row = lambda columns: pl.BlockSpec((block, columns), lambda r: (r, 0))
    weight = pl.BlockSpec((features, width), lambda r: (0, 0))
    sds = jax.ShapeDtypeStruct
    return pl.pallas_call(
        project_kernel,
        grid=(rows // block,),
        in_specs=[row(features), weight, weight, weight],
        out_specs=[row(width), row(width), row(width), pl.BlockSpec((2, block), lambda r: (0, r))],
        out_shape=[sds((rows, width), f32), sds((rows, width), f32), sds((rows, width), bf16), sds((2, rows), f32)],
        compiler_params=params(),
        cost_estimate=cost(6 * rows * features * width, 2 * (rows + 3 * width) * features),
        name="project",
    )(rows_in, w_query, w_key, w_value)


def project_back_kernel(
    rows_in, dqn, dkn, dvalue, qraw, kraw, q_scale, k_scale, q_dot, k_dot, q_gain, k_gain,
    w_query, w_key, w_value, part_out, dq_out, dk_out, gain_out,
):
    @pl.when(pl.program_id(0) == 0)
    def _():
        gain_out[...] = jnp.zeros_like(gain_out)

    def raw_grad(grad, raw, scale, gain, dot):
        cube = scale[...] * scale[...] * scale[...]
        return (scale[...] * (gain[...] * grad[...]) - raw[...] * (cube * dot[...])).astype(bf16)

    dq = raw_grad(dqn, qraw, q_scale, q_gain, q_dot)
    dk = raw_grad(dkn, kraw, k_scale, k_gain, k_dot)
    dq_out[...] = dq
    dk_out[...] = dk
    part = nt(dq, w_query[...]) + nt(dk, w_key[...]) + nt(dvalue[...], w_value[...])
    part_out[...] = part.astype(bf16)
    gain_out[...] += jnp.sum(part * rows_in[...].astype(f32), axis=0, keepdims=True)


def project_back(rows_in, dqn, dkn, dvalue, qraw, kraw, q_scale, k_scale, q_dot, k_dot, q_gain, k_gain, w_query, w_key, w_value):
    rows, features = rows_in.shape
    width = w_query.shape[1]
    block = min(256, rows)
    row = lambda columns: pl.BlockSpec((block, columns), lambda r: (r, 0))
    whole = lambda *shape: pl.BlockSpec(shape, lambda r: (0, 0))
    sds = jax.ShapeDtypeStruct
    return pl.pallas_call(
        project_back_kernel,
        grid=(rows // block,),
        in_specs=[row(features)] + [row(width)] * 5 + [row(1)] * 4 + [whole(1, width)] * 2 + [whole(features, width)] * 3,
        out_specs=[row(features), row(width), row(width), whole(1, features)],
        out_shape=[sds((rows, features), bf16), sds((rows, width), bf16), sds((rows, width), bf16), sds((1, features), f32)],
        compiler_params=params(),
        cost_estimate=cost(6 * rows * features * width, 2 * (rows + 3 * width) * features),
        name="project_back",
    )(rows_in, dqn, dkn, dvalue, qraw, kraw, q_scale, k_scale, q_dot, k_dot, q_gain[None], k_gain[None], w_query, w_key, w_value)


def attention_wgrad_kernel(added, order, rows_in, middle, *refs):
    sides, (attended,), refs = refs[:3], refs[3:4], refs[4:]
    got, outs = (refs[:added], refs[added:])
    at = pl.program_id(0)
    totals = [tn(rows_in[...], side[...]) for side in sides] + [tn(middle[...], attended[...])]
    if not added:
        for place, out in enumerate(outs):

            @pl.when(at == place)
            def _(out=out):
                for weight, total in enumerate(totals):
                    out[0, weight] = total.astype(bf16)

        return
    half = outs[0].shape[2]
    for place, piece in enumerate(got):

        @pl.when(at == place)
        def _(piece=piece):
            for weight, total in enumerate(totals):
                total = total + piece[0, weight].astype(f32)
                for side, out in enumerate(outs):
                    out[0, weight] = total[side * half : (side + 1) * half, :].astype(bf16)


def attention_wgrad(rows_in, middle, sides, attended, order, blocks, added=()):
    features = rows_in.shape[1]
    width = sides[0].shape[1]
    block = features // blocks
    count = order.shape[0]
    left = lambda values: pl.BlockSpec((values.shape[0], block), lambda i, ids: (0, ids[i]))
    right = lambda values: pl.BlockSpec(values.shape, lambda i, ids: (0, 0))
    group_specs = [pl.BlockSpec((1, 4, block, width), lambda i, ids: (0, 0, 0, 0))] * count
    if added:
        out_specs = [pl.BlockSpec((1, 4, block // 2, width), lambda i, ids: (i, 0, 0, 0))] * 2
        out_shape = [jax.ShapeDtypeStruct((count, 4, block // 2, width), bf16)] * 2
    else:
        out_specs = group_specs
        out_shape = [jax.ShapeDtypeStruct((1, 4, block, width), bf16)] * count
    return pl.pallas_call(
        functools.partial(attention_wgrad_kernel, len(added)),
        grid_spec=pltpu.PrefetchScalarGridSpec(
            num_scalar_prefetch=1,
            grid=(count,),
            in_specs=[left(rows_in), left(middle)] + [right(v) for v in sides] + [right(attended)] + (group_specs if added else []),
            out_specs=out_specs,
        ),
        out_shape=out_shape,
        compiler_params=params(),
        cost_estimate=cost(8 * rows_in.shape[0] * features * width, 4 * features * width),
        name="attention_wgrad",
    )(order, rows_in, middle, *sides, attended, *added)


def attend_kernel(
    block, qraw, kraw, value, q_scale, k_scale, q_gain, k_gain, cosine, sine,
    seg_col, seg_row, keep_row, q_out, k_out, o_out, lse_out, bias,
):
    @pl.when(pl.program_id(0) == 0)
    def _():
        fill_bias(bias, seg_col, seg_row, keep_row, block)

    def rotated(raw, scale, gain):
        normed = raw[...] * scale[...] * gain[...]
        return (normed * cosine[...] + turned(normed) * sine[...]).astype(bf16)

    q_out[...] = rotated(qraw, q_scale, q_gain)
    k_out[...] = rotated(kraw, k_scale, k_gain)
    length = seg_col.shape[0]
    for start in range(0, length, block):
        first, stop = key_start(start), start + block
        scores = nt(q_out[start:stop, :], k_out[first:stop, :]) * HEAD ** (-0.5)
        scores = scores + bias[start:stop, : stop - first]
        top = jnp.max(scores, axis=1, keepdims=True)
        powers = jnp.exp(scores - top)
        total = jnp.sum(powers, axis=1, keepdims=True)
        weights = (powers * (1.0 / total)).astype(bf16)
        o_out[start:stop, :] = nn(weights, value[first:stop, :]).astype(bf16)
        lse_out[start:stop, :] = jnp.broadcast_to(top + jnp.log(total), (block, HEAD))


def attend(qraw, kraw, value, q_scale, k_scale, q_gain, k_gain, cosine, sine, seg, keep):
    length, width = qraw.shape
    block = min(256, length)
    span = min(DOC + block, length)
    head = pl.BlockSpec((length, HEAD), lambda h: (0, h))
    gain = pl.BlockSpec((1, HEAD), lambda h: (0, h))
    whole = lambda *shape: pl.BlockSpec(shape, lambda h: (0, 0))
    return pl.pallas_call(
        functools.partial(attend_kernel, block),
        grid=(width // HEAD,),
        in_specs=[head, head, head, whole(length, 1), whole(length, 1), gain, gain]
        + [whole(length, HEAD), whole(length, HEAD), whole(length, 1), whole(1, length), whole(1, length)],
        out_specs=[head, head, head, head],
        out_shape=[jax.ShapeDtypeStruct((length, width), t) for t in (bf16, bf16, bf16, f32)],
        scratch_shapes=[pltpu.VMEM((length, span), f32)],
        compiler_params=params(),
        cost_estimate=cost(4 * length * span * width, 18 * length * width, length * span * width // HEAD),
        name="attend",
    )(qraw, kraw, value, q_scale, k_scale, q_gain[None], k_gain[None], cosine, sine, seg[:, None], seg[None], keep[None])


def attend_back_kernel(
    block, query, key, value, out_grad, lse, qraw, kraw, q_scale, k_scale, q_gain, k_gain, cosine, sine,
    seg_col, seg_row, keep_row, dq_out, dk_out, dv_out, qdot_out, kdot_out, qg_out, kg_out, bias, dk_sum, dv_sum,
):
    at = pl.program_id(0)

    @pl.when(at == 0)
    def _():
        fill_bias(bias, seg_col, seg_row, keep_row, block)
        qdot_out[...] = jnp.zeros_like(qdot_out)
        kdot_out[...] = jnp.zeros_like(kdot_out)

    dk_sum[...] = jnp.zeros_like(dk_sum)
    dv_sum[...] = jnp.zeros_like(dv_sum)
    length = seg_col.shape[0]
    scale = HEAD ** (-0.5)
    for start in range(0, length, block):
        first, stop = key_start(start), start + block
        rows, keys = slice(start, stop), slice(first, stop)
        scores = nt(query[rows, :], key[keys, :]) * scale + bias[rows, : stop - first]
        weights = jnp.exp(scores - lse[rows, :1])
        prob_grad = nt(out_grad[rows, :], value[keys, :])
        inner = jnp.sum(weights * prob_grad, axis=1, keepdims=True)
        score_grad = (weights * (prob_grad - inner)).astype(bf16)
        dq_out[rows, :] = nn(score_grad, key[keys, :]) * scale
        dk_sum[keys, :] += tn(score_grad, query[rows, :])
        dv_sum[keys, :] += tn(weights.astype(bf16), out_grad[rows, :])

    def unrotated(grad):
        return grad * cosine[...] + turned(grad * sine[...])

    dv_out[...] = dv_sum[...].astype(bf16)
    dq = unrotated(dq_out[...])
    dk = unrotated(dk_sum[...] * scale)
    dq_out[...] = dq
    dk_out[...] = dk
    dq = dq * qraw[...]
    dk = dk * kraw[...]
    qg_out[...] = jnp.sum(dq * q_scale[...], axis=0, keepdims=True)
    kg_out[...] = jnp.sum(dk * k_scale[...], axis=0, keepdims=True)
    qdot_out[...] += jnp.sum(dq * q_gain[...], axis=1, keepdims=True)
    kdot_out[...] += jnp.sum(dk * k_gain[...], axis=1, keepdims=True)


def attend_back(query, key, value, out_grad, lse, qraw, kraw, q_scale, k_scale, q_gain, k_gain, cosine, sine, seg, keep):
    length, width = qraw.shape
    block = min(256, length)
    span = min(DOC + block, length)
    head = pl.BlockSpec((length, HEAD), lambda h: (0, h))
    gain = pl.BlockSpec((1, HEAD), lambda h: (0, h))
    whole = lambda *shape: pl.BlockSpec(shape, lambda h: (0, 0))
    sds = jax.ShapeDtypeStruct
    return pl.pallas_call(
        functools.partial(attend_back_kernel, block),
        grid=(width // HEAD,),
        in_specs=[head] * 7
        + [whole(length, 1), whole(length, 1), gain, gain]
        + [whole(length, HEAD), whole(length, HEAD), whole(length, 1), whole(1, length), whole(1, length)],
        out_specs=[head, head, head, whole(length, 1), whole(length, 1), gain, gain],
        out_shape=[sds((length, width), f32), sds((length, width), f32), sds((length, width), bf16)]
        + [sds((length, 1), f32), sds((length, 1), f32), sds((1, width), f32), sds((1, width), f32)],
        scratch_shapes=[pltpu.VMEM((length, span), f32), pltpu.VMEM((length, HEAD), f32), pltpu.VMEM((length, HEAD), f32)],
        compiler_params=params(),
        cost_estimate=cost(10 * length * span * width, 32 * length * width, length * span * width // HEAD),
        name="attend_back",
    )(query, key, value, out_grad, lse, qraw, kraw, q_scale, k_scale, q_gain[None], k_gain[None], cosine, sine, seg[:, None], seg[None], keep[None])


def up_back_kernel(grad, down_w, out):
    width = down_w.shape[2]
    for at in range(down_w.shape[0]):
        out[:, at * width : (at + 1) * width] = nn(grad[...], down_w[at]).astype(out.dtype)


def up_back(grad, down_w):
    rows, features = grad.shape
    experts, _, width = down_w.shape
    step = 2 if experts % 2 == 0 else 1
    return pl.pallas_call(
        up_back_kernel,
        grid=(experts // step,),
        in_specs=[pl.BlockSpec((rows, features), lambda e: (0, 0)), pl.BlockSpec((step, features, width), lambda e: (e, 0, 0))],
        out_specs=pl.BlockSpec((rows, step * width), lambda e: (0, e)),
        out_shape=jax.ShapeDtypeStruct((rows, experts * width), bf16),
        compiler_params=params(),
        cost_estimate=cost(2 * rows * features * experts * width, 2 * (rows + experts * width) * features),
        name="up_back",
    )(grad, down_w)


def expert_kernel(block, rows_in, back, routed, router, gate_w, up_w, act_out, dgate_out, dup_out, grad_out, comb, dcomb, total):
    at = pl.program_id(0)
    rows, features = rows_in.shape
    lane = lax.broadcasted_iota(jnp.int32, (block, LANES), 1)

    @pl.when(at == 0)
    def _():
        experts = pl.num_programs(0)
        for start in range(0, rows, block):
            here = slice(start, start + block)
            logits = jnp.where(lane < experts, nn(rows_in[here, :], router[...]), MASKED)
            powers = jnp.exp(logits - jnp.max(logits, axis=1, keepdims=True))
            probs = powers / jnp.sum(powers, axis=1, keepdims=True)
            comb[here, :] = probs * routed[here, :]
        total[...] = jnp.zeros_like(total)
        dcomb[...] = jnp.zeros_like(dcomb)

    gate, up = gate_w[0], up_w[0]
    mine = lane == at
    for start in range(0, rows, block):
        here = slice(start, start + block)
        taken = rows_in[here, :]
        pre_gate = nn(taken, gate)
        pre_up = nn(taken, up)
        behind = back[here, :].astype(f32)
        share = jnp.sum(jnp.where(mine, comb[here, :], 0.0), axis=1, keepdims=True)
        sigmoid = 0.5 * jnp.tanh(0.5 * pre_gate) + 0.5
        active = pre_gate * sigmoid
        inner = active * pre_up
        share_grad = jnp.sum(inner * behind, axis=1, keepdims=True)
        dcomb[here, :] = jnp.where(mine, share_grad, dcomb[here, :])
        act_out[here, :] = (inner * share).astype(bf16)
        inner_grad = behind * share
        dgate = (inner_grad * pre_up * (sigmoid + active * (1.0 - sigmoid))).astype(bf16)
        dup = (inner_grad * active).astype(bf16)
        dgate_out[here, :] = dgate
        dup_out[here, :] = dup
        total[here, :] += nt(dgate, gate) + nt(dup, up)

    @pl.when(at == pl.num_programs(0) - 1)
    def _():
        grad_out[:, :features] = total[...].astype(bf16)
        grad_out[:, features:] = dcomb[...].astype(bf16)


def experts_block(rows_in, back, routed, router, gate_w, up_w):
    rows, features = rows_in.shape
    experts, _, width = gate_w.shape
    block = min(512, rows)
    whole = lambda *shape: pl.BlockSpec(shape, lambda e: (0, 0))
    column = pl.BlockSpec((rows, width), lambda e: (0, e))
    weight = pl.BlockSpec((1, features, width), lambda e: (e, 0, 0))
    wide = jax.ShapeDtypeStruct((rows, experts * width), bf16)
    return pl.pallas_call(
        functools.partial(expert_kernel, block),
        grid=(experts,),
        in_specs=[whole(rows, features), column, whole(rows, LANES), whole(features, LANES), weight, weight],
        out_specs=[column, column, column, whole(rows, features + LANES)],
        out_shape=[wide, wide, wide, jax.ShapeDtypeStruct((rows, features + LANES), bf16)],
        scratch_shapes=[pltpu.VMEM((rows, LANES), f32), pltpu.VMEM((rows, LANES), f32), pltpu.VMEM((rows, features), f32)],
        compiler_params=params(),
        cost_estimate=cost(8 * rows * features * experts * width, 4 * experts * width * (features + 2 * rows), rows * experts * width),
        name="experts",
    )(rows_in, back, routed, router, gate_w, up_w)


def wgrad_kernel(count, extra, per, block, order, *refs):
    lefts, rights = refs[:count], refs[count : 2 * count]
    added = refs[2 * count : 2 * count + extra]
    outs = refs[2 * count + extra :]
    at = pl.program_id(0)
    features = lefts[0].shape[1]

    def piece(start, stop):
        total = tn(lefts[0][:, start:stop], rights[0][...])
        for left, right in zip(lefts[1:], rights[1:]):
            total = total + tn(left[:, start:stop], right[...])
        return total

    if not added:
        for place, out in enumerate(outs):

            @pl.when(at // per == place)
            def _(out=out):
                for start in range(0, features, block):
                    out[0, start : start + block, :] = piece(start, start + block).astype(bf16)

        return
    half = features // 2
    for place, got in enumerate(added):

        @pl.when(at // per == place)
        def _(got=got):
            for start in range(0, features, block):
                total = piece(start, start + block) + got[0, start : start + block, :].astype(f32)
                outs[start // half][0, start % half : start % half + block, :] = total.astype(bf16)


def wgrad(lefts, rights, order, width, per, added=()):
    features = lefts[0].shape[1]
    experts = order.shape[0]
    groups = experts // per
    rows = sum(left.shape[0] for left in lefts)

    def group_spec(place):
        return pl.BlockSpec((1, features, width), lambda i, ids: (jnp.clip(i - place * per, 0, per - 1), 0, 0))

    groups_specs = [group_spec(place) for place in range(groups)]
    if added:
        out_specs = [pl.BlockSpec((1, features // 2, width), lambda i, ids: (i, 0, 0))] * 2
        out_shape = [jax.ShapeDtypeStruct((experts, features // 2, width), bf16)] * 2
    else:
        out_specs = groups_specs
        out_shape = [jax.ShapeDtypeStruct((per, features, width), bf16)] * groups
    return pl.pallas_call(
        functools.partial(wgrad_kernel, len(lefts), len(added), per, min(512, features // 2)),
        grid_spec=pltpu.PrefetchScalarGridSpec(
            num_scalar_prefetch=1,
            grid=(experts,),
            in_specs=[pl.BlockSpec(left.shape, lambda i, ids: (0, 0)) for left in lefts]
            + [pl.BlockSpec((right.shape[0], width), lambda i, ids: (0, ids[i])) for right in rights]
            + (groups_specs if added else []),
            out_specs=out_specs,
        ),
        out_shape=out_shape,
        compiler_params=params(),
        cost_estimate=cost(2 * rows * features * experts * width, 2 * (rows + 2 * experts * width) * features),
        name="wgrad",
    )(order, *lefts, *rights, *added)


def down_kernel(parts, down_w, *refs):
    acts, out = refs[:-1], refs[-1]
    joined = jnp.concatenate([down_w[e] for e in range(down_w.shape[0])], axis=1)
    block = acts[0].shape[0] // parts
    for at, act in enumerate(acts):
        result = nt(act[...], joined).astype(out.dtype)
        for part in range(parts):
            start = (part * len(acts) + at) * block
            out[start : start + block, :] = result[part * block : (part + 1) * block, :]


def down(acts, down_w, parts):
    rows = sum(act.shape[0] for act in acts)
    experts, features, width = down_w.shape
    block = min(256, features)
    return pl.pallas_call(
        functools.partial(down_kernel, parts),
        grid=(features // block,),
        in_specs=[pl.BlockSpec((experts, block, width), lambda n: (0, n, 0))]
        + [pl.BlockSpec(act.shape, lambda n: (0, 0)) for act in acts],
        out_specs=pl.BlockSpec((rows, block), lambda n: (0, n)),
        out_shape=jax.ShapeDtypeStruct((rows, features), bf16),
        compiler_params=params(),
        cost_estimate=cost(2 * rows * features * experts * width, 2 * (rows + experts * width) * features),
        name="down",
    )(down_w, *acts)


def gate(value, *others):
    return lax.optimization_barrier((value, others))[0]


def gather_rows(values):
    return lax.all_gather(values, "tensor", axis=0, tiled=True)


def scatter_rows(values):
    return lax.psum_scatter(values, "tensor", scatter_dimension=0, tiled=True)


def join_kernel(parts, slots, own, *refs):
    ups, downs, out = refs[: parts - 1], refs[parts - 1 : 2 * parts - 2], refs[2 * parts - 2]
    at = pl.program_id(0)

    @pl.when(at == 0)
    def _():
        out[...] = own[...]

    for step in range(1, parts):

        @pl.when(at == step)
        def _(step=step):
            out[...] = ups[step - 1][...] + downs[parts - 1 - step][...]


def join(slots, own, ups, downs):
    rows, columns = own.shape
    parts = len(ups) + 1
    whole = pl.BlockSpec((rows, columns), lambda i, to: (0, 0))
    return pl.pallas_call(
        functools.partial(join_kernel, parts),
        grid_spec=pltpu.PrefetchScalarGridSpec(
            num_scalar_prefetch=1,
            grid=(parts,),
            in_specs=[whole] * (2 * parts - 1),
            out_specs=pl.BlockSpec((rows, columns), lambda i, to: (to[i], 0)),
        ),
        out_shape=jax.ShapeDtypeStruct((parts * rows, columns), own.dtype),
        compiler_params=params(),
        cost_estimate=cost(0, 0),
        name="join",
    )(slots, own, *ups, *downs)


class Chain:
    def __init__(self, values):
        self.values = values
        self.parts = lax.axis_size("tensor")
        self.ups, self.downs = [values], [values]

    def hop(self, *others):
        step = len(self.ups)
        if step < self.parts:
            up, down = gate((self.ups[-1], self.downs[-1]), *others) if others else (self.ups[-1], self.downs[-1])
            self.sent = (up, down)
            self.ups.append(lax.ppermute(up, "tensor", [(i, i + 1) for i in range(step - 1, self.parts - 1)]))
            self.downs.append(lax.ppermute(down, "tensor", [(i, i - 1) for i in range(1, self.parts - step + 1)]))
        return self.sent

    def recv(self):
        return self.ups[-1], self.downs[-1]

    def joined(self):
        while len(self.ups) < self.parts:
            self.hop()
        at = lax.axis_index("tensor")
        slots = lax.rem(at - jnp.arange(self.parts, dtype=jnp.int32) + self.parts, self.parts)
        return join(slots, self.values, self.ups[1:], self.downs[1:])


def pair_swap(values, step):
    size = lax.axis_size("dp")
    return lax.ppermute(values, "dp", [(i, i ^ step) for i in range(size)])


class Halving:
    def __init__(self, values):
        bits = list(range(values[0].shape[0].bit_length() - 1))
        self.kept = list(values)
        self.left = [bits[::-1], bits]
        self.got = None

    def send(self):
        if not self.left[0]:
            return ()
        self.got = []
        sent = []
        for side, downward in ((0, True), (1, False)):
            bit = self.left[side].pop(0)
            kept = self.kept[side]
            half = kept.shape[0] // 2
            if downward:
                keep, go = kept[:half], kept[half:]
            else:
                view = kept.reshape((half, 2) + kept.shape[1:])
                keep, go = view[:, 0], view[:, 1]
            sent.append(go)
            self.got.append(pair_swap(go, 2 << bit))
            self.kept[side] = keep
        return tuple(sent)

    def add(self, *others):
        if self.got is not None:
            if others:
                self.got = gate(tuple(self.got), *others)
            last = not self.left[0]
            for side in range(2):
                total = self.kept[side].astype(f32) + self.got[side].astype(f32)
                self.kept[side] = total if last else total.astype(bf16)
            self.got = None
        return tuple(self.kept)

    def done(self):
        self.add()
        while self.left[0]:
            self.send()
            self.add()
        return jnp.concatenate([kept[0].astype(f32) for kept in self.kept], axis=1)


def exchange_sum(values, axes):
    for axis in axes:
        size = lax.axis_size(axis)
        step = 1
        while step < size:
            values = values + lax.ppermute(values, axis, [(i, i ^ step) for i in range(size)])
            step *= 2
    return values


def local(
    tokens, cotangent, seg_ids, keep_mask, routes, attn_gain, w_query, w_key, w_value, w_out,
    q_gain, k_gain, ffn_gain, router, w_gate, w_up, w_down,
):
    parts = lax.axis_size("tensor")
    part_at = lax.axis_index("tensor")
    dp_size = lax.axis_size("dp")
    low_bit = lax.axis_index("dp") % 2
    shard_rows, features = tokens.shape
    group_rows = shard_rows * parts
    _, length = seg_ids.shape
    local_width = w_query.shape[1]
    experts, _, width = w_gate.shape
    per = experts // dp_size
    chunk_rows = shard_rows // CHUNKS
    chunks = range(CHUNKS)
    own = [slice(c * chunk_rows, (c + 1) * chunk_rows) for c in chunks]

    def chunk_of(values, c):
        columns = values.shape[1]
        return values.reshape(parts, CHUNKS, chunk_rows, columns)[:, c].reshape(parts * chunk_rows, columns)

    inputs = tokens.astype(f32)
    first_scale = rms_scale(inputs)
    normed_all = gather_rows((inputs * first_scale * attn_gain).astype(bf16))
    behind = Chain(gate(cotangent, normed_all))

    cosine, sine = rope_tables(length, HEAD)

    relative = jnp.arange(dp_size // 2, dtype=jnp.int32) ^ (lax.axis_index("dp") // 2)
    own_blocks, other_blocks = 2 * relative + low_bit, 2 * relative + 1 - low_bit
    mine, theirs = (
        (blocks[:, None] * per + jnp.arange(per, dtype=jnp.int32)).reshape(-1) for blocks in (own_blocks, other_blocks)
    )

    qraw, kraw, value, squares = project(normed_all, w_query, w_key, w_value)
    squares = exchange_sum(squares, ("tensor",))
    behind.hop()
    q_scale, k_scale = (lax.rsqrt(squares[i] / features + EPSILON)[:, None] for i in range(2))
    query, key, attended, lse = attend(
        qraw, kraw, value, q_scale, k_scale, q_gain, k_gain, cosine, sine, gate(seg_ids[0], *behind.recv()), keep_mask[0]
    )
    behind.hop()
    attended_parts = [chunk_of(gate(attended, *behind.recv()), c) for c in chunks]
    outs = [nt(attended_parts[0], w_out).astype(bf16)]
    summed = [scatter_rows(outs[0])]
    outs.append(nt(gate(attended_parts[1], outs[0]), w_out).astype(bf16))
    summed.append(scatter_rows(outs[1]))
    behind.hop(outs[1])

    idle_routes, idle_router = gate((routes, router), outs[1])
    expert_ids = jnp.arange(LANES)
    routed = jnp.sum((idle_routes[:, :, None] == expert_ids[None, None, :]).astype(f32), axis=1)
    router_wide = jnp.pad(idle_router, ((0, 0), (0, LANES - experts)))
    routed_own = lax.dynamic_slice_in_dim(routed, part_at * shard_rows, shard_rows, 0)[:, :experts]
    grad_group = behind.joined()
    grad_all = [chunk_of(grad_group, c) for c in chunks]
    backs = [up_back(gate(rows, routed, router_wide), w_down) for rows in grad_all]

    middles, scales, ffn_own = [], [], []

    def middle_of(c, total):
        middle = inputs[own[c]] + total.astype(f32)
        scale = rms_scale(middle)
        normed = (middle * scale * ffn_gain).astype(bf16)
        middles.append(middle)
        scales.append(scale)
        ffn_own.append(normed)
        return normed

    ffn_all = [gather_rows(middle_of(0, summed[0]))]
    ffn_all.append(gather_rows(middle_of(1, gate(summed[1], ffn_own[0], *backs))))
    acts, dgates, dups, expert_grads = [], [], [], []
    for c in chunks:
        here = gate(chunk_of(routed, c), *backs, *acts[-1:])
        act, dgate, dup, grads = experts_block(ffn_all[c], backs[c], here, router_wide, w_gate, w_up)
        acts.append(act)
        dgates.append(dgate)
        dups.append(dup)
        expert_grads.append(grads)
    expert_grads = [scatter_rows(grads) for grads in expert_grads]

    ffn_gain_parts, router_parts, middle_grads = [], [], []

    def middle_back(c, grads):
        share_grad = grads[:, features : features + experts] * routed_own[own[c]]
        probs = jax.nn.softmax(nn(ffn_own[c], router), axis=-1)
        logit_grad = (probs * (share_grad - jnp.sum(share_grad * probs, axis=-1, keepdims=True))).astype(bf16)
        ffn_grad = grads[:, :features] + nt(logit_grad, router)
        router_parts.append(tn(ffn_own[c], logit_grad))
        ffn_gain_parts.append(jnp.sum(ffn_grad * middles[c] * scales[c], axis=0))
        middle_grads.append(cotangent[own[c]].astype(f32) + norm_back(ffn_grad, middles[c], scales[c], ffn_gain))
        return middle_grads[c].astype(bf16)

    def expert_sums(lefts, rights, ids, *others, added=()):
        return wgrad(lefts, rights, gate(ids, *others), width, per, added)

    def core_swap(pieces):
        return [pair_swap(piece, 1) for piece in pieces]

    def halving(sums):
        return Halving([half.reshape((dp_size // 2, per) + half.shape[1:]) for half in sums])

    first = middle_back(0, gate(expert_grads[0], acts[1]).astype(f32))
    gate_sent = expert_sums(ffn_all, dgates, theirs, first)
    gate_got = core_swap(gate_sent)
    up_sent = expert_sums(ffn_all, dups, theirs, *gate_sent)
    up_got = core_swap(up_sent)
    second = middle_back(1, gate(expert_grads[1], *up_sent).astype(f32))
    middle_all = gather_rows(jnp.concatenate([first, second]))
    gate_sums = expert_sums(ffn_all, dgates, mine, second, added=gate_got)
    gate_out = halving(gate_sums)
    up_sums = expert_sums(ffn_all, dups, mine, *gate_sums, *gate_out.send(), added=up_got)
    up_out = halving(up_sums)
    moe = down([gate(acts[0], *up_sums, *up_out.send()), acts[1]], w_down, parts)
    moe_sum = scatter_rows(moe)
    gate_late = gate_out.add()
    gate_out.send()
    down_sent = expert_sums(grad_all, acts, theirs, moe, *gate_late)
    down_got = core_swap(down_sent)

    attended_grad = nn(gate(middle_all, *down_sent), w_out).astype(bf16)
    dqn, dkn, dvalue, qdot, kdot, q_gain_part, k_gain_part = attend_back(
        query, key, value, attended_grad, lse, qraw, kraw, q_scale, k_scale, q_gain, k_gain, cosine, sine,
        seg_ids[0], keep_mask[0],
    )
    dots = exchange_sum(jnp.stack([qdot[:, 0], kdot[:, 0]]), ("tensor",)) / features
    up_late = up_out.add()
    up_out.send()
    down_sums = expert_sums(grad_all, acts, mine, dqn, *up_late, added=down_got)
    down_out = halving(down_sums)
    down_out.send()
    normed_part, dqraw, dkraw, attn_gain_part = project_back(
        normed_all, dqn, dkn, dvalue, qraw, kraw, q_scale, k_scale, dots[0][:, None], dots[1][:, None],
        gate(q_gain, *down_sums), k_gain, w_query, w_key, w_value,
    )
    normed_grad = scatter_rows(normed_part)
    def attention_sums(ids, *others, added=()):
        return attention_wgrad(
            normed_all, middle_all, (dqraw, dkraw, dvalue), attended, gate(ids, *others), dp_size, added
        )

    attn_sent = attention_sums(other_blocks, normed_part)
    attn_got = core_swap(attn_sent)

    def placed(part):
        return lax.dynamic_update_slice_in_dim(jnp.zeros((features,), f32), part, part_at * local_width, 0)

    attn_sums = attention_sums(own_blocks, *attn_sent, added=attn_got)
    attn_out = Halving(attn_sums)
    normed_grad = gate(normed_grad, *attn_out.send())
    smalls = [attn_gain_part[0] / attn_gain, placed(q_gain_part[0]), placed(k_gain_part[0]), sum(ffn_gain_parts)]
    smalls = gate(jnp.concatenate([jnp.stack(smalls), sum(router_parts).T]), normed_grad)
    smalls = exchange_sum(smalls, ("dp", "tensor"))
    gate_done = gate_out.done()
    up_done = up_out.done()
    down_done = down_out.done()
    attn_out.add(normed_grad)
    query_done, key_done, value_done, out_done = attn_out.done()
    layer_out = (jnp.concatenate(middles) + moe_sum.astype(f32)).astype(bf16)
    tokens_grad = jnp.concatenate(middle_grads) + norm_back(normed_grad.astype(f32), inputs, first_scale, attn_gain)
    return (
        layer_out, tokens_grad, query_done, key_done, value_done, out_done,
        smalls[0], smalls[1], smalls[2], smalls[3], smalls[4:].T, gate_done, up_done, down_done,
    )


def solution(mesh):
    rows = P(("dp", "tensor"), None)
    column = P(None, "tensor")
    expert = P(None, None, "tensor")
    in_specs = (
        rows, rows, P("dp", None), P("dp", None), P("dp", None), P(), column, column, column, column,
        P("tensor"), P("tensor"), P(), P(), expert, expert, expert,
    )
    block = P("dp", "tensor")
    expert_out = P("dp", None, "tensor")
    out_specs = (
        rows, rows, block, block, block, block, P(), P(), P(), P(), P(), expert_out, expert_out, expert_out,
    )
    return jax.shard_map(local, mesh=mesh, in_specs=in_specs, out_specs=out_specs, check_vma=False)
```

```python
import functools

import jax
import jax.numpy as jnp
import numpy as np
from jax import lax
from jax.experimental import pallas as pl
from jax.experimental.pallas import tpu as pltpu
from jax.sharding import PartitionSpec as P

D = 2048
HEAD = 128
DOC = 512
LANES = 128
EPSILON = 1e-05
MASKED = -1e30
CHUNKS = 2
VMEM = 56 * 1024 * 1024
bf16 = jnp.bfloat16
f32 = jnp.float32


def nn(left, right):
    return lax.dot_general(left, right, (((1,), (0,)), ((), ())), preferred_element_type=f32)


def nt(left, right):
    return lax.dot_general(left, right, (((1,), (1,)), ((), ())), preferred_element_type=f32)


def tn(left, right):
    return lax.dot_general(left, right, (((0,), (0,)), ((), ())), preferred_element_type=f32)


def params():
    return pltpu.CompilerParams(vmem_limit_bytes=VMEM)


PACE = 0.3


def cost(flops, moved, special=0):
    return pl.CostEstimate(flops=int(1.5 * PACE * flops + 6e4 * PACE * special), bytes_accessed=moved // 8, transcendentals=0)


def rms_scale(values):
    return lax.rsqrt(jnp.mean(values * values, axis=-1, keepdims=True) + EPSILON)


def norm_back(grad_values, values, scale_col, gain_vec):
    weighted = grad_values * gain_vec
    inner_mean = jnp.mean(weighted * values, axis=-1, keepdims=True)
    return scale_col * weighted - values * (scale_col * scale_col * scale_col) * inner_mean


def rope_tables(length, width):
    angles = np.arange(length)[:, None] * 10000.0 ** (-np.arange(width // 2) * 2.0 / width)[None, :]
    cosine, sine = np.cos(angles).astype(np.float32), np.sin(angles).astype(np.float32)
    return jnp.asarray(np.concatenate([cosine, cosine], axis=1)), jnp.asarray(np.concatenate([-sine, sine], axis=1))


def key_start(query_start):
    return max(0, query_start - DOC)


def fill_bias(bias, seg_col, seg_row, keep_row, block):
    length = seg_col.shape[0]
    for start in range(0, length, block):
        first, stop = key_start(start), start + block
        query_pos = start + lax.broadcasted_iota(jnp.int32, (block, stop - first), 0)
        key_pos = first + lax.broadcasted_iota(jnp.int32, (block, stop - first), 1)
        same = seg_col[start:stop, :] == seg_row[:, first:stop]
        live = (keep_row[:, first:stop] == 1) | (key_pos == query_pos)
        allowed = same & live & (key_pos <= query_pos)
        bias[start:stop, : stop - first] = jnp.where(allowed, 0.0, MASKED)


def turned(values):
    return pltpu.roll(values, values.shape[1] // 2, 1)


def project_kernel(rows_in, w_query, w_key, w_value, q_out, k_out, v_out, squares_out):
    ones = jnp.ones((8, q_out.shape[1]), f32)
    for at, (weight, out) in enumerate(((w_query, q_out), (w_key, k_out))):
        raw = nn(rows_in[...], weight[...])
        out[...] = raw
        sums = lax.dot_general(
            ones, raw * raw, (((1,), (1,)), ((), ())), precision=lax.Precision.HIGHEST, preferred_element_type=f32
        )
        squares_out[at : at + 1, :] = sums[:1]
    v_out[...] = nn(rows_in[...], w_value[...]).astype(bf16)


def project(rows_in, w_query, w_key, w_value):
    rows, features = rows_in.shape
    width = w_query.shape[1]
    block = min(256, rows)
    row = lambda columns: pl.BlockSpec((block, columns), lambda r: (r, 0))
    weight = pl.BlockSpec((features, width), lambda r: (0, 0))
    sds = jax.ShapeDtypeStruct
    return pl.pallas_call(
        project_kernel,
        grid=(rows // block,),
        in_specs=[row(features), weight, weight, weight],
        out_specs=[row(width), row(width), row(width), pl.BlockSpec((2, block), lambda r: (0, r))],
        out_shape=[sds((rows, width), f32), sds((rows, width), f32), sds((rows, width), bf16), sds((2, rows), f32)],
        compiler_params=params(),
        cost_estimate=cost(6 * rows * features * width, 2 * (rows + 3 * width) * features),
        name="project",
    )(rows_in, w_query, w_key, w_value)


def project_back_kernel(
    rows_in, dqn, dkn, dvalue, qraw, kraw, q_scale, k_scale, q_dot, k_dot, q_gain, k_gain,
    w_query, w_key, w_value, part_out, dq_out, dk_out, gain_out,
):
    @pl.when(pl.program_id(0) == 0)
    def _():
        gain_out[...] = jnp.zeros_like(gain_out)

    def raw_grad(grad, raw, scale, gain, dot):
        cube = scale[...] * scale[...] * scale[...]
        return (scale[...] * (gain[...] * grad[...]) - raw[...] * (cube * dot[...])).astype(bf16)

    dq = raw_grad(dqn, qraw, q_scale, q_gain, q_dot)
    dk = raw_grad(dkn, kraw, k_scale, k_gain, k_dot)
    dq_out[...] = dq
    dk_out[...] = dk
    part = nt(dq, w_query[...]) + nt(dk, w_key[...]) + nt(dvalue[...], w_value[...])
    part_out[...] = part.astype(bf16)
    gain_out[...] += jnp.sum(part * rows_in[...].astype(f32), axis=0, keepdims=True)


def project_back(rows_in, dqn, dkn, dvalue, qraw, kraw, q_scale, k_scale, q_dot, k_dot, q_gain, k_gain, w_query, w_key, w_value):
    rows, features = rows_in.shape
    width = w_query.shape[1]
    block = min(256, rows)
    row = lambda columns: pl.BlockSpec((block, columns), lambda r: (r, 0))
    whole = lambda *shape: pl.BlockSpec(shape, lambda r: (0, 0))
    sds = jax.ShapeDtypeStruct
    return pl.pallas_call(
        project_back_kernel,
        grid=(rows // block,),
        in_specs=[row(features)] + [row(width)] * 5 + [row(1)] * 4 + [whole(1, width)] * 2 + [whole(features, width)] * 3,
        out_specs=[row(features), row(width), row(width), whole(1, features)],
        out_shape=[sds((rows, features), bf16), sds((rows, width), bf16), sds((rows, width), bf16), sds((1, features), f32)],
        compiler_params=params(),
        cost_estimate=cost(6 * rows * features * width, 2 * (rows + 3 * width) * features),
        name="project_back",
    )(rows_in, dqn, dkn, dvalue, qraw, kraw, q_scale, k_scale, q_dot, k_dot, q_gain[None], k_gain[None], w_query, w_key, w_value)


def attention_wgrad_kernel(added, order, rows_in, middle, *refs):
    sides, (attended,), refs = refs[:3], refs[3:4], refs[4:]
    got, outs = (refs[:added], refs[added:])
    at = pl.program_id(0)
    totals = [tn(rows_in[...], side[...]) for side in sides] + [tn(middle[...], attended[...])]
    if not added:
        for place, out in enumerate(outs):

            @pl.when(at == place)
            def _(out=out):
                for weight, total in enumerate(totals):
                    out[0, weight] = total.astype(bf16)

        return
    half = outs[0].shape[2]
    for place, piece in enumerate(got):

        @pl.when(at == place)
        def _(piece=piece):
            for weight, total in enumerate(totals):
                total = total + piece[0, weight].astype(f32)
                for side, out in enumerate(outs):
                    out[0, weight] = total[side * half : (side + 1) * half, :].astype(bf16)


def attention_wgrad(rows_in, middle, sides, attended, order, blocks, added=()):
    features = rows_in.shape[1]
    width = sides[0].shape[1]
    block = features // blocks
    count = order.shape[0]
    left = lambda values: pl.BlockSpec((values.shape[0], block), lambda i, ids: (0, ids[i]))
    right = lambda values: pl.BlockSpec(values.shape, lambda i, ids: (0, 0))
    group_specs = [pl.BlockSpec((1, 4, block, width), lambda i, ids: (0, 0, 0, 0))] * count
    if added:
        out_specs = [pl.BlockSpec((1, 4, block // 2, width), lambda i, ids: (i, 0, 0, 0))] * 2
        out_shape = [jax.ShapeDtypeStruct((count, 4, block // 2, width), bf16)] * 2
    else:
        out_specs = group_specs
        out_shape = [jax.ShapeDtypeStruct((1, 4, block, width), bf16)] * count
    return pl.pallas_call(
        functools.partial(attention_wgrad_kernel, len(added)),
        grid_spec=pltpu.PrefetchScalarGridSpec(
            num_scalar_prefetch=1,
            grid=(count,),
            in_specs=[left(rows_in), left(middle)] + [right(v) for v in sides] + [right(attended)] + (group_specs if added else []),
            out_specs=out_specs,
        ),
        out_shape=out_shape,
        compiler_params=params(),
        cost_estimate=cost(8 * rows_in.shape[0] * features * width, 4 * features * width),
        name="attention_wgrad",
    )(order, rows_in, middle, *sides, attended, *added)


def attend_kernel(
    block, qraw, kraw, value, q_scale, k_scale, q_gain, k_gain, cosine, sine,
    seg_col, seg_row, keep_row, q_out, k_out, o_out, lse_out, bias,
):
    @pl.when(pl.program_id(0) == 0)
    def _():
        fill_bias(bias, seg_col, seg_row, keep_row, block)

    def rotated(raw, scale, gain):
        normed = raw[...] * scale[...] * gain[...]
        return (normed * cosine[...] + turned(normed) * sine[...]).astype(bf16)

    q_out[...] = rotated(qraw, q_scale, q_gain)
    k_out[...] = rotated(kraw, k_scale, k_gain)
    length = seg_col.shape[0]
    for start in range(0, length, block):
        first, stop = key_start(start), start + block
        scores = nt(q_out[start:stop, :], k_out[first:stop, :]) * HEAD ** (-0.5)
        scores = scores + bias[start:stop, : stop - first]
        top = jnp.max(scores, axis=1, keepdims=True)
        powers = jnp.exp(scores - top)
        total = jnp.sum(powers, axis=1, keepdims=True)
        weights = (powers * (1.0 / total)).astype(bf16)
        o_out[start:stop, :] = nn(weights, value[first:stop, :]).astype(bf16)
        lse_out[start:stop, :] = jnp.broadcast_to(top + jnp.log(total), (block, HEAD))


def attend(qraw, kraw, value, q_scale, k_scale, q_gain, k_gain, cosine, sine, seg, keep):
    length, width = qraw.shape
    block = min(256, length)
    span = min(DOC + block, length)
    head = pl.BlockSpec((length, HEAD), lambda h: (0, h))
    gain = pl.BlockSpec((1, HEAD), lambda h: (0, h))
    whole = lambda *shape: pl.BlockSpec(shape, lambda h: (0, 0))
    return pl.pallas_call(
        functools.partial(attend_kernel, block),
        grid=(width // HEAD,),
        in_specs=[head, head, head, whole(length, 1), whole(length, 1), gain, gain]
        + [whole(length, HEAD), whole(length, HEAD), whole(length, 1), whole(1, length), whole(1, length)],
        out_specs=[head, head, head, head],
        out_shape=[jax.ShapeDtypeStruct((length, width), t) for t in (bf16, bf16, bf16, f32)],
        scratch_shapes=[pltpu.VMEM((length, span), f32)],
        compiler_params=params(),
        cost_estimate=cost(4 * length * span * width, 18 * length * width, length * span * width // HEAD),
        name="attend",
    )(qraw, kraw, value, q_scale, k_scale, q_gain[None], k_gain[None], cosine, sine, seg[:, None], seg[None], keep[None])


def attend_back_kernel(
    block, query, key, value, out_grad, lse, qraw, kraw, q_scale, k_scale, q_gain, k_gain, cosine, sine,
    seg_col, seg_row, keep_row, dq_out, dk_out, dv_out, qdot_out, kdot_out, qg_out, kg_out, bias, dk_sum, dv_sum,
):
    at = pl.program_id(0)

    @pl.when(at == 0)
    def _():
        fill_bias(bias, seg_col, seg_row, keep_row, block)
        qdot_out[...] = jnp.zeros_like(qdot_out)
        kdot_out[...] = jnp.zeros_like(kdot_out)

    dk_sum[...] = jnp.zeros_like(dk_sum)
    dv_sum[...] = jnp.zeros_like(dv_sum)
    length = seg_col.shape[0]
    scale = HEAD ** (-0.5)
    for start in range(0, length, block):
        first, stop = key_start(start), start + block
        rows, keys = slice(start, stop), slice(first, stop)
        scores = nt(query[rows, :], key[keys, :]) * scale + bias[rows, : stop - first]
        weights = jnp.exp(scores - lse[rows, :1])
        prob_grad = nt(out_grad[rows, :], value[keys, :])
        inner = jnp.sum(weights * prob_grad, axis=1, keepdims=True)
        score_grad = (weights * (prob_grad - inner)).astype(bf16)
        dq_out[rows, :] = nn(score_grad, key[keys, :]) * scale
        dk_sum[keys, :] += tn(score_grad, query[rows, :])
        dv_sum[keys, :] += tn(weights.astype(bf16), out_grad[rows, :])

    def unrotated(grad):
        return grad * cosine[...] + turned(grad * sine[...])

    dv_out[...] = dv_sum[...].astype(bf16)
    dq = unrotated(dq_out[...])
    dk = unrotated(dk_sum[...] * scale)
    dq_out[...] = dq
    dk_out[...] = dk
    dq = dq * qraw[...]
    dk = dk * kraw[...]
    qg_out[...] = jnp.sum(dq * q_scale[...], axis=0, keepdims=True)
    kg_out[...] = jnp.sum(dk * k_scale[...], axis=0, keepdims=True)
    qdot_out[...] += jnp.sum(dq * q_gain[...], axis=1, keepdims=True)
    kdot_out[...] += jnp.sum(dk * k_gain[...], axis=1, keepdims=True)


def attend_back(query, key, value, out_grad, lse, qraw, kraw, q_scale, k_scale, q_gain, k_gain, cosine, sine, seg, keep):
    length, width = qraw.shape
    block = min(256, length)
    span = min(DOC + block, length)
    head = pl.BlockSpec((length, HEAD), lambda h: (0, h))
    gain = pl.BlockSpec((1, HEAD), lambda h: (0, h))
    whole = lambda *shape: pl.BlockSpec(shape, lambda h: (0, 0))
    sds = jax.ShapeDtypeStruct
    return pl.pallas_call(
        functools.partial(attend_back_kernel, block),
        grid=(width // HEAD,),
        in_specs=[head] * 7
        + [whole(length, 1), whole(length, 1), gain, gain]
        + [whole(length, HEAD), whole(length, HEAD), whole(length, 1), whole(1, length), whole(1, length)],
        out_specs=[head, head, head, whole(length, 1), whole(length, 1), gain, gain],
        out_shape=[sds((length, width), f32), sds((length, width), f32), sds((length, width), bf16)]
        + [sds((length, 1), f32), sds((length, 1), f32), sds((1, width), f32), sds((1, width), f32)],
        scratch_shapes=[pltpu.VMEM((length, span), f32), pltpu.VMEM((length, HEAD), f32), pltpu.VMEM((length, HEAD), f32)],
        compiler_params=params(),
        cost_estimate=cost(10 * length * span * width, 32 * length * width, length * span * width // HEAD),
        name="attend_back",
    )(query, key, value, out_grad, lse, qraw, kraw, q_scale, k_scale, q_gain[None], k_gain[None], cosine, sine, seg[:, None], seg[None], keep[None])


def up_back_kernel(grad, down_w, out):
    width = down_w.shape[2]
    for at in range(down_w.shape[0]):
        out[:, at * width : (at + 1) * width] = nn(grad[...], down_w[at]).astype(out.dtype)


def up_back(grad, down_w):
    rows, features = grad.shape
    experts, _, width = down_w.shape
    step = 2 if experts % 2 == 0 else 1
    return pl.pallas_call(
        up_back_kernel,
        grid=(experts // step,),
        in_specs=[pl.BlockSpec((rows, features), lambda e: (0, 0)), pl.BlockSpec((step, features, width), lambda e: (e, 0, 0))],
        out_specs=pl.BlockSpec((rows, step * width), lambda e: (0, e)),
        out_shape=jax.ShapeDtypeStruct((rows, experts * width), bf16),
        compiler_params=params(),
        cost_estimate=cost(2 * rows * features * experts * width, 2 * (rows + experts * width) * features),
        name="up_back",
    )(grad, down_w)


def expert_kernel(block, rows_in, back, routed, router, gate_w, up_w, act_out, dgate_out, dup_out, grad_out, comb, dcomb, total):
    at = pl.program_id(0)
    rows, features = rows_in.shape
    lane = lax.broadcasted_iota(jnp.int32, (block, LANES), 1)

    @pl.when(at == 0)
    def _():
        experts = pl.num_programs(0)
        for start in range(0, rows, block):
            here = slice(start, start + block)
            logits = jnp.where(lane < experts, nn(rows_in[here, :], router[...]), MASKED)
            powers = jnp.exp(logits - jnp.max(logits, axis=1, keepdims=True))
            probs = powers / jnp.sum(powers, axis=1, keepdims=True)
            comb[here, :] = probs * routed[here, :]
        total[...] = jnp.zeros_like(total)
        dcomb[...] = jnp.zeros_like(dcomb)

    gate, up = gate_w[0], up_w[0]
    mine = lane == at
    for start in range(0, rows, block):
        here = slice(start, start + block)
        taken = rows_in[here, :]
        pre_gate = nn(taken, gate)
        pre_up = nn(taken, up)
        behind = back[here, :].astype(f32)
        share = jnp.sum(jnp.where(mine, comb[here, :], 0.0), axis=1, keepdims=True)
        sigmoid = 0.5 * jnp.tanh(0.5 * pre_gate) + 0.5
        active = pre_gate * sigmoid
        inner = active * pre_up
        share_grad = jnp.sum(inner * behind, axis=1, keepdims=True)
        dcomb[here, :] = jnp.where(mine, share_grad, dcomb[here, :])
        act_out[here, :] = (inner * share).astype(bf16)
        inner_grad = behind * share
        dgate = (inner_grad * pre_up * (sigmoid + active * (1.0 - sigmoid))).astype(bf16)
        dup = (inner_grad * active).astype(bf16)
        dgate_out[here, :] = dgate
        dup_out[here, :] = dup
        total[here, :] += nt(dgate, gate) + nt(dup, up)

    @pl.when(at == pl.num_programs(0) - 1)
    def _():
        grad_out[:, :features] = total[...].astype(bf16)
        grad_out[:, features:] = dcomb[...].astype(bf16)


def experts_block(rows_in, back, routed, router, gate_w, up_w):
    rows, features = rows_in.shape
    experts, _, width = gate_w.shape
    block = min(512, rows)
    whole = lambda *shape: pl.BlockSpec(shape, lambda e: (0, 0))
    column = pl.BlockSpec((rows, width), lambda e: (0, e))
    weight = pl.BlockSpec((1, features, width), lambda e: (e, 0, 0))
    wide = jax.ShapeDtypeStruct((rows, experts * width), bf16)
    return pl.pallas_call(
        functools.partial(expert_kernel, block),
        grid=(experts,),
        in_specs=[whole(rows, features), column, whole(rows, LANES), whole(features, LANES), weight, weight],
        out_specs=[column, column, column, whole(rows, features + LANES)],
        out_shape=[wide, wide, wide, jax.ShapeDtypeStruct((rows, features + LANES), bf16)],
        scratch_shapes=[pltpu.VMEM((rows, LANES), f32), pltpu.VMEM((rows, LANES), f32), pltpu.VMEM((rows, features), f32)],
        compiler_params=params(),
        cost_estimate=cost(8 * rows * features * experts * width, 4 * experts * width * (features + 2 * rows), rows * experts * width),
        name="experts",
    )(rows_in, back, routed, router, gate_w, up_w)


def wgrad_kernel(count, extra, per, block, order, *refs):
    lefts, rights = refs[:count], refs[count : 2 * count]
    added = refs[2 * count : 2 * count + extra]
    outs = refs[2 * count + extra :]
    at = pl.program_id(0)
    features = lefts[0].shape[1]

    def piece(start, stop):
        total = tn(lefts[0][:, start:stop], rights[0][...])
        for left, right in zip(lefts[1:], rights[1:]):
            total = total + tn(left[:, start:stop], right[...])
        return total

    if not added:
        for place, out in enumerate(outs):

            @pl.when(at // per == place)
            def _(out=out):
                for start in range(0, features, block):
                    out[0, start : start + block, :] = piece(start, start + block).astype(bf16)

        return
    half = features // 2
    for place, got in enumerate(added):

        @pl.when(at // per == place)
        def _(got=got):
            for start in range(0, features, block):
                total = piece(start, start + block) + got[0, start : start + block, :].astype(f32)
                outs[start // half][0, start % half : start % half + block, :] = total.astype(bf16)


def wgrad(lefts, rights, order, width, per, added=()):
    features = lefts[0].shape[1]
    experts = order.shape[0]
    groups = experts // per
    rows = sum(left.shape[0] for left in lefts)

    def group_spec(place):
        return pl.BlockSpec((1, features, width), lambda i, ids: (jnp.clip(i - place * per, 0, per - 1), 0, 0))

    groups_specs = [group_spec(place) for place in range(groups)]
    if added:
        out_specs = [pl.BlockSpec((1, features // 2, width), lambda i, ids: (i, 0, 0))] * 2
        out_shape = [jax.ShapeDtypeStruct((experts, features // 2, width), bf16)] * 2
    else:
        out_specs = groups_specs
        out_shape = [jax.ShapeDtypeStruct((per, features, width), bf16)] * groups
    return pl.pallas_call(
        functools.partial(wgrad_kernel, len(lefts), len(added), per, min(512, features // 2)),
        grid_spec=pltpu.PrefetchScalarGridSpec(
            num_scalar_prefetch=1,
            grid=(experts,),
            in_specs=[pl.BlockSpec(left.shape, lambda i, ids: (0, 0)) for left in lefts]
            + [pl.BlockSpec((right.shape[0], width), lambda i, ids: (0, ids[i])) for right in rights]
            + (groups_specs if added else []),
            out_specs=out_specs,
        ),
        out_shape=out_shape,
        compiler_params=params(),
        cost_estimate=cost(2 * rows * features * experts * width, 2 * (rows + 2 * experts * width) * features),
        name="wgrad",
    )(order, *lefts, *rights, *added)


def down_kernel(parts, down_w, *refs):
    acts, out = refs[:-1], refs[-1]
    joined = jnp.concatenate([down_w[e] for e in range(down_w.shape[0])], axis=1)
    block = acts[0].shape[0] // parts
    for at, act in enumerate(acts):
        result = nt(act[...], joined).astype(out.dtype)
        for part in range(parts):
            start = (part * len(acts) + at) * block
            out[start : start + block, :] = result[part * block : (part + 1) * block, :]


def down(acts, down_w, parts):
    rows = sum(act.shape[0] for act in acts)
    experts, features, width = down_w.shape
    block = min(256, features)
    return pl.pallas_call(
        functools.partial(down_kernel, parts),
        grid=(features // block,),
        in_specs=[pl.BlockSpec((experts, block, width), lambda n: (0, n, 0))]
        + [pl.BlockSpec(act.shape, lambda n: (0, 0)) for act in acts],
        out_specs=pl.BlockSpec((rows, block), lambda n: (0, n)),
        out_shape=jax.ShapeDtypeStruct((rows, features), bf16),
        compiler_params=params(),
        cost_estimate=cost(2 * rows * features * experts * width, 2 * (rows + experts * width) * features),
        name="down",
    )(down_w, *acts)


def gate(value, *others):
    return lax.optimization_barrier((value, others))[0]


def gather_rows(values):
    return lax.all_gather(values, "tensor", axis=0, tiled=True)


def scatter_rows(values):
    return lax.psum_scatter(values, "tensor", scatter_dimension=0, tiled=True)


def join_kernel(parts, slots, own, *refs):
    ups, downs, out = refs[: parts - 1], refs[parts - 1 : 2 * parts - 2], refs[2 * parts - 2]
    at = pl.program_id(0)

    @pl.when(at == 0)
    def _():
        out[...] = own[...]

    for step in range(1, parts):

        @pl.when(at == step)
        def _(step=step):
            out[...] = ups[step - 1][...] + downs[parts - 1 - step][...]


def join(slots, own, ups, downs):
    rows, columns = own.shape
    parts = len(ups) + 1
    whole = pl.BlockSpec((rows, columns), lambda i, to: (0, 0))
    return pl.pallas_call(
        functools.partial(join_kernel, parts),
        grid_spec=pltpu.PrefetchScalarGridSpec(
            num_scalar_prefetch=1,
            grid=(parts,),
            in_specs=[whole] * (2 * parts - 1),
            out_specs=pl.BlockSpec((rows, columns), lambda i, to: (to[i], 0)),
        ),
        out_shape=jax.ShapeDtypeStruct((parts * rows, columns), own.dtype),
        compiler_params=params(),
        cost_estimate=cost(0, 0),
        name="join",
    )(slots, own, *ups, *downs)


class Chain:
    def __init__(self, values):
        self.values = values
        self.parts = lax.axis_size("tensor")
        self.ups, self.downs = [values], [values]

    def hop(self, *others):
        step = len(self.ups)
        if step < self.parts:
            up, down = gate((self.ups[-1], self.downs[-1]), *others) if others else (self.ups[-1], self.downs[-1])
            self.sent = (up, down)
            self.ups.append(lax.ppermute(up, "tensor", [(i, i + 1) for i in range(step - 1, self.parts - 1)]))
            self.downs.append(lax.ppermute(down, "tensor", [(i, i - 1) for i in range(1, self.parts - step + 1)]))
        return self.sent

    def recv(self):
        return self.ups[-1], self.downs[-1]

    def joined(self):
        while len(self.ups) < self.parts:
            self.hop()
        at = lax.axis_index("tensor")
        slots = lax.rem(at - jnp.arange(self.parts, dtype=jnp.int32) + self.parts, self.parts)
        return join(slots, self.values, self.ups[1:], self.downs[1:])


def pair_swap(values, step):
    size = lax.axis_size("dp")
    return lax.ppermute(values, "dp", [(i, i ^ step) for i in range(size)])


class Halving:
    def __init__(self, values):
        bits = list(range(values[0].shape[0].bit_length() - 1))
        self.kept = list(values)
        self.left = [bits[::-1], bits]
        self.got = None

    def send(self):
        if not self.left[0]:
            return ()
        self.got = []
        sent = []
        for side, downward in ((0, True), (1, False)):
            bit = self.left[side].pop(0)
            kept = self.kept[side]
            half = kept.shape[0] // 2
            if downward:
                keep, go = kept[:half], kept[half:]
            else:
                view = kept.reshape((half, 2) + kept.shape[1:])
                keep, go = view[:, 0], view[:, 1]
            sent.append(go)
            self.got.append(pair_swap(go, 2 << bit))
            self.kept[side] = keep
        return tuple(sent)

    def add(self, *others):
        if self.got is not None:
            if others:
                self.got = gate(tuple(self.got), *others)
            last = not self.left[0]
            for side in range(2):
                total = self.kept[side].astype(f32) + self.got[side].astype(f32)
                self.kept[side] = total if last else total.astype(bf16)
            self.got = None
        return tuple(self.kept)

    def done(self):
        self.add()
        while self.left[0]:
            self.send()
            self.add()
        return jnp.concatenate([kept[0].astype(f32) for kept in self.kept], axis=1)


def exchange_sum(values, axes):
    for axis in axes:
        size = lax.axis_size(axis)
        step = 1
        while step < size:
            values = values + lax.ppermute(values, axis, [(i, i ^ step) for i in range(size)])
            step *= 2
    return values


def local(
    tokens, cotangent, seg_ids, keep_mask, routes, attn_gain, w_query, w_key, w_value, w_out,
    q_gain, k_gain, ffn_gain, router, w_gate, w_up, w_down,
):
    parts = lax.axis_size("tensor")
    part_at = lax.axis_index("tensor")
    dp_size = lax.axis_size("dp")
    low_bit = lax.axis_index("dp") % 2
    shard_rows, features = tokens.shape
    group_rows = shard_rows * parts
    _, length = seg_ids.shape
    local_width = w_query.shape[1]
    experts, _, width = w_gate.shape
    per = experts // dp_size
    chunk_rows = shard_rows // CHUNKS
    chunks = range(CHUNKS)
    own = [slice(c * chunk_rows, (c + 1) * chunk_rows) for c in chunks]

    def chunk_of(values, c):
        columns = values.shape[1]
        return values.reshape(parts, CHUNKS, chunk_rows, columns)[:, c].reshape(parts * chunk_rows, columns)

    inputs = tokens.astype(f32)
    first_scale = rms_scale(inputs)
    normed_all = gather_rows((inputs * first_scale * attn_gain).astype(bf16))
    behind = Chain(gate(cotangent, normed_all))

    cosine, sine = rope_tables(length, HEAD)

    relative = jnp.arange(dp_size // 2, dtype=jnp.int32) ^ (lax.axis_index("dp") // 2)
    own_blocks, other_blocks = 2 * relative + low_bit, 2 * relative + 1 - low_bit
    mine, theirs = (
        (blocks[:, None] * per + jnp.arange(per, dtype=jnp.int32)).reshape(-1) for blocks in (own_blocks, other_blocks)
    )

    qraw, kraw, value, squares = project(normed_all, w_query, w_key, w_value)
    squares = exchange_sum(squares, ("tensor",))
    behind.hop()
    q_scale, k_scale = (lax.rsqrt(squares[i] / features + EPSILON)[:, None] for i in range(2))
    query, key, attended, lse = attend(
        qraw, kraw, value, q_scale, k_scale, q_gain, k_gain, cosine, sine, gate(seg_ids[0], *behind.recv()), keep_mask[0]
    )
    behind.hop()
    attended_parts = [chunk_of(gate(attended, *behind.recv()), c) for c in chunks]
    outs = [nt(attended_parts[0], w_out).astype(bf16)]
    summed = [scatter_rows(outs[0])]
    outs.append(nt(gate(attended_parts[1], outs[0]), w_out).astype(bf16))
    summed.append(scatter_rows(outs[1]))
    behind.hop(outs[1])

    idle_routes, idle_router = gate((routes, router), outs[1])
    expert_ids = jnp.arange(LANES)
    routed = jnp.sum((idle_routes[:, :, None] == expert_ids[None, None, :]).astype(f32), axis=1)
    router_wide = jnp.pad(idle_router, ((0, 0), (0, LANES - experts)))
    routed_own = lax.dynamic_slice_in_dim(routed, part_at * shard_rows, shard_rows, 0)[:, :experts]
    grad_group = behind.joined()
    grad_all = [chunk_of(grad_group, c) for c in chunks]
    backs = [up_back(gate(rows, routed, router_wide), w_down) for rows in grad_all]

    middles, scales, ffn_own = [], [], []

    def middle_of(c, total):
        middle = inputs[own[c]] + total.astype(f32)
        scale = rms_scale(middle)
        normed = (middle * scale * ffn_gain).astype(bf16)
        middles.append(middle)
        scales.append(scale)
        ffn_own.append(normed)
        return normed

    ffn_all = [gather_rows(middle_of(0, summed[0]))]
    ffn_all.append(gather_rows(middle_of(1, gate(summed[1], ffn_own[0], *backs))))
    acts, dgates, dups, expert_grads = [], [], [], []
    for c in chunks:
        here = gate(chunk_of(routed, c), *backs, *acts[-1:])
        act, dgate, dup, grads = experts_block(ffn_all[c], backs[c], here, router_wide, w_gate, w_up)
        acts.append(act)
        dgates.append(dgate)
        dups.append(dup)
        expert_grads.append(grads)
    expert_grads = [scatter_rows(grads) for grads in expert_grads]

    ffn_gain_parts, router_parts, middle_grads = [], [], []

    def middle_back(c, grads):
        share_grad = grads[:, features : features + experts] * routed_own[own[c]]
        probs = jax.nn.softmax(nn(ffn_own[c], router), axis=-1)
        logit_grad = (probs * (share_grad - jnp.sum(share_grad * probs, axis=-1, keepdims=True))).astype(bf16)
        ffn_grad = grads[:, :features] + nt(logit_grad, router)
        router_parts.append(tn(ffn_own[c], logit_grad))
        ffn_gain_parts.append(jnp.sum(ffn_grad * middles[c] * scales[c], axis=0))
        middle_grads.append(cotangent[own[c]].astype(f32) + norm_back(ffn_grad, middles[c], scales[c], ffn_gain))
        return middle_grads[c].astype(bf16)

    def expert_sums(lefts, rights, ids, *others, added=()):
        return wgrad(lefts, rights, gate(ids, *others), width, per, added)

    def core_swap(pieces):
        return [pair_swap(piece, 1) for piece in pieces]

    def halving(sums):
        return Halving([half.reshape((dp_size // 2, per) + half.shape[1:]) for half in sums])

    first = middle_back(0, gate(expert_grads[0], acts[1]).astype(f32))
    gate_sent = expert_sums(ffn_all, dgates, theirs, first)
    gate_got = core_swap(gate_sent)
    up_sent = expert_sums(ffn_all, dups, theirs, *gate_sent)
    up_got = core_swap(up_sent)
    second = middle_back(1, gate(expert_grads[1], *up_sent).astype(f32))
    middle_all = gather_rows(jnp.concatenate([first, second]))
    gate_sums = expert_sums(ffn_all, dgates, mine, second, added=gate_got)
    gate_out = halving(gate_sums)
    up_sums = expert_sums(ffn_all, dups, mine, *gate_sums, *gate_out.send(), added=up_got)
    up_out = halving(up_sums)
    moe = down([gate(acts[0], *up_sums, *up_out.send()), acts[1]], w_down, parts)
    moe_sum = scatter_rows(moe)
    attended_grad = nn(gate(middle_all, moe), w_out).astype(bf16)
    dqn, dkn, dvalue, qdot, kdot, q_gain_part, k_gain_part = attend_back(
        query, key, value, attended_grad, lse, qraw, kraw, q_scale, k_scale, q_gain, k_gain, cosine, sine,
        seg_ids[0], keep_mask[0],
    )
    dots = exchange_sum(jnp.stack([qdot[:, 0], kdot[:, 0]]), ("tensor",)) / features
    gate_late = gate_out.add(dqn)
    gate_out.send()
    down_sent = expert_sums(grad_all, acts, theirs, *gate_late)
    down_got = core_swap(down_sent)
    normed_part, dqraw, dkraw, attn_gain_part = project_back(
        normed_all, dqn, dkn, dvalue, qraw, kraw, q_scale, k_scale, dots[0][:, None], dots[1][:, None],
        gate(q_gain, *down_sent), k_gain, w_query, w_key, w_value,
    )
    normed_grad = scatter_rows(normed_part)
    up_late = up_out.add(normed_part)
    up_out.send()
    down_sums = expert_sums(grad_all, acts, mine, *up_late, added=down_got)
    down_out = halving(down_sums)
    def attention_sums(ids, *others, added=()):
        return attention_wgrad(
            normed_all, middle_all, (dqraw, dkraw, dvalue), attended, gate(ids, *others), dp_size, added
        )

    attn_sent = attention_sums(other_blocks, *down_out.send())
    attn_got = core_swap(attn_sent)

    def placed(part):
        return lax.dynamic_update_slice_in_dim(jnp.zeros((features,), f32), part, part_at * local_width, 0)

    attn_sums = attention_sums(own_blocks, *attn_sent, added=attn_got)
    attn_out = Halving(attn_sums)
    normed_grad = gate(normed_grad, *attn_out.send())
    smalls = [attn_gain_part[0] / attn_gain, placed(q_gain_part[0]), placed(k_gain_part[0]), sum(ffn_gain_parts)]
    smalls = gate(jnp.concatenate([jnp.stack(smalls), sum(router_parts).T]), normed_grad)
    smalls = exchange_sum(smalls, ("dp", "tensor"))
    gate_done = gate_out.done()
    up_done = up_out.done()
    down_done = down_out.done()
    attn_out.add(normed_grad)
    query_done, key_done, value_done, out_done = attn_out.done()
    layer_out = (jnp.concatenate(middles) + moe_sum.astype(f32)).astype(bf16)
    tokens_grad = jnp.concatenate(middle_grads) + norm_back(normed_grad.astype(f32), inputs, first_scale, attn_gain)
    return (
        layer_out, tokens_grad, query_done, key_done, value_done, out_done,
        smalls[0], smalls[1], smalls[2], smalls[3], smalls[4:].T, gate_done, up_done, down_done,
    )


def solution(mesh):
    rows = P(("dp", "tensor"), None)
    column = P(None, "tensor")
    expert = P(None, None, "tensor")
    in_specs = (
        rows, rows, P("dp", None), P("dp", None), P("dp", None), P(), column, column, column, column,
        P("tensor"), P("tensor"), P(), P(), expert, expert, expert,
    )
    block = P("dp", "tensor")
    expert_out = P("dp", None, "tensor")
    out_specs = (
        rows, rows, block, block, block, block, P(), P(), P(), P(), P(), expert_out, expert_out, expert_out,
    )
    return jax.shard_map(local, mesh=mesh, in_specs=in_specs, out_specs=out_specs, check_vma=False)
```

```python
import functools

import jax
import jax.numpy as jnp
import numpy as np
from jax import lax
from jax.experimental import pallas as pl
from jax.experimental.pallas import tpu as pltpu
from jax.sharding import PartitionSpec as P

D = 2048
HEAD = 128
DOC = 512
LANES = 128
EPSILON = 1e-05
MASKED = -1e30
CHUNKS = 2
VMEM = 56 * 1024 * 1024
bf16 = jnp.bfloat16
f32 = jnp.float32


def nn(left, right):
    return lax.dot_general(left, right, (((1,), (0,)), ((), ())), preferred_element_type=f32)


def nt(left, right):
    return lax.dot_general(left, right, (((1,), (1,)), ((), ())), preferred_element_type=f32)


def tn(left, right):
    return lax.dot_general(left, right, (((0,), (0,)), ((), ())), preferred_element_type=f32)


def params():
    return pltpu.CompilerParams(vmem_limit_bytes=VMEM)


PACE = 0.3


def cost(flops, moved, special=0):
    return pl.CostEstimate(flops=int(1.5 * PACE * flops), bytes_accessed=moved // 8, transcendentals=0)


def rms_scale(values):
    return lax.rsqrt(jnp.mean(values * values, axis=-1, keepdims=True) + EPSILON)


def norm_back(grad_values, values, scale_col, gain_vec):
    weighted = grad_values * gain_vec
    inner_mean = jnp.mean(weighted * values, axis=-1, keepdims=True)
    return scale_col * weighted - values * (scale_col * scale_col * scale_col) * inner_mean


def rope_tables(length, width):
    angles = np.arange(length)[:, None] * 10000.0 ** (-np.arange(width // 2) * 2.0 / width)[None, :]
    cosine, sine = np.cos(angles).astype(np.float32), np.sin(angles).astype(np.float32)
    return jnp.asarray(np.concatenate([cosine, cosine], axis=1)), jnp.asarray(np.concatenate([-sine, sine], axis=1))


def key_start(query_start):
    return max(0, query_start - DOC)


def fill_bias(bias, seg_col, seg_row, keep_row, block):
    length = seg_col.shape[0]
    for start in range(0, length, block):
        first, stop = key_start(start), start + block
        query_pos = start + lax.broadcasted_iota(jnp.int32, (block, stop - first), 0)
        key_pos = first + lax.broadcasted_iota(jnp.int32, (block, stop - first), 1)
        same = seg_col[start:stop, :] == seg_row[:, first:stop]
        live = (keep_row[:, first:stop] == 1) | (key_pos == query_pos)
        allowed = same & live & (key_pos <= query_pos)
        bias[start:stop, : stop - first] = jnp.where(allowed, 0.0, MASKED)


def turned(values):
    return pltpu.roll(values, values.shape[1] // 2, 1)


def project_kernel(rows_in, w_query, w_key, w_value, q_out, k_out, v_out, squares_out):
    ones = jnp.ones((8, q_out.shape[1]), f32)
    for at, (weight, out) in enumerate(((w_query, q_out), (w_key, k_out))):
        raw = nn(rows_in[...], weight[...])
        out[...] = raw
        sums = lax.dot_general(
            ones, raw * raw, (((1,), (1,)), ((), ())), precision=lax.Precision.HIGHEST, preferred_element_type=f32
        )
        squares_out[at : at + 1, :] = sums[:1]
    v_out[...] = nn(rows_in[...], w_value[...]).astype(bf16)


def project(rows_in, w_query, w_key, w_value):
    rows, features = rows_in.shape
    width = w_query.shape[1]
    block = min(256, rows)
    row = lambda columns: pl.BlockSpec((block, columns), lambda r: (r, 0))
    weight = pl.BlockSpec((features, width), lambda r: (0, 0))
    sds = jax.ShapeDtypeStruct
    return pl.pallas_call(
        project_kernel,
        grid=(rows // block,),
        in_specs=[row(features), weight, weight, weight],
        out_specs=[row(width), row(width), row(width), pl.BlockSpec((2, block), lambda r: (0, r))],
        out_shape=[sds((rows, width), f32), sds((rows, width), f32), sds((rows, width), bf16), sds((2, rows), f32)],
        compiler_params=params(),
        cost_estimate=cost(6 * rows * features * width, 2 * (rows + 3 * width) * features),
        name="project",
    )(rows_in, w_query, w_key, w_value)


def project_back_kernel(
    rows_in, dqn, dkn, dvalue, qraw, kraw, q_scale, k_scale, q_dot, k_dot, q_gain, k_gain,
    w_query, w_key, w_value, part_out, dq_out, dk_out, gain_out,
):
    @pl.when(pl.program_id(0) == 0)
    def _():
        gain_out[...] = jnp.zeros_like(gain_out)

    def raw_grad(grad, raw, scale, gain, dot):
        cube = scale[...] * scale[...] * scale[...]
        return (scale[...] * (gain[...] * grad[...]) - raw[...] * (cube * dot[...])).astype(bf16)

    dq = raw_grad(dqn, qraw, q_scale, q_gain, q_dot)
    dk = raw_grad(dkn, kraw, k_scale, k_gain, k_dot)
    dq_out[...] = dq
    dk_out[...] = dk
    part = nt(dq, w_query[...]) + nt(dk, w_key[...]) + nt(dvalue[...], w_value[...])
    part_out[...] = part.astype(bf16)
    gain_out[...] += jnp.sum(part * rows_in[...].astype(f32), axis=0, keepdims=True)


def project_back(rows_in, dqn, dkn, dvalue, qraw, kraw, q_scale, k_scale, q_dot, k_dot, q_gain, k_gain, w_query, w_key, w_value):
    rows, features = rows_in.shape
    width = w_query.shape[1]
    block = min(256, rows)
    row = lambda columns: pl.BlockSpec((block, columns), lambda r: (r, 0))
    whole = lambda *shape: pl.BlockSpec(shape, lambda r: (0, 0))
    sds = jax.ShapeDtypeStruct
    return pl.pallas_call(
        project_back_kernel,
        grid=(rows // block,),
        in_specs=[row(features)] + [row(width)] * 5 + [row(1)] * 4 + [whole(1, width)] * 2 + [whole(features, width)] * 3,
        out_specs=[row(features), row(width), row(width), whole(1, features)],
        out_shape=[sds((rows, features), bf16), sds((rows, width), bf16), sds((rows, width), bf16), sds((1, features), f32)],
        compiler_params=params(),
        cost_estimate=cost(6 * rows * features * width, 2 * (rows + 3 * width) * features),
        name="project_back",
    )(rows_in, dqn, dkn, dvalue, qraw, kraw, q_scale, k_scale, q_dot, k_dot, q_gain[None], k_gain[None], w_query, w_key, w_value)


def attention_wgrad_kernel(added, order, rows_in, middle, *refs):
    sides, (attended,), refs = refs[:3], refs[3:4], refs[4:]
    got, outs = (refs[:added], refs[added:])
    at = pl.program_id(0)
    totals = [tn(rows_in[...], side[...]) for side in sides] + [tn(middle[...], attended[...])]
    if not added:
        for place, out in enumerate(outs):

            @pl.when(at == place)
            def _(out=out):
                for weight, total in enumerate(totals):
                    out[0, weight] = total.astype(bf16)

        return
    half = outs[0].shape[2]
    for place, piece in enumerate(got):

        @pl.when(at == place)
        def _(piece=piece):
            for weight, total in enumerate(totals):
                total = total + piece[0, weight].astype(f32)
                for side, out in enumerate(outs):
                    out[0, weight] = total[side * half : (side + 1) * half, :].astype(bf16)


def attention_wgrad(rows_in, middle, sides, attended, order, blocks, added=()):
    features = rows_in.shape[1]
    width = sides[0].shape[1]
    block = features // blocks
    count = order.shape[0]
    left = lambda values: pl.BlockSpec((values.shape[0], block), lambda i, ids: (0, ids[i]))
    right = lambda values: pl.BlockSpec(values.shape, lambda i, ids: (0, 0))
    group_specs = [pl.BlockSpec((1, 4, block, width), lambda i, ids: (0, 0, 0, 0))] * count
    if added:
        out_specs = [pl.BlockSpec((1, 4, block // 2, width), lambda i, ids: (i, 0, 0, 0))] * 2
        out_shape = [jax.ShapeDtypeStruct((count, 4, block // 2, width), bf16)] * 2
    else:
        out_specs = group_specs
        out_shape = [jax.ShapeDtypeStruct((1, 4, block, width), bf16)] * count
    return pl.pallas_call(
        functools.partial(attention_wgrad_kernel, len(added)),
        grid_spec=pltpu.PrefetchScalarGridSpec(
            num_scalar_prefetch=1,
            grid=(count,),
            in_specs=[left(rows_in), left(middle)] + [right(v) for v in sides] + [right(attended)] + (group_specs if added else []),
            out_specs=out_specs,
        ),
        out_shape=out_shape,
        compiler_params=params(),
        cost_estimate=cost(0, 0),
        name="attention_wgrad",
    )(order, rows_in, middle, *sides, attended, *added)


def attend_kernel(
    block, qraw, kraw, value, q_scale, k_scale, q_gain, k_gain, cosine, sine,
    seg_col, seg_row, keep_row, q_out, k_out, o_out, lse_out, bias,
):
    @pl.when(pl.program_id(0) == 0)
    def _():
        fill_bias(bias, seg_col, seg_row, keep_row, block)

    def rotated(raw, scale, gain):
        normed = raw[...] * scale[...] * gain[...]
        return (normed * cosine[...] + turned(normed) * sine[...]).astype(bf16)

    q_out[...] = rotated(qraw, q_scale, q_gain)
    k_out[...] = rotated(kraw, k_scale, k_gain)
    length = seg_col.shape[0]
    for start in range(0, length, block):
        first, stop = key_start(start), start + block
        scores = nt(q_out[start:stop, :], k_out[first:stop, :]) * HEAD ** (-0.5)
        scores = scores + bias[start:stop, : stop - first]
        top = jnp.max(scores, axis=1, keepdims=True)
        powers = jnp.exp(scores - top)
        total = jnp.sum(powers, axis=1, keepdims=True)
        weights = (powers * (1.0 / total)).astype(bf16)
        o_out[start:stop, :] = nn(weights, value[first:stop, :]).astype(bf16)
        lse_out[start:stop, :] = jnp.broadcast_to(top + jnp.log(total), (block, HEAD))


def attend(qraw, kraw, value, q_scale, k_scale, q_gain, k_gain, cosine, sine, seg, keep):
    length, width = qraw.shape
    block = min(256, length)
    span = min(DOC + block, length)
    head = pl.BlockSpec((length, HEAD), lambda h: (0, h))
    gain = pl.BlockSpec((1, HEAD), lambda h: (0, h))
    whole = lambda *shape: pl.BlockSpec(shape, lambda h: (0, 0))
    return pl.pallas_call(
        functools.partial(attend_kernel, block),
        grid=(width // HEAD,),
        in_specs=[head, head, head, whole(length, 1), whole(length, 1), gain, gain]
        + [whole(length, HEAD), whole(length, HEAD), whole(length, 1), whole(1, length), whole(1, length)],
        out_specs=[head, head, head, head],
        out_shape=[jax.ShapeDtypeStruct((length, width), t) for t in (bf16, bf16, bf16, f32)],
        scratch_shapes=[pltpu.VMEM((length, span), f32)],
        compiler_params=params(),
        cost_estimate=cost(4 * length * span * width, 18 * length * width, length * span * width // HEAD),
        name="attend",
    )(qraw, kraw, value, q_scale, k_scale, q_gain[None], k_gain[None], cosine, sine, seg[:, None], seg[None], keep[None])


def attend_back_kernel(
    block, query, key, value, out_grad, lse, qraw, kraw, q_scale, k_scale, q_gain, k_gain, cosine, sine,
    seg_col, seg_row, keep_row, dq_out, dk_out, dv_out, qdot_out, kdot_out, qg_out, kg_out, bias, dk_sum, dv_sum,
):
    at = pl.program_id(0)

    @pl.when(at == 0)
    def _():
        fill_bias(bias, seg_col, seg_row, keep_row, block)
        qdot_out[...] = jnp.zeros_like(qdot_out)
        kdot_out[...] = jnp.zeros_like(kdot_out)

    dk_sum[...] = jnp.zeros_like(dk_sum)
    dv_sum[...] = jnp.zeros_like(dv_sum)
    length = seg_col.shape[0]
    scale = HEAD ** (-0.5)
    for start in range(0, length, block):
        first, stop = key_start(start), start + block
        rows, keys = slice(start, stop), slice(first, stop)
        scores = nt(query[rows, :], key[keys, :]) * scale + bias[rows, : stop - first]
        weights = jnp.exp(scores - lse[rows, :1])
        prob_grad = nt(out_grad[rows, :], value[keys, :])
        inner = jnp.sum(weights * prob_grad, axis=1, keepdims=True)
        score_grad = (weights * (prob_grad - inner)).astype(bf16)
        dq_out[rows, :] = nn(score_grad, key[keys, :]) * scale
        dk_sum[keys, :] += tn(score_grad, query[rows, :])
        dv_sum[keys, :] += tn(weights.astype(bf16), out_grad[rows, :])

    def unrotated(grad):
        return grad * cosine[...] + turned(grad * sine[...])

    dv_out[...] = dv_sum[...].astype(bf16)
    dq = unrotated(dq_out[...])
    dk = unrotated(dk_sum[...] * scale)
    dq_out[...] = dq
    dk_out[...] = dk
    dq = dq * qraw[...]
    dk = dk * kraw[...]
    qg_out[...] = jnp.sum(dq * q_scale[...], axis=0, keepdims=True)
    kg_out[...] = jnp.sum(dk * k_scale[...], axis=0, keepdims=True)
    qdot_out[...] += jnp.sum(dq * q_gain[...], axis=1, keepdims=True)
    kdot_out[...] += jnp.sum(dk * k_gain[...], axis=1, keepdims=True)


def attend_back(query, key, value, out_grad, lse, qraw, kraw, q_scale, k_scale, q_gain, k_gain, cosine, sine, seg, keep):
    length, width = qraw.shape
    block = min(256, length)
    span = min(DOC + block, length)
    head = pl.BlockSpec((length, HEAD), lambda h: (0, h))
    gain = pl.BlockSpec((1, HEAD), lambda h: (0, h))
    whole = lambda *shape: pl.BlockSpec(shape, lambda h: (0, 0))
    sds = jax.ShapeDtypeStruct
    return pl.pallas_call(
        functools.partial(attend_back_kernel, block),
        grid=(width // HEAD,),
        in_specs=[head] * 7
        + [whole(length, 1), whole(length, 1), gain, gain]
        + [whole(length, HEAD), whole(length, HEAD), whole(length, 1), whole(1, length), whole(1, length)],
        out_specs=[head, head, head, whole(length, 1), whole(length, 1), gain, gain],
        out_shape=[sds((length, width), f32), sds((length, width), f32), sds((length, width), bf16)]
        + [sds((length, 1), f32), sds((length, 1), f32), sds((1, width), f32), sds((1, width), f32)],
        scratch_shapes=[pltpu.VMEM((length, span), f32), pltpu.VMEM((length, HEAD), f32), pltpu.VMEM((length, HEAD), f32)],
        compiler_params=params(),
        cost_estimate=cost(10 * length * span * width, 32 * length * width, length * span * width // HEAD),
        name="attend_back",
    )(query, key, value, out_grad, lse, qraw, kraw, q_scale, k_scale, q_gain[None], k_gain[None], cosine, sine, seg[:, None], seg[None], keep[None])


def up_back_kernel(grad, down_w, out):
    width = down_w.shape[2]
    for at in range(down_w.shape[0]):
        out[:, at * width : (at + 1) * width] = nn(grad[...], down_w[at]).astype(out.dtype)


def up_back(grad, down_w):
    rows, features = grad.shape
    experts, _, width = down_w.shape
    step = 2 if experts % 2 == 0 else 1
    return pl.pallas_call(
        up_back_kernel,
        grid=(experts // step,),
        in_specs=[pl.BlockSpec((rows, features), lambda e: (0, 0)), pl.BlockSpec((step, features, width), lambda e: (e, 0, 0))],
        out_specs=pl.BlockSpec((rows, step * width), lambda e: (0, e)),
        out_shape=jax.ShapeDtypeStruct((rows, experts * width), bf16),
        compiler_params=params(),
        cost_estimate=cost(2 * rows * features * experts * width, 2 * (rows + experts * width) * features),
        name="up_back",
    )(grad, down_w)


def expert_kernel(block, peers, per, order, rows_in, back, routed, router, gate_w, up_w, *refs):
    acts, (dgate_out, dup_out, grad_out, comb, dcomb, total) = refs[-6 - peers : -6], refs[-6:]
    at = pl.program_id(0)
    rows, features = rows_in.shape
    lane = lax.broadcasted_iota(jnp.int32, (block, LANES), 1)

    @pl.when(at == 0)
    def _():
        experts = pl.num_programs(0)
        for start in range(0, rows, block):
            here = slice(start, start + block)
            logits = jnp.where(lane < experts, nn(rows_in[here, :], router[...]), MASKED)
            powers = jnp.exp(logits - jnp.max(logits, axis=1, keepdims=True))
            probs = powers / jnp.sum(powers, axis=1, keepdims=True)
            comb[here, :] = probs * routed[here, :]
        total[...] = jnp.zeros_like(total)
        dcomb[...] = jnp.zeros_like(dcomb)

    gate, up = gate_w[0], up_w[0]
    mine = lane == order[at]
    for start in range(0, rows, block):
        here = slice(start, start + block)
        taken = rows_in[here, :]
        pre_gate = nn(taken, gate)
        pre_up = nn(taken, up)
        behind = back[here, :].astype(f32)
        share = jnp.sum(jnp.where(mine, comb[here, :], 0.0), axis=1, keepdims=True)
        sigmoid = 0.5 * jnp.tanh(0.5 * pre_gate) + 0.5
        active = pre_gate * sigmoid
        inner = active * pre_up
        share_grad = jnp.sum(inner * behind, axis=1, keepdims=True)
        dcomb[here, :] = jnp.where(mine, share_grad, dcomb[here, :])
        act = (inner * share).astype(bf16)
        for peer in range(peers):

            @pl.when(at // per == peer)
            def _(peer=peer):
                acts[peer][here, :] = act

        inner_grad = behind * share
        dgate = (inner_grad * pre_up * (sigmoid + active * (1.0 - sigmoid))).astype(bf16)
        dup = (inner_grad * active).astype(bf16)
        dgate_out[here, :] = dgate
        dup_out[here, :] = dup
        total[here, :] += nt(dgate, gate) + nt(dup, up)

    @pl.when(at == pl.num_programs(0) - 1)
    def _():
        grad_out[:, :features] = total[...].astype(bf16)
        grad_out[:, features:] = dcomb[...].astype(bf16)


def experts_chunk(chunk, order, per, rows_in, back, routed, router, gate_w, up_w, filled=()):
    rows, features = rows_in.shape
    experts, _, width = gate_w.shape
    peers = experts // per
    block = min(512, rows)
    whole = lambda *shape: pl.BlockSpec(shape, lambda i, ids: (0, 0))
    column = pl.BlockSpec((rows, width), lambda i, ids: (chunk, ids[i]))
    act = lambda peer: pl.BlockSpec((rows, width), lambda i, ids: (chunk, jnp.clip(i - peer * per, 0, per - 1)))
    weight = pl.BlockSpec((1, features, width), lambda i, ids: (ids[i], 0, 0))
    sds = lambda *shape: jax.ShapeDtypeStruct(shape, bf16)
    result = pl.pallas_call(
        functools.partial(expert_kernel, block, peers, per),
        grid_spec=pltpu.PrefetchScalarGridSpec(
            num_scalar_prefetch=1,
            grid=(experts,),
            in_specs=[whole(rows, features), column, whole(rows, LANES), whole(features, LANES), weight, weight]
            + [pl.BlockSpec(memory_space=pl.ANY)] * len(filled),
            out_specs=[act(peer) for peer in range(peers)] + [column, column, whole(rows, features + LANES)],
            scratch_shapes=[pltpu.VMEM((rows, LANES), f32), pltpu.VMEM((rows, LANES), f32), pltpu.VMEM((rows, features), f32)],
        ),
        out_shape=[sds(CHUNKS * rows, per * width)] * peers
        + [sds(CHUNKS * rows, experts * width)] * 2
        + [sds(rows, features + LANES)],
        input_output_aliases={7 + at: at for at in range(len(filled))},
        compiler_params=params(),
        cost_estimate=cost(8 * rows * features * experts * width, 4 * experts * width * (features + 2 * rows)),
        name="experts",
    )(order, rows_in, back, routed, router, gate_w, up_w, *filled)
    return result[:-1], result[-1]


def wgrad_kernel(count, extra, per, block, order, *refs):
    lefts, right = refs[:count], refs[count]
    added = refs[count + 1 : count + 1 + extra]
    outs = refs[count + 1 + extra :]
    at = pl.program_id(0)
    features = lefts[0].shape[1]

    def piece(start, stop):
        total, row = None, 0
        for left in lefts:
            part = tn(left[:, start:stop], right[row : row + left.shape[0], :])
            total = part if total is None else total + part
            row += left.shape[0]
        return total

    if not added:
        for place, out in enumerate(outs):

            @pl.when(at // per == place)
            def _(out=out):
                for start in range(0, features, block):
                    out[0, start : start + block, :] = piece(start, start + block).astype(bf16)

        return
    half = features // 2
    for place, got in enumerate(added):

        @pl.when(at // per == place)
        def _(got=got):
            for start in range(0, features, block):
                total = piece(start, start + block) + got[0, start : start + block, :].astype(f32)
                outs[start // half][0, start % half : start % half + block, :] = total.astype(bf16)


def wgrad(lefts, right, order, width, per, added=()):
    features = lefts[0].shape[1]
    experts = order.shape[0]
    groups = experts // per
    rows = sum(left.shape[0] for left in lefts)

    def group_spec(place):
        return pl.BlockSpec((1, features, width), lambda i, ids: (jnp.clip(i - place * per, 0, per - 1), 0, 0))

    groups_specs = [group_spec(place) for place in range(groups)]
    if added:
        out_specs = [pl.BlockSpec((1, features // 2, width), lambda i, ids: (i, 0, 0))] * 2
        out_shape = [jax.ShapeDtypeStruct((experts, features // 2, width), bf16)] * 2
    else:
        out_specs = groups_specs
        out_shape = [jax.ShapeDtypeStruct((per, features, width), bf16)] * groups
    return pl.pallas_call(
        functools.partial(wgrad_kernel, len(lefts), len(added), per, min(512, features // 2)),
        grid_spec=pltpu.PrefetchScalarGridSpec(
            num_scalar_prefetch=1,
            grid=(experts,),
            in_specs=[pl.BlockSpec(left.shape, lambda i, ids: (0, 0)) for left in lefts]
            + [pl.BlockSpec((right.shape[0], width), lambda i, ids: (0, ids[i]))]
            + (groups_specs if added else []),
            out_specs=out_specs,
        ),
        out_shape=out_shape,
        compiler_params=params(),
        cost_estimate=cost(2 * rows * features * experts * width, 2 * (rows + 2 * experts * width) * features),
        name="wgrad",
    )(order, *lefts, right, *added)


def down_kernel(parts, per, order, down_w, *refs):
    acts, out = refs[:-1], refs[-1]
    total = None
    for peer, act in enumerate(acts):
        joined = jnp.concatenate([down_w[order[peer * per + at]] for at in range(per)], axis=1)
        part = nt(act[...], joined)
        total = part if total is None else total + part
    block = total.shape[0] // (parts * CHUNKS)
    for chunk in range(CHUNKS):
        for part in range(parts):
            to, start = (part * CHUNKS + chunk) * block, (chunk * parts + part) * block
            out[to : to + block, :] = total[start : start + block, :].astype(out.dtype)


def down(acts, order, down_w, parts):
    rows = acts[0].shape[0]
    experts, features, width = down_w.shape
    block = min(256, features)
    return pl.pallas_call(
        functools.partial(down_kernel, parts, experts // len(acts)),
        grid_spec=pltpu.PrefetchScalarGridSpec(
            num_scalar_prefetch=1,
            grid=(features // block,),
            in_specs=[pl.BlockSpec((experts, block, width), lambda n, ids: (0, n, 0))]
            + [pl.BlockSpec(act.shape, lambda n, ids: (0, 0)) for act in acts],
            out_specs=pl.BlockSpec((rows, block), lambda n, ids: (0, n)),
        ),
        out_shape=jax.ShapeDtypeStruct((rows, features), bf16),
        compiler_params=params(),
        cost_estimate=cost(2 * rows * features * experts * width, 2 * (rows + experts * width) * features),
        name="down",
    )(order, down_w, *acts)


def owner_wgrad_kernel(count, *refs):
    lefts, rights, out = refs[:count], refs[count : 2 * count], refs[2 * count]
    width = out.shape[2]
    total = tn(lefts[0][...], rights[0][...])
    for left, right in zip(lefts[1:], rights[1:]):
        total = total + tn(left[...], right[...])
    for at in range(out.shape[0]):
        out[at] = total[:, at * width : (at + 1) * width]


def owner_wgrad(lefts, rights, width):
    rows, features = lefts[0].shape
    columns = rights[0].shape[1]
    block = min(256, features)
    return pl.pallas_call(
        functools.partial(owner_wgrad_kernel, len(lefts)),
        grid=(features // block,),
        in_specs=[pl.BlockSpec((rows, block), lambda n: (0, n)) for _ in lefts]
        + [pl.BlockSpec((rows, columns), lambda n: (0, 0)) for _ in rights],
        out_specs=pl.BlockSpec((columns // width, block, width), lambda n: (0, n, 0)),
        out_shape=jax.ShapeDtypeStruct((columns // width, features, width), f32),
        compiler_params=params(),
        cost_estimate=cost(0, 0),
        name="owner_wgrad",
    )(*lefts, *rights)


def gate(value, *others):
    return lax.optimization_barrier((value, others))[0]


def gather_rows(values):
    return lax.all_gather(values, "tensor", axis=0, tiled=True)


def scatter_rows(values):
    return lax.psum_scatter(values, "tensor", scatter_dimension=0, tiled=True)


def join_kernel(parts, slots, own, *refs):
    ups, downs, out = refs[: parts - 1], refs[parts - 1 : 2 * parts - 2], refs[2 * parts - 2]
    at = pl.program_id(0)

    @pl.when(at == 0)
    def _():
        out[...] = own[...]

    for step in range(1, parts):

        @pl.when(at == step)
        def _(step=step):
            out[...] = ups[step - 1][...] + downs[parts - 1 - step][...]


def join(slots, own, ups, downs):
    parts = len(ups) + 1
    rows, columns = own.shape
    split = (CHUNKS, rows // CHUNKS, columns)
    whole = pl.BlockSpec(split, lambda i, to: (0, 0, 0))
    return pl.pallas_call(
        functools.partial(join_kernel, parts),
        grid_spec=pltpu.PrefetchScalarGridSpec(
            num_scalar_prefetch=1,
            grid=(parts,),
            in_specs=[whole] * (2 * parts - 1),
            out_specs=pl.BlockSpec(split, lambda i, to: (0, to[i], 0)),
        ),
        out_shape=jax.ShapeDtypeStruct((CHUNKS, parts * rows // CHUNKS, columns), own.dtype),
        compiler_params=params(),
        cost_estimate=cost(0, 0),
        name="join",
    )(slots, *(piece.reshape(split) for piece in (own, *ups, *downs)))


class Chain:
    def __init__(self, values):
        self.values = values
        self.parts = lax.axis_size("tensor")
        self.ups, self.downs = [values], [values]

    def hop(self, *others):
        step = len(self.ups)
        if step < self.parts:
            up, down = gate((self.ups[-1], self.downs[-1]), *others) if others else (self.ups[-1], self.downs[-1])
            self.sent = (up, down)
            self.ups.append(lax.ppermute(up, "tensor", [(i, i + 1) for i in range(step - 1, self.parts - 1)]))
            self.downs.append(lax.ppermute(down, "tensor", [(i, i - 1) for i in range(1, self.parts - step + 1)]))
        return self.sent

    def recv(self):
        return self.ups[-1], self.downs[-1]

    def joined(self):
        while len(self.ups) < self.parts:
            self.hop()
        at = lax.axis_index("tensor")
        slots = lax.rem(at - jnp.arange(self.parts, dtype=jnp.int32) + self.parts, self.parts)
        return join(slots, self.values, self.ups[1:], self.downs[1:])


def pair_swap(values, step):
    size = lax.axis_size("dp")
    return lax.ppermute(values, "dp", [(i, i ^ step) for i in range(size)])


class Halving:
    def __init__(self, values):
        bits = list(range(values[0].shape[0].bit_length() - 1))
        self.kept = list(values)
        self.left = [bits[::-1], bits]
        self.got = None

    def send(self):
        if not self.left[0]:
            return ()
        self.got = []
        sent = []
        for side, downward in ((0, True), (1, False)):
            bit = self.left[side].pop(0)
            kept = self.kept[side]
            half = kept.shape[0] // 2
            if downward:
                keep, go = kept[:half], kept[half:]
            else:
                view = kept.reshape((half, 2) + kept.shape[1:])
                keep, go = view[:, 0], view[:, 1]
            sent.append(go)
            self.got.append(pair_swap(go, 2 << bit))
            self.kept[side] = keep
        return tuple(sent)

    def add(self, *others):
        if self.got is not None:
            if others:
                self.got = gate(tuple(self.got), *others)
            last = not self.left[0]
            for side in range(2):
                total = self.kept[side].astype(f32) + self.got[side].astype(f32)
                self.kept[side] = total if last else total.astype(bf16)
            self.got = None
        return tuple(self.kept)

    def done(self):
        self.add()
        while self.left[0]:
            self.send()
            self.add()
        return jnp.concatenate([kept[0].astype(f32) for kept in self.kept], axis=1)


class Spread:
    def __init__(self, values):
        self.pieces = {0: values}
        self.steps = sorted((k for k in range(2, lax.axis_size("dp"), 2)), key=lambda k: (k.bit_count(), k))

    def first(self):
        near = [k for k in self.steps if k.bit_count() == 1]
        for k in near:
            self.pieces[k] = pair_swap(self.pieces[0], k)
        return [self.pieces[k] for k in near]

    def rest(self):
        half = self.pieces[0].shape[0] // 2
        got = []
        for k in self.steps:
            if k not in self.pieces:
                low, high = k & -k, 1 << (k.bit_length() - 1)
                got += [pair_swap(self.pieces[k ^ high][:half], high), pair_swap(self.pieces[k ^ low][half:], low)]
                self.pieces[k] = jnp.concatenate(got[-2:])
        return got

    def all(self):
        for k in [0] + self.steps:
            self.pieces[k ^ 1] = pair_swap(self.pieces[k], 1)
        return [self.pieces[k] for k in range(len(self.pieces))]


def exchange_sum(values, axes):
    for axis in axes:
        size = lax.axis_size(axis)
        step = 1
        while step < size:
            values = values + lax.ppermute(values, axis, [(i, i ^ step) for i in range(size)])
            step *= 2
    return values


def local(
    tokens, cotangent, seg_ids, keep_mask, routes, attn_gain, w_query, w_key, w_value, w_out,
    q_gain, k_gain, ffn_gain, router, w_gate, w_up, w_down,
):
    parts = lax.axis_size("tensor")
    part_at = lax.axis_index("tensor")
    dp_size = lax.axis_size("dp")
    low_bit = lax.axis_index("dp") % 2
    shard_rows, features = tokens.shape
    group_rows = shard_rows * parts
    _, length = seg_ids.shape
    local_width = w_query.shape[1]
    experts, _, width = w_gate.shape
    per = experts // dp_size
    chunk_rows = shard_rows // CHUNKS
    chunks = range(CHUNKS)
    own = [slice(c * chunk_rows, (c + 1) * chunk_rows) for c in chunks]

    def chunk_of(values, c):
        columns = values.shape[1]
        return values.reshape(parts, CHUNKS, chunk_rows, columns)[:, c].reshape(parts * chunk_rows, columns)

    inputs = tokens.astype(f32)
    first_scale = rms_scale(inputs)
    normed_all = gather_rows((inputs * first_scale * attn_gain).astype(bf16))
    behind = Chain(gate(cotangent, normed_all))

    cosine, sine = rope_tables(length, HEAD)

    relative = jnp.arange(dp_size // 2, dtype=jnp.int32) ^ (lax.axis_index("dp") // 2)
    own_blocks, other_blocks = 2 * relative + low_bit, 2 * relative + 1 - low_bit
    mine, theirs = (
        (blocks[:, None] * per + jnp.arange(per, dtype=jnp.int32)).reshape(-1) for blocks in (own_blocks, other_blocks)
    )

    qraw, kraw, value, squares = project(normed_all, w_query, w_key, w_value)
    squares = exchange_sum(squares, ("tensor",))
    behind.hop()
    q_scale, k_scale = (lax.rsqrt(squares[i] / features + EPSILON)[:, None] for i in range(2))
    query, key, attended, lse = attend(
        qraw, kraw, value, q_scale, k_scale, q_gain, k_gain, cosine, sine, gate(seg_ids[0], *behind.recv()), keep_mask[0]
    )
    behind.hop()
    attended_parts = [chunk_of(gate(attended, *behind.recv()), c) for c in chunks]
    outs = [nt(attended_parts[0], w_out).astype(bf16)]
    summed = [scatter_rows(outs[0])]
    outs.append(nt(gate(attended_parts[1], outs[0]), w_out).astype(bf16))
    summed.append(scatter_rows(outs[1]))
    behind.hop(outs[1])

    idle_routes, idle_router = gate((routes, router), outs[1])
    expert_ids = jnp.arange(LANES)
    routed = jnp.sum((idle_routes[:, :, None] == expert_ids[None, None, :]).astype(f32), axis=1)
    router_wide = jnp.pad(idle_router, ((0, 0), (0, LANES - experts)))
    routed_own = lax.dynamic_slice_in_dim(routed, part_at * shard_rows, shard_rows, 0)[:, :experts]
    grad_rows = behind.joined().reshape(group_rows, features)
    back = up_back(gate(grad_rows, routed, router_wide), w_down)
    spread = Spread(grad_rows)
    spread_first = spread.first()

    middles, scales, ffn_own = [], [], []

    def middle_of(c, total):
        middle = inputs[own[c]] + total.astype(f32)
        scale = rms_scale(middle)
        normed = (middle * scale * ffn_gain).astype(bf16)
        middles.append(middle)
        scales.append(scale)
        ffn_own.append(normed)
        return normed

    ffn_all = [gather_rows(middle_of(0, summed[0]))]
    ffn_all.append(gather_rows(middle_of(1, gate(summed[1], ffn_own[0], back))))
    dp_at = lax.axis_index("dp")
    owners = jnp.arange(dp_size, dtype=jnp.int32) ^ dp_at
    order = (owners[:, None] * per + jnp.arange(per, dtype=jnp.int32)).reshape(-1)
    filled, expert_grads = (), []
    for c in chunks:
        here = gate(chunk_of(routed, c), back, *filled, *(spread_first if c else ()))
        filled, grads = experts_chunk(c, order, per, ffn_all[c], back, here, router_wide, w_gate, w_up, filled)
        expert_grads.append(scatter_rows(grads))
    acts, (dgates, dups) = filled[:-2], filled[-2:]
    spread_rest = spread.rest()
    peers = sorted(range(1, dp_size), key=lambda k: (k.bit_count(), k))
    act_pieces = {k: pair_swap(acts[k], k) for k in peers}
    act_slots = [[act_pieces[k] for k in peers[at * 3 * dp_size // 8 : (at + 1) * 3 * dp_size // 8]] for at in range(3)]

    ffn_gain_parts, router_parts, middle_grads = [], [], []

    def middle_back(c, grads):
        share_grad = grads[:, features : features + experts] * routed_own[own[c]]
        probs = jax.nn.softmax(nn(ffn_own[c], router), axis=-1)
        logit_grad = (probs * (share_grad - jnp.sum(share_grad * probs, axis=-1, keepdims=True))).astype(bf16)
        ffn_grad = grads[:, :features] + nt(logit_grad, router)
        router_parts.append(tn(ffn_own[c], logit_grad))
        ffn_gain_parts.append(jnp.sum(ffn_grad * middles[c] * scales[c], axis=0))
        middle_grads.append(cotangent[own[c]].astype(f32) + norm_back(ffn_grad, middles[c], scales[c], ffn_gain))
        return middle_grads[c].astype(bf16)

    def expert_sums(lefts, rights, ids, *others, added=()):
        return wgrad(lefts, rights, gate(ids, *others), width, per, added)

    def core_swap(pieces):
        return [pair_swap(piece, 1) for piece in pieces]

    def halving(sums):
        return Halving([half.reshape((dp_size // 2, per) + half.shape[1:]) for half in sums])

    first = middle_back(0, gate(expert_grads[0], dups, *spread_rest).astype(f32))
    gate_sent = expert_sums(ffn_all, dgates, theirs, first)
    gate_got = core_swap(gate_sent)
    up_sent = expert_sums(ffn_all, dups, theirs, *gate_sent, *act_slots[0])
    up_got = core_swap(up_sent)
    second = middle_back(1, gate(expert_grads[1], *up_sent).astype(f32))
    middle_all = gather_rows(jnp.concatenate([first, second]))
    gate_sums = expert_sums(ffn_all, dgates, mine, second, *act_slots[1], added=gate_got)
    gate_out = halving(gate_sums)
    moe = down(acts, gate(order, *gate_sums, *gate_out.send(), *act_slots[2]), w_down, parts)
    moe_sum = scatter_rows(moe)
    up_sums = expert_sums(ffn_all, dups, mine, moe, added=up_got)
    up_out = halving(up_sums)

    attended_grad = nn(gate(middle_all, *up_out.send()), w_out).astype(bf16)
    dqn, dkn, dvalue, qdot, kdot, q_gain_part, k_gain_part = attend_back(
        query, key, value, attended_grad, lse, qraw, kraw, q_scale, k_scale, q_gain, k_gain, cosine, sine,
        seg_ids[0], keep_mask[0],
    )
    dots = exchange_sum(jnp.stack([qdot[:, 0], kdot[:, 0]]), ("tensor",)) / features
    gate_late = gate_out.add(dqn)
    gate_out.send()
    normed_part, dqraw, dkraw, attn_gain_part = project_back(
        normed_all, dqn, dkn, dvalue, qraw, kraw, q_scale, k_scale, dots[0][:, None], dots[1][:, None],
        gate(q_gain, *gate_late), k_gain, w_query, w_key, w_value,
    )
    normed_grad = scatter_rows(normed_part)

    def attention_sums(ids, *others, added=()):
        return attention_wgrad(
            normed_all, middle_all, (dqraw, dkraw, dvalue), attended, gate(ids, *others), dp_size, added
        )

    attn_sent = attention_sums(other_blocks, normed_part, moe_sum)
    attn_got = core_swap(attn_sent)
    up_late = up_out.add(*attn_sent)
    up_out.send()
    down_done = owner_wgrad(
        spread.all(), [gate(acts[0], *up_late)] + [act_pieces[k] for k in range(1, dp_size)], width
    )

    def placed(part):
        return lax.dynamic_update_slice_in_dim(jnp.zeros((features,), f32), part, part_at * local_width, 0)

    attn_sums = attention_sums(own_blocks, down_done, added=attn_got)
    attn_out = Halving(attn_sums)
    normed_grad = gate(normed_grad, *attn_out.send())
    smalls = [attn_gain_part[0] / attn_gain, placed(q_gain_part[0]), placed(k_gain_part[0]), sum(ffn_gain_parts)]
    smalls = gate(jnp.concatenate([jnp.stack(smalls), sum(router_parts).T]), normed_grad)
    smalls = exchange_sum(smalls, ("dp", "tensor"))
    gate_done = gate_out.done()
    up_done = up_out.done()
    attn_out.add(normed_grad)
    query_done, key_done, value_done, out_done = attn_out.done()
    layer_out = (jnp.concatenate(middles) + moe_sum.astype(f32)).astype(bf16)
    tokens_grad = jnp.concatenate(middle_grads) + norm_back(normed_grad.astype(f32), inputs, first_scale, attn_gain)
    return (
        layer_out, tokens_grad, query_done, key_done, value_done, out_done,
        smalls[0], smalls[1], smalls[2], smalls[3], smalls[4:].T, gate_done, up_done, down_done,
    )


def solution(mesh):
    rows = P(("dp", "tensor"), None)
    column = P(None, "tensor")
    expert = P(None, None, "tensor")
    in_specs = (
        rows, rows, P("dp", None), P("dp", None), P("dp", None), P(), column, column, column, column,
        P("tensor"), P("tensor"), P(), P(), expert, expert, expert,
    )
    block = P("dp", "tensor")
    expert_out = P("dp", None, "tensor")
    out_specs = (
        rows, rows, block, block, block, block, P(), P(), P(), P(), P(), expert_out, expert_out, expert_out,
    )
    return jax.shard_map(local, mesh=mesh, in_specs=in_specs, out_specs=out_specs, check_vma=False)
```

```python
import functools

import jax
import jax.numpy as jnp
import numpy as np
from jax import lax
from jax.experimental import pallas as pl
from jax.experimental.pallas import tpu as pltpu
from jax.sharding import PartitionSpec as P

D = 2048
HEAD = 128
DOC = 512
LANES = 128
EPSILON = 1e-05
MASKED = -1e30
CHUNKS = 2
VMEM = 56 * 1024 * 1024
bf16 = jnp.bfloat16
f32 = jnp.float32


def nn(left, right):
    return lax.dot_general(left, right, (((1,), (0,)), ((), ())), preferred_element_type=f32)


def nt(left, right):
    return lax.dot_general(left, right, (((1,), (1,)), ((), ())), preferred_element_type=f32)


def tn(left, right):
    return lax.dot_general(left, right, (((0,), (0,)), ((), ())), preferred_element_type=f32)


def params():
    return pltpu.CompilerParams(vmem_limit_bytes=VMEM)


PACE = 0.3


def cost(flops, moved, special=0):
    return pl.CostEstimate(flops=int(1.5 * PACE * flops + 6e4 * PACE * special), bytes_accessed=moved // 8, transcendentals=0)


def rms_scale(values):
    return lax.rsqrt(jnp.mean(values * values, axis=-1, keepdims=True) + EPSILON)


def norm_back(grad_values, values, scale_col, gain_vec):
    weighted = grad_values * gain_vec
    inner_mean = jnp.mean(weighted * values, axis=-1, keepdims=True)
    return scale_col * weighted - values * (scale_col * scale_col * scale_col) * inner_mean


def rope_tables(length, width):
    angles = np.arange(length)[:, None] * 10000.0 ** (-np.arange(width // 2) * 2.0 / width)[None, :]
    cosine, sine = np.cos(angles).astype(np.float32), np.sin(angles).astype(np.float32)
    return jnp.asarray(np.concatenate([cosine, cosine], axis=1)), jnp.asarray(np.concatenate([-sine, sine], axis=1))


def key_start(query_start):
    return max(0, query_start - DOC)


def fill_bias(bias, seg_col, seg_row, keep_row, block):
    length = seg_col.shape[0]
    for start in range(0, length, block):
        first, stop = key_start(start), start + block
        query_pos = start + lax.broadcasted_iota(jnp.int32, (block, stop - first), 0)
        key_pos = first + lax.broadcasted_iota(jnp.int32, (block, stop - first), 1)
        same = seg_col[start:stop, :] == seg_row[:, first:stop]
        live = (keep_row[:, first:stop] == 1) | (key_pos == query_pos)
        allowed = same & live & (key_pos <= query_pos)
        bias[start:stop, : stop - first] = jnp.where(allowed, 0.0, MASKED)


def turned(values):
    return pltpu.roll(values, values.shape[1] // 2, 1)


def project_kernel(rows_in, w_query, w_key, w_value, q_out, k_out, v_out, squares_out):
    ones = jnp.ones((8, q_out.shape[1]), f32)
    for at, (weight, out) in enumerate(((w_query, q_out), (w_key, k_out))):
        raw = nn(rows_in[...], weight[...])
        out[...] = raw
        sums = lax.dot_general(
            ones, raw * raw, (((1,), (1,)), ((), ())), precision=lax.Precision.HIGHEST, preferred_element_type=f32
        )
        squares_out[at : at + 1, :] = sums[:1]
    v_out[...] = nn(rows_in[...], w_value[...]).astype(bf16)


def project(rows_in, w_query, w_key, w_value):
    rows, features = rows_in.shape
    width = w_query.shape[1]
    block = min(256, rows)
    row = lambda columns: pl.BlockSpec((block, columns), lambda r: (r, 0))
    weight = pl.BlockSpec((features, width), lambda r: (0, 0))
    sds = jax.ShapeDtypeStruct
    return pl.pallas_call(
        project_kernel,
        grid=(rows // block,),
        in_specs=[row(features), weight, weight, weight],
        out_specs=[row(width), row(width), row(width), pl.BlockSpec((2, block), lambda r: (0, r))],
        out_shape=[sds((rows, width), f32), sds((rows, width), f32), sds((rows, width), bf16), sds((2, rows), f32)],
        compiler_params=params(),
        cost_estimate=cost(6 * rows * features * width, 2 * (rows + 3 * width) * features),
        name="project",
    )(rows_in, w_query, w_key, w_value)


def project_back_kernel(
    rows_in, dqn, dkn, dvalue, qraw, kraw, q_scale, k_scale, q_dot, k_dot, q_gain, k_gain,
    w_query, w_key, w_value, part_out, dq_out, dk_out, gain_out,
):
    @pl.when(pl.program_id(0) == 0)
    def _():
        gain_out[...] = jnp.zeros_like(gain_out)

    def raw_grad(grad, raw, scale, gain, dot):
        cube = scale[...] * scale[...] * scale[...]
        return (scale[...] * (gain[...] * grad[...]) - raw[...] * (cube * dot[...])).astype(bf16)

    dq = raw_grad(dqn, qraw, q_scale, q_gain, q_dot)
    dk = raw_grad(dkn, kraw, k_scale, k_gain, k_dot)
    dq_out[...] = dq
    dk_out[...] = dk
    part = nt(dq, w_query[...]) + nt(dk, w_key[...]) + nt(dvalue[...], w_value[...])
    part_out[...] = part.astype(bf16)
    gain_out[...] += jnp.sum(part * rows_in[...].astype(f32), axis=0, keepdims=True)


def project_back(rows_in, dqn, dkn, dvalue, qraw, kraw, q_scale, k_scale, q_dot, k_dot, q_gain, k_gain, w_query, w_key, w_value):
    rows, features = rows_in.shape
    width = w_query.shape[1]
    block = min(256, rows)
    row = lambda columns: pl.BlockSpec((block, columns), lambda r: (r, 0))
    whole = lambda *shape: pl.BlockSpec(shape, lambda r: (0, 0))
    sds = jax.ShapeDtypeStruct
    return pl.pallas_call(
        project_back_kernel,
        grid=(rows // block,),
        in_specs=[row(features)] + [row(width)] * 5 + [row(1)] * 4 + [whole(1, width)] * 2 + [whole(features, width)] * 3,
        out_specs=[row(features), row(width), row(width), whole(1, features)],
        out_shape=[sds((rows, features), bf16), sds((rows, width), bf16), sds((rows, width), bf16), sds((1, features), f32)],
        compiler_params=params(),
        cost_estimate=cost(6 * rows * features * width, 2 * (rows + 3 * width) * features),
        name="project_back",
    )(rows_in, dqn, dkn, dvalue, qraw, kraw, q_scale, k_scale, q_dot, k_dot, q_gain[None], k_gain[None], w_query, w_key, w_value)


def attention_wgrad_kernel(added, order, tables, rows_in, middle, *refs):
    sides, (attended,), refs = refs[:3], refs[3:4], refs[4:]
    got, outs = (refs[:added], refs[added:])
    at = pl.program_id(0)
    totals = [tn(rows_in[...], side[...]) for side in sides] + [tn(middle[...], attended[...])]
    if not added:
        for place, out in enumerate(outs):

            @pl.when(at == place)
            def _(out=out):
                for weight, total in enumerate(totals):
                    out[0, weight] = total.astype(bf16)

        return
    scratch, outs = outs[-1], outs[:-1]
    half = outs[0].shape[2]
    for place, piece in enumerate(got):

        @pl.when(at == place)
        def _(piece=piece):
            for weight, total in enumerate(totals):
                scratch[weight] = (total + piece[0, weight].astype(f32)).astype(bf16)

    for side, out in enumerate(outs):
        start = side * 2 // len(outs) * half

        @pl.when(tables[1, side, at] == 1)
        def _(out=out, start=start):
            out[0] = scratch[:, start : start + half, :]


def attention_wgrad(rows_in, middle, sides, attended, order, blocks, added=()):
    features = rows_in.shape[1]
    width = sides[0].shape[1]
    block = features // blocks
    count = order.shape[0]
    tables, sizes = split_tables(count, 1)
    left = lambda values: pl.BlockSpec((values.shape[0], block), lambda i, ids, to: (0, ids[i]))
    right = lambda values: pl.BlockSpec(values.shape, lambda i, ids, to: (0, 0))

    def half_spec(side):
        return pl.BlockSpec((1, 4, block // 2, width), lambda i, ids, to: (to[0, side, i], 0, 0, 0))

    group_specs = [pl.BlockSpec((1, 4, block, width), lambda i, ids, to: (0, 0, 0, 0))] * count
    if added:
        out_specs = [half_spec(side) for side in range(len(sizes))]
        out_shape = [jax.ShapeDtypeStruct((size, 4, block // 2, width), bf16) for size in sizes]
    else:
        out_specs = group_specs
        out_shape = [jax.ShapeDtypeStruct((1, 4, block, width), bf16)] * count
    return pl.pallas_call(
        functools.partial(attention_wgrad_kernel, len(added)),
        grid_spec=pltpu.PrefetchScalarGridSpec(
            num_scalar_prefetch=2,
            grid=(count,),
            in_specs=[left(rows_in), left(middle)] + [right(v) for v in sides] + [right(attended)] + (group_specs if added else []),
            out_specs=out_specs,
            scratch_shapes=[pltpu.VMEM((4, block, width), bf16)] if added else [],
        ),
        out_shape=out_shape,
        compiler_params=params(),
        cost_estimate=cost(0, 0),
        name="attention_wgrad",
    )(order, tables, rows_in, middle, *sides, attended, *added)


def attend_kernel(
    block, qraw, kraw, value, q_scale, k_scale, q_gain, k_gain, cosine, sine,
    seg_col, seg_row, keep_row, q_out, k_out, o_out, lse_out, bias,
):
    @pl.when(pl.program_id(0) == 0)
    def _():
        fill_bias(bias, seg_col, seg_row, keep_row, block)

    def rotated(raw, scale, gain):
        normed = raw[...] * scale[...] * gain[...]
        return (normed * cosine[...] + turned(normed) * sine[...]).astype(bf16)

    q_out[...] = rotated(qraw, q_scale, q_gain)
    k_out[...] = rotated(kraw, k_scale, k_gain)
    length = seg_col.shape[0]
    for start in range(0, length, block):
        first, stop = key_start(start), start + block
        scores = nt(q_out[start:stop, :], k_out[first:stop, :]) * HEAD ** (-0.5)
        scores = scores + bias[start:stop, : stop - first]
        top = jnp.max(scores, axis=1, keepdims=True)
        powers = jnp.exp(scores - top)
        total = jnp.sum(powers, axis=1, keepdims=True)
        weights = (powers * (1.0 / total)).astype(bf16)
        o_out[start:stop, :] = nn(weights, value[first:stop, :]).astype(bf16)
        lse_out[start:stop, :] = jnp.broadcast_to(top + jnp.log(total), (block, HEAD))


def attend(qraw, kraw, value, q_scale, k_scale, q_gain, k_gain, cosine, sine, seg, keep):
    length, width = qraw.shape
    block = min(256, length)
    span = min(DOC + block, length)
    head = pl.BlockSpec((length, HEAD), lambda h: (0, h))
    gain = pl.BlockSpec((1, HEAD), lambda h: (0, h))
    whole = lambda *shape: pl.BlockSpec(shape, lambda h: (0, 0))
    return pl.pallas_call(
        functools.partial(attend_kernel, block),
        grid=(width // HEAD,),
        in_specs=[head, head, head, whole(length, 1), whole(length, 1), gain, gain]
        + [whole(length, HEAD), whole(length, HEAD), whole(length, 1), whole(1, length), whole(1, length)],
        out_specs=[head, head, head, head],
        out_shape=[jax.ShapeDtypeStruct((length, width), t) for t in (bf16, bf16, bf16, f32)],
        scratch_shapes=[pltpu.VMEM((length, span), f32)],
        compiler_params=params(),
        cost_estimate=cost(4 * length * span * width, 18 * length * width, length * span * width // HEAD),
        name="attend",
    )(qraw, kraw, value, q_scale, k_scale, q_gain[None], k_gain[None], cosine, sine, seg[:, None], seg[None], keep[None])


def attend_back_kernel(
    block, query, key, value, out_grad, lse, qraw, kraw, q_scale, k_scale, q_gain, k_gain, cosine, sine,
    seg_col, seg_row, keep_row, dq_out, dk_out, dv_out, qdot_out, kdot_out, qg_out, kg_out, bias, dk_sum, dv_sum,
):
    at = pl.program_id(0)

    @pl.when(at == 0)
    def _():
        fill_bias(bias, seg_col, seg_row, keep_row, block)
        qdot_out[...] = jnp.zeros_like(qdot_out)
        kdot_out[...] = jnp.zeros_like(kdot_out)

    dk_sum[...] = jnp.zeros_like(dk_sum)
    dv_sum[...] = jnp.zeros_like(dv_sum)
    length = seg_col.shape[0]
    scale = HEAD ** (-0.5)
    for start in range(0, length, block):
        first, stop = key_start(start), start + block
        rows, keys = slice(start, stop), slice(first, stop)
        scores = nt(query[rows, :], key[keys, :]) * scale + bias[rows, : stop - first]
        weights = jnp.exp(scores - lse[rows, :1])
        prob_grad = nt(out_grad[rows, :], value[keys, :])
        inner = jnp.sum(weights * prob_grad, axis=1, keepdims=True)
        score_grad = (weights * (prob_grad - inner)).astype(bf16)
        dq_out[rows, :] = nn(score_grad, key[keys, :]) * scale
        dk_sum[keys, :] += tn(score_grad, query[rows, :])
        dv_sum[keys, :] += tn(weights.astype(bf16), out_grad[rows, :])

    def unrotated(grad):
        return grad * cosine[...] + turned(grad * sine[...])

    dv_out[...] = dv_sum[...].astype(bf16)
    dq = unrotated(dq_out[...])
    dk = unrotated(dk_sum[...] * scale)
    dq_out[...] = dq
    dk_out[...] = dk
    dq = dq * qraw[...]
    dk = dk * kraw[...]
    qg_out[...] = jnp.sum(dq * q_scale[...], axis=0, keepdims=True)
    kg_out[...] = jnp.sum(dk * k_scale[...], axis=0, keepdims=True)
    qdot_out[...] += jnp.sum(dq * q_gain[...], axis=1, keepdims=True)
    kdot_out[...] += jnp.sum(dk * k_gain[...], axis=1, keepdims=True)


def attend_back(query, key, value, out_grad, lse, qraw, kraw, q_scale, k_scale, q_gain, k_gain, cosine, sine, seg, keep):
    length, width = qraw.shape
    block = min(256, length)
    span = min(DOC + block, length)
    head = pl.BlockSpec((length, HEAD), lambda h: (0, h))
    gain = pl.BlockSpec((1, HEAD), lambda h: (0, h))
    whole = lambda *shape: pl.BlockSpec(shape, lambda h: (0, 0))
    sds = jax.ShapeDtypeStruct
    return pl.pallas_call(
        functools.partial(attend_back_kernel, block),
        grid=(width // HEAD,),
        in_specs=[head] * 7
        + [whole(length, 1), whole(length, 1), gain, gain]
        + [whole(length, HEAD), whole(length, HEAD), whole(length, 1), whole(1, length), whole(1, length)],
        out_specs=[head, head, head, whole(length, 1), whole(length, 1), gain, gain],
        out_shape=[sds((length, width), f32), sds((length, width), f32), sds((length, width), bf16)]
        + [sds((length, 1), f32), sds((length, 1), f32), sds((1, width), f32), sds((1, width), f32)],
        scratch_shapes=[pltpu.VMEM((length, span), f32), pltpu.VMEM((length, HEAD), f32), pltpu.VMEM((length, HEAD), f32)],
        compiler_params=params(),
        cost_estimate=cost(20 * length * span * width, 0),
        name="attend_back",
    )(query, key, value, out_grad, lse, qraw, kraw, q_scale, k_scale, q_gain[None], k_gain[None], cosine, sine, seg[:, None], seg[None], keep[None])


def middle_kernel(tokens, summed, gain, middle_out, scale_out, normed_out):
    middle = tokens[...].astype(f32) + summed[...].astype(f32)
    scale = lax.rsqrt(jnp.mean(middle * middle, axis=1, keepdims=True) + EPSILON)
    middle_out[...] = middle
    scale_out[...] = scale
    normed_out[...] = (middle * scale * gain[...]).astype(bf16)


def middle_rows(chunk, tokens, summed, gain):
    rows, features = summed.shape
    sds = jax.ShapeDtypeStruct
    whole = lambda *shape: pl.BlockSpec(shape, lambda i: (0, 0))
    return pl.pallas_call(
        middle_kernel,
        grid=(1,),
        in_specs=[pl.BlockSpec((rows, features), lambda i: (chunk, 0)), whole(rows, features), whole(1, features)],
        out_specs=[whole(rows, features), whole(rows, 1), whole(rows, features)],
        out_shape=[sds((rows, features), f32), sds((rows, 1), f32), sds((rows, features), bf16)],
        compiler_params=params(),
        cost_estimate=cost(0, 0),
        name="middle",
    )(tokens, summed, gain[None])


def middle_back_kernel(
    experts, grads, middle, scale, normed, routed, router, cotangent, gain, *refs
):
    grad_out, low_out, gain_out, logit_out = refs[-4:]
    features = middle.shape[1]
    lane = lax.broadcasted_iota(jnp.int32, routed.shape, 1)
    logits = jnp.where(lane < experts, nn(normed[...], router[...]), MASKED)
    powers = jnp.exp(logits - jnp.max(logits, axis=1, keepdims=True))
    probs = powers / jnp.sum(powers, axis=1, keepdims=True)
    share_grad = grads[:, features:].astype(f32) * routed[...]
    logit_grad = (probs * (share_grad - jnp.sum(share_grad * probs, axis=1, keepdims=True))).astype(bf16)
    logit_out[...] = logit_grad
    ffn_grad = grads[:, :features].astype(f32) + nt(logit_grad, router[...])
    along = middle[...] * scale[...]
    gain_out[...] = jnp.sum(ffn_grad * along, axis=0, keepdims=True)
    weighted = ffn_grad * gain[...]
    inner = jnp.mean(weighted * along, axis=1, keepdims=True)
    total = cotangent[...].astype(f32) + scale[...] * (weighted - along * inner)
    grad_out[...] = total
    low_out[...] = total.astype(bf16)


def middle_back(chunk, grads, middle, scale, normed, routed, router, cotangent, gain, experts, filled=()):
    rows, features = middle.shape
    sds = jax.ShapeDtypeStruct
    whole = lambda *shape: pl.BlockSpec(shape, lambda i: (0, 0))
    part = lambda columns: pl.BlockSpec((rows, columns), lambda i: (chunk, 0))
    return pl.pallas_call(
        functools.partial(middle_back_kernel, experts),
        grid=(1,),
        in_specs=[whole(rows, features + LANES), whole(rows, features), whole(rows, 1), whole(rows, features), part(LANES)]
        + [whole(features, LANES), part(features), whole(1, features)]
        + [pl.BlockSpec(memory_space=pl.ANY)] * len(filled),
        out_specs=[part(features), part(features), whole(1, features), whole(rows, LANES)],
        out_shape=[sds(cotangent.shape, f32), sds(cotangent.shape, bf16), sds((1, features), f32), sds((rows, LANES), bf16)],
        input_output_aliases={8 + at: at for at in range(len(filled))},
        compiler_params=params(),
        cost_estimate=cost(0, 0),
        name="middle_back",
    )(grads, middle, scale, normed, routed, router, cotangent, gain[None], *filled)


def up_back_kernel(grad, down_w, out):
    width = down_w.shape[2]
    for at in range(down_w.shape[0]):
        out[:, at * width : (at + 1) * width] = nn(grad[...], down_w[at]).astype(out.dtype)


def up_back(grad, down_w):
    rows, features = grad.shape
    experts, _, width = down_w.shape
    step = 2 if experts % 2 == 0 else 1
    return pl.pallas_call(
        up_back_kernel,
        grid=(experts // step,),
        in_specs=[pl.BlockSpec((rows, features), lambda e: (0, 0)), pl.BlockSpec((step, features, width), lambda e: (e, 0, 0))],
        out_specs=pl.BlockSpec((rows, step * width), lambda e: (0, e)),
        out_shape=jax.ShapeDtypeStruct((rows, experts * width), bf16),
        compiler_params=params(),
        cost_estimate=cost(2 * rows * features * experts * width, 2 * (rows + experts * width) * features),
        name="up_back",
    )(grad, down_w)


def expert_kernel(block, rows_in, back, routed, router, gate_w, up_w, act_out, dgate_out, dup_out, grad_out, comb, dcomb, total):
    at = pl.program_id(0)
    rows, features = rows_in.shape
    lane = lax.broadcasted_iota(jnp.int32, (block, LANES), 1)

    @pl.when(at == 0)
    def _():
        experts = pl.num_programs(0)
        for start in range(0, rows, block):
            here = slice(start, start + block)
            logits = jnp.where(lane < experts, nn(rows_in[here, :], router[...]), MASKED)
            powers = jnp.exp(logits - jnp.max(logits, axis=1, keepdims=True))
            probs = powers / jnp.sum(powers, axis=1, keepdims=True)
            comb[here, :] = probs * routed[here, :]
        total[...] = jnp.zeros_like(total)
        dcomb[...] = jnp.zeros_like(dcomb)

    gate, up = gate_w[0], up_w[0]
    mine = lane == at
    for start in range(0, rows, block):
        here = slice(start, start + block)
        taken = rows_in[here, :]
        pre_gate = nn(taken, gate)
        pre_up = nn(taken, up)
        behind = back[here, :].astype(f32)
        share = jnp.sum(jnp.where(mine, comb[here, :], 0.0), axis=1, keepdims=True)
        sigmoid = 0.5 * jnp.tanh(0.5 * pre_gate) + 0.5
        active = pre_gate * sigmoid
        inner = active * pre_up
        share_grad = jnp.sum(inner * behind, axis=1, keepdims=True)
        dcomb[here, :] = jnp.where(mine, share_grad, dcomb[here, :])
        act_out[here, :] = (inner * share).astype(bf16)
        inner_grad = behind * share
        dgate = (inner_grad * pre_up * (sigmoid + active * (1.0 - sigmoid))).astype(bf16)
        dup = (inner_grad * active).astype(bf16)
        dgate_out[here, :] = dgate
        dup_out[here, :] = dup
        total[here, :] += nt(dgate, gate) + nt(dup, up)

    @pl.when(at == pl.num_programs(0) - 1)
    def _():
        grad_out[:, :features] = total[...].astype(bf16)
        grad_out[:, features:] = dcomb[...].astype(bf16)


def experts_block(chunk, rows_in, back, routed, router, gate_w, up_w):
    rows, features = rows_in.shape
    experts, _, width = gate_w.shape
    block = min(512, rows)
    whole = lambda *shape: pl.BlockSpec(shape, lambda e: (0, 0))
    column = pl.BlockSpec((rows, width), lambda e: (0, e))
    weight = pl.BlockSpec((1, features, width), lambda e: (e, 0, 0))
    wide = jax.ShapeDtypeStruct((rows, experts * width), bf16)
    return pl.pallas_call(
        functools.partial(expert_kernel, block),
        grid=(experts,),
        in_specs=[whole(rows, features), pl.BlockSpec((rows, width), lambda e: (chunk, e)), whole(rows, LANES), whole(features, LANES), weight, weight],
        out_specs=[column, column, column, whole(rows, features + LANES)],
        out_shape=[wide, wide, wide, jax.ShapeDtypeStruct((rows, features + LANES), bf16)],
        scratch_shapes=[pltpu.VMEM((rows, LANES), f32), pltpu.VMEM((rows, LANES), f32), pltpu.VMEM((rows, features), f32)],
        compiler_params=params(),
        cost_estimate=cost(8 * rows * features * experts * width, 4 * experts * width * (features + 2 * rows), rows * experts * width),
        name="experts",
    )(rows_in, back, routed, router, gate_w, up_w)


def block_order(blocks):
    return [3, 2, 0, 1] if blocks == 4 else list(range(blocks))


def split_tables(blocks, per):
    order = block_order(blocks)
    if blocks == 4:
        picks = [{0: 0, 1: 1}, {2: 0, 3: 1}, {0: 0, 2: 1}, {1: 0, 3: 1}]
    else:
        picks = [{block: block for block in order}] * 2
    places, fills = [], []
    for pick in picks:
        filled = [pick[block] * per + at if block in pick else None for block in order for at in range(per)]
        last = next(place for place in filled if place is not None)
        row = []
        for place in filled:
            last = last if place is None else place
            row.append(last)
        places.append(row)
        fills.append([int(place is not None) for place in filled])
    return jnp.asarray(np.array([places, fills], np.int32)), [len(pick) for pick in picks]


def wgrad_kernel(count, extra, per, block, order, tables, *refs):
    lefts, rights = refs[:count], refs[count : 2 * count]
    added = refs[2 * count : 2 * count + extra]
    outs = refs[2 * count + extra :]
    at = pl.program_id(0)
    features = lefts[0].shape[1]

    def piece(start, stop):
        total = tn(lefts[0][:, start:stop], rights[0][...])
        for left, right in zip(lefts[1:], rights[1:]):
            total = total + tn(left[:, start:stop], right[...])
        return total

    if not added:
        for place, out in enumerate(outs):

            @pl.when(at // per == place)
            def _(out=out):
                for start in range(0, features, block):
                    out[0, start : start + block, :] = piece(start, start + block).astype(bf16)

        return
    half = features // 2
    got = outs[-1]
    outs = outs[:-1]
    for place, arrived in enumerate(added):

        @pl.when(at // per == place)
        def _(arrived=arrived):
            for start in range(0, features, block):
                total = piece(start, start + block) + arrived[0, start : start + block, :].astype(f32)
                got[start : start + block, :] = total.astype(bf16)

    for side, out in enumerate(outs):
        start = side * 2 // len(outs) * half

        @pl.when(tables[1, side, at] == 1)
        def _(out=out, start=start):
            out[0] = got[start : start + half, :]


def wgrad(lefts, rights, order, width, per, added=()):
    features = lefts[0][0].shape[1]
    experts = order.shape[0]
    groups = experts // per
    tables, sizes = split_tables(groups, per)

    def group_spec(place):
        return pl.BlockSpec((1, features, width), lambda i, ids, to: (jnp.clip(i - place * per, 0, per - 1), 0, 0))

    def half_spec(side):
        return pl.BlockSpec((1, features // 2, width), lambda i, ids, to: (to[0, side, i], 0, 0))

    groups_specs = [group_spec(place) for place in range(groups)]
    if added:
        out_specs = [half_spec(side) for side in range(len(sizes))]
        out_shape = [jax.ShapeDtypeStruct((size * per, features // 2, width), bf16) for size in sizes]
    else:
        out_specs = groups_specs
        out_shape = [jax.ShapeDtypeStruct((per, features, width), bf16)] * groups
    return pl.pallas_call(
        functools.partial(wgrad_kernel, len(lefts), len(added), per, min(512, features // 2)),
        grid_spec=pltpu.PrefetchScalarGridSpec(
            num_scalar_prefetch=2,
            grid=(experts,),
            in_specs=[pl.BlockSpec((right.shape[0], features), lambda i, ids, to, at=at: (at, 0)) for (_, at), right in zip(lefts, rights)]
            + [pl.BlockSpec((right.shape[0], width), lambda i, ids, to: (0, ids[i])) for right in rights]
            + (groups_specs if added else []),
            out_specs=out_specs,
            scratch_shapes=[pltpu.VMEM((features, width), bf16)] if added else [],
        ),
        out_shape=out_shape,
        compiler_params=params(),
        cost_estimate=cost(2 * sum(right.shape[0] for right in rights) * features * experts * width, 0),
        name="wgrad",
    )(order, tables, *(left for left, _ in lefts), *rights, *added)


def down_kernel(parts, down_w, *refs):
    acts, out = refs[:-1], refs[-1]
    joined = jnp.concatenate([down_w[e] for e in range(down_w.shape[0])], axis=1)
    block = acts[0].shape[0] // parts
    for at, act in enumerate(acts):
        result = nt(act[...], joined).astype(out.dtype)
        for part in range(parts):
            start = (part * len(acts) + at) * block
            out[start : start + block, :] = result[part * block : (part + 1) * block, :]


def down(acts, down_w, parts):
    rows = sum(act.shape[0] for act in acts)
    experts, features, width = down_w.shape
    block = min(256, features)
    return pl.pallas_call(
        functools.partial(down_kernel, parts),
        grid=(features // block,),
        in_specs=[pl.BlockSpec((experts, block, width), lambda n: (0, n, 0))]
        + [pl.BlockSpec(act.shape, lambda n: (0, 0)) for act in acts],
        out_specs=pl.BlockSpec((rows, block), lambda n: (0, n)),
        out_shape=jax.ShapeDtypeStruct((rows, features), bf16),
        compiler_params=params(),
        cost_estimate=cost(2 * rows * features * experts * width, 2 * (rows + experts * width) * features),
        name="down",
    )(down_w, *acts)


def gate(value, *others):
    return lax.optimization_barrier((value, others))[0]


def gather_rows(values):
    return lax.all_gather(values, "tensor", axis=0, tiled=True)


def scatter_rows(values):
    return lax.psum_scatter(values, "tensor", scatter_dimension=0, tiled=True)


def join_kernel(parts, slots, own, *refs):
    ups, downs, out = refs[: parts - 1], refs[parts - 1 : 2 * parts - 2], refs[2 * parts - 2]
    at = pl.program_id(0)

    @pl.when(at == 0)
    def _():
        out[...] = own[...]

    for step in range(1, parts):

        @pl.when(at == step)
        def _(step=step):
            out[...] = ups[step - 1][...] + downs[parts - 1 - step][...]


def join(slots, own, ups, downs):
    parts = len(ups) + 1
    rows, columns = own.shape
    split = (CHUNKS, rows // CHUNKS, columns)
    whole = pl.BlockSpec(split, lambda i, to: (0, 0, 0))
    return pl.pallas_call(
        functools.partial(join_kernel, parts),
        grid_spec=pltpu.PrefetchScalarGridSpec(
            num_scalar_prefetch=1,
            grid=(parts,),
            in_specs=[whole] * (2 * parts - 1),
            out_specs=pl.BlockSpec(split, lambda i, to: (0, to[i], 0)),
        ),
        out_shape=jax.ShapeDtypeStruct((CHUNKS, parts * rows // CHUNKS, columns), own.dtype),
        compiler_params=params(),
        cost_estimate=cost(0, 0),
        name="join",
    )(slots, *(piece.reshape(split) for piece in (own, *ups, *downs)))


class Chain:
    def __init__(self, values):
        self.values = values
        self.parts = lax.axis_size("tensor")
        self.ups, self.downs = [values], [values]

    def hop(self, *others):
        step = len(self.ups)
        if step < self.parts:
            up, down = gate((self.ups[-1], self.downs[-1]), *others) if others else (self.ups[-1], self.downs[-1])
            self.sent = (up, down)
            self.ups.append(lax.ppermute(up, "tensor", [(i, i + 1) for i in range(step - 1, self.parts - 1)]))
            self.downs.append(lax.ppermute(down, "tensor", [(i, i - 1) for i in range(1, self.parts - step + 1)]))
        return self.sent

    def recv(self):
        return self.ups[-1], self.downs[-1]

    def joined(self):
        while len(self.ups) < self.parts:
            self.hop()
        at = lax.axis_index("tensor")
        slots = lax.rem(at - jnp.arange(self.parts, dtype=jnp.int32) + self.parts, self.parts)
        return join(slots, self.values, self.ups[1:], self.downs[1:])


def pair_swap(values, step):
    size = lax.axis_size("dp")
    return lax.ppermute(values, "dp", [(i, i ^ step) for i in range(size)])


class Halving:
    def __init__(self, values):
        if len(values) == 2:
            self.kept = list(values)
            self.going = None
        else:
            self.kept, self.going = list(values[::2]), list(values[1::2])
        bits = list(range(values[0].shape[0].bit_length() - (1 if self.going is None else 0)))
        self.left = [bits[::-1], bits]
        self.got = None

    def send(self):
        if not self.left[0]:
            return ()
        self.got = []
        sent = []
        for side, downward in ((0, True), (1, False)):
            bit = self.left[side].pop(0)
            if self.going is not None:
                go = self.going[side]
            else:
                kept = self.kept[side]
                half = kept.shape[0] // 2
                if downward:
                    self.kept[side], go = kept[:half], kept[half:]
                else:
                    view = kept.reshape((half, 2) + kept.shape[1:])
                    self.kept[side], go = view[:, 0], view[:, 1]
            sent.append(go)
            self.got.append(pair_swap(go, 2 << bit))
        self.going = None
        return tuple(sent)

    def add(self, *others):
        if self.got is not None:
            if others:
                self.got = gate(tuple(self.got), *others)
            last = not self.left[0]
            for side in range(2):
                total = self.kept[side].astype(f32) + self.got[side].astype(f32)
                self.kept[side] = total if last else total.astype(bf16)
            self.got = None
        return tuple(self.kept)

    def done(self):
        self.add()
        while self.left[0]:
            self.send()
            self.add()
        return jnp.concatenate([kept[0].astype(f32) for kept in self.kept], axis=1)


def exchange_sum(values, axes):
    for axis in axes:
        size = lax.axis_size(axis)
        step = 1
        while step < size:
            values = values + lax.ppermute(values, axis, [(i, i ^ step) for i in range(size)])
            step *= 2
    return values


def local(
    tokens, cotangent, seg_ids, keep_mask, routes, attn_gain, w_query, w_key, w_value, w_out,
    q_gain, k_gain, ffn_gain, router, w_gate, w_up, w_down,
):
    parts = lax.axis_size("tensor")
    part_at = lax.axis_index("tensor")
    dp_size = lax.axis_size("dp")
    low_bit = lax.axis_index("dp") % 2
    shard_rows, features = tokens.shape
    group_rows = shard_rows * parts
    _, length = seg_ids.shape
    local_width = w_query.shape[1]
    experts, _, width = w_gate.shape
    per = experts // dp_size
    chunk_rows = shard_rows // CHUNKS
    chunks = range(CHUNKS)
    own = [slice(c * chunk_rows, (c + 1) * chunk_rows) for c in chunks]

    def chunk_of(values, c):
        columns = values.shape[1]
        return values.reshape(parts, CHUNKS, chunk_rows, columns)[:, c].reshape(parts * chunk_rows, columns)

    inputs = tokens.astype(f32)
    first_scale = rms_scale(inputs)
    normed_all = gather_rows((inputs * first_scale * attn_gain).astype(bf16))
    behind = Chain(gate(cotangent, normed_all))

    cosine, sine = rope_tables(length, HEAD)

    relative = jnp.asarray(block_order(dp_size // 2), jnp.int32) ^ (lax.axis_index("dp") // 2)
    own_blocks, other_blocks = 2 * relative + low_bit, 2 * relative + 1 - low_bit
    mine, theirs = (
        (blocks[:, None] * per + jnp.arange(per, dtype=jnp.int32)).reshape(-1) for blocks in (own_blocks, other_blocks)
    )

    qraw, kraw, value, squares = project(normed_all, w_query, w_key, w_value)
    squares = exchange_sum(squares, ("tensor",))
    behind.hop()
    q_scale, k_scale = (lax.rsqrt(squares[i] / features + EPSILON)[:, None] for i in range(2))
    query, key, attended, lse = attend(
        qraw, kraw, value, q_scale, k_scale, q_gain, k_gain, cosine, sine, gate(seg_ids[0], *behind.recv()), keep_mask[0]
    )
    behind.hop()
    attended_parts = [chunk_of(gate(attended, *behind.recv()), c) for c in chunks]
    outs = [nt(attended_parts[0], w_out).astype(bf16)]
    summed = [scatter_rows(outs[0])]
    outs.append(nt(gate(attended_parts[1], outs[0]), w_out).astype(bf16))
    summed.append(scatter_rows(outs[1]))
    behind.hop(outs[1])

    idle_routes, idle_router = gate((routes, router), outs[1])
    expert_ids = jnp.arange(LANES)
    routed = jnp.sum((idle_routes[:, :, None] == expert_ids[None, None, :]).astype(f32), axis=1)
    router_wide = jnp.pad(idle_router, ((0, 0), (0, LANES - experts)))
    routed_own = lax.dynamic_slice_in_dim(routed, part_at * shard_rows, shard_rows, 0)
    grad_rows = behind.joined().reshape(group_rows, features)
    back = up_back(gate(grad_rows, routed, router_wide), w_down)
    grad_parts = [(grad_rows, c) for c in chunks]

    norms = [middle_rows(0, tokens, summed[0], ffn_gain)]
    ffn_all = [gather_rows(norms[0][2])]
    norms.append(middle_rows(1, tokens, gate(summed[1], norms[0][2], back), ffn_gain))
    ffn_all.append(gather_rows(norms[1][2]))
    ffn_parts = [(rows, 0) for rows in ffn_all]
    acts, dgates, dups, expert_grads = [], [], [], []
    for c in chunks:
        here = gate(chunk_of(routed, c), back, *acts[-1:])
        act, dgate, dup, grads = experts_block(c, ffn_all[c], back, here, router_wide, w_gate, w_up)
        acts.append(act)
        dgates.append(dgate)
        dups.append(dup)
        expert_grads.append(grads)
    expert_grads = [scatter_rows(grads) for grads in expert_grads]

    def back_of(c, grads, filled=()):
        return middle_back(c, grads, *norms[c], routed_own, router_wide, cotangent, ffn_gain, experts, filled)

    def expert_sums(lefts, rights, ids, *others, added=()):
        return wgrad(lefts, rights, gate(ids, *others), width, per, added)

    def core_swap(pieces):
        return [pair_swap(piece, 1) for piece in pieces]

    def halving(sums):
        return Halving([part.reshape((part.shape[0] // per, per) + part.shape[1:]) for part in sums])

    first = back_of(0, gate(expert_grads[0], acts[1]))
    gate_sent = expert_sums(ffn_parts, dgates, theirs, first[1])
    gate_got = core_swap(gate_sent)
    up_sent = expert_sums(ffn_parts, dups, theirs, *gate_sent)
    up_got = core_swap(up_sent)
    second = back_of(1, gate(expert_grads[1], *up_sent), first[:2])
    middle_grad, middle_low = second[:2]
    middle_all = gather_rows(middle_low)
    gate_sums = expert_sums(ffn_parts, dgates, mine, middle_low, added=gate_got)
    gate_out = halving(gate_sums)
    gate_out.send()
    up_sums = expert_sums(ffn_parts, dups, mine, *gate_sums, added=up_got)
    up_out = halving(up_sums)
    up_out.send()
    moe = down([gate(acts[0], *up_sums), acts[1]], w_down, parts)
    gate_late = gate_out.add(moe)
    gate_out.send()
    moe_sum = scatter_rows(gate(moe, *gate_late))
    down_sent = expert_sums(grad_parts, acts, theirs, moe, *gate_late)
    down_got = core_swap(down_sent)

    attended_grad = nn(gate(middle_all, *down_sent), w_out).astype(bf16)
    dqn, dkn, dvalue, qdot, kdot, q_gain_part, k_gain_part = attend_back(
        query, key, value, attended_grad, lse, qraw, kraw, q_scale, k_scale, q_gain, k_gain, cosine, sine,
        seg_ids[0], keep_mask[0],
    )
    dots = exchange_sum(jnp.stack([qdot[:, 0], kdot[:, 0]]), ("tensor",)) / features
    up_late = up_out.add(dqn)
    up_out.send()
    down_sums = expert_sums(grad_parts, acts, mine, *up_late, added=down_got)
    down_out = halving(down_sums)
    down_out.send()
    normed_part, dqraw, dkraw, attn_gain_part = project_back(
        normed_all, dqn, dkn, dvalue, qraw, kraw, q_scale, k_scale, dots[0][:, None], dots[1][:, None],
        gate(q_gain, *down_sums, *gate_out.got), k_gain, w_query, w_key, w_value,
    )
    normed_grad = scatter_rows(normed_part)
    def attention_sums(ids, *others, added=()):
        return attention_wgrad(
            normed_all, middle_all, (dqraw, dkraw, dvalue), attended, gate(ids, *others), dp_size, added
        )

    attn_sent = attention_sums(other_blocks, normed_part)
    attn_got = core_swap(attn_sent)

    def placed(part):
        return lax.dynamic_update_slice_in_dim(jnp.zeros((features,), f32), part, part_at * local_width, 0)

    attn_sums = attention_sums(own_blocks, *attn_sent, added=attn_got)
    attn_out = Halving(attn_sums)
    normed_grad = gate(normed_grad, *attn_out.send())
    down_out.add(*attn_sums)
    down_out.send()
    smalls = [attn_gain_part[0] / attn_gain, placed(q_gain_part[0]), placed(k_gain_part[0]), (first[2] + second[2])[0]]
    router_part = sum(tn(late[3], norms[c][2]) for c, late in enumerate((first, second)))[:experts]
    smalls = gate(jnp.concatenate([jnp.stack(smalls), router_part]), normed_grad)
    smalls = exchange_sum(smalls, ("dp", "tensor"))
    gate_done = gate_out.done()
    up_done = up_out.done()
    down_done = down_out.done()
    attn_out.add(normed_grad)
    query_done, key_done, value_done, out_done = attn_out.done()
    layer_out = (jnp.concatenate([norms[c][0] for c in chunks]) + moe_sum.astype(f32)).astype(bf16)
    tokens_grad = middle_grad + norm_back(normed_grad.astype(f32), inputs, first_scale, attn_gain)
    return (
        layer_out, tokens_grad, query_done, key_done, value_done, out_done,
        smalls[0], smalls[1], smalls[2], smalls[3], smalls[4:].T, gate_done, up_done, down_done,
    )


def solution(mesh):
    rows = P(("dp", "tensor"), None)
    column = P(None, "tensor")
    expert = P(None, None, "tensor")
    in_specs = (
        rows, rows, P("dp", None), P("dp", None), P("dp", None), P(), column, column, column, column,
        P("tensor"), P("tensor"), P(), P(), expert, expert, expert,
    )
    block = P("dp", "tensor")
    expert_out = P("dp", None, "tensor")
    out_specs = (
        rows, rows, block, block, block, block, P(), P(), P(), P(), P(), expert_out, expert_out, expert_out,
    )
    return jax.shard_map(local, mesh=mesh, in_specs=in_specs, out_specs=out_specs, check_vma=False)
```

```python
import functools

import jax
import jax.numpy as jnp
import numpy as np
from jax import lax
from jax.experimental import pallas as pl
from jax.experimental.pallas import tpu as pltpu
from jax.sharding import PartitionSpec as P

D = 2048
HEAD = 128
DOC = 512
LANES = 128
EPSILON = 1e-05
MASKED = -1e30
CHUNKS = 2
VMEM = 56 * 1024 * 1024
bf16 = jnp.bfloat16
f32 = jnp.float32


def nn(left, right):
    return lax.dot_general(left, right, (((1,), (0,)), ((), ())), preferred_element_type=f32)


def nt(left, right):
    return lax.dot_general(left, right, (((1,), (1,)), ((), ())), preferred_element_type=f32)


def tn(left, right):
    return lax.dot_general(left, right, (((0,), (0,)), ((), ())), preferred_element_type=f32)


def params():
    return pltpu.CompilerParams(vmem_limit_bytes=VMEM)


PACE = 0.3


def cost(flops, moved, special=0):
    return pl.CostEstimate(flops=int(1.5 * PACE * flops + 6e4 * PACE * special), bytes_accessed=moved // 8, transcendentals=0)


def rms_scale(values):
    return lax.rsqrt(jnp.mean(values * values, axis=-1, keepdims=True) + EPSILON)


def norm_back(grad_values, values, scale_col, gain_vec):
    weighted = grad_values * gain_vec
    inner_mean = jnp.mean(weighted * values, axis=-1, keepdims=True)
    return scale_col * weighted - values * (scale_col * scale_col * scale_col) * inner_mean


def rope_tables(length, width):
    angles = np.arange(length)[:, None] * 10000.0 ** (-np.arange(width // 2) * 2.0 / width)[None, :]
    cosine, sine = np.cos(angles).astype(np.float32), np.sin(angles).astype(np.float32)
    return jnp.asarray(np.concatenate([cosine, cosine], axis=1)), jnp.asarray(np.concatenate([-sine, sine], axis=1))


def key_start(query_start):
    return max(0, query_start - DOC)


def fill_bias(bias, seg_col, seg_row, keep_row, block):
    length = seg_col.shape[0]
    for start in range(0, length, block):
        first, stop = key_start(start), start + block
        query_pos = start + lax.broadcasted_iota(jnp.int32, (block, stop - first), 0)
        key_pos = first + lax.broadcasted_iota(jnp.int32, (block, stop - first), 1)
        same = seg_col[start:stop, :] == seg_row[:, first:stop]
        live = (keep_row[:, first:stop] == 1) | (key_pos == query_pos)
        allowed = same & live & (key_pos <= query_pos)
        bias[start:stop, : stop - first] = jnp.where(allowed, 0.0, MASKED)


def turned(values):
    return pltpu.roll(values, values.shape[1] // 2, 1)


def project_kernel(rows_in, w_query, w_key, w_value, q_out, k_out, v_out, squares_out):
    ones = jnp.ones((8, q_out.shape[1]), f32)
    for at, (weight, out) in enumerate(((w_query, q_out), (w_key, k_out))):
        raw = nn(rows_in[...], weight[...])
        out[...] = raw
        sums = lax.dot_general(
            ones, raw * raw, (((1,), (1,)), ((), ())), precision=lax.Precision.HIGHEST, preferred_element_type=f32
        )
        squares_out[at : at + 1, :] = sums[:1]
    v_out[...] = nn(rows_in[...], w_value[...]).astype(bf16)


def project(rows_in, w_query, w_key, w_value):
    rows, features = rows_in.shape
    width = w_query.shape[1]
    block = min(256, rows)
    row = lambda columns: pl.BlockSpec((block, columns), lambda r: (r, 0))
    weight = pl.BlockSpec((features, width), lambda r: (0, 0))
    sds = jax.ShapeDtypeStruct
    return pl.pallas_call(
        project_kernel,
        grid=(rows // block,),
        in_specs=[row(features), weight, weight, weight],
        out_specs=[row(width), row(width), row(width), pl.BlockSpec((2, block), lambda r: (0, r))],
        out_shape=[sds((rows, width), f32), sds((rows, width), f32), sds((rows, width), bf16), sds((2, rows), f32)],
        compiler_params=params(),
        cost_estimate=cost(6 * rows * features * width, 2 * (rows + 3 * width) * features),
        name="project",
    )(rows_in, w_query, w_key, w_value)


def project_back_kernel(
    rows_in, dqn, dkn, dvalue, qraw, kraw, q_scale, k_scale, q_dot, k_dot, q_gain, k_gain,
    w_query, w_key, w_value, part_out, dq_out, dk_out, gain_out,
):
    @pl.when(pl.program_id(0) == 0)
    def _():
        gain_out[...] = jnp.zeros_like(gain_out)

    def raw_grad(grad, raw, scale, gain, dot):
        cube = scale[...] * scale[...] * scale[...]
        return (scale[...] * (gain[...] * grad[...]) - raw[...] * (cube * dot[...])).astype(bf16)

    dq = raw_grad(dqn, qraw, q_scale, q_gain, q_dot)
    dk = raw_grad(dkn, kraw, k_scale, k_gain, k_dot)
    dq_out[...] = dq
    dk_out[...] = dk
    part = nt(dq, w_query[...]) + nt(dk, w_key[...]) + nt(dvalue[...], w_value[...])
    part_out[...] = part.astype(bf16)
    gain_out[...] += jnp.sum(part * rows_in[...].astype(f32), axis=0, keepdims=True)


def project_back(rows_in, dqn, dkn, dvalue, qraw, kraw, q_scale, k_scale, q_dot, k_dot, q_gain, k_gain, w_query, w_key, w_value):
    rows, features = rows_in.shape
    width = w_query.shape[1]
    block = min(256, rows)
    row = lambda columns: pl.BlockSpec((block, columns), lambda r: (r, 0))
    whole = lambda *shape: pl.BlockSpec(shape, lambda r: (0, 0))
    sds = jax.ShapeDtypeStruct
    return pl.pallas_call(
        project_back_kernel,
        grid=(rows // block,),
        in_specs=[row(features)] + [row(width)] * 5 + [row(1)] * 4 + [whole(1, width)] * 2 + [whole(features, width)] * 3,
        out_specs=[row(features), row(width), row(width), whole(1, features)],
        out_shape=[sds((rows, features), bf16), sds((rows, width), bf16), sds((rows, width), bf16), sds((1, features), f32)],
        compiler_params=params(),
        cost_estimate=cost(6 * rows * features * width, 2 * (rows + 3 * width) * features),
        name="project_back",
    )(rows_in, dqn, dkn, dvalue, qraw, kraw, q_scale, k_scale, q_dot, k_dot, q_gain[None], k_gain[None], w_query, w_key, w_value)


def attention_wgrad_kernel(added, order, tables, rows_in, middle, *refs):
    sides, (attended,), refs = refs[:3], refs[3:4], refs[4:]
    got, outs = (refs[:added], refs[added:])
    at = pl.program_id(0)
    totals = [tn(rows_in[...], side[...]) for side in sides] + [tn(middle[...], attended[...])]
    if not added:
        for place, out in enumerate(outs):

            @pl.when(at == place)
            def _(out=out):
                for weight, total in enumerate(totals):
                    out[0, weight] = total.astype(bf16)

        return
    scratch, outs = outs[-1], outs[:-1]
    half = outs[0].shape[2]
    for place, piece in enumerate(got):

        @pl.when(at == place)
        def _(piece=piece):
            for weight, total in enumerate(totals):
                scratch[weight] = (total + piece[0, weight].astype(f32)).astype(bf16)

    for side, out in enumerate(outs):
        start = side * 2 // len(outs) * half

        @pl.when(tables[1, side, at] == 1)
        def _(out=out, start=start):
            out[0] = scratch[:, start : start + half, :]


def attention_wgrad(rows_in, middle, sides, attended, order, blocks, added=()):
    features = rows_in.shape[1]
    width = sides[0].shape[1]
    block = features // blocks
    count = order.shape[0]
    tables, sizes = split_tables(count, 1)
    left = lambda values: pl.BlockSpec((values.shape[0], block), lambda i, ids, to: (0, ids[i]))
    right = lambda values: pl.BlockSpec(values.shape, lambda i, ids, to: (0, 0))

    def half_spec(side):
        return pl.BlockSpec((1, 4, block // 2, width), lambda i, ids, to: (to[0, side, i], 0, 0, 0))

    group_specs = [pl.BlockSpec((1, 4, block, width), lambda i, ids, to: (0, 0, 0, 0))] * count
    if added:
        out_specs = [half_spec(side) for side in range(len(sizes))]
        out_shape = [jax.ShapeDtypeStruct((size, 4, block // 2, width), bf16) for size in sizes]
    else:
        out_specs = group_specs
        out_shape = [jax.ShapeDtypeStruct((1, 4, block, width), bf16)] * count
    return pl.pallas_call(
        functools.partial(attention_wgrad_kernel, len(added)),
        grid_spec=pltpu.PrefetchScalarGridSpec(
            num_scalar_prefetch=2,
            grid=(count,),
            in_specs=[left(rows_in), left(middle)] + [right(v) for v in sides] + [right(attended)] + (group_specs if added else []),
            out_specs=out_specs,
            scratch_shapes=[pltpu.VMEM((4, block, width), bf16)] if added else [],
        ),
        out_shape=out_shape,
        compiler_params=params(),
        cost_estimate=cost(0, 0),
        name="attention_wgrad",
    )(order, tables, rows_in, middle, *sides, attended, *added)


def attend_kernel(
    block, qraw, kraw, value, q_scale, k_scale, q_gain, k_gain, cosine, sine,
    seg_col, seg_row, keep_row, q_out, k_out, o_out, lse_out, bias,
):
    @pl.when(pl.program_id(0) == 0)
    def _():
        fill_bias(bias, seg_col, seg_row, keep_row, block)

    def rotated(raw, scale, gain):
        normed = raw[...] * scale[...] * gain[...]
        return (normed * cosine[...] + turned(normed) * sine[...]).astype(bf16)

    q_out[...] = rotated(qraw, q_scale, q_gain)
    k_out[...] = rotated(kraw, k_scale, k_gain)
    length = seg_col.shape[0]
    for start in range(0, length, block):
        first, stop = key_start(start), start + block
        scores = nt(q_out[start:stop, :], k_out[first:stop, :]) * HEAD ** (-0.5)
        scores = scores + bias[start:stop, : stop - first]
        top = jnp.max(scores, axis=1, keepdims=True)
        powers = jnp.exp(scores - top)
        total = jnp.sum(powers, axis=1, keepdims=True)
        weights = (powers * (1.0 / total)).astype(bf16)
        o_out[start:stop, :] = nn(weights, value[first:stop, :]).astype(bf16)
        lse_out[start:stop, :] = jnp.broadcast_to(top + jnp.log(total), (block, HEAD))


def attend(qraw, kraw, value, q_scale, k_scale, q_gain, k_gain, cosine, sine, seg, keep):
    length, width = qraw.shape
    block = min(256, length)
    span = min(DOC + block, length)
    head = pl.BlockSpec((length, HEAD), lambda h: (0, h))
    gain = pl.BlockSpec((1, HEAD), lambda h: (0, h))
    whole = lambda *shape: pl.BlockSpec(shape, lambda h: (0, 0))
    return pl.pallas_call(
        functools.partial(attend_kernel, block),
        grid=(width // HEAD,),
        in_specs=[head, head, head, whole(length, 1), whole(length, 1), gain, gain]
        + [whole(length, HEAD), whole(length, HEAD), whole(length, 1), whole(1, length), whole(1, length)],
        out_specs=[head, head, head, head],
        out_shape=[jax.ShapeDtypeStruct((length, width), t) for t in (bf16, bf16, bf16, f32)],
        scratch_shapes=[pltpu.VMEM((length, span), f32)],
        compiler_params=params(),
        cost_estimate=cost(4 * length * span * width, 18 * length * width, length * span * width // HEAD),
        name="attend",
    )(qraw, kraw, value, q_scale, k_scale, q_gain[None], k_gain[None], cosine, sine, seg[:, None], seg[None], keep[None])


def attend_back_kernel(
    block, query, key, value, out_grad, lse, qraw, kraw, q_scale, k_scale, q_gain, k_gain, cosine, sine,
    seg_col, seg_row, keep_row, dq_out, dk_out, dv_out, qdot_out, kdot_out, qg_out, kg_out, bias, dk_sum, dv_sum,
):
    at = pl.program_id(0)

    @pl.when(at == 0)
    def _():
        fill_bias(bias, seg_col, seg_row, keep_row, block)
        qdot_out[...] = jnp.zeros_like(qdot_out)
        kdot_out[...] = jnp.zeros_like(kdot_out)

    dk_sum[...] = jnp.zeros_like(dk_sum)
    dv_sum[...] = jnp.zeros_like(dv_sum)
    length = seg_col.shape[0]
    scale = HEAD ** (-0.5)
    for start in range(0, length, block):
        first, stop = key_start(start), start + block
        rows, keys = slice(start, stop), slice(first, stop)
        scores = nt(query[rows, :], key[keys, :]) * scale + bias[rows, : stop - first]
        weights = jnp.exp(scores - lse[rows, :1])
        prob_grad = nt(out_grad[rows, :], value[keys, :])
        inner = jnp.sum(weights * prob_grad, axis=1, keepdims=True)
        score_grad = (weights * (prob_grad - inner)).astype(bf16)
        dq_out[rows, :] = nn(score_grad, key[keys, :]) * scale
        dk_sum[keys, :] += tn(score_grad, query[rows, :])
        dv_sum[keys, :] += tn(weights.astype(bf16), out_grad[rows, :])

    def unrotated(grad):
        return grad * cosine[...] + turned(grad * sine[...])

    dv_out[...] = dv_sum[...].astype(bf16)
    dq = unrotated(dq_out[...])
    dk = unrotated(dk_sum[...] * scale)
    dq_out[...] = dq
    dk_out[...] = dk
    dq = dq * qraw[...]
    dk = dk * kraw[...]
    qg_out[...] = jnp.sum(dq * q_scale[...], axis=0, keepdims=True)
    kg_out[...] = jnp.sum(dk * k_scale[...], axis=0, keepdims=True)
    qdot_out[...] += jnp.sum(dq * q_gain[...], axis=1, keepdims=True)
    kdot_out[...] += jnp.sum(dk * k_gain[...], axis=1, keepdims=True)


def attend_back(query, key, value, out_grad, lse, qraw, kraw, q_scale, k_scale, q_gain, k_gain, cosine, sine, seg, keep):
    length, width = qraw.shape
    block = min(256, length)
    span = min(DOC + block, length)
    head = pl.BlockSpec((length, HEAD), lambda h: (0, h))
    gain = pl.BlockSpec((1, HEAD), lambda h: (0, h))
    whole = lambda *shape: pl.BlockSpec(shape, lambda h: (0, 0))
    sds = jax.ShapeDtypeStruct
    return pl.pallas_call(
        functools.partial(attend_back_kernel, block),
        grid=(width // HEAD,),
        in_specs=[head] * 7
        + [whole(length, 1), whole(length, 1), gain, gain]
        + [whole(length, HEAD), whole(length, HEAD), whole(length, 1), whole(1, length), whole(1, length)],
        out_specs=[head, head, head, whole(length, 1), whole(length, 1), gain, gain],
        out_shape=[sds((length, width), f32), sds((length, width), f32), sds((length, width), bf16)]
        + [sds((length, 1), f32), sds((length, 1), f32), sds((1, width), f32), sds((1, width), f32)],
        scratch_shapes=[pltpu.VMEM((length, span), f32), pltpu.VMEM((length, HEAD), f32), pltpu.VMEM((length, HEAD), f32)],
        compiler_params=params(),
        cost_estimate=cost(20 * length * span * width, 0),
        name="attend_back",
    )(query, key, value, out_grad, lse, qraw, kraw, q_scale, k_scale, q_gain[None], k_gain[None], cosine, sine, seg[:, None], seg[None], keep[None])


def middle_kernel(tokens, summed, gain, middle_out, scale_out, normed_out):
    middle = tokens[...].astype(f32) + summed[...].astype(f32)
    scale = lax.rsqrt(jnp.mean(middle * middle, axis=1, keepdims=True) + EPSILON)
    middle_out[...] = middle
    scale_out[...] = scale
    normed_out[...] = (middle * scale * gain[...]).astype(bf16)


def middle_rows(chunk, tokens, summed, gain):
    rows, features = summed.shape
    sds = jax.ShapeDtypeStruct
    whole = lambda *shape: pl.BlockSpec(shape, lambda i: (0, 0))
    return pl.pallas_call(
        middle_kernel,
        grid=(1,),
        in_specs=[pl.BlockSpec((rows, features), lambda i: (chunk, 0)), whole(rows, features), whole(1, features)],
        out_specs=[whole(rows, features), whole(rows, 1), whole(rows, features)],
        out_shape=[sds((rows, features), f32), sds((rows, 1), f32), sds((rows, features), bf16)],
        compiler_params=params(),
        cost_estimate=cost(0, 0),
        name="middle",
    )(tokens, summed, gain[None])


def middle_back_kernel(
    experts, grads, middle, scale, normed, routed, router, cotangent, gain, *refs
):
    grad_out, low_out, gain_out, logit_out = refs[-4:]
    features = middle.shape[1]
    lane = lax.broadcasted_iota(jnp.int32, routed.shape, 1)
    logits = jnp.where(lane < experts, nn(normed[...], router[...]), MASKED)
    powers = jnp.exp(logits - jnp.max(logits, axis=1, keepdims=True))
    probs = powers / jnp.sum(powers, axis=1, keepdims=True)
    share_grad = grads[:, features:].astype(f32) * routed[...]
    logit_grad = (probs * (share_grad - jnp.sum(share_grad * probs, axis=1, keepdims=True))).astype(bf16)
    logit_out[...] = logit_grad
    ffn_grad = grads[:, :features].astype(f32) + nt(logit_grad, router[...])
    along = middle[...] * scale[...]
    gain_out[...] = jnp.sum(ffn_grad * along, axis=0, keepdims=True)
    weighted = ffn_grad * gain[...]
    inner = jnp.mean(weighted * along, axis=1, keepdims=True)
    total = cotangent[...].astype(f32) + scale[...] * (weighted - along * inner)
    grad_out[...] = total
    low_out[...] = total.astype(bf16)


def middle_back(chunk, grads, middle, scale, normed, routed, router, cotangent, gain, experts, filled=()):
    rows, features = middle.shape
    sds = jax.ShapeDtypeStruct
    whole = lambda *shape: pl.BlockSpec(shape, lambda i: (0, 0))
    part = lambda columns: pl.BlockSpec((rows, columns), lambda i: (chunk, 0))
    return pl.pallas_call(
        functools.partial(middle_back_kernel, experts),
        grid=(1,),
        in_specs=[whole(rows, features + LANES), whole(rows, features), whole(rows, 1), whole(rows, features), part(LANES)]
        + [whole(features, LANES), part(features), whole(1, features)]
        + [pl.BlockSpec(memory_space=pl.ANY)] * len(filled),
        out_specs=[part(features), part(features), whole(1, features), whole(rows, LANES)],
        out_shape=[sds(cotangent.shape, f32), sds(cotangent.shape, bf16), sds((1, features), f32), sds((rows, LANES), bf16)],
        input_output_aliases={8 + at: at for at in range(len(filled))},
        compiler_params=params(),
        cost_estimate=cost(0, 0),
        name="middle_back",
    )(grads, middle, scale, normed, routed, router, cotangent, gain[None], *filled)


def up_back_kernel(grad, down_w, out):
    width = down_w.shape[2]
    for at in range(down_w.shape[0]):
        out[:, at * width : (at + 1) * width] = nn(grad[...], down_w[at]).astype(out.dtype)


def up_back(grad, down_w):
    rows, features = grad.shape
    experts, _, width = down_w.shape
    step = 2 if experts % 2 == 0 else 1
    return pl.pallas_call(
        up_back_kernel,
        grid=(experts // step,),
        in_specs=[pl.BlockSpec((rows, features), lambda e: (0, 0)), pl.BlockSpec((step, features, width), lambda e: (e, 0, 0))],
        out_specs=pl.BlockSpec((rows, step * width), lambda e: (0, e)),
        out_shape=jax.ShapeDtypeStruct((rows, experts * width), bf16),
        compiler_params=params(),
        cost_estimate=cost(2 * rows * features * experts * width, 2 * (rows + experts * width) * features),
        name="up_back",
    )(grad, down_w)


def expert_kernel(block, rows_in, back, routed, router, gate_w, up_w, act_out, dgate_out, dup_out, grad_out, comb, dcomb, total):
    at = pl.program_id(0)
    rows, features = rows_in.shape
    lane = lax.broadcasted_iota(jnp.int32, (block, LANES), 1)

    @pl.when(at == 0)
    def _():
        experts = pl.num_programs(0)
        for start in range(0, rows, block):
            here = slice(start, start + block)
            logits = jnp.where(lane < experts, nn(rows_in[here, :], router[...]), MASKED)
            powers = jnp.exp(logits - jnp.max(logits, axis=1, keepdims=True))
            probs = powers / jnp.sum(powers, axis=1, keepdims=True)
            comb[here, :] = probs * routed[here, :]
        total[...] = jnp.zeros_like(total)
        dcomb[...] = jnp.zeros_like(dcomb)

    gate, up = gate_w[0], up_w[0]
    mine = lane == at
    for start in range(0, rows, block):
        here = slice(start, start + block)
        taken = rows_in[here, :]
        pre_gate = nn(taken, gate)
        pre_up = nn(taken, up)
        behind = back[...].reshape(rows, back.shape[3])[here, :].astype(f32)
        share = jnp.sum(jnp.where(mine, comb[here, :], 0.0), axis=1, keepdims=True)
        sigmoid = 0.5 * jnp.tanh(0.5 * pre_gate) + 0.5
        active = pre_gate * sigmoid
        inner = active * pre_up
        share_grad = jnp.sum(inner * behind, axis=1, keepdims=True)
        dcomb[here, :] = jnp.where(mine, share_grad, dcomb[here, :])
        act_out[here, :] = (inner * share).astype(bf16)
        inner_grad = behind * share
        dgate = (inner_grad * pre_up * (sigmoid + active * (1.0 - sigmoid))).astype(bf16)
        dup = (inner_grad * active).astype(bf16)
        dgate_out[here, :] = dgate
        dup_out[here, :] = dup
        total[here, :] += nt(dgate, gate) + nt(dup, up)

    @pl.when(at == pl.num_programs(0) - 1)
    def _():
        grad_out[:, :features] = total[...].astype(bf16)
        grad_out[:, features:] = dcomb[...].astype(bf16)


def experts_block(chunk, rows_in, back, routed, router, gate_w, up_w):
    rows, features = rows_in.shape
    parts, _, chunk_rows, _ = back.shape
    experts, _, width = gate_w.shape
    block = min(512, rows)
    whole = lambda *shape: pl.BlockSpec(shape, lambda e: (0, 0))
    column = pl.BlockSpec((rows, width), lambda e: (0, e))
    weight = pl.BlockSpec((1, features, width), lambda e: (e, 0, 0))
    wide = jax.ShapeDtypeStruct((rows, experts * width), bf16)
    return pl.pallas_call(
        functools.partial(expert_kernel, block),
        grid=(experts,),
        in_specs=[whole(rows, features), pl.BlockSpec((parts, 1, chunk_rows, width), lambda e: (0, chunk, 0, e)), whole(rows, LANES), whole(features, LANES), weight, weight],
        out_specs=[column, column, column, whole(rows, features + LANES)],
        out_shape=[wide, wide, wide, jax.ShapeDtypeStruct((rows, features + LANES), bf16)],
        scratch_shapes=[pltpu.VMEM((rows, LANES), f32), pltpu.VMEM((rows, LANES), f32), pltpu.VMEM((rows, features), f32)],
        compiler_params=params(),
        cost_estimate=cost(8 * rows * features * experts * width, 4 * experts * width * (features + 2 * rows), rows * experts * width),
        name="experts",
    )(rows_in, back, routed, router, gate_w, up_w)


def block_order(blocks):
    return [3, 2, 0, 1] if blocks == 4 else list(range(blocks))


def split_tables(blocks, per):
    order = block_order(blocks)
    if blocks == 4:
        picks = [{0: 0, 1: 1}, {2: 0, 3: 1}, {0: 0, 2: 1}, {1: 0, 3: 1}]
    else:
        picks = [{block: block for block in order}] * 2
    places, fills = [], []
    for pick in picks:
        filled = [pick[block] * per + at if block in pick else None for block in order for at in range(per)]
        last = next(place for place in filled if place is not None)
        row = []
        for place in filled:
            last = last if place is None else place
            row.append(last)
        places.append(row)
        fills.append([int(place is not None) for place in filled])
    return jnp.asarray(np.array([places, fills], np.int32)), [len(pick) for pick in picks]


def wgrad_kernel(count, extra, per, block, order, tables, *refs):
    lefts, rights = refs[:count], refs[count : 2 * count]
    added = refs[2 * count : 2 * count + extra]
    outs = refs[2 * count + extra :]
    at = pl.program_id(0)
    features = lefts[0].shape[-1]

    def piece(start, stop):
        total = None
        for left, right in zip(lefts, rights):
            columns = left[:, start:stop] if len(left.shape) == 2 else left[:, :, :, start:stop].reshape(-1, stop - start)
            part = tn(columns, right[...])
            total = part if total is None else total + part
        return total

    if not added:
        for place, out in enumerate(outs):

            @pl.when(at // per == place)
            def _(out=out):
                for start in range(0, features, block):
                    out[0, start : start + block, :] = piece(start, start + block).astype(bf16)

        return
    half = features // 2
    got = outs[-1]
    outs = outs[:-1]
    for place, arrived in enumerate(added):

        @pl.when(at // per == place)
        def _(arrived=arrived):
            for start in range(0, features, block):
                total = piece(start, start + block) + arrived[0, start : start + block, :].astype(f32)
                got[start : start + block, :] = total.astype(bf16)

    for side, out in enumerate(outs):
        start = side * 2 // len(outs) * half

        @pl.when(tables[1, side, at] == 1)
        def _(out=out, start=start):
            out[0] = got[start : start + half, :]


def wgrad(lefts, rights, order, width, per, added=(), weight=1):
    features = lefts[0][0].shape[-1]
    experts = order.shape[0]
    groups = experts // per
    tables, sizes = split_tables(groups, per)

    def group_spec(place):
        return pl.BlockSpec((1, features, width), lambda i, ids, to: (jnp.clip(i - place * per, 0, per - 1), 0, 0))

    def half_spec(side):
        return pl.BlockSpec((1, features // 2, width), lambda i, ids, to: (to[0, side, i], 0, 0))

    def left_spec(left, chunk):
        if left.ndim == 2:
            return pl.BlockSpec(left.shape, lambda i, ids, to: (0, 0))
        return pl.BlockSpec((left.shape[0], 1) + left.shape[2:], lambda i, ids, to: (0, chunk, 0, 0))

    groups_specs = [group_spec(place) for place in range(groups)]
    if added:
        out_specs = [half_spec(side) for side in range(len(sizes))]
        out_shape = [jax.ShapeDtypeStruct((size * per, features // 2, width), bf16) for size in sizes]
    else:
        out_specs = groups_specs
        out_shape = [jax.ShapeDtypeStruct((per, features, width), bf16)] * groups
    return pl.pallas_call(
        functools.partial(wgrad_kernel, len(lefts), len(added), per, min(512, features // 2)),
        grid_spec=pltpu.PrefetchScalarGridSpec(
            num_scalar_prefetch=2,
            grid=(experts,),
            in_specs=[left_spec(*left) for left in lefts]
            + [pl.BlockSpec((right.shape[0], width), lambda i, ids, to: (0, ids[i])) for right in rights]
            + (groups_specs if added else []),
            out_specs=out_specs,
            scratch_shapes=[pltpu.VMEM((features, width), bf16)] if added else [],
        ),
        out_shape=out_shape,
        compiler_params=params(),
        cost_estimate=cost(2 * weight * sum(right.shape[0] for right in rights) * features * experts * width, 0),
        name="wgrad",
    )(order, tables, *(left for left, _ in lefts), *rights, *added)


def down_kernel(parts, down_w, *refs):
    acts, out = refs[:-1], refs[-1]
    joined = jnp.concatenate([down_w[e] for e in range(down_w.shape[0])], axis=1)
    block = acts[0].shape[0] // parts
    for at, act in enumerate(acts):
        result = nt(act[...], joined).astype(out.dtype)
        for part in range(parts):
            start = (part * len(acts) + at) * block
            out[start : start + block, :] = result[part * block : (part + 1) * block, :]


def down(acts, down_w, parts):
    rows = sum(act.shape[0] for act in acts)
    experts, features, width = down_w.shape
    block = min(256, features)
    return pl.pallas_call(
        functools.partial(down_kernel, parts),
        grid=(features // block,),
        in_specs=[pl.BlockSpec((experts, block, width), lambda n: (0, n, 0))]
        + [pl.BlockSpec(act.shape, lambda n: (0, 0)) for act in acts],
        out_specs=pl.BlockSpec((rows, block), lambda n: (0, n)),
        out_shape=jax.ShapeDtypeStruct((rows, features), bf16),
        compiler_params=params(),
        cost_estimate=cost(2 * rows * features * experts * width, 2 * (rows + experts * width) * features),
        name="down",
    )(down_w, *acts)


def gate(value, *others):
    return lax.optimization_barrier((value, others))[0]


def gather_rows(values):
    return lax.all_gather(values, "tensor", axis=0, tiled=True)


def scatter_rows(values):
    return lax.psum_scatter(values, "tensor", scatter_dimension=0, tiled=True)


def pair_swap(values, step):
    size = lax.axis_size("dp")
    return lax.ppermute(values, "dp", [(i, i ^ step) for i in range(size)])


class Halving:
    def __init__(self, values):
        if len(values) == 2:
            self.kept = list(values)
            self.going = None
        else:
            self.kept, self.going = list(values[::2]), list(values[1::2])
        bits = list(range(values[0].shape[0].bit_length() - (1 if self.going is None else 0)))
        self.left = [bits[::-1], bits]
        self.got = None

    def send(self):
        if not self.left[0]:
            return ()
        self.got = []
        sent = []
        for side, downward in ((0, True), (1, False)):
            bit = self.left[side].pop(0)
            if self.going is not None:
                go = self.going[side]
            else:
                kept = self.kept[side]
                half = kept.shape[0] // 2
                if downward:
                    self.kept[side], go = kept[:half], kept[half:]
                else:
                    view = kept.reshape((half, 2) + kept.shape[1:])
                    self.kept[side], go = view[:, 0], view[:, 1]
            sent.append(go)
            self.got.append(pair_swap(go, 2 << bit))
        self.going = None
        return tuple(sent)

    def add(self, *others):
        if self.got is not None:
            if others:
                self.got = gate(tuple(self.got), *others)
            last = not self.left[0]
            for side in range(2):
                total = self.kept[side].astype(f32) + self.got[side].astype(f32)
                self.kept[side] = total if last else total.astype(bf16)
            self.got = None
        return tuple(self.kept)

    def done(self):
        self.add()
        while self.left[0]:
            self.send()
            self.add()
        return jnp.concatenate([kept[0].astype(f32) for kept in self.kept], axis=1)


def exchange_sum(values, axes):
    for axis in axes:
        size = lax.axis_size(axis)
        step = 1
        while step < size:
            values = values + lax.ppermute(values, axis, [(i, i ^ step) for i in range(size)])
            step *= 2
    return values


def local(
    tokens, cotangent, seg_ids, keep_mask, routes, attn_gain, w_query, w_key, w_value, w_out,
    q_gain, k_gain, ffn_gain, router, w_gate, w_up, w_down,
):
    parts = lax.axis_size("tensor")
    part_at = lax.axis_index("tensor")
    dp_size = lax.axis_size("dp")
    low_bit = lax.axis_index("dp") % 2
    shard_rows, features = tokens.shape
    group_rows = shard_rows * parts
    _, length = seg_ids.shape
    local_width = w_query.shape[1]
    experts, _, width = w_gate.shape
    per = experts // dp_size
    chunk_rows = shard_rows // CHUNKS
    chunks = range(CHUNKS)
    own = [slice(c * chunk_rows, (c + 1) * chunk_rows) for c in chunks]

    def chunk_of(values, c):
        columns = values.shape[1]
        return values.reshape(parts, CHUNKS, chunk_rows, columns)[:, c].reshape(parts * chunk_rows, columns)

    inputs = tokens.astype(f32)
    first_scale = rms_scale(inputs)
    normed_all = gather_rows((inputs * first_scale * attn_gain).astype(bf16))
    grad_rows = gather_rows(gate(cotangent, normed_all))

    cosine, sine = rope_tables(length, HEAD)

    relative = jnp.asarray(block_order(dp_size // 2), jnp.int32) ^ (lax.axis_index("dp") // 2)
    own_blocks, other_blocks = 2 * relative + low_bit, 2 * relative + 1 - low_bit
    mine, theirs = (
        (blocks[:, None] * per + jnp.arange(per, dtype=jnp.int32)).reshape(-1) for blocks in (own_blocks, other_blocks)
    )

    qraw, kraw, value, squares = project(normed_all, w_query, w_key, w_value)
    squares = exchange_sum(squares, ("tensor",))
    q_scale, k_scale = (lax.rsqrt(squares[i] / features + EPSILON)[:, None] for i in range(2))
    query, key, attended, lse = attend(
        qraw, kraw, value, q_scale, k_scale, q_gain, k_gain, cosine, sine, seg_ids[0], keep_mask[0]
    )
    attended_parts = [chunk_of(gate(attended, grad_rows), c) for c in chunks]
    outs = [nt(attended_parts[0], w_out).astype(bf16)]
    summed = [scatter_rows(outs[0])]
    outs.append(nt(gate(attended_parts[1], outs[0]), w_out).astype(bf16))
    summed.append(scatter_rows(outs[1]))

    idle_routes, idle_router = gate((routes, router), outs[1])
    expert_ids = jnp.arange(LANES)
    routed = jnp.sum((idle_routes[:, :, None] == expert_ids[None, None, :]).astype(f32), axis=1)
    router_wide = jnp.pad(idle_router, ((0, 0), (0, LANES - experts)))
    routed_own = lax.dynamic_slice_in_dim(routed, part_at * shard_rows, shard_rows, 0)
    back = up_back(gate(grad_rows, routed, router_wide), w_down).reshape(parts, CHUNKS, chunk_rows, -1)
    grad_rows = grad_rows.reshape(parts, CHUNKS, chunk_rows, features)
    grad_parts = [(grad_rows, c) for c in chunks]

    norms = [middle_rows(0, tokens, summed[0], ffn_gain)]
    ffn_all = [gather_rows(norms[0][2])]
    norms.append(middle_rows(1, tokens, gate(summed[1], norms[0][2], back), ffn_gain))
    ffn_all.append(gather_rows(norms[1][2]))
    ffn_parts = [(rows, 0) for rows in ffn_all]
    acts, dgates, dups, expert_grads = [], [], [], []
    for c in chunks:
        here = gate(chunk_of(routed, c), back, *acts[-1:])
        act, dgate, dup, grads = experts_block(c, ffn_all[c], back, here, router_wide, w_gate, w_up)
        acts.append(act)
        dgates.append(dgate)
        dups.append(dup)
        expert_grads.append(grads)
    expert_grads = [scatter_rows(grads) for grads in expert_grads]

    def back_of(c, grads, filled=()):
        return middle_back(c, grads, *norms[c], routed_own, router_wide, cotangent, ffn_gain, experts, filled)

    def expert_sums(lefts, rights, ids, *others, added=(), weight=1):
        return wgrad(lefts, rights, gate(ids, *others), width, per, added, weight)

    def core_swap(pieces):
        return [pair_swap(piece, 1) for piece in pieces]

    def halving(sums):
        return Halving([part.reshape((part.shape[0] // per, per) + part.shape[1:]) for part in sums])

    first = back_of(0, gate(expert_grads[0], acts[1]))
    gate_sent = expert_sums(ffn_parts, dgates, theirs, first[1])
    gate_got = core_swap(gate_sent)
    up_sent = expert_sums(ffn_parts, dups, theirs, *gate_sent)
    up_got = core_swap(up_sent)
    second = back_of(1, gate(expert_grads[1], *up_sent), first[:2])
    middle_grad, middle_low = second[:2]
    middle_all = gather_rows(middle_low)
    gate_sums = expert_sums(ffn_parts, dgates, mine, middle_low, added=gate_got)
    gate_out = halving(gate_sums)
    gate_out.send()
    up_sums = expert_sums(ffn_parts, dups, mine, *gate_sums, added=up_got)
    up_out = halving(up_sums)
    up_out.send()
    moe = down([gate(acts[0], *up_sums), acts[1]], w_down, parts)
    moe_sum = scatter_rows(moe)
    attended_grad = nn(gate(middle_all, moe), w_out).astype(bf16)
    dqn, dkn, dvalue, qdot, kdot, q_gain_part, k_gain_part = attend_back(
        query, key, value, attended_grad, lse, qraw, kraw, q_scale, k_scale, q_gain, k_gain, cosine, sine,
        seg_ids[0], keep_mask[0],
    )
    dots = exchange_sum(jnp.stack([qdot[:, 0], kdot[:, 0]]), ("tensor",)) / features
    gate_late = gate_out.add(dqn)
    gate_out.send()
    down_sent = expert_sums(grad_parts, acts, theirs, *gate_late)
    down_got = core_swap(down_sent)
    up_late = up_out.add(*down_sent)
    up_out.send()
    down_sums = expert_sums(grad_parts, acts, mine, *up_late, *gate_out.got, added=down_got, weight=13.0)
    down_out = halving(down_sums)
    down_out.send()
    normed_part, dqraw, dkraw, attn_gain_part = project_back(
        normed_all, dqn, dkn, dvalue, qraw, kraw, q_scale, k_scale, dots[0][:, None], dots[1][:, None],
        gate(q_gain, *down_sums, *up_out.got), k_gain, w_query, w_key, w_value,
    )
    normed_grad = scatter_rows(normed_part)
    def attention_sums(ids, *others, added=()):
        return attention_wgrad(
            normed_all, middle_all, (dqraw, dkraw, dvalue), attended, gate(ids, *others), dp_size, added
        )

    attn_sent = attention_sums(other_blocks, normed_part)
    attn_got = core_swap(attn_sent)

    def placed(part):
        return lax.dynamic_update_slice_in_dim(jnp.zeros((features,), f32), part, part_at * local_width, 0)

    attn_sums = attention_sums(own_blocks, *attn_sent, added=attn_got)
    attn_out = Halving(attn_sums)
    normed_grad = gate(normed_grad, *attn_out.send())
    down_out.add(*attn_sums)
    down_out.send()
    smalls = [attn_gain_part[0] / attn_gain, placed(q_gain_part[0]), placed(k_gain_part[0]), (first[2] + second[2])[0]]
    router_part = sum(tn(late[3], norms[c][2]) for c, late in enumerate((first, second)))[:experts]
    smalls = gate(jnp.concatenate([jnp.stack(smalls), router_part]), *attn_sums)
    smalls = exchange_sum(smalls, ("dp", "tensor"))
    late_got = tuple(down_out.got)
    gate_done = gate_out.done()
    up_done = up_out.done()
    down_done = down_out.done()
    attn_out.add(normed_grad)
    query_done, key_done, value_done, out_done = attn_out.done()
    layer_out = (jnp.concatenate([norms[c][0] for c in chunks]) + gate(moe_sum, *late_got).astype(f32)).astype(bf16)
    tokens_grad = middle_grad + norm_back(normed_grad.astype(f32), inputs, first_scale, attn_gain)
    return (
        layer_out, tokens_grad, query_done, key_done, value_done, out_done,
        smalls[0], smalls[1], smalls[2], smalls[3], smalls[4:].T, gate_done, up_done, down_done,
    )


def solution(mesh):
    rows = P(("dp", "tensor"), None)
    column = P(None, "tensor")
    expert = P(None, None, "tensor")
    in_specs = (
        rows, rows, P("dp", None), P("dp", None), P("dp", None), P(), column, column, column, column,
        P("tensor"), P("tensor"), P(), P(), expert, expert, expert,
    )
    block = P("dp", "tensor")
    expert_out = P("dp", None, "tensor")
    out_specs = (
        rows, rows, block, block, block, block, P(), P(), P(), P(), P(), expert_out, expert_out, expert_out,
    )
    return jax.shard_map(local, mesh=mesh, in_specs=in_specs, out_specs=out_specs, check_vma=False)
```

```python
import functools

import jax
import jax.numpy as jnp
import numpy as np
from jax import lax
from jax.experimental import pallas as pl
from jax.experimental.pallas import tpu as pltpu
from jax.sharding import PartitionSpec as P

D = 2048
HEAD = 128
DOC = 512
LANES = 128
EPSILON = 1e-05
MASKED = -1e30
CHUNKS = 2
VMEM = 56 * 1024 * 1024
bf16 = jnp.bfloat16
f32 = jnp.float32


def nn(left, right):
    return lax.dot_general(left, right, (((1,), (0,)), ((), ())), preferred_element_type=f32)


def nt(left, right):
    return lax.dot_general(left, right, (((1,), (1,)), ((), ())), preferred_element_type=f32)


def tn(left, right):
    return lax.dot_general(left, right, (((0,), (0,)), ((), ())), preferred_element_type=f32)


def params():
    return pltpu.CompilerParams(vmem_limit_bytes=VMEM)


PACE = 0.3


def cost(flops, moved, special=0):
    return pl.CostEstimate(flops=int(1.5 * PACE * flops + 6e4 * PACE * special), bytes_accessed=moved // 8, transcendentals=0)


def rms_scale(values):
    return lax.rsqrt(jnp.mean(values * values, axis=-1, keepdims=True) + EPSILON)


def norm_back(grad_values, values, scale_col, gain_vec):
    weighted = grad_values * gain_vec
    inner_mean = jnp.mean(weighted * values, axis=-1, keepdims=True)
    return scale_col * weighted - values * (scale_col * scale_col * scale_col) * inner_mean


def rope_tables(length, width):
    angles = np.arange(length)[:, None] * 10000.0 ** (-np.arange(width // 2) * 2.0 / width)[None, :]
    cosine, sine = np.cos(angles).astype(np.float32), np.sin(angles).astype(np.float32)
    return jnp.asarray(np.concatenate([cosine, cosine], axis=1)), jnp.asarray(np.concatenate([-sine, sine], axis=1))


def key_start(query_start):
    return max(0, query_start - DOC)


def fill_bias(bias, seg_col, seg_row, keep_row, block):
    length = seg_col.shape[0]
    for start in range(0, length, block):
        first, stop = key_start(start), start + block
        query_pos = start + lax.broadcasted_iota(jnp.int32, (block, stop - first), 0)
        key_pos = first + lax.broadcasted_iota(jnp.int32, (block, stop - first), 1)
        same = seg_col[start:stop, :] == seg_row[:, first:stop]
        live = (keep_row[:, first:stop] == 1) | (key_pos == query_pos)
        allowed = same & live & (key_pos <= query_pos)
        bias[start:stop, : stop - first] = jnp.where(allowed, 0.0, MASKED)


def turned(values):
    return pltpu.roll(values, values.shape[1] // 2, 1)


def project_kernel(rows_in, w_query, w_key, w_value, q_out, k_out, v_out, squares_out):
    ones = jnp.ones((8, q_out.shape[1]), f32)
    for at, (weight, out) in enumerate(((w_query, q_out), (w_key, k_out))):
        raw = nn(rows_in[...], weight[...])
        out[...] = raw
        sums = lax.dot_general(
            ones, raw * raw, (((1,), (1,)), ((), ())), precision=lax.Precision.HIGHEST, preferred_element_type=f32
        )
        squares_out[at : at + 1, :] = sums[:1]
    v_out[...] = nn(rows_in[...], w_value[...]).astype(bf16)


def project(rows_in, w_query, w_key, w_value):
    rows, features = rows_in.shape
    width = w_query.shape[1]
    block = min(256, rows)
    row = lambda columns: pl.BlockSpec((block, columns), lambda r: (r, 0))
    weight = pl.BlockSpec((features, width), lambda r: (0, 0))
    sds = jax.ShapeDtypeStruct
    return pl.pallas_call(
        project_kernel,
        grid=(rows // block,),
        in_specs=[row(features), weight, weight, weight],
        out_specs=[row(width), row(width), row(width), pl.BlockSpec((2, block), lambda r: (0, r))],
        out_shape=[sds((rows, width), f32), sds((rows, width), f32), sds((rows, width), bf16), sds((2, rows), f32)],
        compiler_params=params(),
        cost_estimate=cost(6 * rows * features * width, 2 * (rows + 3 * width) * features),
        name="project",
    )(rows_in, w_query, w_key, w_value)


def project_back_kernel(
    rows_in, dqn, dkn, dvalue, qraw, kraw, q_scale, k_scale, q_dot, k_dot, q_gain, k_gain,
    w_query, w_key, w_value, part_out, dq_out, dk_out, gain_out,
):
    @pl.when(pl.program_id(0) == 0)
    def _():
        gain_out[...] = jnp.zeros_like(gain_out)

    def raw_grad(grad, raw, scale, gain, dot):
        cube = scale[...] * scale[...] * scale[...]
        return (scale[...] * (gain[...] * grad[...]) - raw[...] * (cube * dot[...])).astype(bf16)

    dq = raw_grad(dqn, qraw, q_scale, q_gain, q_dot)
    dk = raw_grad(dkn, kraw, k_scale, k_gain, k_dot)
    dq_out[...] = dq
    dk_out[...] = dk
    part = nt(dq, w_query[...]) + nt(dk, w_key[...]) + nt(dvalue[...], w_value[...])
    part_out[...] = part.astype(bf16)
    gain_out[...] += jnp.sum(part * rows_in[...].astype(f32), axis=0, keepdims=True)


def project_back(rows_in, dqn, dkn, dvalue, qraw, kraw, q_scale, k_scale, q_dot, k_dot, q_gain, k_gain, w_query, w_key, w_value):
    rows, features = rows_in.shape
    width = w_query.shape[1]
    block = min(256, rows)
    row = lambda columns: pl.BlockSpec((block, columns), lambda r: (r, 0))
    whole = lambda *shape: pl.BlockSpec(shape, lambda r: (0, 0))
    sds = jax.ShapeDtypeStruct
    return pl.pallas_call(
        project_back_kernel,
        grid=(rows // block,),
        in_specs=[row(features)] + [row(width)] * 5 + [row(1)] * 4 + [whole(1, width)] * 2 + [whole(features, width)] * 3,
        out_specs=[row(features), row(width), row(width), whole(1, features)],
        out_shape=[sds((rows, features), bf16), sds((rows, width), bf16), sds((rows, width), bf16), sds((1, features), f32)],
        compiler_params=params(),
        cost_estimate=cost(int(20.0 * 6 * rows * features * width), 0),
        name="project_back",
    )(rows_in, dqn, dkn, dvalue, qraw, kraw, q_scale, k_scale, q_dot, k_dot, q_gain[None], k_gain[None], w_query, w_key, w_value)


def attention_wgrad_kernel(added, order, tables, rows_in, middle, *refs):
    sides, (attended,), refs = refs[:3], refs[3:4], refs[4:]
    got, outs = (refs[:added], refs[added:])
    at = pl.program_id(0)
    totals = [tn(rows_in[...], side[...]) for side in sides] + [tn(middle[...], attended[...])]
    if not added:
        for place, out in enumerate(outs):

            @pl.when(at == place)
            def _(out=out):
                for weight, total in enumerate(totals):
                    out[0, weight] = total.astype(bf16)

        return
    scratch, outs = outs[-1], outs[:-1]
    half = outs[0].shape[2]
    for place, piece in enumerate(got):

        @pl.when(at == place)
        def _(piece=piece):
            for weight, total in enumerate(totals):
                scratch[weight] = (total + piece[0, weight].astype(f32)).astype(bf16)

    for side, out in enumerate(outs):
        start = side * 2 // len(outs) * half

        @pl.when(tables[1, side, at] == 1)
        def _(out=out, start=start):
            out[0] = scratch[:, start : start + half, :]


def attention_wgrad(rows_in, middle, sides, attended, order, blocks, added=()):
    features = rows_in.shape[1]
    width = sides[0].shape[1]
    block = features // blocks
    count = order.shape[0]
    tables, sizes = split_tables(count, 1)
    left = lambda values: pl.BlockSpec((values.shape[0], block), lambda i, ids, to: (0, ids[i]))
    right = lambda values: pl.BlockSpec(values.shape, lambda i, ids, to: (0, 0))

    def half_spec(side):
        return pl.BlockSpec((1, 4, block // 2, width), lambda i, ids, to: (to[0, side, i], 0, 0, 0))

    group_specs = [pl.BlockSpec((1, 4, block, width), lambda i, ids, to: (0, 0, 0, 0))] * count
    if added:
        out_specs = [half_spec(side) for side in range(len(sizes))]
        out_shape = [jax.ShapeDtypeStruct((size, 4, block // 2, width), bf16) for size in sizes]
    else:
        out_specs = group_specs
        out_shape = [jax.ShapeDtypeStruct((1, 4, block, width), bf16)] * count
    return pl.pallas_call(
        functools.partial(attention_wgrad_kernel, len(added)),
        grid_spec=pltpu.PrefetchScalarGridSpec(
            num_scalar_prefetch=2,
            grid=(count,),
            in_specs=[left(rows_in), left(middle)] + [right(v) for v in sides] + [right(attended)] + (group_specs if added else []),
            out_specs=out_specs,
            scratch_shapes=[pltpu.VMEM((4, block, width), bf16)] if added else [],
        ),
        out_shape=out_shape,
        compiler_params=params(),
        cost_estimate=cost(0, 0),
        name="attention_wgrad",
    )(order, tables, rows_in, middle, *sides, attended, *added)


def attend_kernel(
    block, qraw, kraw, value, q_scale, k_scale, q_gain, k_gain, cosine, sine,
    seg_col, seg_row, keep_row, q_out, k_out, o_out, lse_out, bias,
):
    @pl.when(pl.program_id(0) == 0)
    def _():
        fill_bias(bias, seg_col, seg_row, keep_row, block)

    def rotated(raw, scale, gain):
        normed = raw[...] * scale[...] * gain[...]
        return (normed * cosine[...] + turned(normed) * sine[...]).astype(bf16)

    q_out[...] = rotated(qraw, q_scale, q_gain)
    k_out[...] = rotated(kraw, k_scale, k_gain)
    length = seg_col.shape[0]
    for start in range(0, length, block):
        first, stop = key_start(start), start + block
        scores = nt(q_out[start:stop, :], k_out[first:stop, :]) * HEAD ** (-0.5)
        scores = scores + bias[start:stop, : stop - first]
        top = jnp.max(scores, axis=1, keepdims=True)
        powers = jnp.exp(scores - top)
        total = jnp.sum(powers, axis=1, keepdims=True)
        weights = (powers * (1.0 / total)).astype(bf16)
        o_out[start:stop, :] = nn(weights, value[first:stop, :]).astype(bf16)
        lse_out[start:stop, :] = jnp.broadcast_to(top + jnp.log(total), (block, HEAD))


def attend(qraw, kraw, value, q_scale, k_scale, q_gain, k_gain, cosine, sine, seg, keep):
    length, width = qraw.shape
    block = min(256, length)
    span = min(DOC + block, length)
    head = pl.BlockSpec((length, HEAD), lambda h: (0, h))
    gain = pl.BlockSpec((1, HEAD), lambda h: (0, h))
    whole = lambda *shape: pl.BlockSpec(shape, lambda h: (0, 0))
    return pl.pallas_call(
        functools.partial(attend_kernel, block),
        grid=(width // HEAD,),
        in_specs=[head, head, head, whole(length, 1), whole(length, 1), gain, gain]
        + [whole(length, HEAD), whole(length, HEAD), whole(length, 1), whole(1, length), whole(1, length)],
        out_specs=[head, head, head, head],
        out_shape=[jax.ShapeDtypeStruct((length, width), t) for t in (bf16, bf16, bf16, f32)],
        scratch_shapes=[pltpu.VMEM((length, span), f32)],
        compiler_params=params(),
        cost_estimate=cost(4 * length * span * width, 18 * length * width, length * span * width // HEAD),
        name="attend",
    )(qraw, kraw, value, q_scale, k_scale, q_gain[None], k_gain[None], cosine, sine, seg[:, None], seg[None], keep[None])


def attend_back_kernel(
    block, query, key, value, out_grad, lse, qraw, kraw, q_scale, k_scale, q_gain, k_gain, cosine, sine,
    seg_col, seg_row, keep_row, dq_out, dk_out, dv_out, qdot_out, kdot_out, qg_out, kg_out, bias, dk_sum, dv_sum,
):
    at = pl.program_id(0)

    @pl.when(at == 0)
    def _():
        fill_bias(bias, seg_col, seg_row, keep_row, block)
        qdot_out[...] = jnp.zeros_like(qdot_out)
        kdot_out[...] = jnp.zeros_like(kdot_out)

    dk_sum[...] = jnp.zeros_like(dk_sum)
    dv_sum[...] = jnp.zeros_like(dv_sum)
    length = seg_col.shape[0]
    scale = HEAD ** (-0.5)
    for start in range(0, length, block):
        first, stop = key_start(start), start + block
        rows, keys = slice(start, stop), slice(first, stop)
        scores = nt(query[rows, :], key[keys, :]) * scale + bias[rows, : stop - first]
        weights = jnp.exp(scores - lse[rows, :1])
        prob_grad = nt(out_grad[rows, :], value[keys, :])
        inner = jnp.sum(weights * prob_grad, axis=1, keepdims=True)
        score_grad = (weights * (prob_grad - inner)).astype(bf16)
        dq_out[rows, :] = nn(score_grad, key[keys, :]) * scale
        dk_sum[keys, :] += tn(score_grad, query[rows, :])
        dv_sum[keys, :] += tn(weights.astype(bf16), out_grad[rows, :])

    def unrotated(grad):
        return grad * cosine[...] + turned(grad * sine[...])

    dv_out[...] = dv_sum[...].astype(bf16)
    dq = unrotated(dq_out[...])
    dk = unrotated(dk_sum[...] * scale)
    dq_out[...] = dq
    dk_out[...] = dk
    dq = dq * qraw[...]
    dk = dk * kraw[...]
    qg_out[...] = jnp.sum(dq * q_scale[...], axis=0, keepdims=True)
    kg_out[...] = jnp.sum(dk * k_scale[...], axis=0, keepdims=True)
    qdot_out[...] += jnp.sum(dq * q_gain[...], axis=1, keepdims=True)
    kdot_out[...] += jnp.sum(dk * k_gain[...], axis=1, keepdims=True)


def attend_back(query, key, value, out_grad, lse, qraw, kraw, q_scale, k_scale, q_gain, k_gain, cosine, sine, seg, keep):
    length, width = qraw.shape
    block = min(256, length)
    span = min(DOC + block, length)
    head = pl.BlockSpec((length, HEAD), lambda h: (0, h))
    gain = pl.BlockSpec((1, HEAD), lambda h: (0, h))
    whole = lambda *shape: pl.BlockSpec(shape, lambda h: (0, 0))
    sds = jax.ShapeDtypeStruct
    return pl.pallas_call(
        functools.partial(attend_back_kernel, block),
        grid=(width // HEAD,),
        in_specs=[head] * 7
        + [whole(length, 1), whole(length, 1), gain, gain]
        + [whole(length, HEAD), whole(length, HEAD), whole(length, 1), whole(1, length), whole(1, length)],
        out_specs=[head, head, head, whole(length, 1), whole(length, 1), gain, gain],
        out_shape=[sds((length, width), f32), sds((length, width), f32), sds((length, width), bf16)]
        + [sds((length, 1), f32), sds((length, 1), f32), sds((1, width), f32), sds((1, width), f32)],
        scratch_shapes=[pltpu.VMEM((length, span), f32), pltpu.VMEM((length, HEAD), f32), pltpu.VMEM((length, HEAD), f32)],
        compiler_params=params(),
        cost_estimate=cost(0, 0),
        name="attend_back",
    )(query, key, value, out_grad, lse, qraw, kraw, q_scale, k_scale, q_gain[None], k_gain[None], cosine, sine, seg[:, None], seg[None], keep[None])


def middle_kernel(tokens, summed, gain, middle_out, scale_out, normed_out):
    middle = tokens[...].astype(f32) + summed[...].astype(f32)
    scale = lax.rsqrt(jnp.mean(middle * middle, axis=1, keepdims=True) + EPSILON)
    middle_out[...] = middle
    scale_out[...] = scale
    normed_out[...] = (middle * scale * gain[...]).astype(bf16)


def middle_rows(chunk, tokens, summed, gain):
    rows, features = summed.shape
    sds = jax.ShapeDtypeStruct
    whole = lambda *shape: pl.BlockSpec(shape, lambda i: (0, 0))
    return pl.pallas_call(
        middle_kernel,
        grid=(1,),
        in_specs=[pl.BlockSpec((rows, features), lambda i: (chunk, 0)), whole(rows, features), whole(1, features)],
        out_specs=[whole(rows, features), whole(rows, 1), whole(rows, features)],
        out_shape=[sds((rows, features), f32), sds((rows, 1), f32), sds((rows, features), bf16)],
        compiler_params=params(),
        cost_estimate=cost(0, 0),
        name="middle",
    )(tokens, summed, gain[None])


def middle_back_kernel(
    experts, grads, middle, scale, normed, routed, router, cotangent, gain, *refs
):
    grad_out, low_out, gain_out, logit_out = refs[-4:]
    features = middle.shape[1]
    lane = lax.broadcasted_iota(jnp.int32, routed.shape, 1)
    logits = jnp.where(lane < experts, nn(normed[...], router[...]), MASKED)
    powers = jnp.exp(logits - jnp.max(logits, axis=1, keepdims=True))
    probs = powers / jnp.sum(powers, axis=1, keepdims=True)
    share_grad = grads[:, features:].astype(f32) * routed[...]
    logit_grad = (probs * (share_grad - jnp.sum(share_grad * probs, axis=1, keepdims=True))).astype(bf16)
    logit_out[...] = logit_grad
    ffn_grad = grads[:, :features].astype(f32) + nt(logit_grad, router[...])
    along = middle[...] * scale[...]
    gain_out[...] = jnp.sum(ffn_grad * along, axis=0, keepdims=True)
    weighted = ffn_grad * gain[...]
    inner = jnp.mean(weighted * along, axis=1, keepdims=True)
    total = cotangent[...].astype(f32) + scale[...] * (weighted - along * inner)
    grad_out[...] = total
    low_out[...] = total.astype(bf16)


def middle_back(chunk, grads, middle, scale, normed, routed, router, cotangent, gain, experts, filled=()):
    rows, features = middle.shape
    sds = jax.ShapeDtypeStruct
    whole = lambda *shape: pl.BlockSpec(shape, lambda i: (0, 0))
    part = lambda columns: pl.BlockSpec((rows, columns), lambda i: (chunk, 0))
    return pl.pallas_call(
        functools.partial(middle_back_kernel, experts),
        grid=(1,),
        in_specs=[whole(rows, features + LANES), whole(rows, features), whole(rows, 1), whole(rows, features), part(LANES)]
        + [whole(features, LANES), part(features), whole(1, features)]
        + [pl.BlockSpec(memory_space=pl.ANY)] * len(filled),
        out_specs=[part(features), part(features), whole(1, features), whole(rows, LANES)],
        out_shape=[sds(cotangent.shape, f32), sds(cotangent.shape, bf16), sds((1, features), f32), sds((rows, LANES), bf16)],
        input_output_aliases={8 + at: at for at in range(len(filled))},
        compiler_params=params(),
        cost_estimate=cost(0, 0),
        name="middle_back",
    )(grads, middle, scale, normed, routed, router, cotangent, gain[None], *filled)


def up_back_kernel(grad, down_w, out):
    width = down_w.shape[2]
    for at in range(down_w.shape[0]):
        out[:, at * width : (at + 1) * width] = nn(grad[...], down_w[at]).astype(out.dtype)


def up_back(grad, down_w):
    rows, features = grad.shape
    experts, _, width = down_w.shape
    step = 2 if experts % 2 == 0 else 1
    return pl.pallas_call(
        up_back_kernel,
        grid=(experts // step,),
        in_specs=[pl.BlockSpec((rows, features), lambda e: (0, 0)), pl.BlockSpec((step, features, width), lambda e: (e, 0, 0))],
        out_specs=pl.BlockSpec((rows, step * width), lambda e: (0, e)),
        out_shape=jax.ShapeDtypeStruct((rows, experts * width), bf16),
        compiler_params=params(),
        cost_estimate=cost(2 * rows * features * experts * width, 2 * (rows + experts * width) * features),
        name="up_back",
    )(grad, down_w)


def expert_kernel(block, rows_in, back, routed, router, gate_w, up_w, act_out, dgate_out, dup_out, grad_out, comb, dcomb, total):
    at = pl.program_id(0)
    rows, features = rows_in.shape
    lane = lax.broadcasted_iota(jnp.int32, (block, LANES), 1)

    @pl.when(at == 0)
    def _():
        experts = pl.num_programs(0)
        for start in range(0, rows, block):
            here = slice(start, start + block)
            logits = jnp.where(lane < experts, nn(rows_in[here, :], router[...]), MASKED)
            powers = jnp.exp(logits - jnp.max(logits, axis=1, keepdims=True))
            probs = powers / jnp.sum(powers, axis=1, keepdims=True)
            comb[here, :] = probs * routed[here, :]
        total[...] = jnp.zeros_like(total)
        dcomb[...] = jnp.zeros_like(dcomb)

    gate, up = gate_w[0], up_w[0]
    mine = lane == at
    for start in range(0, rows, block):
        here = slice(start, start + block)
        taken = rows_in[here, :]
        pre_gate = nn(taken, gate)
        pre_up = nn(taken, up)
        behind = back[...].reshape(rows, back.shape[3])[here, :].astype(f32)
        share = jnp.sum(jnp.where(mine, comb[here, :], 0.0), axis=1, keepdims=True)
        sigmoid = 0.5 * jnp.tanh(0.5 * pre_gate) + 0.5
        active = pre_gate * sigmoid
        inner = active * pre_up
        share_grad = jnp.sum(inner * behind, axis=1, keepdims=True)
        dcomb[here, :] = jnp.where(mine, share_grad, dcomb[here, :])
        act_out[here, :] = (inner * share).astype(bf16)
        inner_grad = behind * share
        dgate = (inner_grad * pre_up * (sigmoid + active * (1.0 - sigmoid))).astype(bf16)
        dup = (inner_grad * active).astype(bf16)
        dgate_out[here, :] = dgate
        dup_out[here, :] = dup
        total[here, :] += nt(dgate, gate) + nt(dup, up)

    @pl.when(at == pl.num_programs(0) - 1)
    def _():
        grad_out[:, :features] = total[...].astype(bf16)
        grad_out[:, features:] = dcomb[...].astype(bf16)


def experts_block(chunk, rows_in, back, routed, router, gate_w, up_w):
    rows, features = rows_in.shape
    parts, _, chunk_rows, _ = back.shape
    experts, _, width = gate_w.shape
    block = min(512, rows)
    whole = lambda *shape: pl.BlockSpec(shape, lambda e: (0, 0))
    column = pl.BlockSpec((rows, width), lambda e: (0, e))
    weight = pl.BlockSpec((1, features, width), lambda e: (e, 0, 0))
    wide = jax.ShapeDtypeStruct((rows, experts * width), bf16)
    return pl.pallas_call(
        functools.partial(expert_kernel, block),
        grid=(experts,),
        in_specs=[whole(rows, features), pl.BlockSpec((parts, 1, chunk_rows, width), lambda e: (0, chunk, 0, e)), whole(rows, LANES), whole(features, LANES), weight, weight],
        out_specs=[column, column, column, whole(rows, features + LANES)],
        out_shape=[wide, wide, wide, jax.ShapeDtypeStruct((rows, features + LANES), bf16)],
        scratch_shapes=[pltpu.VMEM((rows, LANES), f32), pltpu.VMEM((rows, LANES), f32), pltpu.VMEM((rows, features), f32)],
        compiler_params=params(),
        cost_estimate=cost(8 * rows * features * experts * width, 4 * experts * width * (features + 2 * rows), rows * experts * width),
        name="experts",
    )(rows_in, back, routed, router, gate_w, up_w)


def block_order(blocks):
    return [3, 2, 0, 1] if blocks == 4 else list(range(blocks))


def split_tables(blocks, per):
    order = block_order(blocks)
    if blocks == 4:
        picks = [{0: 0, 1: 1}, {2: 0, 3: 1}, {0: 0, 2: 1}, {1: 0, 3: 1}]
    else:
        picks = [{block: block for block in order}] * 2
    places, fills = [], []
    for pick in picks:
        filled = [pick[block] * per + at if block in pick else None for block in order for at in range(per)]
        last = next(place for place in filled if place is not None)
        row = []
        for place in filled:
            last = last if place is None else place
            row.append(last)
        places.append(row)
        fills.append([int(place is not None) for place in filled])
    return jnp.asarray(np.array([places, fills], np.int32)), [len(pick) for pick in picks]


def wgrad_kernel(count, extra, per, block, order, tables, *refs):
    lefts, rights = refs[:count], refs[count : 2 * count]
    added = refs[2 * count : 2 * count + extra]
    outs = refs[2 * count + extra :]
    at = pl.program_id(0)
    features = lefts[0].shape[-1]

    def piece(start, stop):
        total = None
        for left, right in zip(lefts, rights):
            columns = left[:, start:stop] if len(left.shape) == 2 else left[:, :, :, start:stop].reshape(-1, stop - start)
            part = tn(columns, right[...])
            total = part if total is None else total + part
        return total

    if not added:
        for place, out in enumerate(outs):

            @pl.when(at // per == place)
            def _(out=out):
                for start in range(0, features, block):
                    out[0, start : start + block, :] = piece(start, start + block).astype(bf16)

        return
    half = features // 2
    got = outs[-1]
    outs = outs[:-1]
    for place, arrived in enumerate(added):

        @pl.when(at // per == place)
        def _(arrived=arrived):
            for start in range(0, features, block):
                total = piece(start, start + block) + arrived[0, start : start + block, :].astype(f32)
                got[start : start + block, :] = total.astype(bf16)

    for side, out in enumerate(outs):
        start = side * 2 // len(outs) * half

        @pl.when(tables[1, side, at] == 1)
        def _(out=out, start=start):
            out[0] = got[start : start + half, :]


def wgrad(lefts, rights, order, width, per, added=(), weight=1, pieces=0):
    features = lefts[0][0].shape[-1]
    experts = order.shape[0]
    groups = experts // per
    tables, sizes = split_tables(groups, per)
    pieces = len(added) or pieces or groups
    held = experts // pieces

    def piece_spec(place):
        return pl.BlockSpec((1, features, width), lambda i, ids, to: (jnp.clip(i - place * held, 0, held - 1), 0, 0))

    def half_spec(side):
        return pl.BlockSpec((1, features // 2, width), lambda i, ids, to: (to[0, side, i], 0, 0))

    def left_spec(left, chunk):
        if left.ndim == 2:
            return pl.BlockSpec(left.shape, lambda i, ids, to: (0, 0))
        return pl.BlockSpec((left.shape[0], 1) + left.shape[2:], lambda i, ids, to: (0, chunk, 0, 0))

    piece_specs = [piece_spec(place) for place in range(pieces)]
    if added:
        out_specs = [half_spec(side) for side in range(len(sizes))]
        out_shape = [jax.ShapeDtypeStruct((size * per, features // 2, width), bf16) for size in sizes]
    else:
        out_specs = piece_specs
        out_shape = [jax.ShapeDtypeStruct((held, features, width), bf16)] * pieces
    return pl.pallas_call(
        functools.partial(wgrad_kernel, len(lefts), len(added), held, min(512, features // 2)),
        grid_spec=pltpu.PrefetchScalarGridSpec(
            num_scalar_prefetch=2,
            grid=(experts,),
            in_specs=[left_spec(*left) for left in lefts]
            + [pl.BlockSpec((right.shape[0], width), lambda i, ids, to: (0, ids[i])) for right in rights]
            + (piece_specs if added else []),
            out_specs=out_specs,
            scratch_shapes=[pltpu.VMEM((features, width), bf16)] if added else [],
        ),
        out_shape=out_shape,
        compiler_params=params(),
        cost_estimate=cost(2 * weight * sum(right.shape[0] for right in rights) * features * experts * width, 0),
        name="wgrad",
    )(order, tables, *(left for left, _ in lefts), *rights, *added)


def down_kernel(parts, down_w, *refs):
    acts, out = refs[:-1], refs[-1]
    joined = jnp.concatenate([down_w[e] for e in range(down_w.shape[0])], axis=1)
    block = acts[0].shape[0] // parts
    for at, act in enumerate(acts):
        result = nt(act[...], joined).astype(out.dtype)
        for part in range(parts):
            start = (part * len(acts) + at) * block
            out[start : start + block, :] = result[part * block : (part + 1) * block, :]


def down(acts, down_w, parts):
    rows = sum(act.shape[0] for act in acts)
    experts, features, width = down_w.shape
    block = min(256, features)
    return pl.pallas_call(
        functools.partial(down_kernel, parts),
        grid=(features // block,),
        in_specs=[pl.BlockSpec((experts, block, width), lambda n: (0, n, 0))]
        + [pl.BlockSpec(act.shape, lambda n: (0, 0)) for act in acts],
        out_specs=pl.BlockSpec((rows, block), lambda n: (0, n)),
        out_shape=jax.ShapeDtypeStruct((rows, features), bf16),
        compiler_params=params(),
        cost_estimate=cost(0 * 2 * rows * features * experts * width, 0),
        name="down",
    )(down_w, *acts)


def gate(value, *others):
    return lax.optimization_barrier((value, others))[0]


def gather_rows(values):
    return lax.all_gather(values, "tensor", axis=0, tiled=True)


def scatter_rows(values):
    return lax.psum_scatter(values, "tensor", scatter_dimension=0, tiled=True)


def pair_swap(values, step):
    size = lax.axis_size("dp")
    return lax.ppermute(values, "dp", [(i, i ^ step) for i in range(size)])


class Halving:
    def __init__(self, values):
        if len(values) == 2:
            self.kept = list(values)
            self.going = None
        else:
            self.kept, self.going = list(values[::2]), list(values[1::2])
        bits = list(range(values[0].shape[0].bit_length() - (1 if self.going is None else 0)))
        self.left = [bits[::-1], bits]
        self.got = None

    def send(self):
        if not self.left[0]:
            return ()
        self.got = []
        sent = []
        for side, downward in ((0, True), (1, False)):
            bit = self.left[side].pop(0)
            if self.going is not None:
                go = self.going[side]
            else:
                kept = self.kept[side]
                half = kept.shape[0] // 2
                if downward:
                    self.kept[side], go = kept[:half], kept[half:]
                else:
                    view = kept.reshape((half, 2) + kept.shape[1:])
                    self.kept[side], go = view[:, 0], view[:, 1]
            sent.append(go)
            self.got.append(pair_swap(go, 2 << bit))
        self.going = None
        return tuple(sent)

    def add(self, *others):
        if self.got is not None:
            if others:
                self.got = gate(tuple(self.got), *others)
            last = not self.left[0]
            for side in range(2):
                total = self.kept[side].astype(f32) + self.got[side].astype(f32)
                self.kept[side] = total if last else total.astype(bf16)
            self.got = None
        return tuple(self.kept)

    def done(self):
        self.add()
        while self.left[0]:
            self.send()
            self.add()
        return jnp.concatenate([kept[0].astype(f32) for kept in self.kept], axis=1)


def exchange_sum(values, steps):
    for axis, step in steps:
        values = values + lax.ppermute(values, axis, [(i, i ^ step) for i in range(lax.axis_size(axis))])
    return values


def doublings(axis):
    return [(axis, 1 << bit) for bit in range(lax.axis_size(axis).bit_length() - 1)]


def local(
    tokens, cotangent, seg_ids, keep_mask, routes, attn_gain, w_query, w_key, w_value, w_out,
    q_gain, k_gain, ffn_gain, router, w_gate, w_up, w_down,
):
    parts = lax.axis_size("tensor")
    part_at = lax.axis_index("tensor")
    dp_size = lax.axis_size("dp")
    low_bit = lax.axis_index("dp") % 2
    shard_rows, features = tokens.shape
    group_rows = shard_rows * parts
    _, length = seg_ids.shape
    local_width = w_query.shape[1]
    experts, _, width = w_gate.shape
    per = experts // dp_size
    chunk_rows = shard_rows // CHUNKS
    chunks = range(CHUNKS)
    own = [slice(c * chunk_rows, (c + 1) * chunk_rows) for c in chunks]

    def chunk_of(values, c):
        columns = values.shape[1]
        return values.reshape(parts, CHUNKS, chunk_rows, columns)[:, c].reshape(parts * chunk_rows, columns)

    inputs = tokens.astype(f32)
    first_scale = rms_scale(inputs)
    normed_all = gather_rows((inputs * first_scale * attn_gain).astype(bf16))
    grad_rows = gather_rows(gate(cotangent, normed_all))

    cosine, sine = rope_tables(length, HEAD)

    relative = jnp.asarray(block_order(dp_size // 2), jnp.int32) ^ (lax.axis_index("dp") // 2)
    own_blocks, other_blocks = 2 * relative + low_bit, 2 * relative + 1 - low_bit
    mine, theirs = (
        (blocks[:, None] * per + jnp.arange(per, dtype=jnp.int32)).reshape(-1) for blocks in (own_blocks, other_blocks)
    )

    qraw, kraw, value, squares = project(normed_all, w_query, w_key, w_value)
    squares = exchange_sum(squares, doublings("tensor"))
    q_scale, k_scale = (lax.rsqrt(squares[i] / features + EPSILON)[:, None] for i in range(2))
    query, key, attended, lse = attend(
        qraw, kraw, value, q_scale, k_scale, q_gain, k_gain, cosine, sine, seg_ids[0], keep_mask[0]
    )
    attended_parts = [chunk_of(gate(attended, grad_rows), c) for c in chunks]
    outs = [nt(attended_parts[0], w_out).astype(bf16)]
    summed = [scatter_rows(outs[0])]
    outs.append(nt(gate(attended_parts[1], outs[0]), w_out).astype(bf16))
    summed.append(scatter_rows(outs[1]))

    idle_routes, idle_router = gate((routes, router), outs[1])
    expert_ids = jnp.arange(LANES)
    routed = jnp.sum((idle_routes[:, :, None] == expert_ids[None, None, :]).astype(f32), axis=1)
    router_wide = jnp.pad(idle_router, ((0, 0), (0, LANES - experts)))
    routed_own = lax.dynamic_slice_in_dim(routed, part_at * shard_rows, shard_rows, 0)
    back = up_back(gate(grad_rows, routed, router_wide), w_down).reshape(parts, CHUNKS, chunk_rows, -1)
    grad_rows = grad_rows.reshape(parts, CHUNKS, chunk_rows, features)
    grad_parts = [(grad_rows, c) for c in chunks]

    norms = [middle_rows(0, tokens, summed[0], ffn_gain)]
    ffn_all = [gather_rows(norms[0][2])]
    norms.append(middle_rows(1, tokens, gate(summed[1], norms[0][2], back), ffn_gain))
    ffn_all.append(gather_rows(norms[1][2]))
    ffn_parts = [(rows, 0) for rows in ffn_all]
    acts, dgates, dups, expert_grads = [], [], [], []
    for c in chunks:
        here = gate(chunk_of(routed, c), back, *acts[-1:])
        act, dgate, dup, grads = experts_block(c, ffn_all[c], back, here, router_wide, w_gate, w_up)
        acts.append(act)
        dgates.append(dgate)
        dups.append(dup)
        expert_grads.append(grads)
    expert_grads = [scatter_rows(grads) for grads in expert_grads]

    def back_of(c, grads, filled=()):
        return middle_back(c, grads, *norms[c], routed_own, router_wide, cotangent, ffn_gain, experts, filled)

    def expert_sums(lefts, rights, ids, *others, added=(), weight=1, pieces=0):
        return wgrad(lefts, rights, gate(ids, *others), width, per, added, weight, pieces)

    def core_swap(pieces):
        return [pair_swap(piece, 1) for piece in pieces]

    def halving(sums):
        return Halving([part.reshape((part.shape[0] // per, per) + part.shape[1:]) for part in sums])

    first = back_of(0, gate(expert_grads[0], acts[1]))
    gate_sent = expert_sums(ffn_parts, dgates, theirs, first[1], weight=0)
    gate_got = core_swap(gate_sent)
    up_sent = expert_sums(ffn_parts, dups, theirs, *gate_sent, weight=4)
    up_got = core_swap(up_sent)
    gate_sums = expert_sums(ffn_parts, dgates, mine, *up_sent, added=gate_got, weight=4)
    gate_out = halving(gate_sums)
    gate_out.send()
    second = back_of(1, gate(expert_grads[1], *gate_sums), first[:2])
    middle_grad, middle_low = second[:2]
    middle_all = gather_rows(middle_low)
    up_sums = expert_sums(ffn_parts, dups, mine, middle_low, added=up_got, weight=0)
    up_out = halving(up_sums)
    up_out.send()
    moe = down([gate(acts[0], *up_sums), acts[1]], w_down, parts)
    moe_sum = scatter_rows(moe)
    gate_late = gate_out.add(moe)
    gate_out.send()
    down_sent = expert_sums(grad_parts, acts, theirs, *gate_late, pieces=4, weight=0.0)
    down_got = core_swap(down_sent)
    attended_grad = nn(gate(middle_all, *down_sent), w_out).astype(bf16)
    dqn, dkn, dvalue, qdot, kdot, q_gain_part, k_gain_part = attend_back(
        query, key, value, attended_grad, lse, qraw, kraw, q_scale, k_scale, q_gain, k_gain, cosine, sine,
        seg_ids[0], keep_mask[0],
    )
    dots = exchange_sum(jnp.stack([qdot[:, 0], kdot[:, 0]]), doublings("tensor")) / features
    up_late = up_out.add(dqn)
    up_out.send()
    normed_part, dqraw, dkraw, attn_gain_part = project_back(
        normed_all, dqn, dkn, dvalue, qraw, kraw, q_scale, k_scale, dots[0][:, None], dots[1][:, None],
        gate(q_gain, *up_late, *gate_out.got), k_gain, w_query, w_key, w_value,
    )
    normed_grad = scatter_rows(normed_part)
    down_sums = expert_sums(grad_parts, acts, mine, normed_part, added=down_got, weight=0.0)
    down_out = halving(down_sums)
    down_out.send()
    def attention_sums(ids, *others, added=()):
        return attention_wgrad(
            normed_all, middle_all, (dqraw, dkraw, dvalue), attended, gate(ids, *others), dp_size, added
        )

    attn_sent = attention_sums(other_blocks, *down_sums)
    attn_got = core_swap(attn_sent)

    def placed(part):
        return lax.dynamic_update_slice_in_dim(jnp.zeros((features,), f32), part, part_at * local_width, 0)

    attn_sums = attention_sums(own_blocks, *attn_sent, *up_out.got, added=attn_got)
    attn_out = Halving(attn_sums)
    normed_grad = gate(normed_grad, *attn_out.send())
    down_out.add(*attn_sums)
    down_out.send()
    smalls = [attn_gain_part[0] / attn_gain, placed(q_gain_part[0]), placed(k_gain_part[0]), (first[2] + second[2])[0]]
    router_part = sum(tn(late[3], norms[c][2]) for c, late in enumerate((first, second)))[:experts]
    smalls = gate(jnp.concatenate([jnp.stack(smalls), router_part]), *attn_sums)
    smalls = exchange_sum(smalls, doublings("dp")[:1] + doublings("tensor"))
    attn_late = attn_out.add()
    attn_out.send()
    smalls = exchange_sum(gate(smalls, *attn_late), doublings("dp")[1:])
    late_got = tuple(down_out.got)
    gate_done = gate_out.done()
    up_done = up_out.done()
    down_done = down_out.done()
    query_done, key_done, value_done, out_done = attn_out.done()
    layer_out = (jnp.concatenate([norms[c][0] for c in chunks]) + gate(moe_sum, *late_got).astype(f32)).astype(bf16)
    tokens_grad = middle_grad + norm_back(normed_grad.astype(f32), inputs, first_scale, attn_gain)
    return (
        layer_out, tokens_grad, query_done, key_done, value_done, out_done,
        smalls[0], smalls[1], smalls[2], smalls[3], smalls[4:].T, gate_done, up_done, down_done,
    )


def solution(mesh):
    rows = P(("dp", "tensor"), None)
    column = P(None, "tensor")
    expert = P(None, None, "tensor")
    in_specs = (
        rows, rows, P("dp", None), P("dp", None), P("dp", None), P(), column, column, column, column,
        P("tensor"), P("tensor"), P(), P(), expert, expert, expert,
    )
    block = P("dp", "tensor")
    expert_out = P("dp", None, "tensor")
    out_specs = (
        rows, rows, block, block, block, block, P(), P(), P(), P(), P(), expert_out, expert_out, expert_out,
    )
    return jax.shard_map(local, mesh=mesh, in_specs=in_specs, out_specs=out_specs, check_vma=False)
```

```python
import functools

import jax
import jax.numpy as jnp
import numpy as np
from jax import lax
from jax.experimental import pallas as pl
from jax.experimental.pallas import tpu as pltpu
from jax.sharding import PartitionSpec as P

D = 2048
HEAD = 128
DOC = 512
LANES = 128
EPSILON = 1e-05
MASKED = -1e30
CHUNKS = 2
VMEM = 56 * 1024 * 1024
bf16 = jnp.bfloat16
f32 = jnp.float32


def nn(left, right):
    return lax.dot_general(left, right, (((1,), (0,)), ((), ())), preferred_element_type=f32)


def nt(left, right):
    return lax.dot_general(left, right, (((1,), (1,)), ((), ())), preferred_element_type=f32)


def tn(left, right):
    return lax.dot_general(left, right, (((0,), (0,)), ((), ())), preferred_element_type=f32)


def params():
    return pltpu.CompilerParams(vmem_limit_bytes=VMEM)


PACE = 0.3


def cost(flops, moved, special=0):
    return pl.CostEstimate(flops=int(1.5 * PACE * flops + 6e4 * PACE * special), bytes_accessed=moved // 8, transcendentals=0)


def rms_scale(values):
    return lax.rsqrt(jnp.mean(values * values, axis=-1, keepdims=True) + EPSILON)


def norm_back(grad_values, values, scale_col, gain_vec):
    weighted = grad_values * gain_vec
    inner_mean = jnp.mean(weighted * values, axis=-1, keepdims=True)
    return scale_col * weighted - values * (scale_col * scale_col * scale_col) * inner_mean


def rope_tables(length, width):
    angles = np.arange(length)[:, None] * 10000.0 ** (-np.arange(width // 2) * 2.0 / width)[None, :]
    cosine, sine = np.cos(angles).astype(np.float32), np.sin(angles).astype(np.float32)
    return jnp.asarray(np.concatenate([cosine, cosine], axis=1)), jnp.asarray(np.concatenate([-sine, sine], axis=1))


def key_start(query_start):
    return max(0, query_start - DOC)


def fill_bias(bias, seg_col, seg_row, keep_row, block):
    length = seg_col.shape[0]
    for start in range(0, length, block):
        first, stop = key_start(start), start + block
        query_pos = start + lax.broadcasted_iota(jnp.int32, (block, stop - first), 0)
        key_pos = first + lax.broadcasted_iota(jnp.int32, (block, stop - first), 1)
        same = seg_col[start:stop, :] == seg_row[:, first:stop]
        live = (keep_row[:, first:stop] == 1) | (key_pos == query_pos)
        allowed = same & live & (key_pos <= query_pos)
        bias[start:stop, : stop - first] = jnp.where(allowed, 0.0, MASKED)


def turned(values):
    return pltpu.roll(values, values.shape[1] // 2, 1)


def project_kernel(rows_in, w_query, w_key, w_value, q_out, k_out, v_out, squares_out):
    ones = jnp.ones((8, q_out.shape[1]), f32)
    for at, (weight, out) in enumerate(((w_query, q_out), (w_key, k_out))):
        raw = nn(rows_in[...], weight[...])
        out[...] = raw
        sums = lax.dot_general(
            ones, raw * raw, (((1,), (1,)), ((), ())), precision=lax.Precision.HIGHEST, preferred_element_type=f32
        )
        squares_out[at : at + 1, :] = sums[:1]
    v_out[...] = nn(rows_in[...], w_value[...]).astype(bf16)


def project(rows_in, w_query, w_key, w_value):
    rows, features = rows_in.shape
    width = w_query.shape[1]
    block = min(256, rows)
    row = lambda columns: pl.BlockSpec((block, columns), lambda r: (r, 0))
    weight = pl.BlockSpec((features, width), lambda r: (0, 0))
    sds = jax.ShapeDtypeStruct
    return pl.pallas_call(
        project_kernel,
        grid=(rows // block,),
        in_specs=[row(features), weight, weight, weight],
        out_specs=[row(width), row(width), row(width), pl.BlockSpec((2, block), lambda r: (0, r))],
        out_shape=[sds((rows, width), f32), sds((rows, width), f32), sds((rows, width), bf16), sds((2, rows), f32)],
        compiler_params=params(),
        cost_estimate=cost(6 * rows * features * width, 2 * (rows + 3 * width) * features),
        name="project",
    )(rows_in, w_query, w_key, w_value)


def project_back_kernel(
    rows_in, dqn, dkn, dvalue, qraw, kraw, q_scale, k_scale, q_dot, k_dot, q_gain, k_gain,
    w_query, w_key, w_value, part_out, dq_out, dk_out, gain_out,
):
    @pl.when(pl.program_id(0) == 0)
    def _():
        gain_out[...] = jnp.zeros_like(gain_out)

    def raw_grad(grad, raw, scale, gain, dot):
        cube = scale[...] * scale[...] * scale[...]
        return (scale[...] * (gain[...] * grad[...]) - raw[...] * (cube * dot[...])).astype(bf16)

    dq = raw_grad(dqn, qraw, q_scale, q_gain, q_dot)
    dk = raw_grad(dkn, kraw, k_scale, k_gain, k_dot)
    dq_out[...] = dq
    dk_out[...] = dk
    part = nt(dq, w_query[...]) + nt(dk, w_key[...]) + nt(dvalue[...], w_value[...])
    part_out[...] = part.astype(bf16)
    gain_out[...] += jnp.sum(part * rows_in[...].astype(f32), axis=0, keepdims=True)


def project_back(rows_in, dqn, dkn, dvalue, qraw, kraw, q_scale, k_scale, q_dot, k_dot, q_gain, k_gain, w_query, w_key, w_value):
    rows, features = rows_in.shape
    width = w_query.shape[1]
    block = min(256, rows)
    row = lambda columns: pl.BlockSpec((block, columns), lambda r: (r, 0))
    whole = lambda *shape: pl.BlockSpec(shape, lambda r: (0, 0))
    sds = jax.ShapeDtypeStruct
    return pl.pallas_call(
        project_back_kernel,
        grid=(rows // block,),
        in_specs=[row(features)] + [row(width)] * 5 + [row(1)] * 4 + [whole(1, width)] * 2 + [whole(features, width)] * 3,
        out_specs=[row(features), row(width), row(width), whole(1, features)],
        out_shape=[sds((rows, features), bf16), sds((rows, width), bf16), sds((rows, width), bf16), sds((1, features), f32)],
        compiler_params=params(),
        cost_estimate=cost(int(20.0 * 6 * rows * features * width), 0),
        name="project_back",
    )(rows_in, dqn, dkn, dvalue, qraw, kraw, q_scale, k_scale, q_dot, k_dot, q_gain[None], k_gain[None], w_query, w_key, w_value)


def attention_wgrad_kernel(added, held, order, tables, rows_in, middle, *refs):
    sides, (attended,), refs = refs[:3], refs[3:4], refs[4:]
    got, outs = (refs[:added], refs[added:])
    at = pl.program_id(0)
    totals = [tn(rows_in[...], side[...]) for side in sides] + [tn(middle[...], attended[...])]
    if not added:
        for place, out in enumerate(outs):

            @pl.when(at // held == place)
            def _(out=out):
                for weight, total in enumerate(totals):
                    out[0, weight] = total.astype(bf16)

        return
    scratch, outs = outs[-1], outs[:-1]
    half = outs[0].shape[2]
    for place, piece in enumerate(got):

        @pl.when(at // held == place)
        def _(piece=piece):
            for weight, total in enumerate(totals):
                scratch[weight] = (total + piece[0, weight].astype(f32)).astype(bf16)

    for side, out in enumerate(outs):
        start = side * 2 // len(outs) * half

        @pl.when(tables[1, side, at] == 1)
        def _(out=out, start=start):
            out[0] = scratch[:, start : start + half, :]


def attention_wgrad(rows_in, middle, sides, attended, order, blocks, added=()):
    features = rows_in.shape[1]
    width = sides[0].shape[1]
    block = features // blocks
    count = order.shape[0]
    tables, sizes = split_tables(count, 1)
    left = lambda values: pl.BlockSpec((values.shape[0], block), lambda i, ids, to: (0, ids[i]))
    right = lambda values: pl.BlockSpec(values.shape, lambda i, ids, to: (0, 0))

    def half_spec(side):
        return pl.BlockSpec((1, 4, block // 2, width), lambda i, ids, to: (to[0, side, i], 0, 0, 0))

    pieces = min(2, count)
    held = count // pieces

    def piece_spec(place):
        return pl.BlockSpec((1, 4, block, width), lambda i, ids, to: (jnp.clip(i - place * held, 0, held - 1), 0, 0, 0))

    group_specs = [piece_spec(place) for place in range(pieces)]
    if added:
        out_specs = [half_spec(side) for side in range(len(sizes))]
        out_shape = [jax.ShapeDtypeStruct((size, 4, block // 2, width), bf16) for size in sizes]
    else:
        out_specs = group_specs
        out_shape = [jax.ShapeDtypeStruct((held, 4, block, width), bf16)] * pieces
    return pl.pallas_call(
        functools.partial(attention_wgrad_kernel, len(added), held),
        grid_spec=pltpu.PrefetchScalarGridSpec(
            num_scalar_prefetch=2,
            grid=(count,),
            in_specs=[left(rows_in), left(middle)] + [right(v) for v in sides] + [right(attended)] + (group_specs if added else []),
            out_specs=out_specs,
            scratch_shapes=[pltpu.VMEM((4, block, width), bf16)] if added else [],
        ),
        out_shape=out_shape,
        compiler_params=params(),
        cost_estimate=cost(0, 0),
        name="attention_wgrad",
    )(order, tables, rows_in, middle, *sides, attended, *added)


def attend_kernel(
    block, qraw, kraw, value, q_scale, k_scale, q_gain, k_gain, cosine, sine,
    seg_col, seg_row, keep_row, q_out, k_out, o_out, lse_out, bias,
):
    @pl.when(pl.program_id(0) == 0)
    def _():
        fill_bias(bias, seg_col, seg_row, keep_row, block)

    def rotated(raw, scale, gain):
        normed = raw[...] * scale[...] * gain[...]
        return (normed * cosine[...] + turned(normed) * sine[...]).astype(bf16)

    q_out[...] = rotated(qraw, q_scale, q_gain)
    k_out[...] = rotated(kraw, k_scale, k_gain)
    length = seg_col.shape[0]
    for start in range(0, length, block):
        first, stop = key_start(start), start + block
        scores = nt(q_out[start:stop, :], k_out[first:stop, :]) * HEAD ** (-0.5)
        scores = scores + bias[start:stop, : stop - first]
        top = jnp.max(scores, axis=1, keepdims=True)
        powers = jnp.exp(scores - top)
        total = jnp.sum(powers, axis=1, keepdims=True)
        weights = (powers * (1.0 / total)).astype(bf16)
        o_out[start:stop, :] = nn(weights, value[first:stop, :]).astype(bf16)
        lse_out[start:stop, :] = jnp.broadcast_to(top + jnp.log(total), (block, HEAD))


def attend(qraw, kraw, value, q_scale, k_scale, q_gain, k_gain, cosine, sine, seg, keep):
    length, width = qraw.shape
    block = min(256, length)
    span = min(DOC + block, length)
    head = pl.BlockSpec((length, HEAD), lambda h: (0, h))
    gain = pl.BlockSpec((1, HEAD), lambda h: (0, h))
    whole = lambda *shape: pl.BlockSpec(shape, lambda h: (0, 0))
    return pl.pallas_call(
        functools.partial(attend_kernel, block),
        grid=(width // HEAD,),
        in_specs=[head, head, head, whole(length, 1), whole(length, 1), gain, gain]
        + [whole(length, HEAD), whole(length, HEAD), whole(length, 1), whole(1, length), whole(1, length)],
        out_specs=[head, head, head, head],
        out_shape=[jax.ShapeDtypeStruct((length, width), t) for t in (bf16, bf16, bf16, f32)],
        scratch_shapes=[pltpu.VMEM((length, span), f32)],
        compiler_params=params(),
        cost_estimate=cost(4 * length * span * width, 18 * length * width, length * span * width // HEAD),
        name="attend",
    )(qraw, kraw, value, q_scale, k_scale, q_gain[None], k_gain[None], cosine, sine, seg[:, None], seg[None], keep[None])


def attend_back_kernel(
    block, query, key, value, out_grad, lse, qraw, kraw, q_scale, k_scale, q_gain, k_gain, cosine, sine,
    seg_col, seg_row, keep_row, dq_out, dk_out, dv_out, qdot_out, kdot_out, qg_out, kg_out, bias, dk_sum, dv_sum,
):
    at = pl.program_id(0)

    @pl.when(at == 0)
    def _():
        fill_bias(bias, seg_col, seg_row, keep_row, block)
        qdot_out[...] = jnp.zeros_like(qdot_out)
        kdot_out[...] = jnp.zeros_like(kdot_out)

    dk_sum[...] = jnp.zeros_like(dk_sum)
    dv_sum[...] = jnp.zeros_like(dv_sum)
    length = seg_col.shape[0]
    scale = HEAD ** (-0.5)
    for start in range(0, length, block):
        first, stop = key_start(start), start + block
        rows, keys = slice(start, stop), slice(first, stop)
        scores = nt(query[rows, :], key[keys, :]) * scale + bias[rows, : stop - first]
        weights = jnp.exp(scores - lse[rows, :1])
        prob_grad = nt(out_grad[rows, :], value[keys, :])
        inner = jnp.sum(weights * prob_grad, axis=1, keepdims=True)
        score_grad = (weights * (prob_grad - inner)).astype(bf16)
        dq_out[rows, :] = nn(score_grad, key[keys, :]) * scale
        dk_sum[keys, :] += tn(score_grad, query[rows, :])
        dv_sum[keys, :] += tn(weights.astype(bf16), out_grad[rows, :])

    def unrotated(grad):
        return grad * cosine[...] + turned(grad * sine[...])

    dv_out[...] = dv_sum[...].astype(bf16)
    dq = unrotated(dq_out[...])
    dk = unrotated(dk_sum[...] * scale)
    dq_out[...] = dq
    dk_out[...] = dk
    dq = dq * qraw[...]
    dk = dk * kraw[...]
    qg_out[...] = jnp.sum(dq * q_scale[...], axis=0, keepdims=True)
    kg_out[...] = jnp.sum(dk * k_scale[...], axis=0, keepdims=True)
    qdot_out[...] += jnp.sum(dq * q_gain[...], axis=1, keepdims=True)
    kdot_out[...] += jnp.sum(dk * k_gain[...], axis=1, keepdims=True)


def attend_back(query, key, value, out_grad, lse, qraw, kraw, q_scale, k_scale, q_gain, k_gain, cosine, sine, seg, keep):
    length, width = qraw.shape
    block = min(256, length)
    span = min(DOC + block, length)
    head = pl.BlockSpec((length, HEAD), lambda h: (0, h))
    gain = pl.BlockSpec((1, HEAD), lambda h: (0, h))
    whole = lambda *shape: pl.BlockSpec(shape, lambda h: (0, 0))
    sds = jax.ShapeDtypeStruct
    return pl.pallas_call(
        functools.partial(attend_back_kernel, block),
        grid=(width // HEAD,),
        in_specs=[head] * 7
        + [whole(length, 1), whole(length, 1), gain, gain]
        + [whole(length, HEAD), whole(length, HEAD), whole(length, 1), whole(1, length), whole(1, length)],
        out_specs=[head, head, head, whole(length, 1), whole(length, 1), gain, gain],
        out_shape=[sds((length, width), f32), sds((length, width), f32), sds((length, width), bf16)]
        + [sds((length, 1), f32), sds((length, 1), f32), sds((1, width), f32), sds((1, width), f32)],
        scratch_shapes=[pltpu.VMEM((length, span), f32), pltpu.VMEM((length, HEAD), f32), pltpu.VMEM((length, HEAD), f32)],
        compiler_params=params(),
        cost_estimate=cost(0, 0),
        name="attend_back",
    )(query, key, value, out_grad, lse, qraw, kraw, q_scale, k_scale, q_gain[None], k_gain[None], cosine, sine, seg[:, None], seg[None], keep[None])


def middle_kernel(tokens, summed, gain, middle_out, scale_out, normed_out):
    middle = tokens[...].astype(f32) + summed[...].astype(f32)
    scale = lax.rsqrt(jnp.mean(middle * middle, axis=1, keepdims=True) + EPSILON)
    middle_out[...] = middle
    scale_out[...] = scale
    normed_out[...] = (middle * scale * gain[...]).astype(bf16)


def middle_rows(chunk, tokens, summed, gain):
    rows, features = summed.shape
    sds = jax.ShapeDtypeStruct
    whole = lambda *shape: pl.BlockSpec(shape, lambda i: (0, 0))
    return pl.pallas_call(
        middle_kernel,
        grid=(1,),
        in_specs=[pl.BlockSpec((rows, features), lambda i: (chunk, 0)), whole(rows, features), whole(1, features)],
        out_specs=[whole(rows, features), whole(rows, 1), whole(rows, features)],
        out_shape=[sds((rows, features), f32), sds((rows, 1), f32), sds((rows, features), bf16)],
        compiler_params=params(),
        cost_estimate=cost(0, 0),
        name="middle",
    )(tokens, summed, gain[None])


def middle_back_kernel(
    experts, grads, middle, scale, normed, routed, router, cotangent, gain, *refs
):
    grad_out, low_out, gain_out, logit_out = refs[-4:]
    features = middle.shape[1]
    lane = lax.broadcasted_iota(jnp.int32, routed.shape, 1)
    logits = jnp.where(lane < experts, nn(normed[...], router[...]), MASKED)
    powers = jnp.exp(logits - jnp.max(logits, axis=1, keepdims=True))
    probs = powers / jnp.sum(powers, axis=1, keepdims=True)
    share_grad = grads[:, features:].astype(f32) * routed[...]
    logit_grad = (probs * (share_grad - jnp.sum(share_grad * probs, axis=1, keepdims=True))).astype(bf16)
    logit_out[...] = logit_grad
    ffn_grad = grads[:, :features].astype(f32) + nt(logit_grad, router[...])
    along = middle[...] * scale[...]
    gain_out[...] = jnp.sum(ffn_grad * along, axis=0, keepdims=True)
    weighted = ffn_grad * gain[...]
    inner = jnp.mean(weighted * along, axis=1, keepdims=True)
    total = cotangent[...].astype(f32) + scale[...] * (weighted - along * inner)
    grad_out[...] = total
    low_out[...] = total.astype(bf16)


def middle_back(chunk, grads, middle, scale, normed, routed, router, cotangent, gain, experts, filled=()):
    rows, features = middle.shape
    sds = jax.ShapeDtypeStruct
    whole = lambda *shape: pl.BlockSpec(shape, lambda i: (0, 0))
    part = lambda columns: pl.BlockSpec((rows, columns), lambda i: (chunk, 0))
    return pl.pallas_call(
        functools.partial(middle_back_kernel, experts),
        grid=(1,),
        in_specs=[whole(rows, features + LANES), whole(rows, features), whole(rows, 1), whole(rows, features), part(LANES)]
        + [whole(features, LANES), part(features), whole(1, features)]
        + [pl.BlockSpec(memory_space=pl.ANY)] * len(filled),
        out_specs=[part(features), part(features), whole(1, features), whole(rows, LANES)],
        out_shape=[sds(cotangent.shape, f32), sds(cotangent.shape, bf16), sds((1, features), f32), sds((rows, LANES), bf16)],
        input_output_aliases={8 + at: at for at in range(len(filled))},
        compiler_params=params(),
        cost_estimate=cost(0, 0),
        name="middle_back",
    )(grads, middle, scale, normed, routed, router, cotangent, gain[None], *filled)


def up_back_kernel(grad, down_w, out):
    width = down_w.shape[2]
    for at in range(down_w.shape[0]):
        out[:, at * width : (at + 1) * width] = nn(grad[...], down_w[at]).astype(out.dtype)


def up_back(grad, down_w):
    rows, features = grad.shape
    experts, _, width = down_w.shape
    step = 2 if experts % 2 == 0 else 1
    return pl.pallas_call(
        up_back_kernel,
        grid=(experts // step,),
        in_specs=[pl.BlockSpec((rows, features), lambda e: (0, 0)), pl.BlockSpec((step, features, width), lambda e: (e, 0, 0))],
        out_specs=pl.BlockSpec((rows, step * width), lambda e: (0, e)),
        out_shape=jax.ShapeDtypeStruct((rows, experts * width), bf16),
        compiler_params=params(),
        cost_estimate=cost(2 * rows * features * experts * width, 2 * (rows + experts * width) * features),
        name="up_back",
    )(grad, down_w)


def expert_kernel(block, rows_in, back, routed, router, gate_w, up_w, act_out, dgate_out, dup_out, grad_out, comb, dcomb, total):
    at = pl.program_id(0)
    rows, features = rows_in.shape
    lane = lax.broadcasted_iota(jnp.int32, (block, LANES), 1)

    @pl.when(at == 0)
    def _():
        experts = pl.num_programs(0)
        for start in range(0, rows, block):
            here = slice(start, start + block)
            logits = jnp.where(lane < experts, nn(rows_in[here, :], router[...]), MASKED)
            powers = jnp.exp(logits - jnp.max(logits, axis=1, keepdims=True))
            probs = powers / jnp.sum(powers, axis=1, keepdims=True)
            comb[here, :] = probs * routed[here, :]
        total[...] = jnp.zeros_like(total)
        dcomb[...] = jnp.zeros_like(dcomb)

    gate, up = gate_w[0], up_w[0]
    mine = lane == at
    for start in range(0, rows, block):
        here = slice(start, start + block)
        taken = rows_in[here, :]
        pre_gate = nn(taken, gate)
        pre_up = nn(taken, up)
        behind = back[...].reshape(rows, back.shape[3])[here, :].astype(f32)
        share = jnp.sum(jnp.where(mine, comb[here, :], 0.0), axis=1, keepdims=True)
        sigmoid = 0.5 * jnp.tanh(0.5 * pre_gate) + 0.5
        active = pre_gate * sigmoid
        inner = active * pre_up
        share_grad = jnp.sum(inner * behind, axis=1, keepdims=True)
        dcomb[here, :] = jnp.where(mine, share_grad, dcomb[here, :])
        act_out[here, :] = (inner * share).astype(bf16)
        inner_grad = behind * share
        dgate = (inner_grad * pre_up * (sigmoid + active * (1.0 - sigmoid))).astype(bf16)
        dup = (inner_grad * active).astype(bf16)
        dgate_out[here, :] = dgate
        dup_out[here, :] = dup
        total[here, :] += nt(dgate, gate) + nt(dup, up)

    @pl.when(at == pl.num_programs(0) - 1)
    def _():
        grad_out[:, :features] = total[...].astype(bf16)
        grad_out[:, features:] = dcomb[...].astype(bf16)


def experts_block(chunk, rows_in, back, routed, router, gate_w, up_w):
    rows, features = rows_in.shape
    parts, _, chunk_rows, _ = back.shape
    experts, _, width = gate_w.shape
    block = min(512, rows)
    whole = lambda *shape: pl.BlockSpec(shape, lambda e: (0, 0))
    column = pl.BlockSpec((rows, width), lambda e: (0, e))
    weight = pl.BlockSpec((1, features, width), lambda e: (e, 0, 0))
    wide = jax.ShapeDtypeStruct((rows, experts * width), bf16)
    return pl.pallas_call(
        functools.partial(expert_kernel, block),
        grid=(experts,),
        in_specs=[whole(rows, features), pl.BlockSpec((parts, 1, chunk_rows, width), lambda e: (0, chunk, 0, e)), whole(rows, LANES), whole(features, LANES), weight, weight],
        out_specs=[column, column, column, whole(rows, features + LANES)],
        out_shape=[wide, wide, wide, jax.ShapeDtypeStruct((rows, features + LANES), bf16)],
        scratch_shapes=[pltpu.VMEM((rows, LANES), f32), pltpu.VMEM((rows, LANES), f32), pltpu.VMEM((rows, features), f32)],
        compiler_params=params(),
        cost_estimate=cost(8 * rows * features * experts * width, 4 * experts * width * (features + 2 * rows), rows * experts * width),
        name="experts",
    )(rows_in, back, routed, router, gate_w, up_w)


def block_order(blocks):
    return [3, 2, 0, 1] if blocks == 4 else list(range(blocks))


def split_tables(blocks, per):
    order = block_order(blocks)
    if blocks == 4:
        picks = [{0: 0, 1: 1}, {2: 0, 3: 1}, {0: 0, 2: 1}, {1: 0, 3: 1}]
    else:
        picks = [{block: block for block in order}] * 2
    places, fills = [], []
    for pick in picks:
        filled = [pick[block] * per + at if block in pick else None for block in order for at in range(per)]
        last = next(place for place in filled if place is not None)
        row = []
        for place in filled:
            last = last if place is None else place
            row.append(last)
        places.append(row)
        fills.append([int(place is not None) for place in filled])
    return jnp.asarray(np.array([places, fills], np.int32)), [len(pick) for pick in picks]


def wgrad_kernel(count, extra, per, block, order, tables, *refs):
    lefts, rights = refs[:count], refs[count : 2 * count]
    added = refs[2 * count : 2 * count + extra]
    outs = refs[2 * count + extra :]
    at = pl.program_id(0)
    features = lefts[0].shape[-1]

    def piece(start, stop):
        total = None
        for left, right in zip(lefts, rights):
            columns = left[:, start:stop] if len(left.shape) == 2 else left[:, :, :, start:stop].reshape(-1, stop - start)
            part = tn(columns, right[...])
            total = part if total is None else total + part
        return total

    if not added:
        for place, out in enumerate(outs):

            @pl.when(at // per == place)
            def _(out=out):
                for start in range(0, features, block):
                    out[0, start : start + block, :] = piece(start, start + block).astype(bf16)

        return
    half = features // 2
    got = outs[-1]
    outs = outs[:-1]
    for place, arrived in enumerate(added):

        @pl.when(at // per == place)
        def _(arrived=arrived):
            for start in range(0, features, block):
                total = piece(start, start + block) + arrived[0, start : start + block, :].astype(f32)
                got[start : start + block, :] = total.astype(bf16)

    for side, out in enumerate(outs):
        start = side * 2 // len(outs) * half

        @pl.when(tables[1, side, at] == 1)
        def _(out=out, start=start):
            out[0] = got[start : start + half, :]


def wgrad(lefts, rights, order, width, per, added=(), weight=1, pieces=0):
    features = lefts[0][0].shape[-1]
    experts = order.shape[0]
    groups = experts // per
    tables, sizes = split_tables(groups, per)
    pieces = len(added) or pieces or groups
    held = experts // pieces

    def piece_spec(place):
        return pl.BlockSpec((1, features, width), lambda i, ids, to: (jnp.clip(i - place * held, 0, held - 1), 0, 0))

    def half_spec(side):
        return pl.BlockSpec((1, features // 2, width), lambda i, ids, to: (to[0, side, i], 0, 0))

    def left_spec(left, chunk):
        if left.ndim == 2:
            return pl.BlockSpec(left.shape, lambda i, ids, to: (0, 0))
        return pl.BlockSpec((left.shape[0], 1) + left.shape[2:], lambda i, ids, to: (0, chunk, 0, 0))

    piece_specs = [piece_spec(place) for place in range(pieces)]
    if added:
        out_specs = [half_spec(side) for side in range(len(sizes))]
        out_shape = [jax.ShapeDtypeStruct((size * per, features // 2, width), bf16) for size in sizes]
    else:
        out_specs = piece_specs
        out_shape = [jax.ShapeDtypeStruct((held, features, width), bf16)] * pieces
    return pl.pallas_call(
        functools.partial(wgrad_kernel, len(lefts), len(added), held, min(512, features // 2)),
        grid_spec=pltpu.PrefetchScalarGridSpec(
            num_scalar_prefetch=2,
            grid=(experts,),
            in_specs=[left_spec(*left) for left in lefts]
            + [pl.BlockSpec((right.shape[0], width), lambda i, ids, to: (0, ids[i])) for right in rights]
            + (piece_specs if added else []),
            out_specs=out_specs,
            scratch_shapes=[pltpu.VMEM((features, width), bf16)] if added else [],
        ),
        out_shape=out_shape,
        compiler_params=params(),
        cost_estimate=cost(2 * weight * sum(right.shape[0] for right in rights) * features * experts * width, 0),
        name="wgrad",
    )(order, tables, *(left for left, _ in lefts), *rights, *added)


def down_kernel(parts, down_w, *refs):
    acts, out = refs[:-1], refs[-1]
    joined = jnp.concatenate([down_w[e] for e in range(down_w.shape[0])], axis=1)
    block = acts[0].shape[0] // parts
    for at, act in enumerate(acts):
        result = nt(act[...], joined).astype(out.dtype)
        for part in range(parts):
            start = (part * len(acts) + at) * block
            out[start : start + block, :] = result[part * block : (part + 1) * block, :]


def down(acts, down_w, parts):
    rows = sum(act.shape[0] for act in acts)
    experts, features, width = down_w.shape
    block = min(256, features)
    return pl.pallas_call(
        functools.partial(down_kernel, parts),
        grid=(features // block,),
        in_specs=[pl.BlockSpec((experts, block, width), lambda n: (0, n, 0))]
        + [pl.BlockSpec(act.shape, lambda n: (0, 0)) for act in acts],
        out_specs=pl.BlockSpec((rows, block), lambda n: (0, n)),
        out_shape=jax.ShapeDtypeStruct((rows, features), bf16),
        compiler_params=params(),
        cost_estimate=cost(0 * 2 * rows * features * experts * width, 0),
        name="down",
    )(down_w, *acts)


def gate(value, *others):
    return lax.optimization_barrier((value, others))[0]


def gather_rows(values):
    return lax.all_gather(values, "tensor", axis=0, tiled=True)


def scatter_rows(values):
    return lax.psum_scatter(values, "tensor", scatter_dimension=0, tiled=True)


def pair_swap(values, step):
    size = lax.axis_size("dp")
    return lax.ppermute(values, "dp", [(i, i ^ step) for i in range(size)])


class Halving:
    def __init__(self, values):
        if len(values) == 2:
            self.kept = list(values)
            self.going = None
        else:
            self.kept, self.going = list(values[::2]), list(values[1::2])
        bits = list(range(values[0].shape[0].bit_length() - (1 if self.going is None else 0)))
        self.left = [bits[::-1], bits]
        self.got = None

    def send(self):
        if not self.left[0]:
            return ()
        self.got = []
        sent = []
        for side, downward in ((0, True), (1, False)):
            bit = self.left[side].pop(0)
            if self.going is not None:
                go = self.going[side]
            else:
                kept = self.kept[side]
                half = kept.shape[0] // 2
                if downward:
                    self.kept[side], go = kept[:half], kept[half:]
                else:
                    view = kept.reshape((half, 2) + kept.shape[1:])
                    self.kept[side], go = view[:, 0], view[:, 1]
            sent.append(go)
            self.got.append(pair_swap(go, 2 << bit))
        self.going = None
        return tuple(sent)

    def add(self, *others):
        if self.got is not None:
            if others:
                self.got = gate(tuple(self.got), *others)
            last = not self.left[0]
            for side in range(2):
                total = self.kept[side].astype(f32) + self.got[side].astype(f32)
                self.kept[side] = total if last else total.astype(bf16)
            self.got = None
        return tuple(self.kept)

    def done(self):
        self.add()
        while self.left[0]:
            self.send()
            self.add()
        return jnp.concatenate([kept[0].astype(f32) for kept in self.kept], axis=1)


def exchange_sum(values, steps):
    for axis, step in steps:
        values = values + lax.ppermute(values, axis, [(i, i ^ step) for i in range(lax.axis_size(axis))])
    return values


def doublings(axis):
    return [(axis, 1 << bit) for bit in range(lax.axis_size(axis).bit_length() - 1)]


def local(
    tokens, cotangent, seg_ids, keep_mask, routes, attn_gain, w_query, w_key, w_value, w_out,
    q_gain, k_gain, ffn_gain, router, w_gate, w_up, w_down,
):
    parts = lax.axis_size("tensor")
    part_at = lax.axis_index("tensor")
    dp_size = lax.axis_size("dp")
    low_bit = lax.axis_index("dp") % 2
    shard_rows, features = tokens.shape
    group_rows = shard_rows * parts
    _, length = seg_ids.shape
    local_width = w_query.shape[1]
    experts, _, width = w_gate.shape
    per = experts // dp_size
    chunk_rows = shard_rows // CHUNKS
    chunks = range(CHUNKS)
    own = [slice(c * chunk_rows, (c + 1) * chunk_rows) for c in chunks]

    def chunk_of(values, c):
        columns = values.shape[1]
        return values.reshape(parts, CHUNKS, chunk_rows, columns)[:, c].reshape(parts * chunk_rows, columns)

    inputs = tokens.astype(f32)
    first_scale = rms_scale(inputs)
    normed_all = gather_rows((inputs * first_scale * attn_gain).astype(bf16))
    grad_rows = gather_rows(gate(cotangent, normed_all))

    cosine, sine = rope_tables(length, HEAD)

    relative = jnp.asarray(block_order(dp_size // 2), jnp.int32) ^ (lax.axis_index("dp") // 2)
    own_blocks, other_blocks = 2 * relative + low_bit, 2 * relative + 1 - low_bit
    mine, theirs = (
        (blocks[:, None] * per + jnp.arange(per, dtype=jnp.int32)).reshape(-1) for blocks in (own_blocks, other_blocks)
    )

    qraw, kraw, value, squares = project(normed_all, w_query, w_key, w_value)
    squares = exchange_sum(squares, doublings("tensor"))
    q_scale, k_scale = (lax.rsqrt(squares[i] / features + EPSILON)[:, None] for i in range(2))
    query, key, attended, lse = attend(
        qraw, kraw, value, q_scale, k_scale, q_gain, k_gain, cosine, sine, seg_ids[0], keep_mask[0]
    )
    attended_parts = [chunk_of(gate(attended, grad_rows), c) for c in chunks]
    outs = [nt(attended_parts[0], w_out).astype(bf16)]
    summed = [scatter_rows(outs[0])]
    outs.append(nt(gate(attended_parts[1], outs[0]), w_out).astype(bf16))
    summed.append(scatter_rows(outs[1]))

    idle_routes, idle_router = gate((routes, router), outs[1])
    expert_ids = jnp.arange(LANES)
    routed = jnp.sum((idle_routes[:, :, None] == expert_ids[None, None, :]).astype(f32), axis=1)
    router_wide = jnp.pad(idle_router, ((0, 0), (0, LANES - experts)))
    routed_own = lax.dynamic_slice_in_dim(routed, part_at * shard_rows, shard_rows, 0)
    back = up_back(gate(grad_rows, routed, router_wide), w_down).reshape(parts, CHUNKS, chunk_rows, -1)
    grad_rows = grad_rows.reshape(parts, CHUNKS, chunk_rows, features)
    grad_parts = [(grad_rows, c) for c in chunks]

    norms = [middle_rows(0, tokens, summed[0], ffn_gain)]
    ffn_all = [gather_rows(norms[0][2])]
    norms.append(middle_rows(1, tokens, gate(summed[1], norms[0][2], back), ffn_gain))
    ffn_all.append(gather_rows(norms[1][2]))
    ffn_parts = [(rows, 0) for rows in ffn_all]
    acts, dgates, dups, expert_grads = [], [], [], []
    for c in chunks:
        here = gate(chunk_of(routed, c), back, *acts[-1:])
        act, dgate, dup, grads = experts_block(c, ffn_all[c], back, here, router_wide, w_gate, w_up)
        acts.append(act)
        dgates.append(dgate)
        dups.append(dup)
        expert_grads.append(grads)
    expert_grads = [scatter_rows(grads) for grads in expert_grads]

    def back_of(c, grads, filled=()):
        return middle_back(c, grads, *norms[c], routed_own, router_wide, cotangent, ffn_gain, experts, filled)

    def expert_sums(lefts, rights, ids, *others, added=(), weight=1, pieces=0):
        return wgrad(lefts, rights, gate(ids, *others), width, per, added, weight, pieces)

    def core_swap(pieces):
        return [pair_swap(piece, 1) for piece in pieces]

    def halving(sums):
        return Halving([part.reshape((part.shape[0] // per, per) + part.shape[1:]) for part in sums])

    first = back_of(0, gate(expert_grads[0], acts[1]))
    gate_sent = expert_sums(ffn_parts, dgates, theirs, first[1], weight=0)
    gate_got = core_swap(gate_sent)
    up_sent = expert_sums(ffn_parts, dups, theirs, *gate_sent, weight=4)
    up_got = core_swap(up_sent)
    gate_sums = expert_sums(ffn_parts, dgates, mine, *up_sent, added=gate_got, weight=4)
    gate_out = halving(gate_sums)
    gate_out.send()
    second = back_of(1, gate(expert_grads[1], *gate_sums), first[:2])
    middle_grad, middle_low = second[:2]
    middle_all = gather_rows(middle_low)
    up_sums = expert_sums(ffn_parts, dups, mine, middle_low, added=up_got, weight=0)
    up_out = halving(up_sums)
    up_out.send()
    moe = down([gate(acts[0], *up_sums), acts[1]], w_down, parts)
    moe_sum = scatter_rows(moe)
    gate_late = gate_out.add(moe)
    gate_out.send()
    down_sent = expert_sums(grad_parts, acts, theirs, *gate_late, pieces=2, weight=0.0)
    down_got = core_swap(down_sent)
    attended_grad = nn(gate(middle_all, *down_sent), w_out).astype(bf16)
    dqn, dkn, dvalue, qdot, kdot, q_gain_part, k_gain_part = attend_back(
        query, key, value, attended_grad, lse, qraw, kraw, q_scale, k_scale, q_gain, k_gain, cosine, sine,
        seg_ids[0], keep_mask[0],
    )
    dots = exchange_sum(jnp.stack([qdot[:, 0], kdot[:, 0]]), doublings("tensor")) / features
    up_late = up_out.add(dqn)
    up_out.send()
    normed_part, dqraw, dkraw, attn_gain_part = project_back(
        normed_all, dqn, dkn, dvalue, qraw, kraw, q_scale, k_scale, dots[0][:, None], dots[1][:, None],
        gate(q_gain, *up_late, *gate_out.got), k_gain, w_query, w_key, w_value,
    )
    normed_grad = scatter_rows(normed_part)
    down_sums = expert_sums(grad_parts, acts, mine, normed_part, *up_out.got, added=down_got, weight=0.0)
    down_out = halving(down_sums)
    down_out.send()
    def attention_sums(ids, *others, added=()):
        return attention_wgrad(
            normed_all, middle_all, (dqraw, dkraw, dvalue), attended, gate(ids, *others), dp_size, added
        )

    attn_sent = attention_sums(other_blocks, *down_sums)
    attn_got = core_swap(attn_sent)
    down_late = down_out.add(*attn_sent)
    down_out.send()

    def placed(part):
        return lax.dynamic_update_slice_in_dim(jnp.zeros((features,), f32), part, part_at * local_width, 0)

    attn_sums = attention_sums(own_blocks, *down_late, added=attn_got)
    attn_out = Halving(attn_sums)
    normed_grad = gate(normed_grad, *attn_out.send())
    smalls = [attn_gain_part[0] / attn_gain, placed(q_gain_part[0]), placed(k_gain_part[0]), (first[2] + second[2])[0]]
    router_part = sum(tn(late[3], norms[c][2]) for c, late in enumerate((first, second)))[:experts]
    smalls = gate(jnp.concatenate([jnp.stack(smalls), router_part]), *attn_sums)
    smalls = exchange_sum(smalls, doublings("dp")[:1] + doublings("tensor"))
    attn_late = attn_out.add()
    attn_out.send()
    smalls = exchange_sum(gate(smalls, *attn_late), doublings("dp")[1:])
    late_got = tuple(down_out.got)
    gate_done = gate_out.done()
    up_done = up_out.done()
    down_done = down_out.done()
    query_done, key_done, value_done, out_done = attn_out.done()
    layer_out = (jnp.concatenate([norms[c][0] for c in chunks]) + gate(moe_sum, *late_got).astype(f32)).astype(bf16)
    tokens_grad = middle_grad + norm_back(normed_grad.astype(f32), inputs, first_scale, attn_gain)
    return (
        layer_out, tokens_grad, query_done, key_done, value_done, out_done,
        smalls[0], smalls[1], smalls[2], smalls[3], smalls[4:].T, gate_done, up_done, down_done,
    )


def solution(mesh):
    rows = P(("dp", "tensor"), None)
    column = P(None, "tensor")
    expert = P(None, None, "tensor")
    in_specs = (
        rows, rows, P("dp", None), P("dp", None), P("dp", None), P(), column, column, column, column,
        P("tensor"), P("tensor"), P(), P(), expert, expert, expert,
    )
    block = P("dp", "tensor")
    expert_out = P("dp", None, "tensor")
    out_specs = (
        rows, rows, block, block, block, block, P(), P(), P(), P(), P(), expert_out, expert_out, expert_out,
    )
    return jax.shard_map(local, mesh=mesh, in_specs=in_specs, out_specs=out_specs, check_vma=False)
```

```python
import functools

import jax
import jax.numpy as jnp
import numpy as np
from jax import lax
from jax.experimental import pallas as pl
from jax.experimental.pallas import tpu as pltpu
from jax.sharding import PartitionSpec as P

D = 2048
HEAD = 128
DOC = 512
LANES = 128
EPSILON = 1e-05
MASKED = -1e30
CHUNKS = 2
VMEM = 56 * 1024 * 1024
bf16 = jnp.bfloat16
f32 = jnp.float32


def nn(left, right):
    return lax.dot_general(left, right, (((1,), (0,)), ((), ())), preferred_element_type=f32)


def nt(left, right):
    return lax.dot_general(left, right, (((1,), (1,)), ((), ())), preferred_element_type=f32)


def tn(left, right):
    return lax.dot_general(left, right, (((0,), (0,)), ((), ())), preferred_element_type=f32)


def params():
    return pltpu.CompilerParams(vmem_limit_bytes=VMEM)


PACE = 0.3


def cost(flops, moved, special=0):
    return pl.CostEstimate(flops=int(1.5 * PACE * flops + 6e4 * PACE * special), bytes_accessed=moved // 8, transcendentals=0)


def rms_scale(values):
    return lax.rsqrt(jnp.mean(values * values, axis=-1, keepdims=True) + EPSILON)


def norm_back(grad_values, values, scale_col, gain_vec):
    weighted = grad_values * gain_vec
    inner_mean = jnp.mean(weighted * values, axis=-1, keepdims=True)
    return scale_col * weighted - values * (scale_col * scale_col * scale_col) * inner_mean


def rope_tables(length, width):
    angles = np.arange(length)[:, None] * 10000.0 ** (-np.arange(width // 2) * 2.0 / width)[None, :]
    cosine, sine = np.cos(angles).astype(np.float32), np.sin(angles).astype(np.float32)
    return jnp.asarray(np.concatenate([cosine, cosine], axis=1)), jnp.asarray(np.concatenate([-sine, sine], axis=1))


def key_start(query_start):
    return max(0, query_start - DOC)


def fill_bias(bias, seg_col, seg_row, keep_row, block):
    length = seg_col.shape[0]
    for start in range(0, length, block):
        first, stop = key_start(start), start + block
        query_pos = start + lax.broadcasted_iota(jnp.int32, (block, stop - first), 0)
        key_pos = first + lax.broadcasted_iota(jnp.int32, (block, stop - first), 1)
        same = seg_col[start:stop, :] == seg_row[:, first:stop]
        live = (keep_row[:, first:stop] == 1) | (key_pos == query_pos)
        allowed = same & live & (key_pos <= query_pos)
        bias[start:stop, : stop - first] = jnp.where(allowed, 0.0, MASKED)


def turned(values):
    return pltpu.roll(values, values.shape[1] // 2, 1)


def project_kernel(rows_in, w_query, w_key, w_value, q_out, k_out, v_out, squares_out):
    ones = jnp.ones((8, q_out.shape[1]), f32)
    for at, (weight, out) in enumerate(((w_query, q_out), (w_key, k_out))):
        raw = nn(rows_in[...], weight[...])
        out[...] = raw
        sums = lax.dot_general(
            ones, raw * raw, (((1,), (1,)), ((), ())), precision=lax.Precision.HIGHEST, preferred_element_type=f32
        )
        squares_out[at : at + 1, :] = sums[:1]
    v_out[...] = nn(rows_in[...], w_value[...]).astype(bf16)


def project(rows_in, w_query, w_key, w_value):
    rows, features = rows_in.shape
    width = w_query.shape[1]
    block = min(256, rows)
    row = lambda columns: pl.BlockSpec((block, columns), lambda r: (r, 0))
    weight = pl.BlockSpec((features, width), lambda r: (0, 0))
    sds = jax.ShapeDtypeStruct
    return pl.pallas_call(
        project_kernel,
        grid=(rows // block,),
        in_specs=[row(features), weight, weight, weight],
        out_specs=[row(width), row(width), row(width), pl.BlockSpec((2, block), lambda r: (0, r))],
        out_shape=[sds((rows, width), f32), sds((rows, width), f32), sds((rows, width), bf16), sds((2, rows), f32)],
        compiler_params=params(),
        cost_estimate=cost(6 * rows * features * width, 2 * (rows + 3 * width) * features),
        name="project",
    )(rows_in, w_query, w_key, w_value)


def project_back_kernel(
    rows_in, dqn, dkn, dvalue, qraw, kraw, q_scale, k_scale, q_dot, k_dot, q_gain, k_gain,
    w_query, w_key, w_value, part_out, dq_out, dk_out, gain_out,
):
    @pl.when(pl.program_id(0) == 0)
    def _():
        gain_out[...] = jnp.zeros_like(gain_out)

    def raw_grad(grad, raw, scale, gain, dot):
        cube = scale[...] * scale[...] * scale[...]
        return (scale[...] * (gain[...] * grad[...]) - raw[...] * (cube * dot[...])).astype(bf16)

    dq = raw_grad(dqn, qraw, q_scale, q_gain, q_dot)
    dk = raw_grad(dkn, kraw, k_scale, k_gain, k_dot)
    dq_out[...] = dq
    dk_out[...] = dk
    part = nt(dq, w_query[...]) + nt(dk, w_key[...]) + nt(dvalue[...], w_value[...])
    part_out[...] = part.astype(bf16)
    gain_out[...] += jnp.sum(part * rows_in[...].astype(f32), axis=0, keepdims=True)


def project_back(rows_in, dqn, dkn, dvalue, qraw, kraw, q_scale, k_scale, q_dot, k_dot, q_gain, k_gain, w_query, w_key, w_value):
    rows, features = rows_in.shape
    width = w_query.shape[1]
    block = min(256, rows)
    row = lambda columns: pl.BlockSpec((block, columns), lambda r: (r, 0))
    whole = lambda *shape: pl.BlockSpec(shape, lambda r: (0, 0))
    sds = jax.ShapeDtypeStruct
    return pl.pallas_call(
        project_back_kernel,
        grid=(rows // block,),
        in_specs=[row(features)] + [row(width)] * 5 + [row(1)] * 4 + [whole(1, width)] * 2 + [whole(features, width)] * 3,
        out_specs=[row(features), row(width), row(width), whole(1, features)],
        out_shape=[sds((rows, features), bf16), sds((rows, width), bf16), sds((rows, width), bf16), sds((1, features), f32)],
        compiler_params=params(),
        cost_estimate=cost(int(20.0 * 6 * rows * features * width), 0),
        name="project_back",
    )(rows_in, dqn, dkn, dvalue, qraw, kraw, q_scale, k_scale, q_dot, k_dot, q_gain[None], k_gain[None], w_query, w_key, w_value)


def attention_wgrad_kernel(added, held, order, tables, rows_in, middle, *refs):
    sides, (attended,), refs = refs[:3], refs[3:4], refs[4:]
    got, outs = (refs[:added], refs[added:])
    at = pl.program_id(0)
    totals = [tn(rows_in[...], side[...]) for side in sides] + [tn(middle[...], attended[...])]
    if not added:
        for place, out in enumerate(outs):

            @pl.when(at // held == place)
            def _(out=out):
                for weight, total in enumerate(totals):
                    out[0, weight] = total.astype(bf16)

        return
    scratch, outs = outs[-1], outs[:-1]
    half = outs[0].shape[2]
    for place, piece in enumerate(got):

        @pl.when(at // held == place)
        def _(piece=piece):
            for weight, total in enumerate(totals):
                scratch[weight] = (total + piece[0, weight].astype(f32)).astype(bf16)

    for side, out in enumerate(outs):
        start = side * 2 // len(outs) * half

        @pl.when(tables[1, side, at] == 1)
        def _(out=out, start=start):
            out[0] = scratch[:, start : start + half, :]


def attention_wgrad(rows_in, middle, sides, attended, order, blocks, added=()):
    features = rows_in.shape[1]
    width = sides[0].shape[1]
    block = features // blocks
    count = order.shape[0]
    tables, sizes = split_tables(count, 1)
    left = lambda values: pl.BlockSpec((values.shape[0], block), lambda i, ids, to: (0, ids[i]))
    right = lambda values: pl.BlockSpec(values.shape, lambda i, ids, to: (0, 0))

    def half_spec(side):
        return pl.BlockSpec((1, 4, block // 2, width), lambda i, ids, to: (to[0, side, i], 0, 0, 0))

    pieces = min(2, count)
    held = count // pieces

    def piece_spec(place):
        return pl.BlockSpec((1, 4, block, width), lambda i, ids, to: (jnp.clip(i - place * held, 0, held - 1), 0, 0, 0))

    group_specs = [piece_spec(place) for place in range(pieces)]
    if added:
        out_specs = [half_spec(side) for side in range(len(sizes))]
        out_shape = [jax.ShapeDtypeStruct((size, 4, block // 2, width), bf16) for size in sizes]
    else:
        out_specs = group_specs
        out_shape = [jax.ShapeDtypeStruct((held, 4, block, width), bf16)] * pieces
    return pl.pallas_call(
        functools.partial(attention_wgrad_kernel, len(added), held),
        grid_spec=pltpu.PrefetchScalarGridSpec(
            num_scalar_prefetch=2,
            grid=(count,),
            in_specs=[left(rows_in), left(middle)] + [right(v) for v in sides] + [right(attended)] + (group_specs if added else []),
            out_specs=out_specs,
            scratch_shapes=[pltpu.VMEM((4, block, width), bf16)] if added else [],
        ),
        out_shape=out_shape,
        compiler_params=params(),
        cost_estimate=cost(0, 0),
        name="attention_wgrad",
    )(order, tables, rows_in, middle, *sides, attended, *added)


def attend_kernel(
    block, qraw, kraw, value, q_scale, k_scale, q_gain, k_gain, cosine, sine,
    seg_col, seg_row, keep_row, q_out, k_out, o_out, lse_out, bias,
):
    @pl.when(pl.program_id(0) == 0)
    def _():
        fill_bias(bias, seg_col, seg_row, keep_row, block)

    def rotated(raw, scale, gain):
        normed = raw[...] * scale[...] * gain[...]
        return (normed * cosine[...] + turned(normed) * sine[...]).astype(bf16)

    q_out[...] = rotated(qraw, q_scale, q_gain)
    k_out[...] = rotated(kraw, k_scale, k_gain)
    length = seg_col.shape[0]
    for start in range(0, length, block):
        first, stop = key_start(start), start + block
        scores = nt(q_out[start:stop, :], k_out[first:stop, :]) * HEAD ** (-0.5)
        scores = scores + bias[start:stop, : stop - first]
        top = jnp.max(scores, axis=1, keepdims=True)
        powers = jnp.exp(scores - top)
        total = jnp.sum(powers, axis=1, keepdims=True)
        weights = (powers * (1.0 / total)).astype(bf16)
        o_out[start:stop, :] = nn(weights, value[first:stop, :]).astype(bf16)
        lse_out[start:stop, :] = jnp.broadcast_to(top + jnp.log(total), (block, HEAD))


def attend(qraw, kraw, value, q_scale, k_scale, q_gain, k_gain, cosine, sine, seg, keep):
    length, width = qraw.shape
    block = min(256, length)
    span = min(DOC + block, length)
    head = pl.BlockSpec((length, HEAD), lambda h: (0, h))
    gain = pl.BlockSpec((1, HEAD), lambda h: (0, h))
    whole = lambda *shape: pl.BlockSpec(shape, lambda h: (0, 0))
    return pl.pallas_call(
        functools.partial(attend_kernel, block),
        grid=(width // HEAD,),
        in_specs=[head, head, head, whole(length, 1), whole(length, 1), gain, gain]
        + [whole(length, HEAD), whole(length, HEAD), whole(length, 1), whole(1, length), whole(1, length)],
        out_specs=[head, head, head, head],
        out_shape=[jax.ShapeDtypeStruct((length, width), t) for t in (bf16, bf16, bf16, f32)],
        scratch_shapes=[pltpu.VMEM((length, span), f32)],
        compiler_params=params(),
        cost_estimate=cost(4 * length * span * width, 18 * length * width, length * span * width // HEAD),
        name="attend",
    )(qraw, kraw, value, q_scale, k_scale, q_gain[None], k_gain[None], cosine, sine, seg[:, None], seg[None], keep[None])


def attend_back_kernel(
    block, query, key, value, out_grad, lse, qraw, kraw, q_scale, k_scale, q_gain, k_gain, cosine, sine,
    seg_col, seg_row, keep_row, dq_out, dk_out, dv_out, qdot_out, kdot_out, qg_out, kg_out, bias, dk_sum, dv_sum,
):
    at = pl.program_id(0)

    @pl.when(at == 0)
    def _():
        fill_bias(bias, seg_col, seg_row, keep_row, block)
        qdot_out[...] = jnp.zeros_like(qdot_out)
        kdot_out[...] = jnp.zeros_like(kdot_out)

    dk_sum[...] = jnp.zeros_like(dk_sum)
    dv_sum[...] = jnp.zeros_like(dv_sum)
    length = seg_col.shape[0]
    scale = HEAD ** (-0.5)
    for start in range(0, length, block):
        first, stop = key_start(start), start + block
        rows, keys = slice(start, stop), slice(first, stop)
        scores = nt(query[rows, :], key[keys, :]) * scale + bias[rows, : stop - first]
        weights = jnp.exp(scores - lse[rows, :1])
        prob_grad = nt(out_grad[rows, :], value[keys, :])
        inner = jnp.sum(weights * prob_grad, axis=1, keepdims=True)
        score_grad = (weights * (prob_grad - inner)).astype(bf16)
        dq_out[rows, :] = nn(score_grad, key[keys, :]) * scale
        dk_sum[keys, :] += tn(score_grad, query[rows, :])
        dv_sum[keys, :] += tn(weights.astype(bf16), out_grad[rows, :])

    def unrotated(grad):
        return grad * cosine[...] + turned(grad * sine[...])

    dv_out[...] = dv_sum[...].astype(bf16)
    dq = unrotated(dq_out[...])
    dk = unrotated(dk_sum[...] * scale)
    dq_out[...] = dq
    dk_out[...] = dk
    dq = dq * qraw[...]
    dk = dk * kraw[...]
    qg_out[...] = jnp.sum(dq * q_scale[...], axis=0, keepdims=True)
    kg_out[...] = jnp.sum(dk * k_scale[...], axis=0, keepdims=True)
    qdot_out[...] += jnp.sum(dq * q_gain[...], axis=1, keepdims=True)
    kdot_out[...] += jnp.sum(dk * k_gain[...], axis=1, keepdims=True)


def attend_back(query, key, value, out_grad, lse, qraw, kraw, q_scale, k_scale, q_gain, k_gain, cosine, sine, seg, keep):
    length, width = qraw.shape
    block = min(256, length)
    span = min(DOC + block, length)
    head = pl.BlockSpec((length, HEAD), lambda h: (0, h))
    gain = pl.BlockSpec((1, HEAD), lambda h: (0, h))
    whole = lambda *shape: pl.BlockSpec(shape, lambda h: (0, 0))
    sds = jax.ShapeDtypeStruct
    return pl.pallas_call(
        functools.partial(attend_back_kernel, block),
        grid=(width // HEAD,),
        in_specs=[head] * 7
        + [whole(length, 1), whole(length, 1), gain, gain]
        + [whole(length, HEAD), whole(length, HEAD), whole(length, 1), whole(1, length), whole(1, length)],
        out_specs=[head, head, head, whole(length, 1), whole(length, 1), gain, gain],
        out_shape=[sds((length, width), f32), sds((length, width), f32), sds((length, width), bf16)]
        + [sds((length, 1), f32), sds((length, 1), f32), sds((1, width), f32), sds((1, width), f32)],
        scratch_shapes=[pltpu.VMEM((length, span), f32), pltpu.VMEM((length, HEAD), f32), pltpu.VMEM((length, HEAD), f32)],
        compiler_params=params(),
        cost_estimate=cost(0, 0),
        name="attend_back",
    )(query, key, value, out_grad, lse, qraw, kraw, q_scale, k_scale, q_gain[None], k_gain[None], cosine, sine, seg[:, None], seg[None], keep[None])


def middle_kernel(tokens, summed, gain, middle_out, scale_out, normed_out):
    middle = tokens[...].astype(f32) + summed[...].astype(f32)
    scale = lax.rsqrt(jnp.mean(middle * middle, axis=1, keepdims=True) + EPSILON)
    middle_out[...] = middle
    scale_out[...] = scale
    normed_out[...] = (middle * scale * gain[...]).astype(bf16)


def middle_rows(chunk, tokens, summed, gain):
    rows, features = summed.shape
    sds = jax.ShapeDtypeStruct
    whole = lambda *shape: pl.BlockSpec(shape, lambda i: (0, 0))
    return pl.pallas_call(
        middle_kernel,
        grid=(1,),
        in_specs=[pl.BlockSpec((rows, features), lambda i: (chunk, 0)), whole(rows, features), whole(1, features)],
        out_specs=[whole(rows, features), whole(rows, 1), whole(rows, features)],
        out_shape=[sds((rows, features), f32), sds((rows, 1), f32), sds((rows, features), bf16)],
        compiler_params=params(),
        cost_estimate=cost(0, 0),
        name="middle",
    )(tokens, summed, gain[None])


def middle_back_kernel(
    experts, grads, middle, scale, normed, routed, router, cotangent, gain, *refs
):
    grad_out, low_out, gain_out, logit_out = refs[-4:]
    features = middle.shape[1]
    lane = lax.broadcasted_iota(jnp.int32, routed.shape, 1)
    logits = jnp.where(lane < experts, nn(normed[...], router[...]), MASKED)
    powers = jnp.exp(logits - jnp.max(logits, axis=1, keepdims=True))
    probs = powers / jnp.sum(powers, axis=1, keepdims=True)
    share_grad = grads[:, features:].astype(f32) * routed[...]
    logit_grad = (probs * (share_grad - jnp.sum(share_grad * probs, axis=1, keepdims=True))).astype(bf16)
    logit_out[...] = logit_grad
    ffn_grad = grads[:, :features].astype(f32) + nt(logit_grad, router[...])
    along = middle[...] * scale[...]
    gain_out[...] = jnp.sum(ffn_grad * along, axis=0, keepdims=True)
    weighted = ffn_grad * gain[...]
    inner = jnp.mean(weighted * along, axis=1, keepdims=True)
    total = cotangent[...].astype(f32) + scale[...] * (weighted - along * inner)
    grad_out[...] = total
    low_out[...] = total.astype(bf16)


def middle_back(chunk, grads, middle, scale, normed, routed, router, cotangent, gain, experts, filled=()):
    rows, features = middle.shape
    sds = jax.ShapeDtypeStruct
    whole = lambda *shape: pl.BlockSpec(shape, lambda i: (0, 0))
    part = lambda columns: pl.BlockSpec((rows, columns), lambda i: (chunk, 0))
    return pl.pallas_call(
        functools.partial(middle_back_kernel, experts),
        grid=(1,),
        in_specs=[whole(rows, features + LANES), whole(rows, features), whole(rows, 1), whole(rows, features), part(LANES)]
        + [whole(features, LANES), part(features), whole(1, features)]
        + [pl.BlockSpec(memory_space=pl.ANY)] * len(filled),
        out_specs=[part(features), part(features), whole(1, features), whole(rows, LANES)],
        out_shape=[sds(cotangent.shape, f32), sds(cotangent.shape, bf16), sds((1, features), f32), sds((rows, LANES), bf16)],
        input_output_aliases={8 + at: at for at in range(len(filled))},
        compiler_params=params(),
        cost_estimate=cost(0, 0),
        name="middle_back",
    )(grads, middle, scale, normed, routed, router, cotangent, gain[None], *filled)


def up_back_kernel(grad, down_w, out):
    width = down_w.shape[2]
    for at in range(down_w.shape[0]):
        out[:, at * width : (at + 1) * width] = nn(grad[...], down_w[at]).astype(out.dtype)


def up_back(grad, down_w):
    rows, features = grad.shape
    experts, _, width = down_w.shape
    step = 2 if experts % 2 == 0 else 1
    return pl.pallas_call(
        up_back_kernel,
        grid=(experts // step,),
        in_specs=[pl.BlockSpec((rows, features), lambda e: (0, 0)), pl.BlockSpec((step, features, width), lambda e: (e, 0, 0))],
        out_specs=pl.BlockSpec((rows, step * width), lambda e: (0, e)),
        out_shape=jax.ShapeDtypeStruct((rows, experts * width), bf16),
        compiler_params=params(),
        cost_estimate=cost(2 * rows * features * experts * width, 2 * (rows + experts * width) * features),
        name="up_back",
    )(grad, down_w)


def expert_kernel(block, rows_in, back, routed, router, gate_w, up_w, act_out, dgate_out, dup_out, grad_out, comb, dcomb, total):
    at = pl.program_id(0)
    rows, features = rows_in.shape
    lane = lax.broadcasted_iota(jnp.int32, (block, LANES), 1)

    @pl.when(at == 0)
    def _():
        experts = pl.num_programs(0)
        for start in range(0, rows, block):
            here = slice(start, start + block)
            logits = jnp.where(lane < experts, nn(rows_in[here, :], router[...]), MASKED)
            powers = jnp.exp(logits - jnp.max(logits, axis=1, keepdims=True))
            probs = powers / jnp.sum(powers, axis=1, keepdims=True)
            comb[here, :] = probs * routed[here, :]
        total[...] = jnp.zeros_like(total)
        dcomb[...] = jnp.zeros_like(dcomb)

    gate, up = gate_w[0], up_w[0]
    mine = lane == at
    for start in range(0, rows, block):
        here = slice(start, start + block)
        taken = rows_in[here, :]
        pre_gate = nn(taken, gate)
        pre_up = nn(taken, up)
        behind = back[...].reshape(rows, back.shape[3])[here, :].astype(f32)
        share = jnp.sum(jnp.where(mine, comb[here, :], 0.0), axis=1, keepdims=True)
        sigmoid = 0.5 * jnp.tanh(0.5 * pre_gate) + 0.5
        active = pre_gate * sigmoid
        inner = active * pre_up
        share_grad = jnp.sum(inner * behind, axis=1, keepdims=True)
        dcomb[here, :] = jnp.where(mine, share_grad, dcomb[here, :])
        act_out[here, :] = (inner * share).astype(bf16)
        inner_grad = behind * share
        dgate = (inner_grad * pre_up * (sigmoid + active * (1.0 - sigmoid))).astype(bf16)
        dup = (inner_grad * active).astype(bf16)
        dgate_out[here, :] = dgate
        dup_out[here, :] = dup
        total[here, :] += nt(dgate, gate) + nt(dup, up)

    @pl.when(at == pl.num_programs(0) - 1)
    def _():
        grad_out[:, :features] = total[...].astype(bf16)
        grad_out[:, features:] = dcomb[...].astype(bf16)


def experts_block(chunk, rows_in, back, routed, router, gate_w, up_w):
    rows, features = rows_in.shape
    parts, _, chunk_rows, _ = back.shape
    experts, _, width = gate_w.shape
    block = min(512, rows)
    whole = lambda *shape: pl.BlockSpec(shape, lambda e: (0, 0))
    column = pl.BlockSpec((rows, width), lambda e: (0, e))
    weight = pl.BlockSpec((1, features, width), lambda e: (e, 0, 0))
    wide = jax.ShapeDtypeStruct((rows, experts * width), bf16)
    return pl.pallas_call(
        functools.partial(expert_kernel, block),
        grid=(experts,),
        in_specs=[whole(rows, features), pl.BlockSpec((parts, 1, chunk_rows, width), lambda e: (0, chunk, 0, e)), whole(rows, LANES), whole(features, LANES), weight, weight],
        out_specs=[column, column, column, whole(rows, features + LANES)],
        out_shape=[wide, wide, wide, jax.ShapeDtypeStruct((rows, features + LANES), bf16)],
        scratch_shapes=[pltpu.VMEM((rows, LANES), f32), pltpu.VMEM((rows, LANES), f32), pltpu.VMEM((rows, features), f32)],
        compiler_params=params(),
        cost_estimate=cost(8 * rows * features * experts * width, 4 * experts * width * (features + 2 * rows), rows * experts * width),
        name="experts",
    )(rows_in, back, routed, router, gate_w, up_w)


def block_order(blocks):
    return [3, 2, 0, 1] if blocks == 4 else list(range(blocks))


def split_tables(blocks, per):
    order = block_order(blocks)
    if blocks == 4:
        picks = [{0: 0, 1: 1}, {2: 0, 3: 1}, {0: 0, 2: 1}, {1: 0, 3: 1}]
    else:
        picks = [{block: block for block in order}] * 2
    places, fills = [], []
    for pick in picks:
        filled = [pick[block] * per + at if block in pick else None for block in order for at in range(per)]
        last = next(place for place in filled if place is not None)
        row = []
        for place in filled:
            last = last if place is None else place
            row.append(last)
        places.append(row)
        fills.append([int(place is not None) for place in filled])
    return jnp.asarray(np.array([places, fills], np.int32)), [len(pick) for pick in picks]


def wgrad_kernel(count, extra, per, block, order, tables, *refs):
    lefts, rights = refs[:count], refs[count : 2 * count]
    added = refs[2 * count : 2 * count + extra]
    outs = refs[2 * count + extra :]
    at = pl.program_id(0)
    features = lefts[0].shape[-1]

    def piece(start, stop):
        total = None
        for left, right in zip(lefts, rights):
            columns = left[:, start:stop] if len(left.shape) == 2 else left[:, :, :, start:stop].reshape(-1, stop - start)
            part = tn(columns, right[...])
            total = part if total is None else total + part
        return total

    if not added:
        for place, out in enumerate(outs):

            @pl.when(at // per == place)
            def _(out=out):
                for start in range(0, features, block):
                    out[0, start : start + block, :] = piece(start, start + block).astype(bf16)

        return
    half = features // 2
    got = outs[-1]
    outs = outs[:-1]
    for place, arrived in enumerate(added):

        @pl.when(at // per == place)
        def _(arrived=arrived):
            for start in range(0, features, block):
                total = piece(start, start + block) + arrived[0, start : start + block, :].astype(f32)
                got[start : start + block, :] = total.astype(bf16)

    for side, out in enumerate(outs):
        start = side * 2 // len(outs) * half

        @pl.when(tables[1, side, at] == 1)
        def _(out=out, start=start):
            out[0] = got[start : start + half, :]


def wgrad(lefts, rights, order, width, per, added=(), weight=1, pieces=0):
    features = lefts[0][0].shape[-1]
    experts = order.shape[0]
    groups = experts // per
    tables, sizes = split_tables(groups, per)
    pieces = len(added) or pieces or groups
    held = experts // pieces

    def piece_spec(place):
        return pl.BlockSpec((1, features, width), lambda i, ids, to: (jnp.clip(i - place * held, 0, held - 1), 0, 0))

    def half_spec(side):
        return pl.BlockSpec((1, features // 2, width), lambda i, ids, to: (to[0, side, i], 0, 0))

    def left_spec(left, chunk):
        if left.ndim == 2:
            return pl.BlockSpec(left.shape, lambda i, ids, to: (0, 0))
        return pl.BlockSpec((left.shape[0], 1) + left.shape[2:], lambda i, ids, to: (0, chunk, 0, 0))

    piece_specs = [piece_spec(place) for place in range(pieces)]
    if added:
        out_specs = [half_spec(side) for side in range(len(sizes))]
        out_shape = [jax.ShapeDtypeStruct((size * per, features // 2, width), bf16) for size in sizes]
    else:
        out_specs = piece_specs
        out_shape = [jax.ShapeDtypeStruct((held, features, width), bf16)] * pieces
    return pl.pallas_call(
        functools.partial(wgrad_kernel, len(lefts), len(added), held, min(512, features // 2)),
        grid_spec=pltpu.PrefetchScalarGridSpec(
            num_scalar_prefetch=2,
            grid=(experts,),
            in_specs=[left_spec(*left) for left in lefts]
            + [pl.BlockSpec((right.shape[0], width), lambda i, ids, to: (0, ids[i])) for right in rights]
            + (piece_specs if added else []),
            out_specs=out_specs,
            scratch_shapes=[pltpu.VMEM((features, width), bf16)] if added else [],
        ),
        out_shape=out_shape,
        compiler_params=params(),
        cost_estimate=cost(2 * weight * sum(right.shape[0] for right in rights) * features * experts * width, 0),
        name="wgrad",
    )(order, tables, *(left for left, _ in lefts), *rights, *added)


def down_kernel(parts, down_w, *refs):
    acts, out = refs[:-1], refs[-1]
    joined = jnp.concatenate([down_w[e] for e in range(down_w.shape[0])], axis=1)
    block = acts[0].shape[0] // parts
    for at, act in enumerate(acts):
        result = nt(act[...], joined).astype(out.dtype)
        for part in range(parts):
            start = (part * len(acts) + at) * block
            out[start : start + block, :] = result[part * block : (part + 1) * block, :]


def down(acts, down_w, parts):
    rows = sum(act.shape[0] for act in acts)
    experts, features, width = down_w.shape
    block = min(256, features)
    return pl.pallas_call(
        functools.partial(down_kernel, parts),
        grid=(features // block,),
        in_specs=[pl.BlockSpec((experts, block, width), lambda n: (0, n, 0))]
        + [pl.BlockSpec(act.shape, lambda n: (0, 0)) for act in acts],
        out_specs=pl.BlockSpec((rows, block), lambda n: (0, n)),
        out_shape=jax.ShapeDtypeStruct((rows, features), bf16),
        compiler_params=params(),
        cost_estimate=cost(0 * 2 * rows * features * experts * width, 0),
        name="down",
    )(down_w, *acts)


def gate(value, *others):
    return lax.optimization_barrier((value, others))[0]


def gather_rows(values):
    return lax.all_gather(values, "tensor", axis=0, tiled=True)


def scatter_rows(values):
    return lax.psum_scatter(values, "tensor", scatter_dimension=0, tiled=True)


def pair_swap(values, step):
    size = lax.axis_size("dp")
    return lax.ppermute(values, "dp", [(i, i ^ step) for i in range(size)])


class Halving:
    def __init__(self, values):
        if len(values) == 2:
            self.kept = list(values)
            self.going = None
        else:
            self.kept, self.going = list(values[::2]), list(values[1::2])
        bits = list(range(values[0].shape[0].bit_length() - (1 if self.going is None else 0)))
        self.left = [bits[::-1], bits]
        self.got = None

    def send(self):
        if not self.left[0]:
            return ()
        self.got = []
        sent = []
        for side, downward in ((0, True), (1, False)):
            bit = self.left[side].pop(0)
            if self.going is not None:
                go = self.going[side]
            else:
                kept = self.kept[side]
                half = kept.shape[0] // 2
                if downward:
                    self.kept[side], go = kept[:half], kept[half:]
                else:
                    view = kept.reshape((half, 2) + kept.shape[1:])
                    self.kept[side], go = view[:, 0], view[:, 1]
            sent.append(go)
            self.got.append(pair_swap(go, 2 << bit))
        self.going = None
        return tuple(sent)

    def add(self, *others):
        if self.got is not None:
            if others:
                self.got = gate(tuple(self.got), *others)
            last = not self.left[0]
            for side in range(2):
                total = self.kept[side].astype(f32) + self.got[side].astype(f32)
                self.kept[side] = total if last else total.astype(bf16)
            self.got = None
        return tuple(self.kept)

    def done(self):
        self.add()
        while self.left[0]:
            self.send()
            self.add()
        return jnp.concatenate([kept[0].astype(f32) for kept in self.kept], axis=1)


def exchange_sum(values, steps):
    for axis, step in steps:
        values = values + lax.ppermute(values, axis, [(i, i ^ step) for i in range(lax.axis_size(axis))])
    return values


def doublings(axis):
    return [(axis, 1 << bit) for bit in range(lax.axis_size(axis).bit_length() - 1)]


def local(
    tokens, cotangent, seg_ids, keep_mask, routes, attn_gain, w_query, w_key, w_value, w_out,
    q_gain, k_gain, ffn_gain, router, w_gate, w_up, w_down,
):
    parts = lax.axis_size("tensor")
    part_at = lax.axis_index("tensor")
    dp_size = lax.axis_size("dp")
    low_bit = lax.axis_index("dp") % 2
    shard_rows, features = tokens.shape
    group_rows = shard_rows * parts
    _, length = seg_ids.shape
    local_width = w_query.shape[1]
    experts, _, width = w_gate.shape
    per = experts // dp_size
    chunk_rows = shard_rows // CHUNKS
    chunks = range(CHUNKS)
    own = [slice(c * chunk_rows, (c + 1) * chunk_rows) for c in chunks]

    def chunk_of(values, c):
        columns = values.shape[1]
        return values.reshape(parts, CHUNKS, chunk_rows, columns)[:, c].reshape(parts * chunk_rows, columns)

    inputs = tokens.astype(f32)
    first_scale = rms_scale(inputs)
    normed_all = gather_rows((inputs * first_scale * attn_gain).astype(bf16))
    grad_rows = gather_rows(gate(cotangent, normed_all))

    cosine, sine = rope_tables(length, HEAD)

    relative = jnp.asarray(block_order(dp_size // 2), jnp.int32) ^ (lax.axis_index("dp") // 2)
    own_blocks, other_blocks = 2 * relative + low_bit, 2 * relative + 1 - low_bit
    mine, theirs = (
        (blocks[:, None] * per + jnp.arange(per, dtype=jnp.int32)).reshape(-1) for blocks in (own_blocks, other_blocks)
    )

    qraw, kraw, value, squares = project(normed_all, w_query, w_key, w_value)
    squares = exchange_sum(squares, doublings("tensor"))
    q_scale, k_scale = (lax.rsqrt(squares[i] / features + EPSILON)[:, None] for i in range(2))
    query, key, attended, lse = attend(
        qraw, kraw, value, q_scale, k_scale, q_gain, k_gain, cosine, sine, seg_ids[0], keep_mask[0]
    )
    attended_parts = [chunk_of(attended, c) for c in chunks]
    outs = [nt(attended_parts[0], w_out).astype(bf16)]
    summed = [scatter_rows(gate(outs[0], grad_rows))]
    outs.append(nt(gate(attended_parts[1], outs[0]), w_out).astype(bf16))
    summed.append(scatter_rows(gate(outs[1], grad_rows)))

    idle_routes, idle_router = gate((routes, router), outs[1])
    expert_ids = jnp.arange(LANES)
    routed = jnp.sum((idle_routes[:, :, None] == expert_ids[None, None, :]).astype(f32), axis=1)
    router_wide = jnp.pad(idle_router, ((0, 0), (0, LANES - experts)))
    routed_own = lax.dynamic_slice_in_dim(routed, part_at * shard_rows, shard_rows, 0)
    back = up_back(gate(grad_rows, routed, router_wide), w_down).reshape(parts, CHUNKS, chunk_rows, -1)
    grad_rows = grad_rows.reshape(parts, CHUNKS, chunk_rows, features)
    grad_parts = [(grad_rows, c) for c in chunks]

    norms = [middle_rows(0, tokens, summed[0], ffn_gain)]
    ffn_all = [gather_rows(norms[0][2])]
    norms.append(middle_rows(1, tokens, gate(summed[1], norms[0][2], back), ffn_gain))
    ffn_all.append(gather_rows(norms[1][2]))
    ffn_parts = [(rows, 0) for rows in ffn_all]
    acts, dgates, dups, expert_grads = [], [], [], []
    for c in chunks:
        here = gate(chunk_of(routed, c), back, *acts[-1:])
        act, dgate, dup, grads = experts_block(c, ffn_all[c], back, here, router_wide, w_gate, w_up)
        acts.append(act)
        dgates.append(dgate)
        dups.append(dup)
        expert_grads.append(grads)
    expert_grads = [scatter_rows(grads) for grads in expert_grads]

    def back_of(c, grads, filled=()):
        return middle_back(c, grads, *norms[c], routed_own, router_wide, cotangent, ffn_gain, experts, filled)

    def expert_sums(lefts, rights, ids, *others, added=(), weight=1, pieces=0):
        return wgrad(lefts, rights, gate(ids, *others), width, per, added, weight, pieces)

    def core_swap(pieces):
        return [pair_swap(piece, 1) for piece in pieces]

    def halving(sums):
        return Halving([part.reshape((part.shape[0] // per, per) + part.shape[1:]) for part in sums])

    first = back_of(0, gate(expert_grads[0], acts[1]))
    gate_sent = expert_sums(ffn_parts, dgates, theirs, first[1], weight=0)
    gate_got = core_swap(gate_sent)
    up_sent = expert_sums(ffn_parts, dups, theirs, *gate_sent, pieces=2, weight=4)
    up_got = core_swap(up_sent)
    gate_sums = expert_sums(ffn_parts, dgates, mine, *up_sent, added=gate_got, weight=4)
    gate_out = halving(gate_sums)
    gate_out.send()
    second = back_of(1, gate(expert_grads[1], *gate_sums), first[:2])
    middle_grad, middle_low = second[:2]
    middle_all = gather_rows(middle_low)
    up_sums = expert_sums(ffn_parts, dups, mine, middle_low, added=up_got, weight=0)
    up_out = halving(up_sums)
    up_out.send()
    moe = down([gate(acts[0], *up_sums), acts[1]], w_down, parts)
    moe_sum = scatter_rows(moe)
    gate_late = gate_out.add(moe)
    gate_out.send()
    down_sent = expert_sums(grad_parts, acts, theirs, *gate_late, pieces=2, weight=0.0)
    down_got = core_swap(down_sent)
    attended_grad = nn(gate(middle_all, *down_sent), w_out).astype(bf16)
    dqn, dkn, dvalue, qdot, kdot, q_gain_part, k_gain_part = attend_back(
        query, key, value, attended_grad, lse, qraw, kraw, q_scale, k_scale, q_gain, k_gain, cosine, sine,
        seg_ids[0], keep_mask[0],
    )
    dots = exchange_sum(jnp.stack([qdot[:, 0], kdot[:, 0]]), doublings("tensor")) / features
    up_late = up_out.add(dqn)
    up_out.send()
    normed_part, dqraw, dkraw, attn_gain_part = project_back(
        normed_all, dqn, dkn, dvalue, qraw, kraw, q_scale, k_scale, dots[0][:, None], dots[1][:, None],
        gate(q_gain, *up_late, *gate_out.got), k_gain, w_query, w_key, w_value,
    )
    normed_grad = scatter_rows(normed_part)
    down_sums = expert_sums(grad_parts, acts, mine, normed_part, *up_out.got, added=down_got, weight=0.0)
    down_out = halving(down_sums)
    down_out.send()
    def attention_sums(ids, *others, added=()):
        return attention_wgrad(
            normed_all, middle_all, (dqraw, dkraw, dvalue), attended, gate(ids, *others), dp_size, added
        )

    attn_sent = attention_sums(other_blocks, *down_sums)
    attn_got = core_swap(attn_sent)
    down_late = down_out.add(*attn_sent)
    down_out.send()

    def placed(part):
        return lax.dynamic_update_slice_in_dim(jnp.zeros((features,), f32), part, part_at * local_width, 0)

    attn_sums = attention_sums(own_blocks, *down_late, added=attn_got)
    attn_out = Halving(attn_sums)
    normed_grad = gate(normed_grad, *attn_out.send())
    smalls = [attn_gain_part[0] / attn_gain, placed(q_gain_part[0]), placed(k_gain_part[0]), (first[2] + second[2])[0]]
    router_part = sum(tn(late[3], norms[c][2]) for c, late in enumerate((first, second)))[:experts]
    smalls = gate(jnp.concatenate([jnp.stack(smalls), router_part]), *attn_sums)
    smalls = exchange_sum(smalls, doublings("dp")[:1] + doublings("tensor"))
    attn_late = attn_out.add()
    attn_out.send()
    smalls = exchange_sum(gate(smalls, *attn_late), doublings("dp")[1:])
    late_got = tuple(down_out.got)
    gate_done = gate_out.done()
    up_done = up_out.done()
    down_done = down_out.done()
    query_done, key_done, value_done, out_done = attn_out.done()
    layer_out = (jnp.concatenate([norms[c][0] for c in chunks]) + gate(moe_sum, *late_got).astype(f32)).astype(bf16)
    tokens_grad = middle_grad + norm_back(normed_grad.astype(f32), inputs, first_scale, attn_gain)
    return (
        layer_out, tokens_grad, query_done, key_done, value_done, out_done,
        smalls[0], smalls[1], smalls[2], smalls[3], smalls[4:].T, gate_done, up_done, down_done,
    )


def solution(mesh):
    rows = P(("dp", "tensor"), None)
    column = P(None, "tensor")
    expert = P(None, None, "tensor")
    in_specs = (
        rows, rows, P("dp", None), P("dp", None), P("dp", None), P(), column, column, column, column,
        P("tensor"), P("tensor"), P(), P(), expert, expert, expert,
    )
    block = P("dp", "tensor")
    expert_out = P("dp", None, "tensor")
    out_specs = (
        rows, rows, block, block, block, block, P(), P(), P(), P(), P(), expert_out, expert_out, expert_out,
    )
    return jax.shard_map(local, mesh=mesh, in_specs=in_specs, out_specs=out_specs, check_vma=False)
```

```python
import functools

import jax
import jax.numpy as jnp
import numpy as np
from jax import lax
from jax.experimental import pallas as pl
from jax.experimental.pallas import tpu as pltpu
from jax.sharding import PartitionSpec as P

D = 2048
HEAD = 128
DOC = 512
LANES = 128
EPSILON = 1e-05
MASKED = -1e30
CHUNKS = 2
VMEM = 56 * 1024 * 1024
bf16 = jnp.bfloat16
f32 = jnp.float32


def nn(left, right):
    return lax.dot_general(left, right, (((1,), (0,)), ((), ())), preferred_element_type=f32)


def nt(left, right):
    return lax.dot_general(left, right, (((1,), (1,)), ((), ())), preferred_element_type=f32)


def tn(left, right):
    return lax.dot_general(left, right, (((0,), (0,)), ((), ())), preferred_element_type=f32)


def params():
    return pltpu.CompilerParams(vmem_limit_bytes=VMEM)


PACE = 0.3


def cost(flops, moved, special=0):
    return pl.CostEstimate(flops=int(1.5 * PACE * flops + 6e4 * PACE * special), bytes_accessed=moved // 8, transcendentals=0)


def rms_scale(values):
    return lax.rsqrt(jnp.mean(values * values, axis=-1, keepdims=True) + EPSILON)


def norm_back(grad_values, values, scale_col, gain_vec):
    weighted = grad_values * gain_vec
    inner_mean = jnp.mean(weighted * values, axis=-1, keepdims=True)
    return scale_col * weighted - values * (scale_col * scale_col * scale_col) * inner_mean


def rope_tables(length, width):
    angles = np.arange(length)[:, None] * 10000.0 ** (-np.arange(width // 2) * 2.0 / width)[None, :]
    cosine, sine = np.cos(angles).astype(np.float32), np.sin(angles).astype(np.float32)
    return jnp.asarray(np.concatenate([cosine, cosine], axis=1)), jnp.asarray(np.concatenate([-sine, sine], axis=1))


def key_start(query_start):
    return max(0, query_start - DOC)


def fill_bias(bias, seg_col, seg_row, keep_row, block):
    length = seg_col.shape[0]
    for start in range(0, length, block):
        first, stop = key_start(start), start + block
        query_pos = start + lax.broadcasted_iota(jnp.int32, (block, stop - first), 0)
        key_pos = first + lax.broadcasted_iota(jnp.int32, (block, stop - first), 1)
        same = seg_col[start:stop, :] == seg_row[:, first:stop]
        live = (keep_row[:, first:stop] == 1) | (key_pos == query_pos)
        allowed = same & live & (key_pos <= query_pos)
        bias[start:stop, : stop - first] = jnp.where(allowed, 0.0, MASKED)


def turned(values):
    return pltpu.roll(values, values.shape[1] // 2, 1)


def project_kernel(rows_in, w_query, w_key, w_value, q_out, k_out, v_out, squares_out):
    ones = jnp.ones((8, q_out.shape[1]), f32)
    for at, (weight, out) in enumerate(((w_query, q_out), (w_key, k_out))):
        raw = nn(rows_in[...], weight[...])
        out[...] = raw
        sums = lax.dot_general(
            ones, raw * raw, (((1,), (1,)), ((), ())), precision=lax.Precision.HIGHEST, preferred_element_type=f32
        )
        squares_out[at : at + 1, :] = sums[:1]
    v_out[...] = nn(rows_in[...], w_value[...]).astype(bf16)


def project(rows_in, w_query, w_key, w_value):
    rows, features = rows_in.shape
    width = w_query.shape[1]
    block = min(256, rows)
    row = lambda columns: pl.BlockSpec((block, columns), lambda r: (r, 0))
    weight = pl.BlockSpec((features, width), lambda r: (0, 0))
    sds = jax.ShapeDtypeStruct
    return pl.pallas_call(
        project_kernel,
        grid=(rows // block,),
        in_specs=[row(features), weight, weight, weight],
        out_specs=[row(width), row(width), row(width), pl.BlockSpec((2, block), lambda r: (0, r))],
        out_shape=[sds((rows, width), f32), sds((rows, width), f32), sds((rows, width), bf16), sds((2, rows), f32)],
        compiler_params=params(),
        cost_estimate=cost(6 * rows * features * width, 2 * (rows + 3 * width) * features),
        name="project",
    )(rows_in, w_query, w_key, w_value)


def project_back_kernel(
    rows_in, dqn, dkn, dvalue, qraw, kraw, q_scale, k_scale, q_dot, k_dot, q_gain, k_gain,
    w_query, w_key, w_value, part_out, dq_out, dk_out, gain_out,
):
    @pl.when(pl.program_id(0) == 0)
    def _():
        gain_out[...] = jnp.zeros_like(gain_out)

    def raw_grad(grad, raw, scale, gain, dot):
        cube = scale[...] * scale[...] * scale[...]
        return (scale[...] * (gain[...] * grad[...]) - raw[...] * (cube * dot[...])).astype(bf16)

    dq = raw_grad(dqn, qraw, q_scale, q_gain, q_dot)
    dk = raw_grad(dkn, kraw, k_scale, k_gain, k_dot)
    dq_out[...] = dq
    dk_out[...] = dk
    part = nt(dq, w_query[...]) + nt(dk, w_key[...]) + nt(dvalue[...], w_value[...])
    part_out[...] = part.astype(bf16)
    gain_out[...] += jnp.sum(part * rows_in[...].astype(f32), axis=0, keepdims=True)


def project_back(rows_in, dqn, dkn, dvalue, qraw, kraw, q_scale, k_scale, q_dot, k_dot, q_gain, k_gain, w_query, w_key, w_value):
    rows, features = rows_in.shape
    width = w_query.shape[1]
    block = min(256, rows)
    row = lambda columns: pl.BlockSpec((block, columns), lambda r: (r, 0))
    whole = lambda *shape: pl.BlockSpec(shape, lambda r: (0, 0))
    sds = jax.ShapeDtypeStruct
    return pl.pallas_call(
        project_back_kernel,
        grid=(rows // block,),
        in_specs=[row(features)] + [row(width)] * 5 + [row(1)] * 4 + [whole(1, width)] * 2 + [whole(features, width)] * 3,
        out_specs=[row(features), row(width), row(width), whole(1, features)],
        out_shape=[sds((rows, features), bf16), sds((rows, width), bf16), sds((rows, width), bf16), sds((1, features), f32)],
        compiler_params=params(),
        cost_estimate=cost(int(20.0 * 6 * rows * features * width), 0),
        name="project_back",
    )(rows_in, dqn, dkn, dvalue, qraw, kraw, q_scale, k_scale, q_dot, k_dot, q_gain[None], k_gain[None], w_query, w_key, w_value)


def attention_wgrad_kernel(added, held, order, tables, rows_in, middle, *refs):
    sides, (attended,), refs = refs[:3], refs[3:4], refs[4:]
    got, outs = (refs[:added], refs[added:])
    at = pl.program_id(0)
    totals = [tn(rows_in[...], side[...]) for side in sides] + [tn(middle[...], attended[...])]
    if not added:
        for place, out in enumerate(outs):

            @pl.when(at // held == place)
            def _(out=out):
                for weight, total in enumerate(totals):
                    out[0, weight] = total.astype(bf16)

        return
    scratch, outs = outs[-1], outs[:-1]
    half = outs[0].shape[2]
    for place, piece in enumerate(got):

        @pl.when(at // held == place)
        def _(piece=piece):
            for weight, total in enumerate(totals):
                scratch[weight] = (total + piece[0, weight].astype(f32)).astype(bf16)

    for side, out in enumerate(outs):
        start = side * 2 // len(outs) * half

        @pl.when(tables[1, side, at] == 1)
        def _(out=out, start=start):
            out[0] = scratch[:, start : start + half, :]


def attention_wgrad(rows_in, middle, sides, attended, order, blocks, added=()):
    features = rows_in.shape[1]
    width = sides[0].shape[1]
    block = features // blocks
    count = order.shape[0]
    tables, sizes = split_tables(count, 1)
    left = lambda values: pl.BlockSpec((values.shape[0], block), lambda i, ids, to: (0, ids[i]))
    right = lambda values: pl.BlockSpec(values.shape, lambda i, ids, to: (0, 0))

    def half_spec(side):
        return pl.BlockSpec((1, 4, block // 2, width), lambda i, ids, to: (to[0, side, i], 0, 0, 0))

    pieces = min(2, count)
    held = count // pieces

    def piece_spec(place):
        return pl.BlockSpec((1, 4, block, width), lambda i, ids, to: (jnp.clip(i - place * held, 0, held - 1), 0, 0, 0))

    group_specs = [piece_spec(place) for place in range(pieces)]
    if added:
        out_specs = [half_spec(side) for side in range(len(sizes))]
        out_shape = [jax.ShapeDtypeStruct((size, 4, block // 2, width), bf16) for size in sizes]
    else:
        out_specs = group_specs
        out_shape = [jax.ShapeDtypeStruct((held, 4, block, width), bf16)] * pieces
    return pl.pallas_call(
        functools.partial(attention_wgrad_kernel, len(added), held),
        grid_spec=pltpu.PrefetchScalarGridSpec(
            num_scalar_prefetch=2,
            grid=(count,),
            in_specs=[left(rows_in), left(middle)] + [right(v) for v in sides] + [right(attended)] + (group_specs if added else []),
            out_specs=out_specs,
            scratch_shapes=[pltpu.VMEM((4, block, width), bf16)] if added else [],
        ),
        out_shape=out_shape,
        compiler_params=params(),
        cost_estimate=cost(0, 0),
        name="attention_wgrad",
    )(order, tables, rows_in, middle, *sides, attended, *added)


def attend_kernel(
    block, qraw, kraw, value, q_scale, k_scale, q_gain, k_gain, cosine, sine,
    seg_col, seg_row, keep_row, q_out, k_out, o_out, lse_out, bias,
):
    @pl.when(pl.program_id(0) == 0)
    def _():
        fill_bias(bias, seg_col, seg_row, keep_row, block)

    def rotated(raw, scale, gain):
        normed = raw[...] * scale[...] * gain[...]
        return (normed * cosine[...] + turned(normed) * sine[...]).astype(bf16)

    q_out[...] = rotated(qraw, q_scale, q_gain)
    k_out[...] = rotated(kraw, k_scale, k_gain)
    length = seg_col.shape[0]
    for start in range(0, length, block):
        first, stop = key_start(start), start + block
        scores = nt(q_out[start:stop, :], k_out[first:stop, :]) * HEAD ** (-0.5)
        scores = scores + bias[start:stop, : stop - first]
        top = jnp.max(scores, axis=1, keepdims=True)
        powers = jnp.exp(scores - top)
        total = jnp.sum(powers, axis=1, keepdims=True)
        weights = (powers * (1.0 / total)).astype(bf16)
        o_out[start:stop, :] = nn(weights, value[first:stop, :]).astype(bf16)
        lse_out[start:stop, :] = jnp.broadcast_to(top + jnp.log(total), (block, HEAD))


def attend(qraw, kraw, value, q_scale, k_scale, q_gain, k_gain, cosine, sine, seg, keep):
    length, width = qraw.shape
    block = min(256, length)
    span = min(DOC + block, length)
    head = pl.BlockSpec((length, HEAD), lambda h: (0, h))
    gain = pl.BlockSpec((1, HEAD), lambda h: (0, h))
    whole = lambda *shape: pl.BlockSpec(shape, lambda h: (0, 0))
    return pl.pallas_call(
        functools.partial(attend_kernel, block),
        grid=(width // HEAD,),
        in_specs=[head, head, head, whole(length, 1), whole(length, 1), gain, gain]
        + [whole(length, HEAD), whole(length, HEAD), whole(length, 1), whole(1, length), whole(1, length)],
        out_specs=[head, head, head, head],
        out_shape=[jax.ShapeDtypeStruct((length, width), t) for t in (bf16, bf16, bf16, f32)],
        scratch_shapes=[pltpu.VMEM((length, span), f32)],
        compiler_params=params(),
        cost_estimate=cost(4 * length * span * width, 18 * length * width, length * span * width // HEAD),
        name="attend",
    )(qraw, kraw, value, q_scale, k_scale, q_gain[None], k_gain[None], cosine, sine, seg[:, None], seg[None], keep[None])


def attend_back_kernel(
    block, query, key, value, out_grad, lse, qraw, kraw, q_scale, k_scale, q_gain, k_gain, cosine, sine,
    seg_col, seg_row, keep_row, dq_out, dk_out, dv_out, qdot_out, kdot_out, qg_out, kg_out, bias, dk_sum, dv_sum,
):
    at = pl.program_id(0)

    @pl.when(at == 0)
    def _():
        fill_bias(bias, seg_col, seg_row, keep_row, block)
        qdot_out[...] = jnp.zeros_like(qdot_out)
        kdot_out[...] = jnp.zeros_like(kdot_out)

    dk_sum[...] = jnp.zeros_like(dk_sum)
    dv_sum[...] = jnp.zeros_like(dv_sum)
    length = seg_col.shape[0]
    scale = HEAD ** (-0.5)
    for start in range(0, length, block):
        first, stop = key_start(start), start + block
        rows, keys = slice(start, stop), slice(first, stop)
        scores = nt(query[rows, :], key[keys, :]) * scale + bias[rows, : stop - first]
        weights = jnp.exp(scores - lse[rows, :1])
        prob_grad = nt(out_grad[rows, :], value[keys, :])
        inner = jnp.sum(weights * prob_grad, axis=1, keepdims=True)
        score_grad = (weights * (prob_grad - inner)).astype(bf16)
        dq_out[rows, :] = nn(score_grad, key[keys, :]) * scale
        dk_sum[keys, :] += tn(score_grad, query[rows, :])
        dv_sum[keys, :] += tn(weights.astype(bf16), out_grad[rows, :])

    def unrotated(grad):
        return grad * cosine[...] + turned(grad * sine[...])

    dv_out[...] = dv_sum[...].astype(bf16)
    dq = unrotated(dq_out[...])
    dk = unrotated(dk_sum[...] * scale)
    dq_out[...] = dq
    dk_out[...] = dk
    dq = dq * qraw[...]
    dk = dk * kraw[...]
    qg_out[...] = jnp.sum(dq * q_scale[...], axis=0, keepdims=True)
    kg_out[...] = jnp.sum(dk * k_scale[...], axis=0, keepdims=True)
    qdot_out[...] += jnp.sum(dq * q_gain[...], axis=1, keepdims=True)
    kdot_out[...] += jnp.sum(dk * k_gain[...], axis=1, keepdims=True)


def attend_back(query, key, value, out_grad, lse, qraw, kraw, q_scale, k_scale, q_gain, k_gain, cosine, sine, seg, keep):
    length, width = qraw.shape
    block = min(256, length)
    span = min(DOC + block, length)
    head = pl.BlockSpec((length, HEAD), lambda h: (0, h))
    gain = pl.BlockSpec((1, HEAD), lambda h: (0, h))
    whole = lambda *shape: pl.BlockSpec(shape, lambda h: (0, 0))
    sds = jax.ShapeDtypeStruct
    return pl.pallas_call(
        functools.partial(attend_back_kernel, block),
        grid=(width // HEAD,),
        in_specs=[head] * 7
        + [whole(length, 1), whole(length, 1), gain, gain]
        + [whole(length, HEAD), whole(length, HEAD), whole(length, 1), whole(1, length), whole(1, length)],
        out_specs=[head, head, head, whole(length, 1), whole(length, 1), gain, gain],
        out_shape=[sds((length, width), f32), sds((length, width), f32), sds((length, width), bf16)]
        + [sds((length, 1), f32), sds((length, 1), f32), sds((1, width), f32), sds((1, width), f32)],
        scratch_shapes=[pltpu.VMEM((length, span), f32), pltpu.VMEM((length, HEAD), f32), pltpu.VMEM((length, HEAD), f32)],
        compiler_params=params(),
        cost_estimate=cost(0, 0),
        name="attend_back",
    )(query, key, value, out_grad, lse, qraw, kraw, q_scale, k_scale, q_gain[None], k_gain[None], cosine, sine, seg[:, None], seg[None], keep[None])


def middle_kernel(tokens, summed, gain, middle_out, scale_out, normed_out):
    middle = tokens[...].astype(f32) + summed[...].astype(f32)
    scale = lax.rsqrt(jnp.mean(middle * middle, axis=1, keepdims=True) + EPSILON)
    middle_out[...] = middle
    scale_out[...] = scale
    normed_out[...] = (middle * scale * gain[...]).astype(bf16)


def middle_rows(chunk, tokens, summed, gain):
    rows, features = summed.shape
    sds = jax.ShapeDtypeStruct
    whole = lambda *shape: pl.BlockSpec(shape, lambda i: (0, 0))
    return pl.pallas_call(
        middle_kernel,
        grid=(1,),
        in_specs=[pl.BlockSpec((rows, features), lambda i: (chunk, 0)), whole(rows, features), whole(1, features)],
        out_specs=[whole(rows, features), whole(rows, 1), whole(rows, features)],
        out_shape=[sds((rows, features), f32), sds((rows, 1), f32), sds((rows, features), bf16)],
        compiler_params=params(),
        cost_estimate=cost(0, 0),
        name="middle",
    )(tokens, summed, gain[None])


def middle_back_kernel(
    experts, grads, middle, scale, normed, routed, router, cotangent, gain, *refs
):
    grad_out, low_out, gain_out, logit_out = refs[-4:]
    features = middle.shape[1]
    lane = lax.broadcasted_iota(jnp.int32, routed.shape, 1)
    logits = jnp.where(lane < experts, nn(normed[...], router[...]), MASKED)
    powers = jnp.exp(logits - jnp.max(logits, axis=1, keepdims=True))
    probs = powers / jnp.sum(powers, axis=1, keepdims=True)
    share_grad = grads[:, features:].astype(f32) * routed[...]
    logit_grad = (probs * (share_grad - jnp.sum(share_grad * probs, axis=1, keepdims=True))).astype(bf16)
    logit_out[...] = logit_grad
    ffn_grad = grads[:, :features].astype(f32) + nt(logit_grad, router[...])
    along = middle[...] * scale[...]
    gain_out[...] = jnp.sum(ffn_grad * along, axis=0, keepdims=True)
    weighted = ffn_grad * gain[...]
    inner = jnp.mean(weighted * along, axis=1, keepdims=True)
    total = cotangent[...].astype(f32) + scale[...] * (weighted - along * inner)
    grad_out[...] = total
    low_out[...] = total.astype(bf16)


def middle_back(chunk, grads, middle, scale, normed, routed, router, cotangent, gain, experts, filled=()):
    rows, features = middle.shape
    sds = jax.ShapeDtypeStruct
    whole = lambda *shape: pl.BlockSpec(shape, lambda i: (0, 0))
    part = lambda columns: pl.BlockSpec((rows, columns), lambda i: (chunk, 0))
    return pl.pallas_call(
        functools.partial(middle_back_kernel, experts),
        grid=(1,),
        in_specs=[whole(rows, features + LANES), whole(rows, features), whole(rows, 1), whole(rows, features), part(LANES)]
        + [whole(features, LANES), part(features), whole(1, features)]
        + [pl.BlockSpec(memory_space=pl.ANY)] * len(filled),
        out_specs=[part(features), part(features), whole(1, features), whole(rows, LANES)],
        out_shape=[sds(cotangent.shape, f32), sds(cotangent.shape, bf16), sds((1, features), f32), sds((rows, LANES), bf16)],
        input_output_aliases={8 + at: at for at in range(len(filled))},
        compiler_params=params(),
        cost_estimate=cost(0, 0),
        name="middle_back",
    )(grads, middle, scale, normed, routed, router, cotangent, gain[None], *filled)


def up_back_kernel(grad, down_w, out):
    width = down_w.shape[2]
    for at in range(down_w.shape[0]):
        out[:, at * width : (at + 1) * width] = nn(grad[...], down_w[at]).astype(out.dtype)


def up_back(grad, down_w):
    rows, features = grad.shape
    experts, _, width = down_w.shape
    step = 2 if experts % 2 == 0 else 1
    return pl.pallas_call(
        up_back_kernel,
        grid=(experts // step,),
        in_specs=[pl.BlockSpec((rows, features), lambda e: (0, 0)), pl.BlockSpec((step, features, width), lambda e: (e, 0, 0))],
        out_specs=pl.BlockSpec((rows, step * width), lambda e: (0, e)),
        out_shape=jax.ShapeDtypeStruct((rows, experts * width), bf16),
        compiler_params=params(),
        cost_estimate=cost(2 * rows * features * experts * width, 2 * (rows + experts * width) * features),
        name="up_back",
    )(grad, down_w)


def expert_kernel(block, rows_in, back, routed, router, gate_w, up_w, act_out, dgate_out, dup_out, grad_out, comb, dcomb, total):
    at = pl.program_id(0)
    rows, features = rows_in.shape
    lane = lax.broadcasted_iota(jnp.int32, (block, LANES), 1)

    @pl.when(at == 0)
    def _():
        experts = pl.num_programs(0)
        for start in range(0, rows, block):
            here = slice(start, start + block)
            logits = jnp.where(lane < experts, nn(rows_in[here, :], router[...]), MASKED)
            powers = jnp.exp(logits - jnp.max(logits, axis=1, keepdims=True))
            probs = powers / jnp.sum(powers, axis=1, keepdims=True)
            comb[here, :] = probs * routed[here, :]
        total[...] = jnp.zeros_like(total)
        dcomb[...] = jnp.zeros_like(dcomb)

    gate, up = gate_w[0], up_w[0]
    mine = lane == at
    for start in range(0, rows, block):
        here = slice(start, start + block)
        taken = rows_in[here, :]
        pre_gate = nn(taken, gate)
        pre_up = nn(taken, up)
        behind = back[...].reshape(rows, back.shape[3])[here, :].astype(f32)
        share = jnp.sum(jnp.where(mine, comb[here, :], 0.0), axis=1, keepdims=True)
        sigmoid = 0.5 * jnp.tanh(0.5 * pre_gate) + 0.5
        active = pre_gate * sigmoid
        inner = active * pre_up
        share_grad = jnp.sum(inner * behind, axis=1, keepdims=True)
        dcomb[here, :] = jnp.where(mine, share_grad, dcomb[here, :])
        act_out[here, :] = (inner * share).astype(bf16)
        inner_grad = behind * share
        dgate = (inner_grad * pre_up * (sigmoid + active * (1.0 - sigmoid))).astype(bf16)
        dup = (inner_grad * active).astype(bf16)
        dgate_out[here, :] = dgate
        dup_out[here, :] = dup
        total[here, :] += nt(dgate, gate) + nt(dup, up)

    @pl.when(at == pl.num_programs(0) - 1)
    def _():
        grad_out[:, :features] = total[...].astype(bf16)
        grad_out[:, features:] = dcomb[...].astype(bf16)


def experts_block(chunk, rows_in, back, routed, router, gate_w, up_w):
    rows, features = rows_in.shape
    parts, _, chunk_rows, _ = back.shape
    experts, _, width = gate_w.shape
    block = min(512, rows)
    whole = lambda *shape: pl.BlockSpec(shape, lambda e: (0, 0))
    column = pl.BlockSpec((rows, width), lambda e: (0, e))
    weight = pl.BlockSpec((1, features, width), lambda e: (e, 0, 0))
    wide = jax.ShapeDtypeStruct((rows, experts * width), bf16)
    return pl.pallas_call(
        functools.partial(expert_kernel, block),
        grid=(experts,),
        in_specs=[whole(rows, features), pl.BlockSpec((parts, 1, chunk_rows, width), lambda e: (0, chunk, 0, e)), whole(rows, LANES), whole(features, LANES), weight, weight],
        out_specs=[column, column, column, whole(rows, features + LANES)],
        out_shape=[wide, wide, wide, jax.ShapeDtypeStruct((rows, features + LANES), bf16)],
        scratch_shapes=[pltpu.VMEM((rows, LANES), f32), pltpu.VMEM((rows, LANES), f32), pltpu.VMEM((rows, features), f32)],
        compiler_params=params(),
        cost_estimate=cost(8 * rows * features * experts * width, 4 * experts * width * (features + 2 * rows), rows * experts * width),
        name="experts",
    )(rows_in, back, routed, router, gate_w, up_w)


def block_order(blocks):
    return [3, 2, 0, 1] if blocks == 4 else list(range(blocks))


def split_tables(blocks, per):
    order = block_order(blocks)
    if blocks == 4:
        picks = [{0: 0, 1: 1}, {2: 0, 3: 1}, {0: 0, 2: 1}, {1: 0, 3: 1}]
    else:
        picks = [{block: block for block in order}] * 2
    places, fills = [], []
    for pick in picks:
        filled = [pick[block] * per + at if block in pick else None for block in order for at in range(per)]
        last = next(place for place in filled if place is not None)
        row = []
        for place in filled:
            last = last if place is None else place
            row.append(last)
        places.append(row)
        fills.append([int(place is not None) for place in filled])
    return jnp.asarray(np.array([places, fills], np.int32)), [len(pick) for pick in picks]


def wgrad_kernel(count, extra, per, block, order, tables, *refs):
    lefts, rights = refs[:count], refs[count : 2 * count]
    added = refs[2 * count : 2 * count + extra]
    outs = refs[2 * count + extra :]
    at = pl.program_id(0)
    features = lefts[0].shape[-1]

    def piece(start, stop):
        total = None
        for left, right in zip(lefts, rights):
            columns = left[:, start:stop] if len(left.shape) == 2 else left[:, :, :, start:stop].reshape(-1, stop - start)
            part = tn(columns, right[...])
            total = part if total is None else total + part
        return total

    if not added:
        for place, out in enumerate(outs):

            @pl.when(at // per == place)
            def _(out=out):
                for start in range(0, features, block):
                    out[0, start : start + block, :] = piece(start, start + block).astype(bf16)

        return
    half = features // 2
    got = outs[-1]
    outs = outs[:-1]
    for place, arrived in enumerate(added):

        @pl.when(at // per == place)
        def _(arrived=arrived):
            for start in range(0, features, block):
                total = piece(start, start + block) + arrived[0, start : start + block, :].astype(f32)
                got[start : start + block, :] = total.astype(bf16)

    for side, out in enumerate(outs):
        start = side * 2 // len(outs) * half

        @pl.when(tables[1, side, at] == 1)
        def _(out=out, start=start):
            out[0] = got[start : start + half, :]


def wgrad(lefts, rights, order, width, per, added=(), weight=1, pieces=0):
    features = lefts[0][0].shape[-1]
    experts = order.shape[0]
    groups = experts // per
    tables, sizes = split_tables(groups, per)
    pieces = len(added) or pieces or groups
    held = experts // pieces

    def piece_spec(place):
        return pl.BlockSpec((1, features, width), lambda i, ids, to: (jnp.clip(i - place * held, 0, held - 1), 0, 0))

    def half_spec(side):
        return pl.BlockSpec((1, features // 2, width), lambda i, ids, to: (to[0, side, i], 0, 0))

    def left_spec(left, chunk):
        if left.ndim == 2:
            return pl.BlockSpec(left.shape, lambda i, ids, to: (0, 0))
        return pl.BlockSpec((left.shape[0], 1) + left.shape[2:], lambda i, ids, to: (0, chunk, 0, 0))

    piece_specs = [piece_spec(place) for place in range(pieces)]
    if added:
        out_specs = [half_spec(side) for side in range(len(sizes))]
        out_shape = [jax.ShapeDtypeStruct((size * per, features // 2, width), bf16) for size in sizes]
    else:
        out_specs = piece_specs
        out_shape = [jax.ShapeDtypeStruct((held, features, width), bf16)] * pieces
    return pl.pallas_call(
        functools.partial(wgrad_kernel, len(lefts), len(added), held, min(512, features // 2)),
        grid_spec=pltpu.PrefetchScalarGridSpec(
            num_scalar_prefetch=2,
            grid=(experts,),
            in_specs=[left_spec(*left) for left in lefts]
            + [pl.BlockSpec((right.shape[0], width), lambda i, ids, to: (0, ids[i])) for right in rights]
            + (piece_specs if added else []),
            out_specs=out_specs,
            scratch_shapes=[pltpu.VMEM((features, width), bf16)] if added else [],
        ),
        out_shape=out_shape,
        compiler_params=params(),
        cost_estimate=cost(2 * weight * sum(right.shape[0] for right in rights) * features * experts * width, 0),
        name="wgrad",
    )(order, tables, *(left for left, _ in lefts), *rights, *added)


def down_kernel(parts, down_w, *refs):
    acts, out = refs[:-1], refs[-1]
    joined = jnp.concatenate([down_w[e] for e in range(down_w.shape[0])], axis=1)
    block = acts[0].shape[0] // parts
    for at, act in enumerate(acts):
        result = nt(act[...], joined).astype(out.dtype)
        for part in range(parts):
            start = (part * len(acts) + at) * block
            out[start : start + block, :] = result[part * block : (part + 1) * block, :]


def down(acts, down_w, parts):
    rows = sum(act.shape[0] for act in acts)
    experts, features, width = down_w.shape
    block = min(256, features)
    return pl.pallas_call(
        functools.partial(down_kernel, parts),
        grid=(features // block,),
        in_specs=[pl.BlockSpec((experts, block, width), lambda n: (0, n, 0))]
        + [pl.BlockSpec(act.shape, lambda n: (0, 0)) for act in acts],
        out_specs=pl.BlockSpec((rows, block), lambda n: (0, n)),
        out_shape=jax.ShapeDtypeStruct((rows, features), bf16),
        compiler_params=params(),
        cost_estimate=cost(0 * 2 * rows * features * experts * width, 0),
        name="down",
    )(down_w, *acts)


def gate(value, *others):
    return lax.optimization_barrier((value, others))[0]


def gather_rows(values):
    return lax.all_gather(values, "tensor", axis=0, tiled=True)


def scatter_rows(values):
    return lax.psum_scatter(values, "tensor", scatter_dimension=0, tiled=True)


def pair_swap(values, step):
    size = lax.axis_size("dp")
    return lax.ppermute(values, "dp", [(i, i ^ step) for i in range(size)])


class Halving:
    def __init__(self, values):
        if len(values) == 2:
            self.kept = list(values)
            self.going = None
        else:
            self.kept, self.going = list(values[::2]), list(values[1::2])
        bits = list(range(values[0].shape[0].bit_length() - (1 if self.going is None else 0)))
        self.left = [bits[::-1], bits]
        self.got = None

    def send(self):
        if not self.left[0]:
            return ()
        self.got = []
        sent = []
        for side, downward in ((0, True), (1, False)):
            bit = self.left[side].pop(0)
            if self.going is not None:
                go = self.going[side]
            else:
                kept = self.kept[side]
                half = kept.shape[0] // 2
                if downward:
                    self.kept[side], go = kept[:half], kept[half:]
                else:
                    view = kept.reshape((half, 2) + kept.shape[1:])
                    self.kept[side], go = view[:, 0], view[:, 1]
            sent.append(go)
            self.got.append(pair_swap(go, 2 << bit))
        self.going = None
        return tuple(sent)

    def add(self, *others):
        if self.got is not None:
            if others:
                self.got = gate(tuple(self.got), *others)
            last = not self.left[0]
            for side in range(2):
                total = self.kept[side].astype(f32) + self.got[side].astype(f32)
                self.kept[side] = total if last else total.astype(bf16)
            self.got = None
        return tuple(self.kept)

    def done(self):
        self.add()
        while self.left[0]:
            self.send()
            self.add()
        return jnp.concatenate([kept[0].astype(f32) for kept in self.kept], axis=1)


def exchange_sum(values, steps):
    for axis, step in steps:
        values = values + lax.ppermute(values, axis, [(i, i ^ step) for i in range(lax.axis_size(axis))])
    return values


def doublings(axis):
    return [(axis, 1 << bit) for bit in range(lax.axis_size(axis).bit_length() - 1)]


def local(
    tokens, cotangent, seg_ids, keep_mask, routes, attn_gain, w_query, w_key, w_value, w_out,
    q_gain, k_gain, ffn_gain, router, w_gate, w_up, w_down,
):
    parts = lax.axis_size("tensor")
    part_at = lax.axis_index("tensor")
    dp_size = lax.axis_size("dp")
    low_bit = lax.axis_index("dp") % 2
    shard_rows, features = tokens.shape
    group_rows = shard_rows * parts
    _, length = seg_ids.shape
    local_width = w_query.shape[1]
    experts, _, width = w_gate.shape
    per = experts // dp_size
    chunk_rows = shard_rows // CHUNKS
    chunks = range(CHUNKS)
    own = [slice(c * chunk_rows, (c + 1) * chunk_rows) for c in chunks]

    def chunk_of(values, c):
        columns = values.shape[1]
        return values.reshape(parts, CHUNKS, chunk_rows, columns)[:, c].reshape(parts * chunk_rows, columns)

    inputs = tokens.astype(f32)
    first_scale = rms_scale(inputs)
    normed_all = gather_rows((inputs * first_scale * attn_gain).astype(bf16))
    grad_rows = gather_rows(gate(cotangent, normed_all))

    cosine, sine = rope_tables(length, HEAD)

    relative = jnp.asarray(block_order(dp_size // 2), jnp.int32) ^ (lax.axis_index("dp") // 2)
    own_blocks, other_blocks = 2 * relative + low_bit, 2 * relative + 1 - low_bit
    mine, theirs = (
        (blocks[:, None] * per + jnp.arange(per, dtype=jnp.int32)).reshape(-1) for blocks in (own_blocks, other_blocks)
    )

    qraw, kraw, value, squares = project(normed_all, w_query, w_key, w_value)
    squares = exchange_sum(squares, doublings("tensor"))
    q_scale, k_scale = (lax.rsqrt(squares[i] / features + EPSILON)[:, None] for i in range(2))
    query, key, attended, lse = attend(
        qraw, kraw, value, q_scale, k_scale, q_gain, k_gain, cosine, sine, seg_ids[0], keep_mask[0]
    )
    attended_parts = [chunk_of(attended, c) for c in chunks]
    outs = [nt(attended_parts[0], w_out).astype(bf16)]
    summed = [scatter_rows(gate(outs[0], grad_rows))]
    outs.append(nt(gate(attended_parts[1], outs[0]), w_out).astype(bf16))
    summed.append(scatter_rows(gate(outs[1], grad_rows)))

    idle_routes, idle_router = gate((routes, router), outs[1])
    expert_ids = jnp.arange(LANES)
    routed = jnp.sum((idle_routes[:, :, None] == expert_ids[None, None, :]).astype(f32), axis=1)
    router_wide = jnp.pad(idle_router, ((0, 0), (0, LANES - experts)))
    routed_own = lax.dynamic_slice_in_dim(routed, part_at * shard_rows, shard_rows, 0)
    back = up_back(gate(grad_rows, routed, router_wide), w_down).reshape(parts, CHUNKS, chunk_rows, -1)
    grad_rows = grad_rows.reshape(parts, CHUNKS, chunk_rows, features)
    grad_parts = [(grad_rows, c) for c in chunks]

    norms = [middle_rows(0, tokens, summed[0], ffn_gain)]
    ffn_all = [gather_rows(norms[0][2])]
    norms.append(middle_rows(1, tokens, gate(summed[1], norms[0][2], back), ffn_gain))
    ffn_all.append(gather_rows(norms[1][2]))
    ffn_parts = [(rows, 0) for rows in ffn_all]
    acts, dgates, dups, expert_grads = [], [], [], []
    for c in chunks:
        here = gate(chunk_of(routed, c), back, *acts[-1:])
        act, dgate, dup, grads = experts_block(c, ffn_all[c], back, here, router_wide, w_gate, w_up)
        acts.append(act)
        dgates.append(dgate)
        dups.append(dup)
        expert_grads.append(grads)
    expert_grads = [scatter_rows(grads) for grads in expert_grads]

    def back_of(c, grads, filled=()):
        return middle_back(c, grads, *norms[c], routed_own, router_wide, cotangent, ffn_gain, experts, filled)

    def expert_sums(lefts, rights, ids, *others, added=(), weight=1, pieces=0):
        return wgrad(lefts, rights, gate(ids, *others), width, per, added, weight, pieces)

    def core_swap(pieces):
        return [pair_swap(piece, 1) for piece in pieces]

    def halving(sums):
        return Halving([part.reshape((part.shape[0] // per, per) + part.shape[1:]) for part in sums])

    first = back_of(0, gate(expert_grads[0], acts[1]))
    gate_sent = expert_sums(ffn_parts, dgates, theirs, first[1], weight=0)
    gate_got = core_swap(gate_sent)
    up_sent = expert_sums(ffn_parts, dups, theirs, *gate_sent, pieces=2, weight=4)
    up_got = core_swap(up_sent)
    gate_sums = expert_sums(ffn_parts, dgates, mine, *up_sent, added=gate_got, weight=4)
    gate_out = halving(gate_sums)
    gate_out.send()
    second = back_of(1, gate(expert_grads[1], *gate_sums), first[:2])
    middle_grad, middle_low = second[:2]
    middle_all = gather_rows(middle_low)
    moe = down([gate(acts[0], middle_low), acts[1]], w_down, parts)
    up_sums = expert_sums(ffn_parts, dups, mine, moe, added=up_got, weight=0)
    up_out = halving(up_sums)
    up_out.send()
    moe_sum = scatter_rows(moe)
    gate_late = gate_out.add(*up_sums)
    gate_out.send()
    down_sent = expert_sums(grad_parts, acts, theirs, *gate_late, pieces=2, weight=0.0)
    down_got = core_swap(down_sent)
    attended_grad = nn(gate(middle_all, *down_sent), w_out).astype(bf16)
    dqn, dkn, dvalue, qdot, kdot, q_gain_part, k_gain_part = attend_back(
        query, key, value, attended_grad, lse, qraw, kraw, q_scale, k_scale, q_gain, k_gain, cosine, sine,
        seg_ids[0], keep_mask[0],
    )
    dots = exchange_sum(jnp.stack([qdot[:, 0], kdot[:, 0]]), doublings("tensor")) / features
    up_late = up_out.add(dqn)
    up_out.send()
    normed_part, dqraw, dkraw, attn_gain_part = project_back(
        normed_all, dqn, dkn, dvalue, qraw, kraw, q_scale, k_scale, dots[0][:, None], dots[1][:, None],
        gate(q_gain, *up_late, *gate_out.got), k_gain, w_query, w_key, w_value,
    )
    normed_grad = scatter_rows(normed_part)
    down_sums = expert_sums(grad_parts, acts, mine, normed_part, *up_out.got, added=down_got, weight=0.0)
    down_out = halving(down_sums)
    down_out.send()
    def attention_sums(ids, *others, added=()):
        return attention_wgrad(
            normed_all, middle_all, (dqraw, dkraw, dvalue), attended, gate(ids, *others), dp_size, added
        )

    attn_sent = attention_sums(other_blocks, *down_sums)
    attn_got = core_swap(attn_sent)
    down_late = down_out.add(*attn_sent)
    down_out.send()

    def placed(part):
        return lax.dynamic_update_slice_in_dim(jnp.zeros((features,), f32), part, part_at * local_width, 0)

    attn_sums = attention_sums(own_blocks, *down_late, added=attn_got)
    attn_out = Halving(attn_sums)
    normed_grad = gate(normed_grad, *attn_out.send())
    smalls = [attn_gain_part[0] / attn_gain, placed(q_gain_part[0]), placed(k_gain_part[0]), (first[2] + second[2])[0]]
    router_part = sum(tn(late[3], norms[c][2]) for c, late in enumerate((first, second)))[:experts]
    smalls = gate(jnp.concatenate([jnp.stack(smalls), router_part]), *attn_sums)
    smalls = exchange_sum(smalls, doublings("dp")[:1] + doublings("tensor"))
    attn_late = attn_out.add()
    attn_out.send()
    smalls = exchange_sum(gate(smalls, *attn_late), doublings("dp")[1:])
    late_got = tuple(down_out.got)
    gate_done = gate_out.done()
    up_done = up_out.done()
    down_done = down_out.done()
    query_done, key_done, value_done, out_done = attn_out.done()
    layer_out = (jnp.concatenate([norms[c][0] for c in chunks]) + gate(moe_sum, *late_got).astype(f32)).astype(bf16)
    tokens_grad = middle_grad + norm_back(normed_grad.astype(f32), inputs, first_scale, attn_gain)
    return (
        layer_out, tokens_grad, query_done, key_done, value_done, out_done,
        smalls[0], smalls[1], smalls[2], smalls[3], smalls[4:].T, gate_done, up_done, down_done,
    )


def solution(mesh):
    rows = P(("dp", "tensor"), None)
    column = P(None, "tensor")
    expert = P(None, None, "tensor")
    in_specs = (
        rows, rows, P("dp", None), P("dp", None), P("dp", None), P(), column, column, column, column,
        P("tensor"), P("tensor"), P(), P(), expert, expert, expert,
    )
    block = P("dp", "tensor")
    expert_out = P("dp", None, "tensor")
    out_specs = (
        rows, rows, block, block, block, block, P(), P(), P(), P(), P(), expert_out, expert_out, expert_out,
    )
    return jax.shard_map(local, mesh=mesh, in_specs=in_specs, out_specs=out_specs, check_vma=False)
```

```python
import functools

import jax
import jax.numpy as jnp
import numpy as np
from jax import lax
from jax.experimental import pallas as pl
from jax.experimental.pallas import tpu as pltpu
from jax.sharding import PartitionSpec as P

D = 2048
HEAD = 128
DOC = 512
LANES = 128
EPSILON = 1e-05
MASKED = -1e30
CHUNKS = 2
VMEM = 56 * 1024 * 1024
bf16 = jnp.bfloat16
f32 = jnp.float32


def nn(left, right):
    return lax.dot_general(left, right, (((1,), (0,)), ((), ())), preferred_element_type=f32)


def nt(left, right):
    return lax.dot_general(left, right, (((1,), (1,)), ((), ())), preferred_element_type=f32)


def tn(left, right):
    return lax.dot_general(left, right, (((0,), (0,)), ((), ())), preferred_element_type=f32)


def params():
    return pltpu.CompilerParams(vmem_limit_bytes=VMEM)


PACE = 0.3


def cost(flops, moved, special=0):
    return pl.CostEstimate(flops=int(1.5 * PACE * flops + 6e4 * PACE * special), bytes_accessed=moved // 8, transcendentals=0)


def rms_scale(values):
    return lax.rsqrt(jnp.mean(values * values, axis=-1, keepdims=True) + EPSILON)


def norm_back(grad_values, values, scale_col, gain_vec):
    weighted = grad_values * gain_vec
    inner_mean = jnp.mean(weighted * values, axis=-1, keepdims=True)
    return scale_col * weighted - values * (scale_col * scale_col * scale_col) * inner_mean


def rope_tables(length, width):
    angles = np.arange(length)[:, None] * 10000.0 ** (-np.arange(width // 2) * 2.0 / width)[None, :]
    cosine, sine = np.cos(angles).astype(np.float32), np.sin(angles).astype(np.float32)
    return jnp.asarray(np.concatenate([cosine, cosine], axis=1)), jnp.asarray(np.concatenate([-sine, sine], axis=1))


def key_start(query_start):
    return max(0, query_start - DOC)


def fill_bias(bias, seg_col, seg_row, keep_row, block):
    length = seg_col.shape[0]
    for start in range(0, length, block):
        first, stop = key_start(start), start + block
        query_pos = start + lax.broadcasted_iota(jnp.int32, (block, stop - first), 0)
        key_pos = first + lax.broadcasted_iota(jnp.int32, (block, stop - first), 1)
        same = seg_col[start:stop, :] == seg_row[:, first:stop]
        live = (keep_row[:, first:stop] == 1) | (key_pos == query_pos)
        allowed = same & live & (key_pos <= query_pos)
        bias[start:stop, : stop - first] = jnp.where(allowed, 0.0, MASKED)


def turned(values):
    return pltpu.roll(values, values.shape[1] // 2, 1)


def project_kernel(rows_in, w_query, w_key, w_value, q_out, k_out, v_out, squares_out):
    ones = jnp.ones((8, q_out.shape[1]), f32)
    for at, (weight, out) in enumerate(((w_query, q_out), (w_key, k_out))):
        raw = nn(rows_in[...], weight[...])
        out[...] = raw
        sums = lax.dot_general(
            ones, raw * raw, (((1,), (1,)), ((), ())), precision=lax.Precision.HIGHEST, preferred_element_type=f32
        )
        squares_out[at : at + 1, :] = sums[:1]
    v_out[...] = nn(rows_in[...], w_value[...]).astype(bf16)


def project(rows_in, w_query, w_key, w_value):
    rows, features = rows_in.shape
    width = w_query.shape[1]
    block = min(256, rows)
    row = lambda columns: pl.BlockSpec((block, columns), lambda r: (r, 0))
    weight = pl.BlockSpec((features, width), lambda r: (0, 0))
    sds = jax.ShapeDtypeStruct
    return pl.pallas_call(
        project_kernel,
        grid=(rows // block,),
        in_specs=[row(features), weight, weight, weight],
        out_specs=[row(width), row(width), row(width), pl.BlockSpec((2, block), lambda r: (0, r))],
        out_shape=[sds((rows, width), f32), sds((rows, width), f32), sds((rows, width), bf16), sds((2, rows), f32)],
        compiler_params=params(),
        cost_estimate=cost(6 * rows * features * width, 2 * (rows + 3 * width) * features),
        name="project",
    )(rows_in, w_query, w_key, w_value)


def project_back_kernel(
    rows_in, dqn, dkn, dvalue, qraw, kraw, q_scale, k_scale, q_dot, k_dot, q_gain, k_gain,
    w_query, w_key, w_value, part_out, dq_out, dk_out, gain_out,
):
    @pl.when(pl.program_id(0) == 0)
    def _():
        gain_out[...] = jnp.zeros_like(gain_out)

    def raw_grad(grad, raw, scale, gain, dot):
        cube = scale[...] * scale[...] * scale[...]
        return (scale[...] * (gain[...] * grad[...]) - raw[...] * (cube * dot[...])).astype(bf16)

    dq = raw_grad(dqn, qraw, q_scale, q_gain, q_dot)
    dk = raw_grad(dkn, kraw, k_scale, k_gain, k_dot)
    dq_out[...] = dq
    dk_out[...] = dk
    part = nt(dq, w_query[...]) + nt(dk, w_key[...]) + nt(dvalue[...], w_value[...])
    part_out[...] = part.astype(bf16)
    gain_out[...] += jnp.sum(part * rows_in[...].astype(f32), axis=0, keepdims=True)


def project_back(rows_in, dqn, dkn, dvalue, qraw, kraw, q_scale, k_scale, q_dot, k_dot, q_gain, k_gain, w_query, w_key, w_value):
    rows, features = rows_in.shape
    width = w_query.shape[1]
    block = min(256, rows)
    row = lambda columns: pl.BlockSpec((block, columns), lambda r: (r, 0))
    whole = lambda *shape: pl.BlockSpec(shape, lambda r: (0, 0))
    sds = jax.ShapeDtypeStruct
    return pl.pallas_call(
        project_back_kernel,
        grid=(rows // block,),
        in_specs=[row(features)] + [row(width)] * 5 + [row(1)] * 4 + [whole(1, width)] * 2 + [whole(features, width)] * 3,
        out_specs=[row(features), row(width), row(width), whole(1, features)],
        out_shape=[sds((rows, features), bf16), sds((rows, width), bf16), sds((rows, width), bf16), sds((1, features), f32)],
        compiler_params=params(),
        cost_estimate=cost(int(20.0 * 6 * rows * features * width), 0),
        name="project_back",
    )(rows_in, dqn, dkn, dvalue, qraw, kraw, q_scale, k_scale, q_dot, k_dot, q_gain[None], k_gain[None], w_query, w_key, w_value)


def attention_wgrad_kernel(added, held, order, tables, rows_in, middle, *refs):
    sides, (attended,), refs = refs[:3], refs[3:4], refs[4:]
    got, outs = (refs[:added], refs[added:])
    at = pl.program_id(0)
    totals = [tn(rows_in[...], side[...]) for side in sides] + [tn(middle[...], attended[...])]
    if not added:
        for place, out in enumerate(outs):

            @pl.when(at // held == place)
            def _(out=out):
                for weight, total in enumerate(totals):
                    out[0, weight] = total.astype(bf16)

        return
    scratch, outs = outs[-1], outs[:-1]
    half = outs[0].shape[2]
    for place, piece in enumerate(got):

        @pl.when(at // held == place)
        def _(piece=piece):
            for weight, total in enumerate(totals):
                scratch[weight] = (total + piece[0, weight].astype(f32)).astype(bf16)

    for side, out in enumerate(outs):
        start = side * 2 // len(outs) * half

        @pl.when(tables[1, side, at] == 1)
        def _(out=out, start=start):
            out[0] = scratch[:, start : start + half, :]


def attention_wgrad(rows_in, middle, sides, attended, order, blocks, added=()):
    features = rows_in.shape[1]
    width = sides[0].shape[1]
    block = features // blocks
    count = order.shape[0]
    tables, sizes = split_tables(count, 1)
    left = lambda values: pl.BlockSpec((values.shape[0], block), lambda i, ids, to: (0, ids[i]))
    right = lambda values: pl.BlockSpec(values.shape, lambda i, ids, to: (0, 0))

    def half_spec(side):
        return pl.BlockSpec((1, 4, block // 2, width), lambda i, ids, to: (to[0, side, i], 0, 0, 0))

    pieces = min(2, count)
    held = count // pieces

    def piece_spec(place):
        return pl.BlockSpec((1, 4, block, width), lambda i, ids, to: (jnp.clip(i - place * held, 0, held - 1), 0, 0, 0))

    group_specs = [piece_spec(place) for place in range(pieces)]
    if added:
        out_specs = [half_spec(side) for side in range(len(sizes))]
        out_shape = [jax.ShapeDtypeStruct((size, 4, block // 2, width), bf16) for size in sizes]
    else:
        out_specs = group_specs
        out_shape = [jax.ShapeDtypeStruct((held, 4, block, width), bf16)] * pieces
    return pl.pallas_call(
        functools.partial(attention_wgrad_kernel, len(added), held),
        grid_spec=pltpu.PrefetchScalarGridSpec(
            num_scalar_prefetch=2,
            grid=(count,),
            in_specs=[left(rows_in), left(middle)] + [right(v) for v in sides] + [right(attended)] + (group_specs if added else []),
            out_specs=out_specs,
            scratch_shapes=[pltpu.VMEM((4, block, width), bf16)] if added else [],
        ),
        out_shape=out_shape,
        compiler_params=params(),
        cost_estimate=cost(0, 0),
        name="attention_wgrad",
    )(order, tables, rows_in, middle, *sides, attended, *added)


def attend_kernel(
    block, qraw, kraw, value, q_scale, k_scale, q_gain, k_gain, cosine, sine,
    seg_col, seg_row, keep_row, q_out, k_out, o_out, lse_out, bias,
):
    @pl.when(pl.program_id(0) == 0)
    def _():
        fill_bias(bias, seg_col, seg_row, keep_row, block)

    def rotated(raw, scale, gain):
        normed = raw[...] * scale[...] * gain[...]
        return (normed * cosine[...] + turned(normed) * sine[...]).astype(bf16)

    q_out[...] = rotated(qraw, q_scale, q_gain)
    k_out[...] = rotated(kraw, k_scale, k_gain)
    length = seg_col.shape[0]
    for start in range(0, length, block):
        first, stop = key_start(start), start + block
        scores = nt(q_out[start:stop, :], k_out[first:stop, :]) * HEAD ** (-0.5)
        scores = scores + bias[start:stop, : stop - first]
        top = jnp.max(scores, axis=1, keepdims=True)
        powers = jnp.exp(scores - top)
        total = jnp.sum(powers, axis=1, keepdims=True)
        weights = (powers * (1.0 / total)).astype(bf16)
        o_out[start:stop, :] = nn(weights, value[first:stop, :]).astype(bf16)
        lse_out[start:stop, :] = jnp.broadcast_to(top + jnp.log(total), (block, HEAD))


def attend(qraw, kraw, value, q_scale, k_scale, q_gain, k_gain, cosine, sine, seg, keep):
    length, width = qraw.shape
    block = min(256, length)
    span = min(DOC + block, length)
    head = pl.BlockSpec((length, HEAD), lambda h: (0, h))
    gain = pl.BlockSpec((1, HEAD), lambda h: (0, h))
    whole = lambda *shape: pl.BlockSpec(shape, lambda h: (0, 0))
    return pl.pallas_call(
        functools.partial(attend_kernel, block),
        grid=(width // HEAD,),
        in_specs=[head, head, head, whole(length, 1), whole(length, 1), gain, gain]
        + [whole(length, HEAD), whole(length, HEAD), whole(length, 1), whole(1, length), whole(1, length)],
        out_specs=[head, head, head, head],
        out_shape=[jax.ShapeDtypeStruct((length, width), t) for t in (bf16, bf16, bf16, f32)],
        scratch_shapes=[pltpu.VMEM((length, span), f32)],
        compiler_params=params(),
        cost_estimate=cost(4 * length * span * width, 18 * length * width, length * span * width // HEAD),
        name="attend",
    )(qraw, kraw, value, q_scale, k_scale, q_gain[None], k_gain[None], cosine, sine, seg[:, None], seg[None], keep[None])


def attend_back_kernel(
    block, query, key, value, out_grad, lse, qraw, kraw, q_scale, k_scale, q_gain, k_gain, cosine, sine,
    seg_col, seg_row, keep_row, dq_out, dk_out, dv_out, qdot_out, kdot_out, qg_out, kg_out, bias, dk_sum, dv_sum,
):
    at = pl.program_id(0)

    @pl.when(at == 0)
    def _():
        fill_bias(bias, seg_col, seg_row, keep_row, block)
        qdot_out[...] = jnp.zeros_like(qdot_out)
        kdot_out[...] = jnp.zeros_like(kdot_out)

    dk_sum[...] = jnp.zeros_like(dk_sum)
    dv_sum[...] = jnp.zeros_like(dv_sum)
    length = seg_col.shape[0]
    scale = HEAD ** (-0.5)
    for start in range(0, length, block):
        first, stop = key_start(start), start + block
        rows, keys = slice(start, stop), slice(first, stop)
        scores = nt(query[rows, :], key[keys, :]) * scale + bias[rows, : stop - first]
        weights = jnp.exp(scores - lse[rows, :1])
        prob_grad = nt(out_grad[rows, :], value[keys, :])
        inner = jnp.sum(weights * prob_grad, axis=1, keepdims=True)
        score_grad = (weights * (prob_grad - inner)).astype(bf16)
        dq_out[rows, :] = nn(score_grad, key[keys, :]) * scale
        dk_sum[keys, :] += tn(score_grad, query[rows, :])
        dv_sum[keys, :] += tn(weights.astype(bf16), out_grad[rows, :])

    def unrotated(grad):
        return grad * cosine[...] + turned(grad * sine[...])

    dv_out[...] = dv_sum[...].astype(bf16)
    dq = unrotated(dq_out[...])
    dk = unrotated(dk_sum[...] * scale)
    dq_out[...] = dq
    dk_out[...] = dk
    dq = dq * qraw[...]
    dk = dk * kraw[...]
    qg_out[...] = jnp.sum(dq * q_scale[...], axis=0, keepdims=True)
    kg_out[...] = jnp.sum(dk * k_scale[...], axis=0, keepdims=True)
    qdot_out[...] += jnp.sum(dq * q_gain[...], axis=1, keepdims=True)
    kdot_out[...] += jnp.sum(dk * k_gain[...], axis=1, keepdims=True)


def attend_back(query, key, value, out_grad, lse, qraw, kraw, q_scale, k_scale, q_gain, k_gain, cosine, sine, seg, keep):
    length, width = qraw.shape
    block = min(256, length)
    span = min(DOC + block, length)
    head = pl.BlockSpec((length, HEAD), lambda h: (0, h))
    gain = pl.BlockSpec((1, HEAD), lambda h: (0, h))
    whole = lambda *shape: pl.BlockSpec(shape, lambda h: (0, 0))
    sds = jax.ShapeDtypeStruct
    return pl.pallas_call(
        functools.partial(attend_back_kernel, block),
        grid=(width // HEAD,),
        in_specs=[head] * 7
        + [whole(length, 1), whole(length, 1), gain, gain]
        + [whole(length, HEAD), whole(length, HEAD), whole(length, 1), whole(1, length), whole(1, length)],
        out_specs=[head, head, head, whole(length, 1), whole(length, 1), gain, gain],
        out_shape=[sds((length, width), f32), sds((length, width), f32), sds((length, width), bf16)]
        + [sds((length, 1), f32), sds((length, 1), f32), sds((1, width), f32), sds((1, width), f32)],
        scratch_shapes=[pltpu.VMEM((length, span), f32), pltpu.VMEM((length, HEAD), f32), pltpu.VMEM((length, HEAD), f32)],
        compiler_params=params(),
        cost_estimate=cost(0, 0),
        name="attend_back",
    )(query, key, value, out_grad, lse, qraw, kraw, q_scale, k_scale, q_gain[None], k_gain[None], cosine, sine, seg[:, None], seg[None], keep[None])


def middle_kernel(tokens, summed, gain, middle_out, scale_out, normed_out):
    middle = tokens[...].astype(f32) + summed[...].astype(f32)
    scale = lax.rsqrt(jnp.mean(middle * middle, axis=1, keepdims=True) + EPSILON)
    middle_out[...] = middle
    scale_out[...] = scale
    normed_out[...] = (middle * scale * gain[...]).astype(bf16)


def middle_rows(chunk, tokens, summed, gain):
    rows, features = summed.shape
    sds = jax.ShapeDtypeStruct
    whole = lambda *shape: pl.BlockSpec(shape, lambda i: (0, 0))
    return pl.pallas_call(
        middle_kernel,
        grid=(1,),
        in_specs=[pl.BlockSpec((rows, features), lambda i: (chunk, 0)), whole(rows, features), whole(1, features)],
        out_specs=[whole(rows, features), whole(rows, 1), whole(rows, features)],
        out_shape=[sds((rows, features), f32), sds((rows, 1), f32), sds((rows, features), bf16)],
        compiler_params=params(),
        cost_estimate=cost(0, 0),
        name="middle",
    )(tokens, summed, gain[None])


def middle_back_kernel(
    experts, grads, middle, scale, normed, routed, router, cotangent, gain, *refs
):
    grad_out, low_out, gain_out, logit_out = refs[-4:]
    features = middle.shape[1]
    lane = lax.broadcasted_iota(jnp.int32, routed.shape, 1)
    logits = jnp.where(lane < experts, nn(normed[...], router[...]), MASKED)
    powers = jnp.exp(logits - jnp.max(logits, axis=1, keepdims=True))
    probs = powers / jnp.sum(powers, axis=1, keepdims=True)
    share_grad = grads[:, features:].astype(f32) * routed[...]
    logit_grad = (probs * (share_grad - jnp.sum(share_grad * probs, axis=1, keepdims=True))).astype(bf16)
    logit_out[...] = logit_grad
    ffn_grad = grads[:, :features].astype(f32) + nt(logit_grad, router[...])
    along = middle[...] * scale[...]
    gain_out[...] = jnp.sum(ffn_grad * along, axis=0, keepdims=True)
    weighted = ffn_grad * gain[...]
    inner = jnp.mean(weighted * along, axis=1, keepdims=True)
    total = cotangent[...].astype(f32) + scale[...] * (weighted - along * inner)
    grad_out[...] = total
    low_out[...] = total.astype(bf16)


def middle_back(chunk, grads, middle, scale, normed, routed, router, cotangent, gain, experts, filled=()):
    rows, features = middle.shape
    sds = jax.ShapeDtypeStruct
    whole = lambda *shape: pl.BlockSpec(shape, lambda i: (0, 0))
    part = lambda columns: pl.BlockSpec((rows, columns), lambda i: (chunk, 0))
    return pl.pallas_call(
        functools.partial(middle_back_kernel, experts),
        grid=(1,),
        in_specs=[whole(rows, features + LANES), whole(rows, features), whole(rows, 1), whole(rows, features), part(LANES)]
        + [whole(features, LANES), part(features), whole(1, features)]
        + [pl.BlockSpec(memory_space=pl.ANY)] * len(filled),
        out_specs=[part(features), part(features), whole(1, features), whole(rows, LANES)],
        out_shape=[sds(cotangent.shape, f32), sds(cotangent.shape, bf16), sds((1, features), f32), sds((rows, LANES), bf16)],
        input_output_aliases={8 + at: at for at in range(len(filled))},
        compiler_params=params(),
        cost_estimate=cost(0, 0),
        name="middle_back",
    )(grads, middle, scale, normed, routed, router, cotangent, gain[None], *filled)


def up_back_kernel(grad, down_w, out):
    width = down_w.shape[2]
    for at in range(down_w.shape[0]):
        out[:, at * width : (at + 1) * width] = nn(grad[...], down_w[at]).astype(out.dtype)


def up_back(grad, down_w):
    rows, features = grad.shape
    experts, _, width = down_w.shape
    step = 2 if experts % 2 == 0 else 1
    return pl.pallas_call(
        up_back_kernel,
        grid=(experts // step,),
        in_specs=[pl.BlockSpec((rows, features), lambda e: (0, 0)), pl.BlockSpec((step, features, width), lambda e: (e, 0, 0))],
        out_specs=pl.BlockSpec((rows, step * width), lambda e: (0, e)),
        out_shape=jax.ShapeDtypeStruct((rows, experts * width), bf16),
        compiler_params=params(),
        cost_estimate=cost(2 * rows * features * experts * width, 2 * (rows + experts * width) * features),
        name="up_back",
    )(grad, down_w)


def expert_kernel(block, rows_in, back, routed, router, gate_w, up_w, act_out, dgate_out, dup_out, grad_out, comb, dcomb, total):
    at = pl.program_id(0)
    rows, features = rows_in.shape
    lane = lax.broadcasted_iota(jnp.int32, (block, LANES), 1)

    @pl.when(at == 0)
    def _():
        experts = pl.num_programs(0)
        for start in range(0, rows, block):
            here = slice(start, start + block)
            logits = jnp.where(lane < experts, nn(rows_in[here, :], router[...]), MASKED)
            powers = jnp.exp(logits - jnp.max(logits, axis=1, keepdims=True))
            probs = powers / jnp.sum(powers, axis=1, keepdims=True)
            comb[here, :] = probs * routed[here, :]
        total[...] = jnp.zeros_like(total)
        dcomb[...] = jnp.zeros_like(dcomb)

    gate, up = gate_w[0], up_w[0]
    mine = lane == at
    for start in range(0, rows, block):
        here = slice(start, start + block)
        taken = rows_in[here, :]
        pre_gate = nn(taken, gate)
        pre_up = nn(taken, up)
        behind = back[...].reshape(rows, back.shape[3])[here, :].astype(f32)
        share = jnp.sum(jnp.where(mine, comb[here, :], 0.0), axis=1, keepdims=True)
        sigmoid = 0.5 * jnp.tanh(0.5 * pre_gate) + 0.5
        active = pre_gate * sigmoid
        inner = active * pre_up
        share_grad = jnp.sum(inner * behind, axis=1, keepdims=True)
        dcomb[here, :] = jnp.where(mine, share_grad, dcomb[here, :])
        act_out[here, :] = (inner * share).astype(bf16)
        inner_grad = behind * share
        dgate = (inner_grad * pre_up * (sigmoid + active * (1.0 - sigmoid))).astype(bf16)
        dup = (inner_grad * active).astype(bf16)
        dgate_out[here, :] = dgate
        dup_out[here, :] = dup
        total[here, :] += nt(dgate, gate) + nt(dup, up)

    @pl.when(at == pl.num_programs(0) - 1)
    def _():
        grad_out[:, :features] = total[...].astype(bf16)
        grad_out[:, features:] = dcomb[...].astype(bf16)


def experts_block(chunk, rows_in, back, routed, router, gate_w, up_w):
    rows, features = rows_in.shape
    parts, _, chunk_rows, _ = back.shape
    experts, _, width = gate_w.shape
    block = min(512, rows)
    whole = lambda *shape: pl.BlockSpec(shape, lambda e: (0, 0))
    column = pl.BlockSpec((rows, width), lambda e: (0, e))
    weight = pl.BlockSpec((1, features, width), lambda e: (e, 0, 0))
    wide = jax.ShapeDtypeStruct((rows, experts * width), bf16)
    return pl.pallas_call(
        functools.partial(expert_kernel, block),
        grid=(experts,),
        in_specs=[whole(rows, features), pl.BlockSpec((parts, 1, chunk_rows, width), lambda e: (0, chunk, 0, e)), whole(rows, LANES), whole(features, LANES), weight, weight],
        out_specs=[column, column, column, whole(rows, features + LANES)],
        out_shape=[wide, wide, wide, jax.ShapeDtypeStruct((rows, features + LANES), bf16)],
        scratch_shapes=[pltpu.VMEM((rows, LANES), f32), pltpu.VMEM((rows, LANES), f32), pltpu.VMEM((rows, features), f32)],
        compiler_params=params(),
        cost_estimate=cost(8 * rows * features * experts * width, 4 * experts * width * (features + 2 * rows), rows * experts * width),
        name="experts",
    )(rows_in, back, routed, router, gate_w, up_w)


def block_order(blocks):
    return [3, 2, 0, 1] if blocks == 4 else list(range(blocks))


def split_tables(blocks, per):
    order = block_order(blocks)
    if blocks == 4:
        picks = [{0: 0, 1: 1}, {2: 0, 3: 1}, {0: 0, 2: 1}, {1: 0, 3: 1}]
    else:
        picks = [{block: block for block in order}] * 2
    places, fills = [], []
    for pick in picks:
        filled = [pick[block] * per + at if block in pick else None for block in order for at in range(per)]
        last = next(place for place in filled if place is not None)
        row = []
        for place in filled:
            last = last if place is None else place
            row.append(last)
        places.append(row)
        fills.append([int(place is not None) for place in filled])
    return jnp.asarray(np.array([places, fills], np.int32)), [len(pick) for pick in picks]


def wgrad_kernel(count, extra, per, block, order, tables, *refs):
    lefts, rights = refs[:count], refs[count : 2 * count]
    added = refs[2 * count : 2 * count + extra]
    outs = refs[2 * count + extra :]
    at = pl.program_id(0)
    features = lefts[0].shape[-1]
    width = outs[0].shape[2]

    def piece(start, stop):
        total = None
        for left, right in zip(lefts, rights):
            columns = left[:, start:stop] if len(left.shape) == 2 else left[:, :, :, start:stop].reshape(-1, stop - start)
            part = tn(columns, right[...])
            total = part if total is None else total + part
        return total

    if not added:
        for place, out in enumerate(outs):

            @pl.when(at // per == place)
            def _(out=out):
                for start in range(0, features, block):
                    total = piece(start, start + block).astype(bf16)
                    for entry in range(out.shape[0]):
                        out[entry, start : start + block, :] = total[:, entry * width : (entry + 1) * width]

        return
    half = features // 2
    got = outs[-1]
    outs = outs[:-1]
    for place, arrived in enumerate(added):

        @pl.when(at // per == place)
        def _(arrived=arrived):
            for start in range(0, features, block):
                total = piece(start, start + block)
                for entry in range(got.shape[0]):
                    part = total[:, entry * width : (entry + 1) * width]
                    got[entry, start : start + block, :] = (part + arrived[entry, start : start + block, :].astype(f32)).astype(bf16)

    for side, out in enumerate(outs):
        start = side * 2 // len(outs) * half

        @pl.when(tables[1, side, at] == 1)
        def _(out=out, start=start):
            out[...] = got[:, start : start + half, :]


def wgrad(lefts, rights, order, width, per, added=(), weight=1, pieces=0):
    features = lefts[0][0].shape[-1]
    groups = order.shape[0]
    experts = groups * per
    tables, sizes = split_tables(groups, 1)
    pieces = len(added) or pieces or groups
    held = groups // pieces

    def piece_spec(place):
        return pl.BlockSpec((per, features, width), lambda i, ids, to: (jnp.clip(i - place * held, 0, held - 1), 0, 0))

    def half_spec(side):
        return pl.BlockSpec((per, features // 2, width), lambda i, ids, to: (to[0, side, i], 0, 0))

    def left_spec(left, chunk):
        if left.ndim == 2:
            return pl.BlockSpec(left.shape, lambda i, ids, to: (0, 0))
        return pl.BlockSpec((left.shape[0], 1) + left.shape[2:], lambda i, ids, to: (0, chunk, 0, 0))

    piece_specs = [piece_spec(place) for place in range(pieces)]
    if added:
        out_specs = [half_spec(side) for side in range(len(sizes))]
        out_shape = [jax.ShapeDtypeStruct((size * per, features // 2, width), bf16) for size in sizes]
    else:
        out_specs = piece_specs
        out_shape = [jax.ShapeDtypeStruct((held * per, features, width), bf16)] * pieces
    return pl.pallas_call(
        functools.partial(wgrad_kernel, len(lefts), len(added), held, min(512, features // 2)),
        grid_spec=pltpu.PrefetchScalarGridSpec(
            num_scalar_prefetch=2,
            grid=(groups,),
            in_specs=[left_spec(*left) for left in lefts]
            + [pl.BlockSpec((right.shape[0], per * width), lambda i, ids, to: (0, ids[i])) for right in rights]
            + (piece_specs if added else []),
            out_specs=out_specs,
            scratch_shapes=[pltpu.VMEM((per, features, width), bf16)] if added else [],
        ),
        out_shape=out_shape,
        compiler_params=params(),
        cost_estimate=cost(2 * weight * sum(right.shape[0] for right in rights) * features * experts * width, 0),
        name="wgrad",
    )(order, tables, *(left for left, _ in lefts), *rights, *added)


def down_kernel(parts, down_w, *refs):
    acts, out = refs[:-1], refs[-1]
    joined = jnp.concatenate([down_w[e] for e in range(down_w.shape[0])], axis=1)
    block = acts[0].shape[0] // parts
    for at, act in enumerate(acts):
        result = nt(act[...], joined).astype(out.dtype)
        for part in range(parts):
            start = (part * len(acts) + at) * block
            out[start : start + block, :] = result[part * block : (part + 1) * block, :]


def down(acts, down_w, parts):
    rows = sum(act.shape[0] for act in acts)
    experts, features, width = down_w.shape
    block = min(256, features)
    return pl.pallas_call(
        functools.partial(down_kernel, parts),
        grid=(features // block,),
        in_specs=[pl.BlockSpec((experts, block, width), lambda n: (0, n, 0))]
        + [pl.BlockSpec(act.shape, lambda n: (0, 0)) for act in acts],
        out_specs=pl.BlockSpec((rows, block), lambda n: (0, n)),
        out_shape=jax.ShapeDtypeStruct((rows, features), bf16),
        compiler_params=params(),
        cost_estimate=cost(0 * 2 * rows * features * experts * width, 0),
        name="down",
    )(down_w, *acts)


def gate(value, *others):
    return lax.optimization_barrier((value, others))[0]


def gather_rows(values):
    return lax.all_gather(values, "tensor", axis=0, tiled=True)


def scatter_rows(values):
    return lax.psum_scatter(values, "tensor", scatter_dimension=0, tiled=True)


def pair_swap(values, step):
    size = lax.axis_size("dp")
    return lax.ppermute(values, "dp", [(i, i ^ step) for i in range(size)])


class Halving:
    def __init__(self, values):
        if len(values) == 2:
            self.kept = list(values)
            self.going = None
        else:
            self.kept, self.going = list(values[::2]), list(values[1::2])
        bits = list(range(values[0].shape[0].bit_length() - (1 if self.going is None else 0)))
        self.left = [bits[::-1], bits]
        self.got = None

    def send(self):
        if not self.left[0]:
            return ()
        self.got = []
        sent = []
        for side, downward in ((0, True), (1, False)):
            bit = self.left[side].pop(0)
            if self.going is not None:
                go = self.going[side]
            else:
                kept = self.kept[side]
                half = kept.shape[0] // 2
                if downward:
                    self.kept[side], go = kept[:half], kept[half:]
                else:
                    view = kept.reshape((half, 2) + kept.shape[1:])
                    self.kept[side], go = view[:, 0], view[:, 1]
            sent.append(go)
            self.got.append(pair_swap(go, 2 << bit))
        self.going = None
        return tuple(sent)

    def add(self, *others):
        if self.got is not None:
            if others:
                self.got = gate(tuple(self.got), *others)
            last = not self.left[0]
            for side in range(2):
                total = self.kept[side].astype(f32) + self.got[side].astype(f32)
                self.kept[side] = total if last else total.astype(bf16)
            self.got = None
        return tuple(self.kept)

    def done(self):
        self.add()
        while self.left[0]:
            self.send()
            self.add()
        return jnp.concatenate([kept[0].astype(f32) for kept in self.kept], axis=1)


def exchange_sum(values, steps):
    for axis, step in steps:
        values = values + lax.ppermute(values, axis, [(i, i ^ step) for i in range(lax.axis_size(axis))])
    return values


def doublings(axis):
    return [(axis, 1 << bit) for bit in range(lax.axis_size(axis).bit_length() - 1)]


def local(
    tokens, cotangent, seg_ids, keep_mask, routes, attn_gain, w_query, w_key, w_value, w_out,
    q_gain, k_gain, ffn_gain, router, w_gate, w_up, w_down,
):
    parts = lax.axis_size("tensor")
    part_at = lax.axis_index("tensor")
    dp_size = lax.axis_size("dp")
    low_bit = lax.axis_index("dp") % 2
    shard_rows, features = tokens.shape
    group_rows = shard_rows * parts
    _, length = seg_ids.shape
    local_width = w_query.shape[1]
    experts, _, width = w_gate.shape
    per = experts // dp_size
    chunk_rows = shard_rows // CHUNKS
    chunks = range(CHUNKS)
    own = [slice(c * chunk_rows, (c + 1) * chunk_rows) for c in chunks]

    def chunk_of(values, c):
        columns = values.shape[1]
        return values.reshape(parts, CHUNKS, chunk_rows, columns)[:, c].reshape(parts * chunk_rows, columns)

    inputs = tokens.astype(f32)
    first_scale = rms_scale(inputs)
    normed_all = gather_rows((inputs * first_scale * attn_gain).astype(bf16))
    grad_rows = gather_rows(gate(cotangent, normed_all))

    cosine, sine = rope_tables(length, HEAD)

    relative = jnp.asarray(block_order(dp_size // 2), jnp.int32) ^ (lax.axis_index("dp") // 2)
    own_blocks, other_blocks = 2 * relative + low_bit, 2 * relative + 1 - low_bit
    mine, theirs = own_blocks, other_blocks

    qraw, kraw, value, squares = project(normed_all, w_query, w_key, w_value)
    squares = exchange_sum(squares, doublings("tensor"))
    q_scale, k_scale = (lax.rsqrt(squares[i] / features + EPSILON)[:, None] for i in range(2))
    query, key, attended, lse = attend(
        qraw, kraw, value, q_scale, k_scale, q_gain, k_gain, cosine, sine, seg_ids[0], keep_mask[0]
    )
    attended_parts = [chunk_of(attended, c) for c in chunks]
    outs = [nt(attended_parts[0], w_out).astype(bf16)]
    summed = [scatter_rows(gate(outs[0], grad_rows))]
    outs.append(nt(gate(attended_parts[1], outs[0]), w_out).astype(bf16))
    summed.append(scatter_rows(gate(outs[1], grad_rows)))

    idle_routes, idle_router = gate((routes, router), outs[1])
    expert_ids = jnp.arange(LANES)
    routed = jnp.sum((idle_routes[:, :, None] == expert_ids[None, None, :]).astype(f32), axis=1)
    router_wide = jnp.pad(idle_router, ((0, 0), (0, LANES - experts)))
    routed_own = lax.dynamic_slice_in_dim(routed, part_at * shard_rows, shard_rows, 0)
    back = up_back(gate(grad_rows, routed, router_wide), w_down).reshape(parts, CHUNKS, chunk_rows, -1)
    grad_rows = grad_rows.reshape(parts, CHUNKS, chunk_rows, features)
    grad_parts = [(grad_rows, c) for c in chunks]

    norms = [middle_rows(0, tokens, summed[0], ffn_gain)]
    ffn_all = [gather_rows(norms[0][2])]
    norms.append(middle_rows(1, tokens, gate(summed[1], norms[0][2], back), ffn_gain))
    ffn_all.append(gather_rows(norms[1][2]))
    ffn_parts = [(rows, 0) for rows in ffn_all]
    acts, dgates, dups, expert_grads = [], [], [], []
    for c in chunks:
        here = gate(chunk_of(routed, c), back, *acts[-1:])
        act, dgate, dup, grads = experts_block(c, ffn_all[c], back, here, router_wide, w_gate, w_up)
        acts.append(act)
        dgates.append(dgate)
        dups.append(dup)
        expert_grads.append(grads)
    expert_grads = [scatter_rows(grads) for grads in expert_grads]

    def back_of(c, grads, filled=()):
        return middle_back(c, grads, *norms[c], routed_own, router_wide, cotangent, ffn_gain, experts, filled)

    def expert_sums(lefts, rights, ids, *others, added=(), weight=1, pieces=0):
        return wgrad(lefts, rights, gate(ids, *others), width, per, added, weight, pieces)

    def core_swap(pieces):
        return [pair_swap(piece, 1) for piece in pieces]

    def halving(sums):
        return Halving([part.reshape((part.shape[0] // per, per) + part.shape[1:]) for part in sums])

    first = back_of(0, gate(expert_grads[0], acts[1]))
    gate_sent = expert_sums(ffn_parts, dgates, theirs, first[1], weight=0)
    gate_got = core_swap(gate_sent)
    up_sent = expert_sums(ffn_parts, dups, theirs, *gate_sent, pieces=2, weight=4)
    up_got = core_swap(up_sent)
    gate_sums = expert_sums(ffn_parts, dgates, mine, *up_sent, added=gate_got, weight=4)
    gate_out = halving(gate_sums)
    gate_out.send()
    second = back_of(1, gate(expert_grads[1], *gate_sums), first[:2])
    middle_grad, middle_low = second[:2]
    middle_all = gather_rows(middle_low)
    moe = down([gate(acts[0], middle_low), acts[1]], w_down, parts)
    up_sums = expert_sums(ffn_parts, dups, mine, moe, added=up_got, weight=0)
    up_out = halving(up_sums)
    up_out.send()
    moe_sum = scatter_rows(moe)
    gate_late = gate_out.add(*up_sums)
    gate_out.send()
    down_sent = expert_sums(grad_parts, acts, theirs, *gate_late, pieces=2, weight=0.0)
    down_got = core_swap(down_sent)
    attended_grad = nn(gate(middle_all, *down_sent), w_out).astype(bf16)
    dqn, dkn, dvalue, qdot, kdot, q_gain_part, k_gain_part = attend_back(
        query, key, value, attended_grad, lse, qraw, kraw, q_scale, k_scale, q_gain, k_gain, cosine, sine,
        seg_ids[0], keep_mask[0],
    )
    dots = exchange_sum(jnp.stack([qdot[:, 0], kdot[:, 0]]), doublings("tensor")) / features
    up_late = up_out.add(dqn)
    up_out.send()
    normed_part, dqraw, dkraw, attn_gain_part = project_back(
        normed_all, dqn, dkn, dvalue, qraw, kraw, q_scale, k_scale, dots[0][:, None], dots[1][:, None],
        gate(q_gain, *up_late, *gate_out.got), k_gain, w_query, w_key, w_value,
    )
    normed_grad = scatter_rows(normed_part)
    down_sums = expert_sums(grad_parts, acts, mine, normed_part, *up_out.got, added=down_got, weight=0.0)
    down_out = halving(down_sums)
    down_out.send()
    def attention_sums(ids, *others, added=()):
        return attention_wgrad(
            normed_all, middle_all, (dqraw, dkraw, dvalue), attended, gate(ids, *others), dp_size, added
        )

    attn_sent = attention_sums(other_blocks, *down_sums)
    attn_got = core_swap(attn_sent)
    down_late = down_out.add(*attn_sent)
    down_out.send()

    def placed(part):
        return lax.dynamic_update_slice_in_dim(jnp.zeros((features,), f32), part, part_at * local_width, 0)

    attn_sums = attention_sums(own_blocks, *down_late, added=attn_got)
    attn_out = Halving(attn_sums)
    normed_grad = gate(normed_grad, *attn_out.send())
    smalls = [attn_gain_part[0] / attn_gain, placed(q_gain_part[0]), placed(k_gain_part[0]), (first[2] + second[2])[0]]
    router_part = sum(tn(late[3], norms[c][2]) for c, late in enumerate((first, second)))[:experts]
    smalls = gate(jnp.concatenate([jnp.stack(smalls), router_part]), *attn_sums)
    smalls = exchange_sum(smalls, doublings("dp")[:1] + doublings("tensor"))
    attn_late = attn_out.add()
    attn_out.send()
    smalls = exchange_sum(gate(smalls, *attn_late), doublings("dp")[1:])
    late_got = tuple(down_out.got)
    gate_done = gate_out.done()
    up_done = up_out.done()
    down_done = down_out.done()
    query_done, key_done, value_done, out_done = attn_out.done()
    layer_out = (jnp.concatenate([norms[c][0] for c in chunks]) + gate(moe_sum, *late_got).astype(f32)).astype(bf16)
    tokens_grad = middle_grad + norm_back(normed_grad.astype(f32), inputs, first_scale, attn_gain)
    return (
        layer_out, tokens_grad, query_done, key_done, value_done, out_done,
        smalls[0], smalls[1], smalls[2], smalls[3], smalls[4:].T, gate_done, up_done, down_done,
    )


def solution(mesh):
    rows = P(("dp", "tensor"), None)
    column = P(None, "tensor")
    expert = P(None, None, "tensor")
    in_specs = (
        rows, rows, P("dp", None), P("dp", None), P("dp", None), P(), column, column, column, column,
        P("tensor"), P("tensor"), P(), P(), expert, expert, expert,
    )
    block = P("dp", "tensor")
    expert_out = P("dp", None, "tensor")
    out_specs = (
        rows, rows, block, block, block, block, P(), P(), P(), P(), P(), expert_out, expert_out, expert_out,
    )
    return jax.shard_map(local, mesh=mesh, in_specs=in_specs, out_specs=out_specs, check_vma=False)
```
